32 devices in a mesh: seq: 8 (over y, x, core), tp: 4 (over z).
Axes of the slice: x: 2, y: 2, z: 4, core: 2. Of those that a mesh axis runs over, the one named last changes fastest.
Arguments:
- projected: bfloat16 [18560, 8192], P(('tp', 'seq')), may hold values from -4 to 53
- conv_weight: float32 [4, 8, 1280], P(None, 'tp'), may hold values from -3 to 3
- dt_bias: float32 [128], P('tp'), may hold values from -7 to -1
- a_log: float32 [128], P('tp'), may hold values from -7 to -1
- d_skip: float32 [128], P('tp'), may hold values from 0.5 to 2
- norm_gain: float32 [8192], P('tp'), may hold values from 0.25 to 1.75
Outputs:
- mixer_out: bfloat16 [8192, 8192], P('seq', 'tp')
The draws below stay inside these ranges and needn't reach their ends.
All inputs are finite; a program needn't handle non-finite values.
Results may differ from the reference program's by a relative error of at most 0.0034.
Values may be sent and summed in bfloat16 or wider, within the bound.
No kernel may reach another device: no remote copies, remote signals or barrier semaphores. Data moves between devices by JAX's collectives and lax.ppermute only.
A program may use at most 192 MiB of HBM per device.

```python
import math
import jax
import jax.numpy as jnp
from jax import lax

HEADS = 128
HEAD_DIM = 64
STATE_WIDTH = 128
GROUPS = 8
CONV_TAPS = 4
BLOCK = 256
TOK_DEV = 1024
CONVCH = 1280
INNER = 8192
PROMPT_TOKENS = 8192


def head_kinds(key, fast_share):
    return jax.random.uniform(key, (HEADS,)) < fast_share


def draw_projected(key, part):
    key = jax.random.fold_in(key, 7)
    random_splitkeys = jax.random.split(key, 4)
    heads_group = HEADS // GROUPS
    group_span_width = heads_group * HEAD_DIM
    group_cols = 2 * group_span_width + 2 * STATE_WIDTH + heads_group
    base_draw = jax.random.normal(random_splitkeys[0], (PROMPT_TOKENS, GROUPS, group_cols))
    base_draw = jnp.clip(base_draw, -4.0, 4.0)
    column_entry = jnp.arange(group_cols)
    column_scale = jnp.where(column_entry < 2 * group_span_width, 1.0, 0.5)
    value_rows = base_draw * column_scale[None, None, :]
    regions = PROMPT_TOKENS // TOK_DEV
    offsets = jax.random.uniform(random_splitkeys[2], (regions,), minval=-0.7, maxval=0.35)
    token_position = jnp.arange(PROMPT_TOKENS)
    segment_offset = offsets[token_position // TOK_DEV]
    spike_position = jax.random.randint(random_splitkeys[3], (2,), CONV_TAPS - 1, PROMPT_TOKENS)
    inside_spike = jnp.any(token_position[:, None] == spike_position[None, :], axis=1)
    beside_spike = jnp.any((token_position[:, None] <= spike_position[None, :]) & (token_position[:, None] >= spike_position[None, :] - (CONV_TAPS - 1)), axis=1)
    spike_height = math.floor(math.sqrt(PROMPT_TOKENS) / 2) + 8.0
    is_step = column_entry >= group_cols - heads_group
    carries_state = (column_entry >= group_span_width) & (column_entry < 2 * group_span_width + STATE_WIDTH)
    increment_values = jnp.where(inside_spike[:, None, None], spike_height, segment_offset[:, None, None] + value_rows)
    value_rows = jnp.where(is_step[None, None, :], increment_values, value_rows)
    value_rows = jnp.where(beside_spike[:, None, None] & carries_state[None, None, :], value_rows * 0.001, value_rows)
    return jnp.transpose(value_rows.reshape(PROMPT_TOKENS, GROUPS * group_cols)).astype(jnp.bfloat16)


def draw_dt_bias(key, part):
    fast_share = 0.5
    fast_heads = head_kinds(key, fast_share)
    key = jax.random.fold_in(key, 3)
    random_splitkeys = jax.random.split(key, 4)
    slow_bias = jnp.log(jax.random.uniform(random_splitkeys[0], (HEADS,), minval=0.5, maxval=1.0)) - 0.5 * math.log(PROMPT_TOKENS)
    short_bias = jax.random.uniform(random_splitkeys[1], (HEADS,), minval=-2.2, maxval=-1.4)
    small_bias = jax.random.uniform(random_splitkeys[3], (HEADS,), minval=-7.0, maxval=-6.0)
    small_steps = jax.random.uniform(random_splitkeys[2], (HEADS,)) < 0.5
    fast_bias = jnp.where(small_steps, small_bias, short_bias)
    return jnp.where(fast_heads, fast_bias, slow_bias).astype(jnp.float32)


def draw_a_log(key, part):
    fast_share = 0.5
    fast_heads = head_kinds(key, fast_share)
    key = jax.random.fold_in(key, 5)
    random_splitkeys = jax.random.split(key, 2)
    slow_rate = jnp.log(jax.random.uniform(random_splitkeys[0], (HEADS,), minval=0.5, maxval=1.0)) - 0.5 * math.log(PROMPT_TOKENS)
    fast_rate = jax.random.uniform(random_splitkeys[1], (HEADS,), minval=math.log(0.1), maxval=math.log(0.25))
    return jnp.where(fast_heads, fast_rate, slow_rate).astype(jnp.float32)


def levels(own_key, dims, shards, low, largest):
    factor_of, own = 1.0, jax.random.fold_in(own_key, 6)
    for dim, parts in shards:
        heights = jnp.exp(jax.random.uniform(jax.random.fold_in(own, dim), (parts,), jnp.float32, low / len(shards), largest / len(shards)))
        factor_of = factor_of * jnp.repeat(heights, dims[dim] // parts).reshape([-1 if axis == dim else 1 for axis in range(len(dims))])
    return factor_of


def bell_draw(rng, shape, width, most, cuts=(), dtype=jnp.bfloat16):
    level = levels(rng, shape, cuts, -0.22, 0.18) if cuts else 1.0
    entries = jax.random.normal(rng, shape, jnp.float32) * width * level
    return jnp.minimum(jnp.maximum(entries, -most), most).astype(dtype)


def setup_inputs(seed: int = 0) -> dict:
    key_of = jax.random.split(jax.random.key(seed), 7)
    return {
        "projected": draw_projected(jax.random.fold_in(key_of[6], 71), 0),
        "conv_weight": bell_draw(key_of[1], (CONV_TAPS, GROUPS, CONVCH), CONV_TAPS ** -0.5, 3.0, ((1, 4),), jnp.float32),
        "dt_bias": draw_dt_bias(jax.random.fold_in(key_of[6], 71), 0),
        "a_log": draw_a_log(jax.random.fold_in(key_of[6], 71), 0),
        "d_skip": jnp.clip(0.5 + 1.5 * jax.random.uniform(key_of[4], (HEADS,), jnp.float32) ** levels(key_of[4], (HEADS,), ((0, 4),), -0.2, 0.2), 0.5, 2.0),
        "norm_gain": jnp.clip(1.0 + 0.15 * jax.random.normal(key_of[5], (INNER,), jnp.float32), 0.25, 1.75),
    }


epsilon = 1e-05

def block_step(state_now, pieces):
    block_values, block_input, block_output, block_decay, block_steps = pieces
    f32 = jnp.float32
    running = jnp.cumsum(block_decay, axis=0)
    length = running.shape[0]
    scores = jnp.einsum('tgn,sgn->gts', block_output.astype(f32), block_input.astype(f32), precision=lax.Precision.HIGHEST)
    running_heads = jnp.transpose(running, (1, 2, 0))
    log_gaps = running_heads[:, :, :, None] - running_heads[:, :, None, :]
    row_index = lax.broadcasted_iota(jnp.int32, (length, length), 0)
    col_index = lax.broadcasted_iota(jnp.int32, (length, length), 1)
    decays = jnp.exp(jnp.where(row_index >= col_index, log_gaps, -jnp.inf))
    weights = (scores[:, None] * decays * jnp.transpose(block_steps, (1, 2, 0))[:, :, None, :]).astype(jnp.bfloat16)
    intra_part = jnp.einsum('gjts,sgjp->tgjp', weights.astype(f32), block_values.astype(f32), precision=lax.Precision.HIGHEST)
    carried = jnp.exp(running)[..., None] * jnp.einsum('tgn,gjpn->tgjp', block_output.astype(f32), state_now, precision=lax.Precision.HIGHEST)
    block_end = running[-1]
    carry_scale = jnp.exp(block_end[None] - running) * block_steps
    weighted = (block_values.astype(f32) * carry_scale[..., None]).astype(jnp.bfloat16)
    update = jnp.einsum('sgjp,sgn->gjpn', weighted.astype(f32), block_input.astype(f32), precision=lax.Precision.HIGHEST)
    advanced = jnp.exp(block_end)[..., None, None] * state_now + update
    return (advanced, intra_part + carried)

def reference(projected, conv_weight, dt_bias, a_log, d_skip, norm_gain):
    f32 = jnp.float32
    token_count = projected.shape[1]
    heads_group = HEADS // GROUPS
    group_span_width = heads_group * HEAD_DIM
    conv_channels = group_span_width + 2 * STATE_WIDTH
    columns = jnp.transpose(projected).reshape(token_count, GROUPS, -1)
    gate_part = columns[:, :, :group_span_width]
    conv_input = columns[:, :, group_span_width:group_span_width + conv_channels].astype(f32)
    step_raw = columns[:, :, group_span_width + conv_channels:].astype(f32)
    padded = jnp.concatenate([jnp.zeros((CONV_TAPS - 1, GROUPS, conv_channels), f32), conv_input], axis=0)
    summed = conv_weight[0] * padded[0:token_count]
    for tap_index in range(1, CONV_TAPS):
        summed = summed + conv_weight[tap_index] * padded[tap_index:tap_index + token_count]
    activated = jax.nn.silu(summed).astype(jnp.bfloat16)
    head_values = activated[:, :, :group_span_width].reshape(token_count, GROUPS, heads_group, HEAD_DIM)
    input_map = activated[:, :, group_span_width:group_span_width + STATE_WIDTH]
    output_map = activated[:, :, group_span_width + STATE_WIDTH:]
    step_size = jax.nn.softplus(step_raw + dt_bias.reshape(GROUPS, heads_group))
    log_decay = -jnp.exp(a_log).reshape(GROUPS, heads_group) * step_size
    block_count = token_count // BLOCK

    def to_blocks(tensor):
        return tensor.reshape((block_count, BLOCK) + tensor.shape[1:])
    zero_state = jnp.zeros((GROUPS, heads_group, HEAD_DIM, STATE_WIDTH), f32)
    _, block_outputs = lax.scan(block_step, zero_state, (to_blocks(head_values), to_blocks(input_map), to_blocks(output_map), to_blocks(log_decay), to_blocks(step_size)))
    mixed_out = block_outputs.reshape(token_count, GROUPS, heads_group, HEAD_DIM) + d_skip.reshape(GROUPS, heads_group)[:, :, None] * head_values.astype(f32)
    gated_out = mixed_out.reshape(token_count, GROUPS, group_span_width) * jax.nn.silu(gate_part.astype(f32))
    mean_square = lax.optimization_barrier(jnp.mean(gated_out * gated_out, axis=-1, keepdims=True))
    normed = gated_out * lax.rsqrt(mean_square + epsilon) * norm_gain.reshape(GROUPS, group_span_width)
    return normed.reshape(token_count, GROUPS * group_span_width).astype(jnp.bfloat16)
```

```python
import functools

import jax
import jax.numpy as jnp
from jax import lax
from jax.experimental import pallas as pl
from jax.experimental.pallas import tpu as pltpu
from jax.sharding import PartitionSpec as P

HEAD_DIM = 64
STATE_WIDTH = 128
BLOCK = 256
LANES = 128
HALF = BLOCK // 2
LOG2E = 1.4426950408889634
CAP = 80.0
EPSILON = 1e-05

f32 = jnp.float32
bf16 = jnp.bfloat16
NT = (((1,), (1,)), ((), ()))


def params(mib=48):
    return pltpu.CompilerParams(vmem_limit_bytes=mib * 2**20)


def silu(v):
    return v / (1.0 + jnp.exp(-v))


def softplus(v):
    e = jnp.exp(-jnp.abs(v))
    u = 1.0 + e
    gap = u - 1.0
    tiny = gap == 0.0
    log_part = jnp.where(tiny, e, jnp.log(u) * (e / jnp.where(tiny, 1.0, gap)))
    return jnp.maximum(v, 0.0) + log_part


def cut_kernel(src, dst):
    dst[0] = src[...]


def cut_chunk(projected, seq_count, chunk, chunks):
    rows = projected.shape[0]
    return pl.pallas_call(
        cut_kernel,
        grid=(seq_count,),
        in_specs=[pl.BlockSpec((rows, BLOCK), lambda d: (0, d * chunks + chunk))],
        out_specs=pl.BlockSpec((1, rows, BLOCK), lambda d: (d, 0, 0)),
        out_shape=jax.ShapeDtypeStruct((seq_count, rows, BLOCK), bf16),
        compiler_params=params(16),
        name="cut_chunk",
    )(projected)


def rim_kernel(src, dst):
    row = lax.broadcasted_iota(jnp.int32, (8, LANES), 0)
    col = lax.broadcasted_iota(jnp.int32, (8, LANES), 1)
    pick = jnp.where((col == row + LANES - 8) & (pl.program_id(0) > 0), 1.0, 0.0)
    dst[0] = lax.dot_general(pick.astype(bf16), src[...], NT, preferred_element_type=f32).astype(bf16)


def cut_rims(projected, seq_count, local_tokens):
    rows = projected.shape[0]
    per = local_tokens // LANES
    return pl.pallas_call(
        rim_kernel,
        grid=(seq_count,),
        in_specs=[pl.BlockSpec((rows, LANES), lambda d: (0, jnp.maximum(d * per - 1, 0)))],
        out_specs=pl.BlockSpec((1, 8, rows), lambda d: (d, 0, 0)),
        out_shape=jax.ShapeDtypeStruct((seq_count, 8, rows), bf16),
        compiler_params=params(16),
        name="cut_rims",
    )(projected)


def conv_kernel(dims, last, recv, tail_in, w, bias, a_log, state_in, lead_in, *refs):
    spg, rows, heads, span, piece_heads = dims
    refs = refs[-13:]
    xact, bmap, cmap, run_out, dt_out, tail, state_out, lead_out = refs[:8]
    gate_all, cum_all, c_all = refs[8:11]
    raw, xw = refs[11:]
    conv_rows = span + 2 * STATE_WIDTH

    for s in range(spg):
        raw[rows * s : rows * (s + 1), LANES:] = recv[s].astype(f32)
    raw[span : span + conv_rows, :LANES] = tail_in[0].astype(f32)

    dt = softplus(raw[span + conv_rows :, LANES:] + bias[0])
    log_decay = -jnp.exp(a_log[0]) * dt
    lane = lax.broadcasted_iota(jnp.int32, (heads, BLOCK), 1)
    run = log_decay
    shift = 1
    while shift < BLOCK:
        run = run + jnp.where(lane >= shift, pltpu.roll(run, shift, 1), 0.0)
        shift *= 2
    final = run[:, BLOCK - 1 :]
    scale = jnp.exp(final - run) * dt
    cum = run + lead_in[0][:, :1]
    run_out[0] = run
    dt_out[0] = dt
    cum_all[0] = cum
    lead_out[0] = jnp.broadcast_to(cum[:, BLOCK - 1 :], (heads, LANES))
    keep = jnp.broadcast_to(jnp.exp(final), (heads, LANES))

    def conv_tile(r):
        tile = raw[pl.ds(span + r, HEAD_DIM), :]
        taps = w[0, pl.ds(r, HEAD_DIM), :]
        summed = None
        for k in range(4):
            part = tile if k == 3 else pltpu.roll(tile, 3 - k, 1)
            part = taps[:, k : k + 1] * part[:, LANES:]
            summed = part if summed is None else summed + part
        return silu(summed).astype(bf16)

    for r in range(0, STATE_WIDTH, HEAD_DIM):
        bmap[0, r : r + HEAD_DIM, :] = conv_tile(span + r)
        c_tile = conv_tile(span + STATE_WIDTH + r)
        cmap[0, r : r + HEAD_DIM, :] = c_tile
        c_all[0, r : r + HEAD_DIM, :] = c_tile
    for h in range(heads):
        r = h * HEAD_DIM
        tile = conv_tile(r)
        xact[0, r : r + HEAD_DIM, :] = tile
        xw[r : r + HEAD_DIM, :] = (tile.astype(f32) * scale[h : h + 1, :]).astype(bf16)
    update = lax.dot_general(xw[...], bmap[0], NT, preferred_element_type=f32)
    for h in range(heads):
        r = h * HEAD_DIM
        new = keep[h : h + 1, :] * state_in[0, r : r + HEAD_DIM, :] + update[r : r + HEAD_DIM, :]
        if last:
            at = (h % piece_heads) * HEAD_DIM
            state_out[h // piece_heads, at : at + HEAD_DIM, :] = new
        else:
            state_out[0, r : r + HEAD_DIM, :] = new
    if last:
        decay = jnp.exp(lead_out[0])
        for h in range(heads):
            at = piece_heads * HEAD_DIM + h % piece_heads
            state_out[h // piece_heads, at : at + 1, :] = decay[h : h + 1, :]
    tail[0] = raw[span : span + conv_rows, BLOCK : BLOCK + LANES].astype(bf16)
    gate_all[0] = raw[:span, LANES:].astype(bf16)


def conv_chunk(chunk, chunks, recv, tail, w, bias, a_log, state, lead, wholes, dims):
    spg, rows, heads, span, piece_heads = dims
    groups = w.shape[0]
    conv_rows = span + 2 * STATE_WIDTH
    last = chunk == chunks - 1
    tokens = chunks * BLOCK

    def per_group(*shape):
        return pl.BlockSpec((1,) + shape, lambda g: (g,) + (0,) * len(shape))

    def whole(*shape):
        return pl.BlockSpec((1,) + shape, lambda g: (g, 0, chunk))

    if last:
        packed = piece_heads * HEAD_DIM + 8
        state_shape = jax.ShapeDtypeStruct((groups * spg, packed, STATE_WIDTH), f32)
        state_spec = pl.BlockSpec((spg, packed, STATE_WIDTH), lambda g: (g, 0, 0))
    else:
        state_shape = jax.ShapeDtypeStruct((groups, span, STATE_WIDTH), f32)
        state_spec = per_group(span, STATE_WIDTH)

    def out(dtype, *shape):
        return jax.ShapeDtypeStruct((groups,) + shape, dtype)

    args = [recv, tail, w, bias, a_log, state, lead]
    aliases = {}
    if wholes is not None:
        for i, array in enumerate(wholes):
            aliases[len(args)] = 8 + i
            args.append(array)
    return pl.pallas_call(
        functools.partial(conv_kernel, dims, last),
        grid=(groups,),
        in_specs=[
            pl.BlockSpec((spg, rows, BLOCK), lambda g: (g, 0, 0)),
            per_group(conv_rows, LANES),
            per_group(conv_rows, 4),
            per_group(heads, 1),
            per_group(heads, 1),
            per_group(span, STATE_WIDTH),
            per_group(heads, LANES),
        ]
        + [pl.BlockSpec(memory_space=pl.ANY)] * len(aliases),
        out_specs=[
            per_group(span, BLOCK),
            per_group(STATE_WIDTH, BLOCK),
            per_group(STATE_WIDTH, BLOCK),
            per_group(heads, BLOCK),
            per_group(heads, BLOCK),
            per_group(conv_rows, LANES),
            state_spec,
            per_group(heads, LANES),
            whole(span, BLOCK),
            whole(heads, BLOCK),
            whole(STATE_WIDTH, BLOCK),
        ],
        out_shape=[
            out(bf16, span, BLOCK),
            out(bf16, STATE_WIDTH, BLOCK),
            out(bf16, STATE_WIDTH, BLOCK),
            out(f32, heads, BLOCK),
            out(f32, heads, BLOCK),
            out(bf16, conv_rows, LANES),
            state_shape,
            out(f32, heads, LANES),
            out(bf16, span, tokens),
            out(f32, heads, tokens),
            out(bf16, STATE_WIDTH, tokens),
        ],
        scratch_shapes=[
            pltpu.VMEM((rows * spg, LANES + BLOCK), f32),
            pltpu.VMEM((span, BLOCK), bf16),
        ],
        input_output_aliases=aliases,
        compiler_params=params(),
        cost_estimate=pl.CostEstimate(flops=2 * 10**9, bytes_accessed=10**7, transcendentals=10**6),
        name="conv_chunk",
    )(*args)


def split(v):
    high = v.astype(bf16)
    return high, (v - high.astype(f32)).astype(bf16)


def block_kernel(dims, first, xact, bmap, cmap, run_ref, dt_ref, state, skip, *refs):
    heads, span = dims
    mixed = refs[-1]
    c = cmap[0]
    b_rows = bmap[0].astype(f32).T.astype(bf16)
    scores = jnp.dot(b_rows, c, preferred_element_type=f32)
    src = lax.broadcasted_iota(jnp.int32, (HALF, HALF), 0)
    dst = lax.broadcasted_iota(jnp.int32, (HALF, HALF), 1)
    causal = src <= dst
    s00 = jnp.where(causal, scores[:HALF, :HALF], 0.0)
    s01 = scores[:HALF, HALF:]
    s11 = jnp.where(causal, scores[HALF:, HALF:], 0.0)
    r = run_ref[0] * LOG2E
    q = (r - jnp.log(dt_ref[0]) * LOG2E).T
    if not first:
        cc = jnp.concatenate([c, c], axis=0)
        entered = jnp.exp2(r)
    for h in range(heads):
        at = h * HEAD_DIM
        r0, r1 = r[h : h + 1, :HALF], r[h : h + 1, HALF:]
        q0, q1 = q[:HALF, h : h + 1], q[HALF:, h : h + 1]
        w00 = (s00 * jnp.exp2(jnp.minimum(r0 - q0, CAP))).astype(bf16)
        w01 = (s01 * jnp.exp2(r1 - q0)).astype(bf16)
        w11 = (s11 * jnp.exp2(jnp.minimum(r1 - q1, CAP))).astype(bf16)
        x = xact[0, at : at + HEAD_DIM, :]
        y0 = jnp.dot(x[:, :HALF], w00, preferred_element_type=f32)
        y1 = jnp.dot(x, jnp.concatenate([w01, w11], axis=0), preferred_element_type=f32)
        y = jnp.concatenate([y0, y1], axis=1) + skip[0, h : h + 1, :] * x.astype(f32)
        if not first:
            high, low = split(state[0, at : at + HEAD_DIM, :])
            carried = jnp.dot(
                jnp.concatenate([high, low], axis=1), cc, preferred_element_type=f32
            )
            y = y + entered[h : h + 1, :] * carried
        mixed[0, at : at + HEAD_DIM, :] = y


def block_chunk(chunk, chunks, xact, bmap, cmap, run, dt, state, skip, whole):
    groups, span, _ = xact.shape
    heads = run.shape[1]

    def per_group(*shape):
        return pl.BlockSpec((1,) + shape, lambda g: (g,) + (0,) * len(shape))

    args = [xact, bmap, cmap, run, dt, state, skip]
    specs = [
        per_group(span, BLOCK),
        per_group(STATE_WIDTH, BLOCK),
        per_group(STATE_WIDTH, BLOCK),
        per_group(heads, BLOCK),
        per_group(heads, BLOCK),
        per_group(span, STATE_WIDTH),
        per_group(heads, 1),
    ]
    aliases = {}
    if whole is not None:
        aliases = {len(args): 0}
        args.append(whole)
        specs.append(pl.BlockSpec(memory_space=pl.ANY))
    return pl.pallas_call(
        functools.partial(block_kernel, (heads, span), chunk == 0),
        grid=(groups,),
        in_specs=specs,
        out_specs=pl.BlockSpec((1, span, BLOCK), lambda g: (g, 0, chunk)),
        out_shape=jax.ShapeDtypeStruct((groups, span, chunks * BLOCK), f32),
        input_output_aliases=aliases,
        compiler_params=params(),
        cost_estimate=pl.CostEstimate(flops=4 * 10**9, bytes_accessed=10**7, transcendentals=10**6),
        name="block_chunk",
    )(*args)


def relay_kernel(piece_heads, src, dst):
    count = src.shape[0]
    rows = piece_heads * HEAD_DIM
    for h in range(piece_heads):
        at = h * HEAD_DIM
        held = jnp.zeros((HEAD_DIM, STATE_WIDTH), f32)
        for d in range(count):
            dst[d, at : at + HEAD_DIM, :] = held
            held = src[d, rows + h : rows + h + 1, :] * held + src[d, at : at + HEAD_DIM, :]


def relay(packed, piece_heads):
    count = packed.shape[0]
    rows = piece_heads * HEAD_DIM
    return pl.pallas_call(
        functools.partial(relay_kernel, piece_heads),
        out_shape=jax.ShapeDtypeStruct((count, rows, STATE_WIDTH), f32),
        compiler_params=params(16),
        name="relay",
    )(packed)


def final_kernel(dims, mixed, gate, c_ref, cum, state, gain, out, kept):
    heads, span = dims
    c = c_ref[0]
    cc = jnp.concatenate([c, c], axis=0)
    entered = jnp.exp(cum[0])
    total = jnp.zeros((HEAD_DIM, BLOCK), f32)
    for h in range(heads):
        at = h * HEAD_DIM
        high, low = split(state[0, at : at + HEAD_DIM, :])
        carried = jnp.dot(jnp.concatenate([high, low], axis=1), cc, preferred_element_type=f32)
        v = mixed[0, at : at + HEAD_DIM, :] + entered[h : h + 1, :] * carried
        v = v * silu(gate[0, at : at + HEAD_DIM, :].astype(f32))
        kept[at : at + HEAD_DIM, :] = v
        total = total + v * v
    mean = jnp.sum(total, axis=0, keepdims=True) * (1.0 / span)
    factor = lax.rsqrt(mean + EPSILON)
    for at in range(0, span, 128):
        tile = (kept[at : at + 128, :] * factor).T
        out[:, at : at + 128] = (tile * gain[0, :, at : at + 128]).astype(bf16)


def finish(mixed, gate, c_all, cum, state, gain):
    groups, span, tokens = mixed.shape
    heads = cum.shape[1]

    def tile(rows):
        return pl.BlockSpec((1, rows, BLOCK), lambda g, c: (g, 0, c))

    return pl.pallas_call(
        functools.partial(final_kernel, (heads, span)),
        grid=(groups, tokens // BLOCK),
        in_specs=[
            tile(span),
            tile(span),
            tile(STATE_WIDTH),
            tile(heads),
            pl.BlockSpec((1, span, STATE_WIDTH), lambda g, c: (g, 0, 0)),
            pl.BlockSpec((1, 1, span), lambda g, c: (g, 0, 0)),
        ],
        out_specs=pl.BlockSpec((BLOCK, span), lambda g, c: (c, g)),
        out_shape=jax.ShapeDtypeStruct((tokens, groups * span), bf16),
        scratch_shapes=[pltpu.VMEM((span, BLOCK), f32)],
        compiler_params=params(),
        name="finish",
    )(mixed, gate, c_all, cum, state, gain)


def exchange(array):
    return lax.all_to_all(array, "seq", split_axis=0, concat_axis=0, tiled=True)


def per_device(projected, conv_weight, dt_bias, a_log, d_skip, norm_gain):
    seq_count = lax.axis_size("seq")
    groups = conv_weight.shape[1]
    conv_rows = conv_weight.shape[2]
    heads = dt_bias.shape[0] // groups
    span = heads * HEAD_DIM
    rows, all_tokens = projected.shape
    local_tokens = all_tokens // seq_count
    chunks = local_tokens // BLOCK
    spg = seq_count // groups
    piece_heads = groups * heads // seq_count
    dims = (spg, rows, heads, span, piece_heads)

    got = [exchange(cut_chunk(projected, seq_count, 0, chunks))]
    rims = exchange(cut_rims(projected, seq_count, local_tokens))
    for c in range(1, chunks):
        got.append(exchange(cut_chunk(projected, seq_count, c, chunks)))

    rims = jnp.transpose(rims, (1, 0, 2)).reshape(8, groups, spg * rows)
    rims = jnp.transpose(rims[:, :, span : span + conv_rows], (1, 2, 0))
    tail = jnp.pad(rims, ((0, 0), (0, 0), (LANES - 8, 0)))

    w = jnp.transpose(conv_weight, (1, 2, 0))
    bias = dt_bias.reshape(groups, heads, 1)
    rate = a_log.reshape(groups, heads, 1)
    skip = d_skip.reshape(groups, heads, 1)
    gain = norm_gain.reshape(groups, 1, span)
    state = jnp.zeros((groups, span, STATE_WIDTH), f32)
    lead = jnp.zeros((groups, heads, LANES), f32)
    wholes = mixed = None
    for c in range(chunks):
        xact, bmap, cmap, run, dt, tail, new, lead, *wholes = conv_chunk(
            c, chunks, got[c], tail, w, bias, rate, state, lead, wholes, dims
        )
        mixed = block_chunk(c, chunks, xact, bmap, cmap, run, dt, state, skip, mixed)
        state = new
    entering = exchange(relay(exchange(state), piece_heads)).reshape(groups, span, STATE_WIDTH)
    gate_all, cum_all, c_all = wholes
    return finish(mixed, gate_all, c_all, cum_all, entering, gain)


def solution(mesh):
    in_specs = (P(("tp", "seq"), None), P(None, "tp", None), P("tp"), P("tp"), P("tp"), P("tp"))
    return jax.shard_map(
        per_device, mesh=mesh, in_specs=in_specs, out_specs=P("seq", "tp"), check_vma=False
    )
```

```python
import functools

import jax
import jax.numpy as jnp
from jax import lax
from jax.experimental import pallas as pl
from jax.experimental.pallas import tpu as pltpu
from jax.sharding import PartitionSpec as P

HEAD_DIM = 64
STATE_WIDTH = 128
BLOCK = 256
LANES = 128
HALF = BLOCK // 2
LOG2E = 1.4426950408889634
CAP = 80.0
EPSILON = 1e-05

f32 = jnp.float32
bf16 = jnp.bfloat16
NT = (((1,), (1,)), ((), ()))


def params():
    return pltpu.CompilerParams(vmem_limit_bytes=56 * 2**20)


def silu(v):
    half = 0.5 * v
    return half + half * jnp.tanh(half)


def softplus(v):
    e = jnp.exp(-jnp.abs(v))
    u = 1.0 + e
    gap = u - 1.0
    tiny = gap == 0.0
    log_part = jnp.where(tiny, e, jnp.log(u) * (e / jnp.where(tiny, 1.0, gap)))
    return jnp.maximum(v, 0.0) + log_part


def per_group(*shape):
    return pl.BlockSpec((1,) + shape, lambda g: (g,) + (0,) * len(shape))


def rim_shape(rows):
    first = -(-rows // 16) * 16
    groups = -(-rows // BLOCK)
    return first, groups


def cut_kernel(with_rims, src, *refs):
    dst = refs[-1]
    rows = src.shape[0]
    dst[0, :rows, :] = src[...]
    if with_rims:
        row = lax.broadcasted_iota(jnp.int32, (8, LANES), 0)
        col = lax.broadcasted_iota(jnp.int32, (8, LANES), 1)
        pick = jnp.where((col == row + LANES - 8) & (pl.program_id(0) > 0), 1.0, 0.0)
        rims = lax.dot_general(pick.astype(bf16), refs[0][...], NT, preferred_element_type=f32)
        first, groups = rim_shape(rows)
        for j in range(groups):
            part = rims[:, j * BLOCK : min((j + 1) * BLOCK, rows)]
            part = jnp.concatenate([part, jnp.zeros((8, part.shape[1]), f32)], axis=0)
            dst[0, first + 16 * j : first + 16 * (j + 1), : part.shape[1]] = part.astype(bf16)


def cut_chunk(projected, seq_count, chunk, chunks, token):
    rows = projected.shape[0]
    args = [projected]
    specs = [pl.BlockSpec((rows, BLOCK), lambda d: (0, d * chunks + chunk))]
    out_rows = rows
    if chunk == 0:
        first, groups = rim_shape(rows)
        out_rows = first + 16 * groups
        per = chunks * BLOCK // LANES
        args.append(projected)
        specs.append(pl.BlockSpec((rows, LANES), lambda d: (0, jnp.maximum(d * per - 1, 0))))
    if token is not None:
        args.append(token)
        specs.append(pl.BlockSpec(memory_space=pl.ANY))
    return pl.pallas_call(
        functools.partial(cut_kernel, chunk == 0),
        grid=(seq_count,),
        in_specs=specs,
        out_specs=pl.BlockSpec((1, out_rows, BLOCK), lambda d: (d, 0, 0)),
        out_shape=jax.ShapeDtypeStruct((seq_count, out_rows, BLOCK), bf16),
        compiler_params=params(),
        name="cut_chunk",
    )(*args)


def gather_rows(recv, prev, raw, rows, low, high):
    for s in range(recv.shape[0]):
        a = max(low - s * rows, 0) // 16 * 16
        b = min(-(-(high - s * rows) // 16) * 16, rows)
        if b <= a:
            continue
        at = s * rows + a
        raw[at : at + b - a, LANES:] = recv[s, a:b, :].astype(f32)
        if prev is not None:
            raw[at : at + b - a, :LANES] = prev[s, a:b, :].astype(f32)
        else:
            first, groups = rim_shape(rows)
            pad = jnp.zeros((LANES - 8, BLOCK), f32)
            for j in range(groups):
                c, d = max(a, j * BLOCK), min(b, (j + 1) * BLOCK)
                if d <= c:
                    continue
                rims = recv[s, first + 16 * j : first + 16 * (j + 1), :].astype(f32)[:8]
                tall = jnp.concatenate([pad, rims], axis=0).T
                raw[s * rows + c : s * rows + d, :LANES] = tall[c - j * BLOCK : d - j * BLOCK]


def conv_tile(raw, w, span, r, height):
    tile = raw[span + r : span + r + height, :]
    taps = w[0, r : r + height, :]
    summed = None
    for k in range(4):
        part = tile if k == 3 else pltpu.roll(tile, 3 - k, 1)
        part = taps[:, k : k + 1] * part[:, LANES:]
        summed = part if summed is None else summed + part
    return silu(summed).astype(bf16)


def state_kernel(dims, first, last, recv, *refs):
    spg, rows, heads, span, piece_heads = dims
    prev = None
    if not first:
        prev, refs = refs[0], refs[1:]
    w, bias, a_log, state_in, lead_in = refs[:5]
    xact, bmap, run_out, dt_out, cum_out, state_out, lead_out = refs[5:12]
    raw, xw = refs[12:]
    steps = 2 * span + 2 * STATE_WIDTH

    gather_rows(recv, prev, raw, rows, steps, steps + heads)
    gather_rows(recv, prev, raw, rows, span, 2 * span + STATE_WIDTH)
    dt = softplus(raw[steps : steps + heads, LANES:] + bias[0])
    log_decay = -jnp.exp(a_log[0]) * dt
    lane = lax.broadcasted_iota(jnp.int32, (heads, BLOCK), 1)
    run = log_decay
    shift = 1
    while shift < BLOCK:
        run = run + jnp.where(lane >= shift, pltpu.roll(run, shift, 1), 0.0)
        shift *= 2
    final = run[:, BLOCK - 1 :]
    scale = jnp.exp(final - run) * dt
    cum = run + lead_in[0][:, :1]
    run_out[0] = run
    dt_out[0] = dt
    cum_out[0] = cum
    lead = jnp.broadcast_to(cum[:, BLOCK - 1 :], (heads, LANES))
    lead_out[0] = lead
    keep = jnp.broadcast_to(jnp.exp(final), (heads, LANES))

    for r in range(0, STATE_WIDTH, HEAD_DIM):
        bmap[0, r : r + HEAD_DIM, :] = conv_tile(raw, w, span, span + r, HEAD_DIM)
    for h in range(heads):
        r = h * HEAD_DIM
        tile = conv_tile(raw, w, span, r, HEAD_DIM)
        xact[0, r : r + HEAD_DIM, :] = tile
        xw[r : r + HEAD_DIM, :] = (tile.astype(f32) * scale[h : h + 1, :]).astype(bf16)
    update = lax.dot_general(xw[...], bmap[0], NT, preferred_element_type=f32)
    for h in range(heads):
        r = h * HEAD_DIM
        new = update[r : r + HEAD_DIM, :]
        if not first:
            new = keep[h : h + 1, :] * state_in[0, r : r + HEAD_DIM, :] + new
        if last:
            at = (h % piece_heads) * HEAD_DIM
            state_out[h // piece_heads, at : at + HEAD_DIM, :] = new
        else:
            state_out[0, r : r + HEAD_DIM, :] = new
    if last:
        decay = jnp.exp(lead)
        for h in range(heads):
            at = piece_heads * HEAD_DIM + h % piece_heads
            state_out[h // piece_heads, at : at + 1, :] = decay[h : h + 1, :]


def chunk_specs(got, chunk, dims):
    spg, rows = dims[:2]
    args = [got[chunk]]
    specs = [pl.BlockSpec((spg,) + got[chunk].shape[1:], lambda g: (g, 0, 0))]
    if chunk:
        held = got[chunk - 1].shape[1]
        args.append(got[chunk - 1])
        specs.append(pl.BlockSpec((spg, held, LANES), lambda g: (g, 0, BLOCK // LANES - 1)))
    return args, specs


def state_chunk(chunk, chunks, got, w, bias, a_log, state, lead, dims):
    spg, rows, heads, span, piece_heads = dims
    groups = w.shape[0]
    conv_rows = span + 2 * STATE_WIDTH
    last = chunk == chunks - 1
    if last:
        packed = piece_heads * HEAD_DIM + 8
        state_shape = jax.ShapeDtypeStruct((groups * spg, packed, STATE_WIDTH), f32)
        state_spec = pl.BlockSpec((spg, packed, STATE_WIDTH), lambda g: (g, 0, 0))
    else:
        state_shape = jax.ShapeDtypeStruct((groups, span, STATE_WIDTH), f32)
        state_spec = per_group(span, STATE_WIDTH)

    def out(dtype, *shape):
        return jax.ShapeDtypeStruct((groups,) + shape, dtype)

    args, specs = chunk_specs(got, chunk, dims)
    return pl.pallas_call(
        functools.partial(state_kernel, dims, chunk == 0, last),
        grid=(groups,),
        in_specs=specs
        + [
            per_group(conv_rows, 4),
            per_group(heads, 1),
            per_group(heads, 1),
            per_group(span, STATE_WIDTH),
            per_group(heads, LANES),
        ],
        out_specs=[
            per_group(span, BLOCK),
            per_group(STATE_WIDTH, BLOCK),
            per_group(heads, BLOCK),
            per_group(heads, BLOCK),
            per_group(heads, BLOCK),
            state_spec,
            per_group(heads, LANES),
        ],
        out_shape=[
            out(bf16, span, BLOCK),
            out(bf16, STATE_WIDTH, BLOCK),
            out(f32, heads, BLOCK),
            out(f32, heads, BLOCK),
            out(f32, heads, BLOCK),
            state_shape,
            out(f32, heads, LANES),
        ],
        scratch_shapes=[
            pltpu.VMEM((rows * spg, LANES + BLOCK), f32),
            pltpu.VMEM((span, BLOCK), bf16),
        ],
        compiler_params=params(),
        cost_estimate=pl.CostEstimate(flops=4 * 10**9, bytes_accessed=10**7, transcendentals=10**6),
        name="state_chunk",
    )(*args, w, bias, a_log, state, lead)


def split(v):
    high = v.astype(bf16)
    return high, (v - high.astype(f32)).astype(bf16)


def block_kernel(dims, first, recv, *refs):
    spg, rows, heads, span, piece_heads = dims
    prev = None
    if not first:
        prev, refs = refs[0], refs[1:]
    w, xact, bmap, run_ref, dt_ref, cum_ref, state, skip = refs[:8]
    mixed, gate_all, c_all, cum_all, token, raw = refs[-6:]
    conv_rows = span + 2 * STATE_WIDTH
    gather_rows(recv, prev, raw, rows, 2 * span + STATE_WIDTH, span + conv_rows)
    for s in range(spg):
        b = min(span - s * rows, rows)
        if b > 0:
            b = min(-(-b // 16) * 16, rows)
            raw[s * rows : s * rows + b, LANES:] = recv[s, :b, :].astype(f32)
    gate_all[0] = raw[:span, LANES:].astype(bf16)
    cum_all[0] = cum_ref[0]
    token[0] = cum_ref[0, :8, :LANES]
    c = conv_tile(raw, w, span, span + STATE_WIDTH, STATE_WIDTH)
    c_all[0] = c

    b_rows = bmap[0].astype(f32).T.astype(bf16)
    scores = jnp.dot(b_rows, c, preferred_element_type=f32)
    src = lax.broadcasted_iota(jnp.int32, (HALF, HALF), 0)
    dst = lax.broadcasted_iota(jnp.int32, (HALF, HALF), 1)
    causal = src <= dst
    s00 = jnp.where(causal, scores[:HALF, :HALF], 0.0)
    s01 = scores[:HALF, HALF:]
    s11 = jnp.where(causal, scores[HALF:, HALF:], 0.0)
    r = run_ref[0] * LOG2E
    q = (r - jnp.log(dt_ref[0]) * LOG2E).T
    if not first:
        cc = jnp.concatenate([c, c], axis=0)
        entered = jnp.exp2(r)
    for h in range(heads):
        at = h * HEAD_DIM
        r0, r1 = r[h : h + 1, :HALF], r[h : h + 1, HALF:]
        q0, q1 = q[:HALF, h : h + 1], q[HALF:, h : h + 1]
        w00 = (s00 * jnp.exp2(jnp.minimum(r0 - q0, CAP))).astype(bf16)
        w01 = (s01 * jnp.exp2(r1 - q0)).astype(bf16)
        w11 = (s11 * jnp.exp2(jnp.minimum(r1 - q1, CAP))).astype(bf16)
        x = xact[0, at : at + HEAD_DIM, :]
        y0 = jnp.dot(x[:, :HALF], w00, preferred_element_type=f32)
        y1 = jnp.dot(x, jnp.concatenate([w01, w11], axis=0), preferred_element_type=f32)
        y = jnp.concatenate([y0, y1], axis=1) + skip[0, h : h + 1, :] * x.astype(f32)
        if not first:
            high, low = split(state[0, at : at + HEAD_DIM, :])
            carried = jnp.dot(
                jnp.concatenate([high, low], axis=1), cc, preferred_element_type=f32
            )
            y = y + entered[h : h + 1, :] * carried
        mixed[0, at : at + HEAD_DIM, :] = y


def block_chunk(chunk, chunks, got, w, xact, bmap, run, dt, cum, state, skip, wholes, dims):
    spg, rows, heads, span, piece_heads = dims
    groups = w.shape[0]
    tokens = chunks * BLOCK

    def whole(*shape):
        return pl.BlockSpec((1,) + shape, lambda g: (g, 0, chunk))

    args, specs = chunk_specs(got, chunk, dims)
    args += [w, xact, bmap, run, dt, cum, state, skip]
    specs += [
        per_group(span + 2 * STATE_WIDTH, 4),
        per_group(span, BLOCK),
        per_group(STATE_WIDTH, BLOCK),
        per_group(heads, BLOCK),
        per_group(heads, BLOCK),
        per_group(heads, BLOCK),
        per_group(span, STATE_WIDTH),
        per_group(heads, 1),
    ]
    aliases = {}
    for i, array in enumerate(wholes or ()):
        aliases[len(args)] = i
        args.append(array)
        specs.append(pl.BlockSpec(memory_space=pl.ANY))

    def out(dtype, *shape):
        return jax.ShapeDtypeStruct((groups,) + shape, dtype)

    *wholes, token = pl.pallas_call(
        functools.partial(block_kernel, dims, chunk == 0),
        grid=(groups,),
        in_specs=specs,
        out_specs=[
            whole(span, BLOCK),
            whole(span, BLOCK),
            whole(STATE_WIDTH, BLOCK),
            whole(heads, BLOCK),
            per_group(8, LANES),
        ],
        out_shape=[
            out(f32, span, tokens),
            out(bf16, span, tokens),
            out(bf16, STATE_WIDTH, tokens),
            out(f32, heads, tokens),
            out(f32, 8, LANES),
        ],
        scratch_shapes=[pltpu.VMEM((rows * spg, LANES + BLOCK), f32)],
        input_output_aliases=aliases,
        compiler_params=params(),
        cost_estimate=pl.CostEstimate(flops=4 * 10**9, bytes_accessed=10**7, transcendentals=10**6),
        name="block_chunk",
    )(*args)
    return wholes, token


def relay_kernel(piece_heads, src, dst):
    count = src.shape[0]
    rows = piece_heads * HEAD_DIM
    for h in range(piece_heads):
        at = h * HEAD_DIM
        held = jnp.zeros((HEAD_DIM, STATE_WIDTH), f32)
        for d in range(count):
            high, low = split(held)
            dst[d, at : at + HEAD_DIM, :STATE_WIDTH] = high
            dst[d, at : at + HEAD_DIM, STATE_WIDTH:] = low
            held = src[d, rows + h : rows + h + 1, :] * held + src[d, at : at + HEAD_DIM, :]


def relay(packed, piece_heads):
    count = packed.shape[0]
    rows = piece_heads * HEAD_DIM
    return pl.pallas_call(
        functools.partial(relay_kernel, piece_heads),
        out_shape=jax.ShapeDtypeStruct((count, rows, 2 * STATE_WIDTH), bf16),
        compiler_params=params(),
        name="relay",
    )(packed)


def final_kernel(dims, mixed, gate, c_ref, cum, state, gain, out, kept, gains):
    heads, span = dims

    @pl.when(pl.program_id(1) == 0)
    def _():
        gains[...] = jnp.broadcast_to(gain[0], (span, LANES))

    c = c_ref[0]
    cc = jnp.concatenate([c, c], axis=0)
    entered = jnp.exp(cum[0])
    total = jnp.zeros((HEAD_DIM, BLOCK), f32)
    for h in range(heads):
        at = h * HEAD_DIM
        carried = jnp.dot(state[0, at : at + HEAD_DIM, :], cc, preferred_element_type=f32)
        v = mixed[0, at : at + HEAD_DIM, :] + entered[h : h + 1, :] * carried
        v = v * silu(gate[0, at : at + HEAD_DIM, :].astype(f32))
        kept[at : at + HEAD_DIM, :] = v
        total = total + v * v
    mean = jnp.sum(total, axis=0, keepdims=True) * (1.0 / span)
    factor = lax.rsqrt(mean + EPSILON)
    row = lax.broadcasted_iota(jnp.int32, (BLOCK, BLOCK), 0)
    col = lax.broadcasted_iota(jnp.int32, (BLOCK, BLOCK), 1)
    eye = jnp.where(row == col, 1.0, 0.0).astype(bf16)
    for at in range(0, span, BLOCK):
        scale = gains[at : at + BLOCK, :]
        scale = jnp.concatenate([scale] * (BLOCK // LANES), axis=1)
        tile = (kept[at : at + BLOCK, :] * factor * scale).astype(bf16)
        turned = lax.dot_general(eye, tile, NT, preferred_element_type=f32)
        out[:, at : at + BLOCK] = turned.astype(bf16)


def finish(mixed, gate, c_all, cum, state, gain):
    groups, span, tokens = mixed.shape
    heads = cum.shape[1]

    def tile(rows):
        return pl.BlockSpec((1, rows, BLOCK), lambda g, c: (g, 0, c))

    return pl.pallas_call(
        functools.partial(final_kernel, (heads, span)),
        grid=(groups, tokens // BLOCK),
        in_specs=[
            tile(span),
            tile(span),
            tile(STATE_WIDTH),
            tile(heads),
            pl.BlockSpec((1, span, 2 * STATE_WIDTH), lambda g, c: (g, 0, 0)),
            pl.BlockSpec((1, span, 1), lambda g, c: (g, 0, 0)),
        ],
        out_specs=pl.BlockSpec((BLOCK, span), lambda g, c: (c, g)),
        out_shape=jax.ShapeDtypeStruct((tokens, groups * span), bf16),
        scratch_shapes=[pltpu.VMEM((span, BLOCK), f32), pltpu.VMEM((span, LANES), f32)],
        compiler_params=params(),
        name="finish",
    )(mixed, gate, c_all, cum, state, gain)


def exchange(array):
    return lax.all_to_all(array, "seq", split_axis=0, concat_axis=0, tiled=True)


def per_device(projected, conv_weight, dt_bias, a_log, d_skip, norm_gain):
    seq_count = lax.axis_size("seq")
    groups = conv_weight.shape[1]
    heads = dt_bias.shape[0] // groups
    span = heads * HEAD_DIM
    rows, all_tokens = projected.shape
    local_tokens = all_tokens // seq_count
    chunks = local_tokens // BLOCK
    spg = seq_count // groups
    piece_heads = groups * heads // seq_count
    dims = (spg, rows, heads, span, piece_heads)

    w = jnp.transpose(conv_weight, (1, 2, 0))
    bias = dt_bias.reshape(groups, heads, 1)
    rate = a_log.reshape(groups, heads, 1)
    skip = d_skip.reshape(groups, heads, 1)
    gain = norm_gain.reshape(groups, span, 1)
    state = jnp.zeros((groups, span, STATE_WIDTH), f32)
    lead = jnp.zeros((groups, heads, LANES), f32)

    cut = cut_chunk(projected, seq_count, 0, chunks, None)
    got = [exchange(cut)]
    if chunks > 1:
        got.append(exchange(cut_chunk(projected, seq_count, 1, chunks, cut)))
    wholes = None
    for c in range(chunks):
        xact, bmap, run, dt, cum, new, lead = state_chunk(
            c, chunks, got, w, bias, rate, state, lead, dims
        )
        wholes, token = block_chunk(
            c, chunks, got, w, xact, bmap, run, dt, cum, state, skip, wholes, dims
        )
        if c + 2 < chunks:
            got.append(exchange(cut_chunk(projected, seq_count, c + 2, chunks, token)))
        state = new
    entering = exchange(relay(exchange(state), piece_heads))
    mixed, gate_all, c_all, cum_all = wholes
    entering = entering.reshape(groups, span, 2 * STATE_WIDTH)
    return finish(mixed, gate_all, c_all, cum_all, entering, gain)


def solution(mesh):
    in_specs = (P(("tp", "seq"), None), P(None, "tp", None), P("tp"), P("tp"), P("tp"), P("tp"))
    return jax.shard_map(
        per_device, mesh=mesh, in_specs=in_specs, out_specs=P("seq", "tp"), check_vma=False
    )
```

```python
import functools

import jax
import jax.numpy as jnp
from jax import lax
from jax.experimental import pallas as pl
from jax.experimental.pallas import tpu as pltpu
from jax.sharding import PartitionSpec as P

HEAD_DIM = 64
STATE_WIDTH = 128
BLOCK = 256
LANES = 128
HALF = BLOCK // 2
WIDE = 256
LOG2E = 1.4426950408889634
CAP = 80.0
EPSILON = 1e-05

f32 = jnp.float32
bf16 = jnp.bfloat16
NT = (((1,), (1,)), ((), ()))


def params():
    return pltpu.CompilerParams(vmem_limit_bytes=56 * 2**20)


def silu(v):
    half = 0.5 * v
    return half + half * jnp.tanh(half)


def softplus(v):
    e = jnp.exp(-jnp.abs(v))
    u = 1.0 + e
    gap = u - 1.0
    tiny = gap == 0.0
    log_part = jnp.where(tiny, e, jnp.log(u) * (e / jnp.where(tiny, 1.0, gap)))
    return jnp.maximum(v, 0.0) + log_part


def per_group(*shape):
    return pl.BlockSpec((1,) + shape, lambda g: (g,) + (0,) * len(shape))


def rim_shape(rows):
    first = -(-rows // 16) * 16
    groups = -(-rows // BLOCK)
    return first, groups


def cut_kernel(chunk, chunks, src, *refs):
    rows, all_tokens = src.shape
    if chunk:
        dst, sems = refs[-2:]
    else:
        dst, windows, held, packed, sems, rim_sems, out_sems = refs
    count = dst.shape[0]
    tokens = all_tokens // count

    def copy(d):
        at = d * tokens + chunk * BLOCK
        to = dst if chunk else held
        return pltpu.make_async_copy(src.at[:, at : at + BLOCK], to.at[d], sems.at[d])

    if chunk:
        for d in range(count):
            copy(d).start()
        for d in range(count):
            copy(d).wait()
        return

    def window(d):
        return pltpu.make_async_copy(
            src.at[:, d * tokens - LANES : d * tokens], windows.at[d], rim_sems.at[d]
        )

    def place(d):
        return pltpu.make_async_copy(packed.at[d], dst.at[d], out_sems.at[d])

    for d in range(count):
        if d:
            window(d).start()
        copy(d).start()
    first, groups = rim_shape(rows)
    row = lax.broadcasted_iota(jnp.int32, (16, LANES), 0)
    col = lax.broadcasted_iota(jnp.int32, (16, LANES), 1)
    pick = jnp.where((col == row + LANES - 8) & (row < 8), 1.0, 0.0).astype(bf16)
    for d in range(count):
        packed[d, first : first + 16 * groups, :] = jnp.zeros((16 * groups, BLOCK), bf16)
        if d:
            window(d).wait()
            rims = lax.dot_general(pick, windows[d], NT, preferred_element_type=f32)
            for j in range(groups):
                part = rims[:, j * BLOCK : min((j + 1) * BLOCK, rows)]
                at = first + 16 * j
                packed[d, at : at + 16, : part.shape[1]] = part.astype(bf16)
        copy(d).wait()
        packed[d, :rows, :] = held[d]
        place(d).start()
    for d in range(count):
        place(d).wait()


def cut_chunk(projected, seq_count, chunk, chunks, token):
    rows = projected.shape[0]
    args = [projected]
    out_rows = rows
    scratch = [pltpu.SemaphoreType.DMA((seq_count,))]
    if chunk == 0:
        first, groups = rim_shape(rows)
        out_rows = first + 16 * groups
        scratch = [
            pltpu.VMEM((seq_count, rows, LANES), bf16),
            pltpu.VMEM((seq_count, rows, BLOCK), bf16),
            pltpu.VMEM((seq_count, out_rows, BLOCK), bf16),
        ] + scratch * 3
    if token is not None:
        args.append(token)
    return pl.pallas_call(
        functools.partial(cut_kernel, chunk, chunks),
        in_specs=[pl.BlockSpec(memory_space=pl.ANY)] * len(args),
        out_specs=pl.BlockSpec(memory_space=pl.ANY),
        out_shape=jax.ShapeDtypeStruct((seq_count, out_rows, BLOCK), bf16),
        scratch_shapes=scratch,
        compiler_params=params(),
        name="cut_chunk",
    )(*args)


def gather_rows(recv, prev, raw, rows, low, high):
    for s in range(recv.shape[0]):
        a = max(low - s * rows, 0) // 16 * 16
        b = min(-(-(high - s * rows) // 16) * 16, rows)
        if b <= a:
            continue
        at = s * rows + a
        raw[at : at + b - a, LANES:] = recv[s, a:b, :].astype(f32)
        if prev is not None:
            raw[at : at + b - a, :LANES] = prev[s, a:b, :].astype(f32)
        else:
            first, groups = rim_shape(rows)
            pad = jnp.zeros((LANES - 8, BLOCK), f32)
            for j in range(groups):
                c, d = max(a, j * BLOCK), min(b, (j + 1) * BLOCK)
                if d <= c:
                    continue
                rims = recv[s, first + 16 * j : first + 16 * (j + 1), :].astype(f32)[:8]
                tall = jnp.concatenate([pad, rims], axis=0).T
                raw[s * rows + c : s * rows + d, :LANES] = tall[c - j * BLOCK : d - j * BLOCK]


def band():
    row = lax.broadcasted_iota(jnp.int32, (2 * LANES, 3 * LANES), 0)
    col = lax.broadcasted_iota(jnp.int32, (2 * LANES, 3 * LANES), 1)
    tap = col // LANES
    return jnp.where(row == col - tap * LANES + LANES - 3 + tap, 1.0, 0.0).astype(bf16)


def conv_rows_of(raw, w, picks, span, r, height):
    low = raw[span + r : span + r + height, :].astype(bf16)
    shifted = [
        jnp.dot(low[:, at : at + 2 * LANES], picks, preferred_element_type=f32)
        for at in range(0, BLOCK, LANES)
    ]
    tiles = []
    for q in range(0, height, HEAD_DIM):
        at = r + q
        taps = [
            jnp.broadcast_to(w[0, at : at + HEAD_DIM, k : k + 1], (HEAD_DIM, LANES))
            for k in range(4)
        ]
        parts = []
        for i, three in enumerate(shifted):
            summed = None
            for k in range(3):
                part = taps[k] * three[q : q + HEAD_DIM, k * LANES : (k + 1) * LANES]
                summed = part if summed is None else summed + part
            own = raw[span + at : span + at + HEAD_DIM, (i + 1) * LANES : (i + 2) * LANES]
            parts.append(silu(summed + taps[3] * own).astype(bf16))
        tiles.append(jnp.concatenate(parts, axis=1))
    return tiles


def state_kernel(dims, first, last, recv, *refs):
    spg, rows, heads, span, piece_heads = dims
    prev = None
    if not first:
        prev, refs = refs[0], refs[1:]
    w, bias, a_log, state_in, lead_in = refs[:5]
    xact, bmap, run_out, dt_out, cum_out, state_out, lead_out = refs[5:12]
    raw, xw = refs[12:]
    steps = 2 * span + 2 * STATE_WIDTH

    gather_rows(recv, prev, raw, rows, steps, steps + heads)
    gather_rows(recv, prev, raw, rows, span, 2 * span + STATE_WIDTH)
    dt = softplus(raw[steps : steps + heads, LANES:] + bias[0])
    log_decay = -jnp.exp(a_log[0]) * dt
    lane = lax.broadcasted_iota(jnp.int32, (heads, BLOCK), 1)
    run = log_decay
    shift = 1
    while shift < BLOCK:
        run = run + jnp.where(lane >= shift, pltpu.roll(run, shift, 1), 0.0)
        shift *= 2
    final = run[:, BLOCK - 1 :]
    scale = jnp.exp(final - run) * dt
    cum = run + lead_in[0][:, :1]
    run_out[0] = run
    dt_out[0] = dt
    cum_out[0] = cum
    lead = jnp.broadcast_to(cum[:, BLOCK - 1 :], (heads, LANES))
    lead_out[0] = lead
    keep = jnp.broadcast_to(jnp.exp(final), (heads, LANES))

    picks = band()
    for i, tile in enumerate(conv_rows_of(raw, w, picks, span, span, STATE_WIDTH)):
        bmap[0, i * HEAD_DIM : (i + 1) * HEAD_DIM, :] = tile
    for r in range(0, span, WIDE):
        for i, tile in enumerate(conv_rows_of(raw, w, picks, span, r, WIDE)):
            at = r + i * HEAD_DIM
            h = at // HEAD_DIM
            xact[0, at : at + HEAD_DIM, :] = tile
            xw[at : at + HEAD_DIM, :] = (tile.astype(f32) * scale[h : h + 1, :]).astype(bf16)
    update = lax.dot_general(xw[...], bmap[0], NT, preferred_element_type=f32)
    for h in range(heads):
        r = h * HEAD_DIM
        new = update[r : r + HEAD_DIM, :]
        if not first:
            new = keep[h : h + 1, :] * state_in[0, r : r + HEAD_DIM, :] + new
        if last:
            at = (h % piece_heads) * HEAD_DIM
            state_out[h // piece_heads, at : at + HEAD_DIM, :] = new
        else:
            state_out[0, r : r + HEAD_DIM, :] = new
    if last:
        decay = jnp.exp(lead)
        for h in range(heads):
            at = piece_heads * HEAD_DIM + h % piece_heads
            state_out[h // piece_heads, at : at + 1, :] = decay[h : h + 1, :]


def chunk_specs(got, chunk, dims):
    spg, rows = dims[:2]
    args = [got[chunk]]
    specs = [pl.BlockSpec((spg,) + got[chunk].shape[1:], lambda g: (g, 0, 0))]
    if chunk:
        held = got[chunk - 1].shape[1]
        args.append(got[chunk - 1])
        specs.append(pl.BlockSpec((spg, held, LANES), lambda g: (g, 0, BLOCK // LANES - 1)))
    return args, specs


def state_chunk(chunk, chunks, got, w, bias, a_log, state, lead, dims):
    spg, rows, heads, span, piece_heads = dims
    groups = w.shape[0]
    conv_rows = span + 2 * STATE_WIDTH
    last = chunk == chunks - 1
    if last:
        packed = piece_heads * HEAD_DIM + 8
        state_shape = jax.ShapeDtypeStruct((groups * spg, packed, STATE_WIDTH), f32)
        state_spec = pl.BlockSpec((spg, packed, STATE_WIDTH), lambda g: (g, 0, 0))
    else:
        state_shape = jax.ShapeDtypeStruct((groups, span, STATE_WIDTH), f32)
        state_spec = per_group(span, STATE_WIDTH)

    def out(dtype, *shape):
        return jax.ShapeDtypeStruct((groups,) + shape, dtype)

    args, specs = chunk_specs(got, chunk, dims)
    return pl.pallas_call(
        functools.partial(state_kernel, dims, chunk == 0, last),
        grid=(groups,),
        in_specs=specs
        + [
            per_group(conv_rows, 4),
            per_group(heads, 1),
            per_group(heads, 1),
            per_group(span, STATE_WIDTH),
            per_group(heads, LANES),
        ],
        out_specs=[
            per_group(span, BLOCK),
            per_group(STATE_WIDTH, BLOCK),
            per_group(heads, BLOCK),
            per_group(heads, BLOCK),
            per_group(heads, BLOCK),
            state_spec,
            per_group(heads, LANES),
        ],
        out_shape=[
            out(bf16, span, BLOCK),
            out(bf16, STATE_WIDTH, BLOCK),
            out(f32, heads, BLOCK),
            out(f32, heads, BLOCK),
            out(f32, heads, BLOCK),
            state_shape,
            out(f32, heads, LANES),
        ],
        scratch_shapes=[
            pltpu.VMEM((rows * spg, LANES + BLOCK), f32),
            pltpu.VMEM((span, BLOCK), bf16),
        ],
        compiler_params=params(),
        cost_estimate=pl.CostEstimate(flops=4 * 10**9, bytes_accessed=10**7, transcendentals=10**6),
        name="state_chunk",
    )(*args, w, bias, a_log, state, lead)


def split(v):
    high = v.astype(bf16)
    return high, (v - high.astype(f32)).astype(bf16)


def block_kernel(dims, first, recv, *refs):
    spg, rows, heads, span, piece_heads = dims
    prev = None
    if not first:
        prev, refs = refs[0], refs[1:]
    w, xact, bmap, run_ref, dt_ref, cum_ref, state, skip = refs[:8]
    mixed, gate_all, c_all, cum_all, token, raw = refs[-6:]
    conv_rows = span + 2 * STATE_WIDTH
    gather_rows(recv, prev, raw, rows, 2 * span + STATE_WIDTH, span + conv_rows)
    for s in range(spg):
        b = min(span - s * rows, rows)
        if b > 0:
            b = min(-(-b // 16) * 16, rows)
            raw[s * rows : s * rows + b, LANES:] = recv[s, :b, :].astype(f32)
    gate_all[0, 0] = raw[:span, LANES:].astype(bf16)
    cum_all[0, 0] = cum_ref[0]
    token[0] = cum_ref[0, :8, :LANES]
    c = jnp.concatenate(
        conv_rows_of(raw, w, band(), span, span + STATE_WIDTH, STATE_WIDTH), axis=0
    )
    c_all[0, 0] = c

    b_rows = bmap[0].astype(f32).T.astype(bf16)
    scores = jnp.dot(b_rows, c, preferred_element_type=f32)
    src = lax.broadcasted_iota(jnp.int32, (HALF, HALF), 0)
    dst = lax.broadcasted_iota(jnp.int32, (HALF, HALF), 1)
    causal = src <= dst
    s00 = jnp.where(causal, scores[:HALF, :HALF], 0.0)
    s01 = scores[:HALF, HALF:]
    s11 = jnp.where(causal, scores[HALF:, HALF:], 0.0)
    r = run_ref[0] * LOG2E
    q = (r - jnp.log(dt_ref[0]) * LOG2E).T
    if not first:
        cc = jnp.concatenate([c, c], axis=0)
        entered = jnp.exp2(r)
    for h in range(heads):
        at = h * HEAD_DIM
        r0, r1 = r[h : h + 1, :HALF], r[h : h + 1, HALF:]
        q0, q1 = q[:HALF, h : h + 1], q[HALF:, h : h + 1]
        w00 = (s00 * jnp.exp2(jnp.minimum(r0 - q0, CAP))).astype(bf16)
        w01 = (s01 * jnp.exp2(r1 - q0)).astype(bf16)
        w11 = (s11 * jnp.exp2(jnp.minimum(r1 - q1, CAP))).astype(bf16)
        x = xact[0, at : at + HEAD_DIM, :]
        y0 = jnp.dot(x[:, :HALF], w00, preferred_element_type=f32)
        y1 = jnp.dot(x, jnp.concatenate([w01, w11], axis=0), preferred_element_type=f32)
        y = jnp.concatenate([y0, y1], axis=1) + skip[0, h : h + 1, :] * x.astype(f32)
        if not first:
            if at % WIDE == 0:
                both = jnp.concatenate(split(state[0, at : at + WIDE, :]), axis=1)
                carried = jnp.dot(both, cc, preferred_element_type=f32)
            y = y + entered[h : h + 1, :] * carried[at % WIDE : at % WIDE + HEAD_DIM, :]
        mixed[0, 0, at : at + HEAD_DIM, :] = y


def block_chunk(chunk, chunks, got, w, xact, bmap, run, dt, cum, state, skip, wholes, dims):
    spg, rows, heads, span, piece_heads = dims
    groups = w.shape[0]

    def whole(*shape):
        return pl.BlockSpec((1, 1) + shape, lambda g: (g, chunk, 0, 0))

    args, specs = chunk_specs(got, chunk, dims)
    args += [w, xact, bmap, run, dt, cum, state, skip]
    specs += [
        per_group(span + 2 * STATE_WIDTH, 4),
        per_group(span, BLOCK),
        per_group(STATE_WIDTH, BLOCK),
        per_group(heads, BLOCK),
        per_group(heads, BLOCK),
        per_group(heads, BLOCK),
        per_group(span, STATE_WIDTH),
        per_group(heads, 1),
    ]
    aliases = {}
    for i, array in enumerate(wholes or ()):
        aliases[len(args)] = i
        args.append(array)
        specs.append(pl.BlockSpec(memory_space=pl.ANY))

    def out(dtype, *shape):
        return jax.ShapeDtypeStruct((groups,) + shape, dtype)

    *wholes, token = pl.pallas_call(
        functools.partial(block_kernel, dims, chunk == 0),
        grid=(groups,),
        in_specs=specs,
        out_specs=[
            whole(span, BLOCK),
            whole(span, BLOCK),
            whole(STATE_WIDTH, BLOCK),
            whole(heads, BLOCK),
            per_group(8, LANES),
        ],
        out_shape=[
            out(f32, chunks, span, BLOCK),
            out(bf16, chunks, span, BLOCK),
            out(bf16, chunks, STATE_WIDTH, BLOCK),
            out(f32, chunks, heads, BLOCK),
            out(f32, 8, LANES),
        ],
        scratch_shapes=[pltpu.VMEM((rows * spg, LANES + BLOCK), f32)],
        input_output_aliases=aliases,
        compiler_params=params(),
        cost_estimate=pl.CostEstimate(flops=4 * 10**9, bytes_accessed=10**7, transcendentals=10**6),
        name="block_chunk",
    )(*args)
    return wholes, token


def relay_kernel(piece_heads, src, token, dst):
    count = src.shape[0]
    rows = piece_heads * HEAD_DIM
    for h in range(piece_heads):
        at = h * HEAD_DIM
        held = jnp.zeros((HEAD_DIM, STATE_WIDTH), f32)
        for d in range(count):
            high, low = split(held)
            dst[d, at : at + HEAD_DIM, :STATE_WIDTH] = high
            dst[d, at : at + HEAD_DIM, STATE_WIDTH:] = low
            held = src[d, rows + h : rows + h + 1, :] * held + src[d, at : at + HEAD_DIM, :]


def relay(packed, token, piece_heads):
    count = packed.shape[0]
    rows = piece_heads * HEAD_DIM
    return pl.pallas_call(
        functools.partial(relay_kernel, piece_heads),
        in_specs=[pl.BlockSpec(memory_space=pltpu.VMEM), pl.BlockSpec(memory_space=pl.ANY)],
        out_shape=jax.ShapeDtypeStruct((count, rows, 2 * STATE_WIDTH), bf16),
        compiler_params=params(),
        name="relay",
    )(packed, token)


def final_kernel(dims, mixed, gate, c_ref, cum, state, gain, out, kept, gains):
    heads, span = dims

    @pl.when(pl.program_id(1) == 0)
    def _():
        gains[...] = jnp.broadcast_to(gain[0], (span, LANES))

    c = c_ref[0, 0]
    cc = jnp.concatenate([c, c], axis=0)
    entered = jnp.exp(cum[0, 0])
    total = jnp.zeros((HEAD_DIM, BLOCK), f32)
    for h in range(heads):
        at = h * HEAD_DIM
        if at % WIDE == 0:
            carried = jnp.dot(state[0, at : at + WIDE, :], cc, preferred_element_type=f32)
        v = carried[at % WIDE : at % WIDE + HEAD_DIM, :] * entered[h : h + 1, :]
        v = mixed[0, 0, at : at + HEAD_DIM, :] + v
        v = v * silu(gate[0, 0, at : at + HEAD_DIM, :].astype(f32))
        kept[at : at + HEAD_DIM, :] = v
        total = total + v * v
    mean = jnp.sum(total, axis=0, keepdims=True) * (1.0 / span)
    factor = lax.rsqrt(mean + EPSILON)
    row = lax.broadcasted_iota(jnp.int32, (BLOCK, BLOCK), 0)
    col = lax.broadcasted_iota(jnp.int32, (BLOCK, BLOCK), 1)
    eye = jnp.where(row == col, 1.0, 0.0).astype(bf16)
    for at in range(0, span, BLOCK):
        scale = gains[at : at + BLOCK, :]
        scale = jnp.concatenate([scale] * (BLOCK // LANES), axis=1)
        tile = (kept[at : at + BLOCK, :] * factor * scale).astype(bf16)
        turned = lax.dot_general(eye, tile, NT, preferred_element_type=f32)
        out[:, at : at + BLOCK] = turned.astype(bf16)


def finish(mixed, gate, c_all, cum, state, gain):
    groups, chunks, span, _ = mixed.shape
    heads = cum.shape[2]

    def tile(rows):
        return pl.BlockSpec((1, 1, rows, BLOCK), lambda g, c: (g, c, 0, 0))

    return pl.pallas_call(
        functools.partial(final_kernel, (heads, span)),
        grid=(groups, chunks),
        in_specs=[
            tile(span),
            tile(span),
            tile(STATE_WIDTH),
            tile(heads),
            pl.BlockSpec((1, span, 2 * STATE_WIDTH), lambda g, c: (g, 0, 0)),
            pl.BlockSpec((1, span, 1), lambda g, c: (g, 0, 0)),
        ],
        out_specs=pl.BlockSpec((BLOCK, span), lambda g, c: (c, g)),
        out_shape=jax.ShapeDtypeStruct((chunks * BLOCK, groups * span), bf16),
        scratch_shapes=[pltpu.VMEM((span, BLOCK), f32), pltpu.VMEM((span, LANES), f32)],
        compiler_params=params(),
        name="finish",
    )(mixed, gate, c_all, cum, state, gain)


def exchange(array):
    return lax.all_to_all(array, "seq", split_axis=0, concat_axis=0, tiled=True)


def per_device(projected, conv_weight, dt_bias, a_log, d_skip, norm_gain):
    seq_count = lax.axis_size("seq")
    groups = conv_weight.shape[1]
    heads = dt_bias.shape[0] // groups
    span = heads * HEAD_DIM
    rows, all_tokens = projected.shape
    local_tokens = all_tokens // seq_count
    chunks = local_tokens // BLOCK
    spg = seq_count // groups
    piece_heads = groups * heads // seq_count
    dims = (spg, rows, heads, span, piece_heads)

    w = jnp.transpose(conv_weight, (1, 2, 0))
    bias = dt_bias.reshape(groups, heads, 1)
    rate = a_log.reshape(groups, heads, 1)
    skip = d_skip.reshape(groups, heads, 1)
    gain = norm_gain.reshape(groups, span, 1)
    state = jnp.zeros((groups, span, STATE_WIDTH), f32)
    lead = jnp.zeros((groups, heads, LANES), f32)

    cut = cut_chunk(projected, seq_count, 0, chunks, None)
    got = [exchange(cut)]
    if chunks > 1:
        got.append(exchange(cut_chunk(projected, seq_count, 1, chunks, cut)))
    wholes = None
    for c in range(chunks):
        xact, bmap, run, dt, cum, new, lead = state_chunk(
            c, chunks, got, w, bias, rate, state, lead, dims
        )
        wholes, token = block_chunk(
            c, chunks, got, w, xact, bmap, run, dt, cum, state, skip, wholes, dims
        )
        if c + 2 < chunks:
            got.append(exchange(cut_chunk(projected, seq_count, c + 2, chunks, token)))
        state = new
    entering = exchange(relay(exchange(state), token, piece_heads))
    mixed, gate_all, c_all, cum_all = wholes
    entering = entering.reshape(groups, span, 2 * STATE_WIDTH)
    return finish(mixed, gate_all, c_all, cum_all, entering, gain)


def solution(mesh):
    in_specs = (P(("tp", "seq"), None), P(None, "tp", None), P("tp"), P("tp"), P("tp"), P("tp"))
    return jax.shard_map(
        per_device, mesh=mesh, in_specs=in_specs, out_specs=P("seq", "tp"), check_vma=False
    )
```

```python
import functools

import jax
import jax.numpy as jnp
from jax import lax
from jax.experimental import pallas as pl
from jax.experimental.pallas import tpu as pltpu
from jax.sharding import PartitionSpec as P

HEAD_DIM = 64
STATE_WIDTH = 128
BLOCK = 256
LANES = 128
HALF = BLOCK // 2
WIDE = 256
LOG2E = 1.4426950408889634
CAP = 80.0
EPSILON = 1e-05

f32 = jnp.float32
bf16 = jnp.bfloat16
NT = (((1,), (1,)), ((), ()))


def params():
    return pltpu.CompilerParams(vmem_limit_bytes=60 * 2**20)


def silu(v):
    half = 0.5 * v
    return half + half * jnp.tanh(half)


def softplus(v):
    e = jnp.exp(-jnp.abs(v))
    u = 1.0 + e
    gap = u - 1.0
    tiny = gap == 0.0
    log_part = jnp.where(tiny, e, jnp.log(u) * (e / jnp.where(tiny, 1.0, gap)))
    return jnp.maximum(v, 0.0) + log_part


def per_group(*shape):
    return pl.BlockSpec((1,) + shape, lambda g: (g,) + (0,) * len(shape))


RIM = 4


def rim_row(rows):
    return -(-rows // 16) * 16


def cut_kernel(chunk, chunks, count, me_ref, src, *refs):
    refs = refs[len(refs) - count - (3 if chunk else 6) :]
    dsts, refs = refs[:count], refs[count:]
    rows, all_tokens = src.shape
    tokens = all_tokens // count
    me = me_ref[0]
    order = list(range(1, count)) + [0]
    held, in_sems, out_sems = refs[:3]
    sent = held if chunk else refs[4]

    def fetch(k):
        at = pl.multiple_of((me ^ k) * tokens + chunk * BLOCK, LANES)
        return pltpu.make_async_copy(src.at[:, pl.ds(at, BLOCK)], held.at[k], in_sems.at[k])

    def place(k):
        return pltpu.make_async_copy(sent.at[k], dsts[k], out_sems.at[k])

    if chunk:
        for k in order:
            fetch(k).start()
        for k in order:
            fetch(k).wait()
            place(k).start()
    else:
        windows, rim_sems = refs[3], refs[5]

        def window(k):
            at = jnp.maximum((me ^ k) * tokens - LANES, 0)
            at = pl.multiple_of(at, LANES)
            return pltpu.make_async_copy(src.at[:, pl.ds(at, LANES)], windows.at[k], rim_sems.at[k])

        for k in order:
            window(k).start()
            fetch(k).start()
        row = lax.broadcasted_iota(jnp.int32, (16, LANES), 0)
        col = lax.broadcasted_iota(jnp.int32, (16, LANES), 1)
        wide = lax.broadcasted_iota(jnp.int32, (16, BLOCK), 0) // RIM
        hit = col == lax.rem(row, RIM) + LANES - RIM
        at = rim_row(rows)
        for k in order:
            window(k).wait()
            pick = jnp.where(hit & ((me ^ k) > 0), 1.0, 0.0).astype(bf16)
            rims = lax.dot_general(pick, windows[k], NT, preferred_element_type=f32)
            merged = jnp.zeros((16, BLOCK), f32)
            for j in range(-(-rows // BLOCK)):
                part = rims[:, j * BLOCK : min((j + 1) * BLOCK, rows)]
                if part.shape[1] < BLOCK:
                    fill = jnp.zeros((16, BLOCK - part.shape[1]), f32)
                    part = jnp.concatenate([part, fill], axis=1)
                merged = jnp.where(wide == j, part, merged)
            sent[k, at : at + 16, :] = merged.astype(bf16)
            fetch(k).wait()
            sent[k, :rows, :] = held[k]
            place(k).start()
    for k in order:
        place(k).wait()


def cut_chunk(projected, me, count, chunk, chunks, token):
    rows = projected.shape[0]
    args = [me, projected]
    out_rows = rows
    sems = pltpu.SemaphoreType.DMA((count,))
    scratch = [pltpu.VMEM((count, rows, BLOCK), bf16), sems, sems]
    if chunk == 0:
        out_rows = rim_row(rows) + 16
        scratch += [
            pltpu.VMEM((count, rows, LANES), bf16),
            pltpu.VMEM((count, out_rows, BLOCK), bf16),
            sems,
        ]
    if token is not None:
        args.append(token)
    return pl.pallas_call(
        functools.partial(cut_kernel, chunk, chunks, count),
        in_specs=[pl.BlockSpec(memory_space=pltpu.SMEM)]
        + [pl.BlockSpec(memory_space=pl.ANY)] * (len(args) - 1),
        out_specs=[pl.BlockSpec(memory_space=pl.ANY)] * count,
        out_shape=[jax.ShapeDtypeStruct((out_rows, BLOCK), bf16)] * count,
        scratch_shapes=scratch,
        compiler_params=params(),
        name="cut_chunk",
    )(*args)


def load_slabs(me_ref, recv, prev, slabs, tails, sems, tail_sems, per_group_slabs):
    count = len(recv)
    me = me_ref[0]
    group = pl.program_id(0)

    def copies(k, s):
        moves = [pltpu.make_async_copy(recv[k], slabs.at[s], sems.at[s])]
        if prev:
            moves.append(
                pltpu.make_async_copy(
                    prev[k].at[:, BLOCK - LANES :], tails.at[s], tail_sems.at[s]
                )
            )
        return moves

    @pl.when(group == 0)
    def _():
        for k in range(count):
            for move in copies(k, me ^ k):
                move.start()

    for i in range(per_group_slabs):
        for move in copies(0, group * per_group_slabs + i):
            move.wait()


def gather_rows(slabs, tails, raw, rows, low, high, ahead=True):
    spg = raw.shape[0] // rows
    base = pl.program_id(0) * spg
    for s in range(spg):
        a = max(low - s * rows, 0) // 16 * 16
        b = min(-(-(high - s * rows) // 16) * 16, rows)
        if b <= a:
            continue
        at = s * rows + a
        raw[at : at + b - a, LANES:] = slabs[base + s, a:b, :].astype(f32)
        if not ahead:
            continue
        if tails is not None:
            raw[at : at + b - a, :LANES] = tails[base + s, a:b, :].astype(f32)
            continue
        first = rim_row(rows)
        rims = slabs[base + s, first : first + 16, :].astype(f32)
        tall = jnp.concatenate([jnp.zeros((LANES - 16, BLOCK), f32), rims], axis=0)
        for j in range(-(-rows // BLOCK)):
            c, d = max(a, j * BLOCK), min(b, (j + 1) * BLOCK)
            if d <= c:
                continue
            shift = LANES - RIM - (LANES - 16 + RIM * j)
            moved = (pltpu.roll(tall, shift, 0) if shift else tall).T
            raw[s * rows + c : s * rows + d, :LANES] = moved[c - j * BLOCK : d - j * BLOCK]


def band():
    row = lax.broadcasted_iota(jnp.int32, (2 * LANES, 3 * LANES), 0)
    col = lax.broadcasted_iota(jnp.int32, (2 * LANES, 3 * LANES), 1)
    tap = col // LANES
    return jnp.where(row == col - tap * LANES + LANES - 3 + tap, 1.0, 0.0).astype(bf16)


def conv_rows_of(raw, w, picks, span, r, height):
    low = raw[span + r : span + r + height, :].astype(bf16)
    shifted = [
        jnp.dot(low[:, at : at + 2 * LANES], picks, preferred_element_type=f32)
        for at in range(0, BLOCK, LANES)
    ]
    tiles = []
    for q in range(0, height, HEAD_DIM):
        at = r + q
        taps = [
            jnp.broadcast_to(w[0, at : at + HEAD_DIM, k : k + 1], (HEAD_DIM, LANES))
            for k in range(4)
        ]
        parts = []
        for i, three in enumerate(shifted):
            summed = None
            for k in range(3):
                part = taps[k] * three[q : q + HEAD_DIM, k * LANES : (k + 1) * LANES]
                summed = part if summed is None else summed + part
            own = raw[span + at : span + at + HEAD_DIM, (i + 1) * LANES : (i + 2) * LANES]
            parts.append(silu(summed + taps[3] * own).astype(bf16))
        tiles.append(jnp.concatenate(parts, axis=1))
    return tiles


def take_slabs(count, spg, first, refs):
    recv, refs = refs[:count], refs[count:]
    prev = ()
    if not first:
        prev, refs = refs[:count], refs[count:]
    *refs, slabs, tails, sems, tail_sems = refs
    return refs, (recv, prev, slabs, tails, sems, tail_sems, spg), slabs, tails if prev else None


def state_kernel(dims, first, last, me_ref, *refs):
    count, spg, rows, heads, span, piece_heads = dims
    refs, moves, slabs, tails = take_slabs(count, spg, first, refs)
    w, bias, a_log, state_in, lead_in = refs[:5]
    xact, bmap, run_out, dt_out, cum_out, state_out, lead_out = refs[5:12]
    raw, xw = refs[12:]
    steps = 2 * span + 2 * STATE_WIDTH

    load_slabs(me_ref, *moves)
    gather_rows(slabs, tails, raw, rows, steps, steps + heads, False)
    gather_rows(slabs, tails, raw, rows, span, 2 * span + STATE_WIDTH)
    dt = softplus(raw[steps : steps + heads, LANES:] + bias[0])
    log_decay = -jnp.exp(a_log[0]) * dt
    lane = lax.broadcasted_iota(jnp.int32, (heads, BLOCK), 1)
    run = log_decay
    shift = 1
    while shift < BLOCK:
        run = run + jnp.where(lane >= shift, pltpu.roll(run, shift, 1), 0.0)
        shift *= 2
    final = run[:, BLOCK - 1 :]
    scale = jnp.exp(final - run) * dt
    cum = run + lead_in[0][:, :1]
    run_out[0] = run
    dt_out[0] = dt
    cum_out[0] = cum
    lead = jnp.broadcast_to(cum[:, BLOCK - 1 :], (heads, LANES))
    lead_out[0] = lead
    keep = jnp.broadcast_to(jnp.exp(final), (heads, LANES))

    picks = band()
    for i, tile in enumerate(conv_rows_of(raw, w, picks, span, span, STATE_WIDTH)):
        bmap[0, i * HEAD_DIM : (i + 1) * HEAD_DIM, :] = tile
    for r in range(0, span, WIDE):
        for i, tile in enumerate(conv_rows_of(raw, w, picks, span, r, WIDE)):
            at = r + i * HEAD_DIM
            h = at // HEAD_DIM
            xact[0, at : at + HEAD_DIM, :] = tile
            xw[at : at + HEAD_DIM, :] = (tile.astype(f32) * scale[h : h + 1, :]).astype(bf16)
    update = lax.dot_general(xw[...], bmap[0], NT, preferred_element_type=f32)
    for h in range(heads):
        r = h * HEAD_DIM
        new = update[r : r + HEAD_DIM, :]
        if not first:
            new = keep[h : h + 1, :] * state_in[0, r : r + HEAD_DIM, :] + new
        if last:
            at = (h % piece_heads) * HEAD_DIM
            state_out[h // piece_heads, at : at + HEAD_DIM, :] = new
        else:
            state_out[0, r : r + HEAD_DIM, :] = new
    if last:
        decay = jnp.exp(lead)
        for h in range(heads):
            at = piece_heads * HEAD_DIM + h % piece_heads
            state_out[h // piece_heads, at : at + 1, :] = decay[h : h + 1, :]


def chunk_specs(me, got, chunk, dims):
    count, spg, rows = dims[:3]
    args = [me, *got[chunk]] + (list(got[chunk - 1]) if chunk else [])
    specs = [pl.BlockSpec(memory_space=pltpu.SMEM)]
    specs += [pl.BlockSpec(memory_space=pl.ANY)] * (len(args) - 1)
    held = got[chunk - 1][0].shape[0] if chunk else 16
    scratch = [
        pltpu.VMEM((count,) + got[chunk][0].shape, bf16),
        pltpu.VMEM((count, held, LANES), bf16),
        pltpu.SemaphoreType.DMA((count,)),
        pltpu.SemaphoreType.DMA((count,)),
    ]
    return args, specs, scratch


def state_chunk(chunk, chunks, me, got, w, bias, a_log, state, lead, dims):
    count, spg, rows, heads, span, piece_heads = dims
    groups = w.shape[0]
    conv_rows = span + 2 * STATE_WIDTH
    last = chunk == chunks - 1
    if last:
        packed = piece_heads * HEAD_DIM + 8
        state_shape = jax.ShapeDtypeStruct((groups * spg, packed, STATE_WIDTH), f32)
        state_spec = pl.BlockSpec((spg, packed, STATE_WIDTH), lambda g: (g, 0, 0))
    else:
        state_shape = jax.ShapeDtypeStruct((groups, span, STATE_WIDTH), f32)
        state_spec = per_group(span, STATE_WIDTH)

    def out(dtype, *shape):
        return jax.ShapeDtypeStruct((groups,) + shape, dtype)

    args, specs, scratch = chunk_specs(me, got, chunk, dims)
    return pl.pallas_call(
        functools.partial(state_kernel, dims, chunk == 0, last),
        grid=(groups,),
        in_specs=specs
        + [
            per_group(conv_rows, 4),
            per_group(heads, 1),
            per_group(heads, 1),
            per_group(span, STATE_WIDTH),
            per_group(heads, LANES),
        ],
        out_specs=[
            per_group(span, BLOCK),
            per_group(STATE_WIDTH, BLOCK),
            per_group(heads, BLOCK),
            per_group(heads, BLOCK),
            per_group(heads, BLOCK),
            state_spec,
            per_group(heads, LANES),
        ],
        out_shape=[
            out(bf16, span, BLOCK),
            out(bf16, STATE_WIDTH, BLOCK),
            out(f32, heads, BLOCK),
            out(f32, heads, BLOCK),
            out(f32, heads, BLOCK),
            state_shape,
            out(f32, heads, LANES),
        ],
        scratch_shapes=[
            pltpu.VMEM((rows * spg, LANES + BLOCK), f32),
            pltpu.VMEM((span, BLOCK), bf16),
        ]
        + scratch,
        compiler_params=params(),
        cost_estimate=pl.CostEstimate(flops=4 * 10**9, bytes_accessed=10**7, transcendentals=10**6),
        name="state_chunk",
    )(*args, w, bias, a_log, state, lead)


def split(v):
    high = v.astype(bf16)
    return high, (v - high.astype(f32)).astype(bf16)


def block_kernel(dims, first, me_ref, *refs):
    count, spg, rows, heads, span, piece_heads = dims
    refs, moves, slabs, tails = take_slabs(count, spg, first, refs)
    w, xact, bmap, run_ref, dt_ref, cum_ref, state, skip = refs[:8]
    mixed, gate_all, c_all, cum_all, token, raw = refs[-6:]
    conv_rows = span + 2 * STATE_WIDTH
    load_slabs(me_ref, *moves)
    gather_rows(slabs, tails, raw, rows, 2 * span + STATE_WIDTH, span + conv_rows)
    gather_rows(slabs, tails, raw, rows, 0, span, False)
    gate_all[0, 0] = raw[:span, LANES:].astype(bf16)
    cum_all[0, 0] = cum_ref[0]
    token[0] = cum_ref[0, :8, :LANES]
    c = jnp.concatenate(
        conv_rows_of(raw, w, band(), span, span + STATE_WIDTH, STATE_WIDTH), axis=0
    )
    c_all[0, 0] = c

    b_rows = bmap[0].astype(f32).T.astype(bf16)
    scores = jnp.dot(b_rows, c, preferred_element_type=f32)
    src = lax.broadcasted_iota(jnp.int32, (HALF, HALF), 0)
    dst = lax.broadcasted_iota(jnp.int32, (HALF, HALF), 1)
    causal = src <= dst
    s00 = jnp.where(causal, scores[:HALF, :HALF], 0.0)
    s01 = scores[:HALF, HALF:]
    s11 = jnp.where(causal, scores[HALF:, HALF:], 0.0)
    r = run_ref[0] * LOG2E
    q = (r - jnp.log(dt_ref[0]) * LOG2E).T
    if not first:
        cc = jnp.concatenate([c, c], axis=0)
        entered = jnp.exp2(r)
    for h in range(heads):
        at = h * HEAD_DIM
        r0, r1 = r[h : h + 1, :HALF], r[h : h + 1, HALF:]
        q0, q1 = q[:HALF, h : h + 1], q[HALF:, h : h + 1]
        w00 = (s00 * jnp.exp2(jnp.minimum(r0 - q0, CAP))).astype(bf16)
        w01 = (s01 * jnp.exp2(r1 - q0)).astype(bf16)
        w11 = (s11 * jnp.exp2(jnp.minimum(r1 - q1, CAP))).astype(bf16)
        x = xact[0, at : at + HEAD_DIM, :]
        y0 = jnp.dot(x[:, :HALF], w00, preferred_element_type=f32)
        y1 = jnp.dot(x, jnp.concatenate([w01, w11], axis=0), preferred_element_type=f32)
        y = jnp.concatenate([y0, y1], axis=1) + skip[0, h : h + 1, :] * x.astype(f32)
        if not first:
            if at % WIDE == 0:
                both = jnp.concatenate(split(state[0, at : at + WIDE, :]), axis=1)
                carried = jnp.dot(both, cc, preferred_element_type=f32)
            y = y + entered[h : h + 1, :] * carried[at % WIDE : at % WIDE + HEAD_DIM, :]
        mixed[0, 0, at : at + HEAD_DIM, :] = y


def block_chunk(chunk, chunks, me, got, w, xact, bmap, run, dt, cum, state, skip, wholes, dims):
    count, spg, rows, heads, span, piece_heads = dims
    groups = w.shape[0]

    def whole(*shape):
        return pl.BlockSpec((1, 1) + shape, lambda g: (g, chunk, 0, 0))

    args, specs, scratch = chunk_specs(me, got, chunk, dims)
    args += [w, xact, bmap, run, dt, cum, state, skip]
    specs += [
        per_group(span + 2 * STATE_WIDTH, 4),
        per_group(span, BLOCK),
        per_group(STATE_WIDTH, BLOCK),
        per_group(heads, BLOCK),
        per_group(heads, BLOCK),
        per_group(heads, BLOCK),
        per_group(span, STATE_WIDTH),
        per_group(heads, 1),
    ]
    aliases = {}
    for i, array in enumerate(wholes or ()):
        aliases[len(args)] = i
        args.append(array)
        specs.append(pl.BlockSpec(memory_space=pl.ANY))

    def out(dtype, *shape):
        return jax.ShapeDtypeStruct((groups,) + shape, dtype)

    *wholes, token = pl.pallas_call(
        functools.partial(block_kernel, dims, chunk == 0),
        grid=(groups,),
        in_specs=specs,
        out_specs=[
            whole(span, BLOCK),
            whole(span, BLOCK),
            whole(STATE_WIDTH, BLOCK),
            whole(heads, BLOCK),
            per_group(8, LANES),
        ],
        out_shape=[
            out(f32, chunks, span, BLOCK),
            out(bf16, chunks, span, BLOCK),
            out(bf16, chunks, STATE_WIDTH, BLOCK),
            out(f32, chunks, heads, BLOCK),
            out(f32, 8, LANES),
        ],
        scratch_shapes=[pltpu.VMEM((rows * spg, LANES + BLOCK), f32)] + scratch,
        input_output_aliases=aliases,
        compiler_params=params(),
        cost_estimate=pl.CostEstimate(flops=4 * 10**9, bytes_accessed=10**7, transcendentals=10**6),
        name="block_chunk",
    )(*args)
    return wholes, token


def relay_kernel(piece_heads, src, token, dst):
    count = src.shape[0]
    rows = piece_heads * HEAD_DIM
    for h in range(piece_heads):
        at = h * HEAD_DIM
        held = jnp.zeros((HEAD_DIM, STATE_WIDTH), f32)
        for d in range(count):
            high, low = split(held)
            dst[d, at : at + HEAD_DIM, :STATE_WIDTH] = high
            dst[d, at : at + HEAD_DIM, STATE_WIDTH:] = low
            held = src[d, rows + h : rows + h + 1, :] * held + src[d, at : at + HEAD_DIM, :]


def relay(packed, token, piece_heads):
    count = packed.shape[0]
    rows = piece_heads * HEAD_DIM
    return pl.pallas_call(
        functools.partial(relay_kernel, piece_heads),
        in_specs=[pl.BlockSpec(memory_space=pltpu.VMEM), pl.BlockSpec(memory_space=pl.ANY)],
        out_shape=jax.ShapeDtypeStruct((count, rows, 2 * STATE_WIDTH), bf16),
        compiler_params=params(),
        name="relay",
    )(packed, token)


def final_kernel(dims, mixed, gate, c_ref, cum, state, gain, out, kept, gains):
    heads, span = dims

    @pl.when(pl.program_id(1) == 0)
    def _():
        gains[...] = jnp.broadcast_to(gain[0], (span, LANES))

    c = c_ref[0, 0]
    cc = jnp.concatenate([c, c], axis=0)
    entered = jnp.exp(cum[0, 0])
    total = jnp.zeros((HEAD_DIM, BLOCK), f32)
    for h in range(heads):
        at = h * HEAD_DIM
        if at % WIDE == 0:
            carried = jnp.dot(state[0, at : at + WIDE, :], cc, preferred_element_type=f32)
        v = carried[at % WIDE : at % WIDE + HEAD_DIM, :] * entered[h : h + 1, :]
        v = mixed[0, 0, at : at + HEAD_DIM, :] + v
        v = v * silu(gate[0, 0, at : at + HEAD_DIM, :].astype(f32))
        kept[at : at + HEAD_DIM, :] = v
        total = total + v * v
    mean = jnp.sum(total, axis=0, keepdims=True) * (1.0 / span)
    factor = lax.rsqrt(mean + EPSILON)
    row = lax.broadcasted_iota(jnp.int32, (BLOCK, BLOCK), 0)
    col = lax.broadcasted_iota(jnp.int32, (BLOCK, BLOCK), 1)
    eye = jnp.where(row == col, 1.0, 0.0).astype(bf16)
    for at in range(0, span, BLOCK):
        scale = gains[at : at + BLOCK, :]
        scale = jnp.concatenate([scale] * (BLOCK // LANES), axis=1)
        tile = (kept[at : at + BLOCK, :] * factor * scale).astype(bf16)
        turned = lax.dot_general(eye, tile, NT, preferred_element_type=f32)
        out[:, at : at + BLOCK] = turned.astype(bf16)


def finish(mixed, gate, c_all, cum, state, gain):
    groups, chunks, span, _ = mixed.shape
    heads = cum.shape[2]

    def tile(rows):
        return pl.BlockSpec((1, 1, rows, BLOCK), lambda g, c: (g, c, 0, 0))

    return pl.pallas_call(
        functools.partial(final_kernel, (heads, span)),
        grid=(groups, chunks),
        in_specs=[
            tile(span),
            tile(span),
            tile(STATE_WIDTH),
            tile(heads),
            pl.BlockSpec((1, span, 2 * STATE_WIDTH), lambda g, c: (g, 0, 0)),
            pl.BlockSpec((1, span, 1), lambda g, c: (g, 0, 0)),
        ],
        out_specs=pl.BlockSpec((BLOCK, span), lambda g, c: (c, g)),
        out_shape=jax.ShapeDtypeStruct((chunks * BLOCK, groups * span), bf16),
        scratch_shapes=[pltpu.VMEM((span, BLOCK), f32), pltpu.VMEM((span, LANES), f32)],
        compiler_params=params(),
        name="finish",
    )(mixed, gate, c_all, cum, state, gain)


def swap(pieces):
    count = len(pieces)
    return [pieces[0]] + [
        lax.ppermute(pieces[k], "seq", [(i, i ^ k) for i in range(count)])
        for k in range(1, count)
    ]


def exchange(array):
    return lax.all_to_all(array, "seq", split_axis=0, concat_axis=0, tiled=True)


def per_device(projected, conv_weight, dt_bias, a_log, d_skip, norm_gain):
    seq_count = lax.axis_size("seq")
    groups = conv_weight.shape[1]
    heads = dt_bias.shape[0] // groups
    span = heads * HEAD_DIM
    rows, all_tokens = projected.shape
    local_tokens = all_tokens // seq_count
    chunks = local_tokens // BLOCK
    spg = seq_count // groups
    piece_heads = groups * heads // seq_count
    dims = (seq_count, spg, rows, heads, span, piece_heads)

    w = jnp.transpose(conv_weight, (1, 2, 0))
    bias = dt_bias.reshape(groups, heads, 1)
    rate = a_log.reshape(groups, heads, 1)
    skip = d_skip.reshape(groups, heads, 1)
    gain = norm_gain.reshape(groups, span, 1)
    state = jnp.zeros((groups, span, STATE_WIDTH), f32)
    lead = jnp.zeros((groups, heads, LANES), f32)

    me = lax.axis_index("seq").astype(jnp.int32).reshape(1)
    cut = cut_chunk(projected, me, seq_count, 0, chunks, None)
    got = [swap(cut)]
    if chunks > 1:
        got.append(swap(cut_chunk(projected, me, seq_count, 1, chunks, cut[0])))
    wholes = None
    for c in range(chunks):
        xact, bmap, run, dt, cum, new, lead = state_chunk(
            c, chunks, me, got, w, bias, rate, state, lead, dims
        )
        wholes, token = block_chunk(
            c, chunks, me, got, w, xact, bmap, run, dt, cum, state, skip, wholes, dims
        )
        if c + 2 < chunks:
            got.append(swap(cut_chunk(projected, me, seq_count, c + 2, chunks, token)))
        state = new
    entering = exchange(relay(exchange(state), token, piece_heads))
    mixed, gate_all, c_all, cum_all = wholes
    entering = entering.reshape(groups, span, 2 * STATE_WIDTH)
    return finish(mixed, gate_all, c_all, cum_all, entering, gain)


def solution(mesh):
    in_specs = (P(("tp", "seq"), None), P(None, "tp", None), P("tp"), P("tp"), P("tp"), P("tp"))
    return jax.shard_map(
        per_device, mesh=mesh, in_specs=in_specs, out_specs=P("seq", "tp"), check_vma=False
    )
```

```python
import functools

import jax
import jax.numpy as jnp
from jax import lax
from jax.experimental import pallas as pl
from jax.experimental.pallas import tpu as pltpu
from jax.sharding import PartitionSpec as P

HEAD_DIM = 64
STATE_WIDTH = 128
BLOCK = 256
LANES = 128
HALF = BLOCK // 2
WIDE = 256
LOG2E = 1.4426950408889634
CAP = 80.0
EPSILON = 1e-05

f32 = jnp.float32
bf16 = jnp.bfloat16
NT = (((1,), (1,)), ((), ()))


def params(mib=60):
    return pltpu.CompilerParams(vmem_limit_bytes=mib * 2**20)


def silu(v):
    half = 0.5 * v
    return half + half * jnp.tanh(half)


def softplus(v):
    e = jnp.exp(-jnp.abs(v))
    u = 1.0 + e
    gap = u - 1.0
    tiny = gap == 0.0
    log_part = jnp.where(tiny, e, jnp.log(u) * (e / jnp.where(tiny, 1.0, gap)))
    return jnp.maximum(v, 0.0) + log_part


def per_group(*shape):
    return pl.BlockSpec((1,) + shape, lambda g: (g,) + (0,) * len(shape))


RIM = 4


def rim_rows(rows):
    base = rows // 16 * 16
    height = -(-(rows - base + RIM) // 8) * 8
    assert height <= 16
    return base, height


def cut_kernel(low, count, src, *refs):
    refs = refs[len(refs) - (4 if low else 7) :]
    dst, held, in_sems, out_sems = refs[:4]
    rows, all_tokens = src.shape
    tokens = all_tokens // count
    width = dst.shape[2]
    sent = held if low else refs[5]

    def fetch(d):
        at = d * tokens + low
        return pltpu.make_async_copy(src.at[:, at : at + width], held.at[d], in_sems.at[d])

    def place(d):
        return pltpu.make_async_copy(sent.at[d], dst.at[d], out_sems.at[d])

    if low:
        for d in range(count):
            fetch(d).start()
        for d in range(count):
            fetch(d).wait()
            place(d).start()
    else:
        windows, rim_sems = refs[4], refs[6]

        def window(d):
            at = d * tokens - LANES
            return pltpu.make_async_copy(src.at[:, at : at + LANES], windows.at[d], rim_sems.at[d])

        for d in range(count):
            if d:
                window(d).start()
            fetch(d).start()
        base, height = rim_rows(rows)
        row = lax.broadcasted_iota(jnp.int32, (height, LANES), 0) - (rows - base)
        col = lax.broadcasted_iota(jnp.int32, (height, LANES), 1)
        hit = (col == row + LANES - RIM) & (row >= 0) & (row < RIM)
        pick = jnp.where(hit, 1.0, 0.0).astype(bf16)
        for d in range(count):
            fetch(d).wait()
            sent[d, :base, :] = held[d, :base, :]
            end = held[d, base:rows, :].astype(f32)
            end = jnp.concatenate([end, jnp.zeros((height - end.shape[0], width), f32)], axis=0)
            if d:
                window(d).wait()
                rims = lax.dot_general(pick, windows[d], NT, preferred_element_type=f32)
                fill = jnp.zeros((height, width - rows), f32)
                end = end + jnp.concatenate([rims, fill], axis=1)
            sent[d, base : base + height, :] = end.astype(bf16)
            place(d).start()
    for d in range(count):
        place(d).wait()


def cut_blocks(projected, count, low, high, token):
    rows = projected.shape[0]
    width = high - low
    args = [projected]
    out_rows = rows
    sems = pltpu.SemaphoreType.DMA((count,))
    scratch = [pltpu.VMEM((count, rows, width), bf16), sems, sems]
    if low == 0:
        assert width >= rows
        out_rows = sum(rim_rows(rows))
        scratch += [
            pltpu.VMEM((count, rows, LANES), bf16),
            pltpu.VMEM((count, out_rows, width), bf16),
            sems,
        ]
    if token is not None:
        args.append(token)
    return pl.pallas_call(
        functools.partial(cut_kernel, low, count),
        in_specs=[pl.BlockSpec(memory_space=pl.ANY)] * len(args),
        out_specs=pl.BlockSpec(memory_space=pl.ANY),
        out_shape=jax.ShapeDtypeStruct((count, out_rows, width), bf16),
        scratch_shapes=scratch,
        compiler_params=params(),
        name="cut_blocks",
    )(*args)


def gather_rows(recv, prev, raw, rows, low, high, ahead=True):
    for s in range(recv.shape[0]):
        a = max(low - s * rows, 0) // 16 * 16
        b = min(-(-(high - s * rows) // 16) * 16, rows)
        if b <= a:
            continue
        at = s * rows + a
        raw[at : at + b - a, LANES:] = recv[s, a:b, :BLOCK].astype(f32)
        if not ahead:
            continue
        if prev is not None:
            raw[at : at + b - a, :LANES] = prev[s, a:b, :].astype(f32)
            continue
        base, height = rim_rows(rows)
        wide = -(-rows // LANES) * LANES
        rims = recv[s, base : base + height, :wide].astype(f32)
        shift = height - RIM - (rows - base)
        if shift:
            rims = pltpu.roll(rims, shift, 0)
        tall = jnp.concatenate([jnp.zeros((LANES - height, wide), f32), rims], axis=0).T
        raw[at : at + b - a, :LANES] = tall[a:b]


def band():
    row = lax.broadcasted_iota(jnp.int32, (2 * LANES, 3 * LANES), 0)
    col = lax.broadcasted_iota(jnp.int32, (2 * LANES, 3 * LANES), 1)
    tap = col // LANES
    return jnp.where(row == col - tap * LANES + LANES - 3 + tap, 1.0, 0.0).astype(bf16)


def conv_rows_of(raw, w, picks, span, r, height):
    low = raw[span + r : span + r + height, :].astype(bf16)
    shifted = [
        jnp.dot(low[:, at : at + 2 * LANES], picks, preferred_element_type=f32)
        for at in range(0, BLOCK, LANES)
    ]
    tiles = []
    for q in range(0, height, HEAD_DIM):
        at = r + q
        taps = [
            jnp.broadcast_to(w[0, at : at + HEAD_DIM, k : k + 1], (HEAD_DIM, LANES))
            for k in range(4)
        ]
        parts = []
        for i, three in enumerate(shifted):
            summed = None
            for k in range(3):
                part = taps[k] * three[q : q + HEAD_DIM, k * LANES : (k + 1) * LANES]
                summed = part if summed is None else summed + part
            own = raw[span + at : span + at + HEAD_DIM, (i + 1) * LANES : (i + 2) * LANES]
            parts.append(silu(summed + taps[3] * own).astype(bf16))
        tiles.append(jnp.concatenate(parts, axis=1))
    return tiles


def state_kernel(dims, first, last, recv, *refs):
    spg, rows, heads, span, piece_heads = dims
    prev = None
    if not first:
        prev, refs = refs[0], refs[1:]
    w, bias, a_log, state_in, lead_in = refs[:5]
    xact, bmap, run_out, dt_out, cum_out, state_out, lead_out = refs[5:12]
    raw, xw = refs[12:]
    steps = 2 * span + 2 * STATE_WIDTH

    gather_rows(recv, prev, raw, rows, steps, steps + heads, False)
    gather_rows(recv, prev, raw, rows, span, 2 * span + STATE_WIDTH)
    dt = softplus(raw[steps : steps + heads, LANES:] + bias[0])
    log_decay = -jnp.exp(a_log[0]) * dt
    lane = lax.broadcasted_iota(jnp.int32, (heads, BLOCK), 1)
    run = log_decay
    shift = 1
    while shift < BLOCK:
        run = run + jnp.where(lane >= shift, pltpu.roll(run, shift, 1), 0.0)
        shift *= 2
    final = run[:, BLOCK - 1 :]
    scale = jnp.exp(final - run) * dt
    cum = run + lead_in[0][:, :1]
    run_out[0] = run
    dt_out[0] = dt
    cum_out[0] = cum
    lead = jnp.broadcast_to(cum[:, BLOCK - 1 :], (heads, LANES))
    lead_out[0] = lead
    keep = jnp.broadcast_to(jnp.exp(final), (heads, LANES))

    picks = band()
    for i, tile in enumerate(conv_rows_of(raw, w, picks, span, span, STATE_WIDTH)):
        bmap[0, i * HEAD_DIM : (i + 1) * HEAD_DIM, :] = tile
    for r in range(0, span, WIDE):
        for i, tile in enumerate(conv_rows_of(raw, w, picks, span, r, WIDE)):
            at = r + i * HEAD_DIM
            h = at // HEAD_DIM
            xact[0, at : at + HEAD_DIM, :] = tile
            xw[at : at + HEAD_DIM, :] = (tile.astype(f32) * scale[h : h + 1, :]).astype(bf16)
    update = lax.dot_general(xw[...], bmap[0], NT, preferred_element_type=f32)
    for h in range(heads):
        r = h * HEAD_DIM
        new = update[r : r + HEAD_DIM, :]
        if not first:
            new = keep[h : h + 1, :] * state_in[0, r : r + HEAD_DIM, :] + new
        if last:
            at = (h % piece_heads) * HEAD_DIM
            state_out[h // piece_heads, at : at + HEAD_DIM, :] = new
        else:
            state_out[0, r : r + HEAD_DIM, :] = new
    if last:
        decay = jnp.exp(lead)
        for h in range(heads):
            at = piece_heads * HEAD_DIM + h % piece_heads
            state_out[h // piece_heads, at : at + 1, :] = decay[h : h + 1, :]


def chunk_specs(got, chunk, dims):
    spg, rows = dims[:2]
    first, last = got
    ahead = first.shape[2] // BLOCK
    if chunk == 0:
        return [first], [pl.BlockSpec((spg,) + first.shape[1:], lambda g: (g, 0, 0))]
    at = 2 * chunk - 1
    prev = pl.BlockSpec((spg, first.shape[1], LANES), lambda g: (g, 0, at))
    if chunk < ahead:
        block = pl.BlockSpec((spg, first.shape[1], BLOCK), lambda g: (g, 0, chunk))
        return [first, first], [block, prev]
    return [last, first], [pl.BlockSpec((spg, rows, BLOCK), lambda g: (g, 0, 0)), prev]


def state_chunk(chunk, chunks, got, w, bias, a_log, state, lead, dims):
    spg, rows, heads, span, piece_heads = dims
    groups = w.shape[0]
    conv_rows = span + 2 * STATE_WIDTH
    last = chunk == chunks - 1
    if last:
        packed = piece_heads * HEAD_DIM + 8
        state_shape = jax.ShapeDtypeStruct((groups * spg, packed, STATE_WIDTH), f32)
        state_spec = pl.BlockSpec((spg, packed, STATE_WIDTH), lambda g: (g, 0, 0))
    else:
        state_shape = jax.ShapeDtypeStruct((groups, span, STATE_WIDTH), f32)
        state_spec = per_group(span, STATE_WIDTH)

    def out(dtype, *shape):
        return jax.ShapeDtypeStruct((groups,) + shape, dtype)

    args, specs = chunk_specs(got, chunk, dims)
    return pl.pallas_call(
        functools.partial(state_kernel, dims, chunk == 0, last),
        grid=(groups,),
        in_specs=specs
        + [
            per_group(conv_rows, 4),
            per_group(heads, 1),
            per_group(heads, 1),
            per_group(span, STATE_WIDTH),
            per_group(heads, LANES),
        ],
        out_specs=[
            per_group(span, BLOCK),
            per_group(STATE_WIDTH, BLOCK),
            per_group(heads, BLOCK),
            per_group(heads, BLOCK),
            per_group(heads, BLOCK),
            state_spec,
            per_group(heads, LANES),
        ],
        out_shape=[
            out(bf16, span, BLOCK),
            out(bf16, STATE_WIDTH, BLOCK),
            out(f32, heads, BLOCK),
            out(f32, heads, BLOCK),
            out(f32, heads, BLOCK),
            state_shape,
            out(f32, heads, LANES),
        ],
        scratch_shapes=[
            pltpu.VMEM((rows * spg, LANES + BLOCK), f32),
            pltpu.VMEM((span, BLOCK), bf16),
        ],
        compiler_params=params(),
        cost_estimate=pl.CostEstimate(flops=4 * 10**9, bytes_accessed=10**7, transcendentals=10**6),
        name="state_chunk",
    )(*args, w, bias, a_log, state, lead)


def split(v):
    high = v.astype(bf16)
    return high, (v - high.astype(f32)).astype(bf16)


def block_kernel(dims, first, recv, *refs):
    spg, rows, heads, span, piece_heads = dims
    prev = None
    if not first:
        prev, refs = refs[0], refs[1:]
    w, xact, bmap, run_ref, dt_ref, cum_ref, state, skip = refs[:8]
    mixed, gate_all, c_all, cum_all, token, raw = refs[-6:]
    conv_rows = span + 2 * STATE_WIDTH
    gather_rows(recv, prev, raw, rows, 2 * span + STATE_WIDTH, span + conv_rows)
    gather_rows(recv, prev, raw, rows, 0, span, False)
    gate_all[0, 0] = raw[:span, LANES:].astype(bf16)
    cum_all[0, 0] = cum_ref[0]
    token[0] = cum_ref[0, :8, :LANES]
    c = jnp.concatenate(
        conv_rows_of(raw, w, band(), span, span + STATE_WIDTH, STATE_WIDTH), axis=0
    )
    c_all[0, 0] = c

    b_rows = bmap[0].astype(f32).T.astype(bf16)
    scores = jnp.dot(b_rows, c, preferred_element_type=f32)
    src = lax.broadcasted_iota(jnp.int32, (HALF, HALF), 0)
    dst = lax.broadcasted_iota(jnp.int32, (HALF, HALF), 1)
    causal = src <= dst
    s00 = jnp.where(causal, scores[:HALF, :HALF], 0.0)
    s01 = scores[:HALF, HALF:]
    s11 = jnp.where(causal, scores[HALF:, HALF:], 0.0)
    r = run_ref[0] * LOG2E
    q = (r - jnp.log(dt_ref[0]) * LOG2E).T
    if not first:
        cc = jnp.concatenate([c, c], axis=0)
        entered = jnp.exp2(r)
    for h in range(heads):
        at = h * HEAD_DIM
        r0, r1 = r[h : h + 1, :HALF], r[h : h + 1, HALF:]
        q0, q1 = q[:HALF, h : h + 1], q[HALF:, h : h + 1]
        w00 = (s00 * jnp.exp2(jnp.minimum(r0 - q0, CAP))).astype(bf16)
        w01 = (s01 * jnp.exp2(r1 - q0)).astype(bf16)
        w11 = (s11 * jnp.exp2(jnp.minimum(r1 - q1, CAP))).astype(bf16)
        x = xact[0, at : at + HEAD_DIM, :]
        y0 = jnp.dot(x[:, :HALF], w00, preferred_element_type=f32)
        y1 = jnp.dot(x, jnp.concatenate([w01, w11], axis=0), preferred_element_type=f32)
        y = jnp.concatenate([y0, y1], axis=1) + skip[0, h : h + 1, :] * x.astype(f32)
        if not first:
            if at % WIDE == 0:
                both = jnp.concatenate(split(state[0, at : at + WIDE, :]), axis=1)
                carried = jnp.dot(both, cc, preferred_element_type=f32)
            y = y + entered[h : h + 1, :] * carried[at % WIDE : at % WIDE + HEAD_DIM, :]
        mixed[0, 0, at : at + HEAD_DIM, :] = y


def block_chunk(chunk, chunks, got, w, xact, bmap, run, dt, cum, state, skip, wholes, dims):
    spg, rows, heads, span, piece_heads = dims
    groups = w.shape[0]

    def whole(*shape):
        return pl.BlockSpec((1, 1) + shape, lambda g: (g, chunk, 0, 0))

    args, specs = chunk_specs(got, chunk, dims)
    args += [w, xact, bmap, run, dt, cum, state, skip]
    specs += [
        per_group(span + 2 * STATE_WIDTH, 4),
        per_group(span, BLOCK),
        per_group(STATE_WIDTH, BLOCK),
        per_group(heads, BLOCK),
        per_group(heads, BLOCK),
        per_group(heads, BLOCK),
        per_group(span, STATE_WIDTH),
        per_group(heads, 1),
    ]
    aliases = {}
    for i, array in enumerate(wholes or ()):
        aliases[len(args)] = i
        args.append(array)
        specs.append(pl.BlockSpec(memory_space=pl.ANY))

    def out(dtype, *shape):
        return jax.ShapeDtypeStruct((groups,) + shape, dtype)

    *wholes, token = pl.pallas_call(
        functools.partial(block_kernel, dims, chunk == 0),
        grid=(groups,),
        in_specs=specs,
        out_specs=[
            whole(span, BLOCK),
            whole(span, BLOCK),
            whole(STATE_WIDTH, BLOCK),
            whole(heads, BLOCK),
            per_group(8, LANES),
        ],
        out_shape=[
            out(f32, chunks, span, BLOCK),
            out(bf16, chunks, span, BLOCK),
            out(bf16, chunks, STATE_WIDTH, BLOCK),
            out(f32, chunks, heads, BLOCK),
            out(f32, 8, LANES),
        ],
        scratch_shapes=[pltpu.VMEM((rows * spg, LANES + BLOCK), f32)],
        input_output_aliases=aliases,
        compiler_params=params(),
        cost_estimate=pl.CostEstimate(flops=4 * 10**9, bytes_accessed=10**7, transcendentals=10**6),
        name="block_chunk",
    )(*args)
    return wholes, token


def relay_kernel(src, decays, token, dst):
    held = jnp.zeros((HEAD_DIM, STATE_WIDTH), f32)
    for d in range(src.shape[0]):
        high, low = split(held)
        dst[d, :, :STATE_WIDTH] = high
        dst[d, :, STATE_WIDTH:] = low
        held = decays[d, pl.ds(pl.program_id(0), 1), :] * held + src[d]


def relay(packed, token, piece_heads):
    count = packed.shape[0]
    rows = piece_heads * HEAD_DIM
    return pl.pallas_call(
        relay_kernel,
        grid=(piece_heads,),
        in_specs=[
            pl.BlockSpec((count, HEAD_DIM, STATE_WIDTH), lambda h: (0, h, 0)),
            pl.BlockSpec((count, 8, STATE_WIDTH), lambda h: (0, rows // 8, 0)),
            pl.BlockSpec(memory_space=pl.ANY),
        ],
        out_specs=pl.BlockSpec((count, HEAD_DIM, 2 * STATE_WIDTH), lambda h: (0, h, 0)),
        out_shape=jax.ShapeDtypeStruct((count, rows, 2 * STATE_WIDTH), bf16),
        compiler_params=params(16),
        name="relay",
    )(packed, packed, token)


def final_kernel(dims, mixed, gate, c_ref, cum, state, gain, out, kept, gains, carried):
    heads, span = dims

    @pl.when(pl.program_id(1) == 0)
    def _():
        gains[...] = jnp.broadcast_to(gain[0], (span, LANES))

    c = c_ref[0, 0]
    cc = jnp.concatenate([c, c], axis=0)
    entered = jnp.exp(cum[0, 0])
    total = jnp.zeros((HEAD_DIM, BLOCK), f32)
    carried[...] = jnp.dot(state[0], cc, preferred_element_type=f32)
    for h in range(heads):
        at = h * HEAD_DIM
        v = carried[at : at + HEAD_DIM, :] * entered[h : h + 1, :]
        v = mixed[0, 0, at : at + HEAD_DIM, :] + v
        v = v * silu(gate[0, 0, at : at + HEAD_DIM, :].astype(f32))
        kept[at : at + HEAD_DIM, :] = v
        total = total + v * v
    mean = jnp.sum(total, axis=0, keepdims=True) * (1.0 / span)
    factor = lax.rsqrt(mean + EPSILON)
    for at in range(0, span, BLOCK):
        scale = gains[at : at + BLOCK, :]
        scale = jnp.concatenate([scale] * (BLOCK // LANES), axis=1)
        tile = (kept[at : at + BLOCK, :] * factor * scale).astype(bf16)
        out[:, at : at + BLOCK] = tile.T


def finish(mixed, gate, c_all, cum, state, gain):
    groups, chunks, span, _ = mixed.shape
    heads = cum.shape[2]

    def tile(rows):
        return pl.BlockSpec((1, 1, rows, BLOCK), lambda g, c: (g, c, 0, 0))

    return pl.pallas_call(
        functools.partial(final_kernel, (heads, span)),
        grid=(groups, chunks),
        in_specs=[
            tile(span),
            tile(span),
            tile(STATE_WIDTH),
            tile(heads),
            pl.BlockSpec((1, span, 2 * STATE_WIDTH), lambda g, c: (g, 0, 0)),
            pl.BlockSpec((1, span, 1), lambda g, c: (g, 0, 0)),
        ],
        out_specs=pl.BlockSpec((BLOCK, span), lambda g, c: (c, g)),
        out_shape=jax.ShapeDtypeStruct((chunks * BLOCK, groups * span), bf16),
        scratch_shapes=[
            pltpu.VMEM((span, BLOCK), f32),
            pltpu.VMEM((span, LANES), f32),
            pltpu.VMEM((span, BLOCK), f32),
        ],
        compiler_params=params(24),
        name="finish",
    )(mixed, gate, c_all, cum, state, gain)


def exchange(array):
    return lax.all_to_all(array, "seq", split_axis=0, concat_axis=0, tiled=True)


def per_device(projected, conv_weight, dt_bias, a_log, d_skip, norm_gain):
    seq_count = lax.axis_size("seq")
    groups = conv_weight.shape[1]
    heads = dt_bias.shape[0] // groups
    span = heads * HEAD_DIM
    rows, all_tokens = projected.shape
    local_tokens = all_tokens // seq_count
    chunks = local_tokens // BLOCK
    spg = seq_count // groups
    piece_heads = groups * heads // seq_count
    dims = (spg, rows, heads, span, piece_heads)

    w = jnp.transpose(conv_weight, (1, 2, 0))
    bias = dt_bias.reshape(groups, heads, 1)
    rate = a_log.reshape(groups, heads, 1)
    skip = d_skip.reshape(groups, heads, 1)
    gain = norm_gain.reshape(groups, span, 1)
    state = jnp.zeros((groups, span, STATE_WIDTH), f32)
    lead = jnp.zeros((groups, heads, LANES), f32)

    split_at = local_tokens - BLOCK
    cut = cut_blocks(projected, seq_count, 0, split_at, None)
    got = [exchange(cut)]
    got.append(exchange(cut_blocks(projected, seq_count, split_at, local_tokens, cut)))
    wholes = None
    for c in range(chunks):
        xact, bmap, run, dt, cum, new, lead = state_chunk(
            c, chunks, got, w, bias, rate, state, lead, dims
        )
        wholes, token = block_chunk(
            c, chunks, got, w, xact, bmap, run, dt, cum, state, skip, wholes, dims
        )
        state = new
    entering = exchange(relay(exchange(state), token, piece_heads))
    mixed, gate_all, c_all, cum_all = wholes
    entering = entering.reshape(groups, span, 2 * STATE_WIDTH)
    return finish(mixed, gate_all, c_all, cum_all, entering, gain)


def solution(mesh):
    in_specs = (P(("tp", "seq"), None), P(None, "tp", None), P("tp"), P("tp"), P("tp"), P("tp"))
    return jax.shard_map(
        per_device, mesh=mesh, in_specs=in_specs, out_specs=P("seq", "tp"), check_vma=False
    )
```

```python
import functools

import jax
import jax.numpy as jnp
from jax import lax
from jax.experimental import pallas as pl
from jax.experimental.pallas import tpu as pltpu
from jax.sharding import PartitionSpec as P

HEAD_DIM = 64
STATE_WIDTH = 128
BLOCK = 256
LANES = 128
HALF = BLOCK // 2
WIDE = 256
LOG2E = 1.4426950408889634
CAP = 80.0
EPSILON = 1e-05

f32 = jnp.float32
bf16 = jnp.bfloat16
NT = (((1,), (1,)), ((), ()))


def params(mib=60):
    return pltpu.CompilerParams(vmem_limit_bytes=mib * 2**20)


def silu(v):
    half = 0.5 * v
    return half + half * jnp.tanh(half)


def softplus(v):
    e = jnp.exp(-jnp.abs(v))
    u = 1.0 + e
    gap = u - 1.0
    tiny = gap == 0.0
    log_part = jnp.where(tiny, e, jnp.log(u) * (e / jnp.where(tiny, 1.0, gap)))
    return jnp.maximum(v, 0.0) + log_part


def per_group(*shape):
    return pl.BlockSpec((1,) + shape, lambda g: (g,) + (0,) * len(shape))


RIM = 4


def rim_rows(rows):
    base = rows // 16 * 16
    height = -(-(rows - base + RIM) // 8) * 8
    assert height <= 16
    return base, height


def cut_kernel(low, count, src, *refs):
    refs = refs[len(refs) - (4 if low else 7) :]
    dst, held, in_sems, out_sems = refs[:4]
    rows, all_tokens = src.shape
    tokens = all_tokens // count
    width = dst.shape[2]
    sent = held if low else refs[5]

    def fetch(d):
        at = d * tokens + low
        return pltpu.make_async_copy(src.at[:, at : at + width], held.at[d], in_sems.at[d])

    def place(d):
        return pltpu.make_async_copy(sent.at[d], dst.at[d], out_sems.at[d])

    if low:
        for d in range(count):
            fetch(d).start()
        for d in range(count):
            fetch(d).wait()
            place(d).start()
    else:
        windows, rim_sems = refs[4], refs[6]

        def window(d):
            at = d * tokens - LANES
            return pltpu.make_async_copy(src.at[:, at : at + LANES], windows.at[d], rim_sems.at[d])

        for d in range(count):
            if d:
                window(d).start()
            fetch(d).start()
        base, height = rim_rows(rows)
        row = lax.broadcasted_iota(jnp.int32, (height, LANES), 0) - (rows - base)
        col = lax.broadcasted_iota(jnp.int32, (height, LANES), 1)
        hit = (col == row + LANES - RIM) & (row >= 0) & (row < RIM)
        pick = jnp.where(hit, 1.0, 0.0).astype(bf16)
        for d in range(count):
            fetch(d).wait()
            sent[d, :base, :] = held[d, :base, :]
            end = held[d, base:rows, :].astype(f32)
            end = jnp.concatenate([end, jnp.zeros((height - end.shape[0], width), f32)], axis=0)
            if d:
                window(d).wait()
                rims = lax.dot_general(pick, windows[d], NT, preferred_element_type=f32)
                fill = jnp.zeros((height, width - rows), f32)
                end = end + jnp.concatenate([rims, fill], axis=1)
            sent[d, base : base + height, :] = end.astype(bf16)
            place(d).start()
    for d in range(count):
        place(d).wait()


def cut_blocks(projected, count, low, high, after):
    rows = projected.shape[0]
    width = high - low
    args = [projected]
    out_rows = rows
    sems = pltpu.SemaphoreType.DMA((count,))
    scratch = [pltpu.VMEM((count, rows, width), bf16), sems, sems]
    if low == 0:
        assert width >= rows
        out_rows = sum(rim_rows(rows))
        scratch += [
            pltpu.VMEM((count, rows, LANES), bf16),
            pltpu.VMEM((count, out_rows, width), bf16),
            sems,
        ]
    args += after
    return pl.pallas_call(
        functools.partial(cut_kernel, low, count),
        in_specs=[pl.BlockSpec(memory_space=pl.ANY)] * len(args),
        out_specs=pl.BlockSpec(memory_space=pl.ANY),
        out_shape=jax.ShapeDtypeStruct((count, out_rows, width), bf16),
        scratch_shapes=scratch,
        compiler_params=params(),
        name="cut_blocks",
    )(*args)


def gather_rows(recv, prev, raw, rows, low, high, ahead=True):
    for s in range(recv.shape[0]):
        a = max(low - s * rows, 0) // 16 * 16
        b = min(-(-(high - s * rows) // 16) * 16, rows)
        if b <= a:
            continue
        at = s * rows + a
        raw[at : at + b - a, LANES:] = recv[s, a:b, :BLOCK].astype(f32)
        if not ahead:
            continue
        if prev is not None:
            raw[at : at + b - a, :LANES] = prev[s, a:b, :].astype(f32)
            continue
        base, height = rim_rows(rows)
        wide = -(-rows // LANES) * LANES
        rims = recv[s, base : base + height, :wide].astype(f32)
        shift = height - RIM - (rows - base)
        if shift:
            rims = pltpu.roll(rims, shift, 0)
        tall = jnp.concatenate([jnp.zeros((LANES - height, wide), f32), rims], axis=0).T
        raw[at : at + b - a, :LANES] = tall[a:b]


def band():
    row = lax.broadcasted_iota(jnp.int32, (2 * LANES, 3 * LANES), 0)
    col = lax.broadcasted_iota(jnp.int32, (2 * LANES, 3 * LANES), 1)
    tap = col // LANES
    return jnp.where(row == col - tap * LANES + LANES - 3 + tap, 1.0, 0.0).astype(bf16)


def conv_rows_of(raw, w, picks, span, r, height):
    low = raw[span + r : span + r + height, :].astype(bf16)
    shifted = [
        jnp.dot(low[:, at : at + 2 * LANES], picks, preferred_element_type=f32)
        for at in range(0, BLOCK, LANES)
    ]
    tiles = []
    for q in range(0, height, HEAD_DIM):
        at = r + q
        taps = [
            jnp.broadcast_to(w[0, at : at + HEAD_DIM, k : k + 1], (HEAD_DIM, LANES))
            for k in range(4)
        ]
        parts = []
        for i, three in enumerate(shifted):
            summed = None
            for k in range(3):
                part = taps[k] * three[q : q + HEAD_DIM, k * LANES : (k + 1) * LANES]
                summed = part if summed is None else summed + part
            own = raw[span + at : span + at + HEAD_DIM, (i + 1) * LANES : (i + 2) * LANES]
            parts.append(silu(summed + taps[3] * own).astype(bf16))
        tiles.append(jnp.concatenate(parts, axis=1))
    return tiles


def state_kernel(dims, first, last, recv, *refs):
    spg, rows, heads, span, piece_heads = dims
    prev = None
    if not first:
        prev, refs = refs[0], refs[1:]
    w, bias, a_log, state_in, lead_in = refs[:5]
    xact, bmap, run_out, dt_out, cum_out, state_out, lead_out, raw, xw = refs[-9:]
    steps = 2 * span + 2 * STATE_WIDTH

    gather_rows(recv, prev, raw, rows, steps, steps + heads, False)
    gather_rows(recv, prev, raw, rows, span, 2 * span + STATE_WIDTH)
    dt = softplus(raw[steps : steps + heads, LANES:] + bias[0])
    log_decay = -jnp.exp(a_log[0]) * dt
    lane = lax.broadcasted_iota(jnp.int32, (heads, BLOCK), 1)
    run = log_decay
    shift = 1
    while shift < BLOCK:
        run = run + jnp.where(lane >= shift, pltpu.roll(run, shift, 1), 0.0)
        shift *= 2
    final = run[:, BLOCK - 1 :]
    scale = jnp.exp(final - run) * dt
    cum = run + lead_in[0][:, :1]
    run_out[0] = run
    dt_out[0] = dt
    cum_out[0] = cum
    lead = jnp.broadcast_to(cum[:, BLOCK - 1 :], (heads, LANES))
    lead_out[0] = lead
    keep = jnp.broadcast_to(jnp.exp(final), (heads, LANES))

    picks = band()
    for i, tile in enumerate(conv_rows_of(raw, w, picks, span, span, STATE_WIDTH)):
        bmap[0, i * HEAD_DIM : (i + 1) * HEAD_DIM, :] = tile
    for r in range(0, span, WIDE):
        for i, tile in enumerate(conv_rows_of(raw, w, picks, span, r, WIDE)):
            at = r + i * HEAD_DIM
            h = at // HEAD_DIM
            xact[0, at : at + HEAD_DIM, :] = tile
            xw[at : at + HEAD_DIM, :] = (tile.astype(f32) * scale[h : h + 1, :]).astype(bf16)
    update = lax.dot_general(xw[...], bmap[0], NT, preferred_element_type=f32)
    for h in range(heads):
        r = h * HEAD_DIM
        new = update[r : r + HEAD_DIM, :]
        if not first:
            new = keep[h : h + 1, :] * state_in[0, r : r + HEAD_DIM, :] + new
        if last:
            at = (h % piece_heads) * HEAD_DIM
            state_out[h // piece_heads, at : at + HEAD_DIM, :] = new.astype(bf16)
        else:
            state_out[0, r : r + HEAD_DIM, :] = new
    if last:
        high, low = split(jnp.exp(lead))
        fill = jnp.zeros((8 - piece_heads, LANES), f32)
        for i in range(heads // piece_heads):
            mine = slice(i * piece_heads, (i + 1) * piece_heads)
            parts = [high[mine].astype(f32), fill, low[mine].astype(f32), fill]
            at = piece_heads * HEAD_DIM
            state_out[i, at : at + 16, :] = jnp.concatenate(parts, axis=0).astype(bf16)


def chunk_specs(got, chunk, dims):
    spg, rows = dims[:2]
    first, last = got
    ahead = first.shape[2] // BLOCK
    if chunk == 0:
        return [first], [pl.BlockSpec((spg,) + first.shape[1:], lambda g: (g, 0, 0))]
    at = 2 * chunk - 1
    prev = pl.BlockSpec((spg, first.shape[1], LANES), lambda g: (g, 0, at))
    if chunk < ahead:
        block = pl.BlockSpec((spg, first.shape[1], BLOCK), lambda g: (g, 0, chunk))
        return [first, first], [block, prev]
    return [last, first], [pl.BlockSpec((spg, rows, BLOCK), lambda g: (g, 0, 0)), prev]


def state_chunk(chunk, chunks, got, w, bias, a_log, state, lead, token, dims):
    spg, rows, heads, span, piece_heads = dims
    groups = w.shape[0]
    conv_rows = span + 2 * STATE_WIDTH
    last = chunk == chunks - 1
    if last:
        packed = piece_heads * HEAD_DIM + 16
        state_shape = jax.ShapeDtypeStruct((groups * spg, packed, STATE_WIDTH), bf16)
        state_spec = pl.BlockSpec((spg, packed, STATE_WIDTH), lambda g: (g, 0, 0))
    else:
        state_shape = jax.ShapeDtypeStruct((groups, span, STATE_WIDTH), f32)
        state_spec = per_group(span, STATE_WIDTH)

    def out(dtype, *shape):
        return jax.ShapeDtypeStruct((groups,) + shape, dtype)

    args, specs = chunk_specs(got, chunk, dims)
    after = [] if token is None else [token]
    return pl.pallas_call(
        functools.partial(state_kernel, dims, chunk == 0, last),
        grid=(groups,),
        in_specs=specs
        + [
            per_group(conv_rows, 4),
            per_group(heads, 1),
            per_group(heads, 1),
            per_group(span, STATE_WIDTH),
            per_group(heads, LANES),
        ]
        + [pl.BlockSpec(memory_space=pl.ANY)] * len(after),
        out_specs=[
            per_group(span, BLOCK),
            per_group(STATE_WIDTH, BLOCK),
            per_group(heads, BLOCK),
            per_group(heads, BLOCK),
            per_group(heads, BLOCK),
            state_spec,
            per_group(heads, LANES),
        ],
        out_shape=[
            out(bf16, span, BLOCK),
            out(bf16, STATE_WIDTH, BLOCK),
            out(f32, heads, BLOCK),
            out(f32, heads, BLOCK),
            out(f32, heads, BLOCK),
            state_shape,
            out(f32, heads, LANES),
        ],
        scratch_shapes=[
            pltpu.VMEM((rows * spg, LANES + BLOCK), f32),
            pltpu.VMEM((span, BLOCK), bf16),
        ],
        compiler_params=params(56 if last else 60),
        cost_estimate=pl.CostEstimate(flops=4 * 10**9, bytes_accessed=10**7, transcendentals=10**6),
        name="state_chunk",
    )(*args, w, bias, a_log, state, lead, *after)


def split(v):
    high = v.astype(bf16)
    return high, (v - high.astype(f32)).astype(bf16)


def block_kernel(dims, first, recv, *refs):
    spg, rows, heads, span, piece_heads = dims
    prev = None
    if not first:
        prev, refs = refs[0], refs[1:]
    w, xact, bmap, run_ref, dt_ref, cum_ref, state, skip = refs[:8]
    mixed, gate_all, c_all, cum_all, token, raw = refs[-6:]
    conv_rows = span + 2 * STATE_WIDTH
    gather_rows(recv, prev, raw, rows, 2 * span + STATE_WIDTH, span + conv_rows)
    gather_rows(recv, prev, raw, rows, 0, span, False)
    gate_all[0, 0] = raw[:span, LANES:].astype(bf16)
    cum_all[0, 0] = cum_ref[0]
    token[0] = cum_ref[0, :8, :LANES]
    c = jnp.concatenate(
        conv_rows_of(raw, w, band(), span, span + STATE_WIDTH, STATE_WIDTH), axis=0
    )
    c_all[0, 0] = c

    b_rows = bmap[0].astype(f32).T.astype(bf16)
    scores = jnp.dot(b_rows, c, preferred_element_type=f32)
    src = lax.broadcasted_iota(jnp.int32, (HALF, HALF), 0)
    dst = lax.broadcasted_iota(jnp.int32, (HALF, HALF), 1)
    causal = src <= dst
    s00 = jnp.where(causal, scores[:HALF, :HALF], 0.0)
    s01 = scores[:HALF, HALF:]
    s11 = jnp.where(causal, scores[HALF:, HALF:], 0.0)
    r = run_ref[0] * LOG2E
    q = (r - jnp.log(dt_ref[0]) * LOG2E).T
    if not first:
        cc = jnp.concatenate([c, c], axis=0)
        entered = jnp.exp2(r)
    for h in range(heads):
        at = h * HEAD_DIM
        r0, r1 = r[h : h + 1, :HALF], r[h : h + 1, HALF:]
        q0, q1 = q[:HALF, h : h + 1], q[HALF:, h : h + 1]
        w00 = (s00 * jnp.exp2(jnp.minimum(r0 - q0, CAP))).astype(bf16)
        w01 = (s01 * jnp.exp2(r1 - q0)).astype(bf16)
        w11 = (s11 * jnp.exp2(jnp.minimum(r1 - q1, CAP))).astype(bf16)
        x = xact[0, at : at + HEAD_DIM, :]
        y0 = jnp.dot(x[:, :HALF], w00, preferred_element_type=f32)
        y1 = jnp.dot(x, jnp.concatenate([w01, w11], axis=0), preferred_element_type=f32)
        y = jnp.concatenate([y0, y1], axis=1) + skip[0, h : h + 1, :] * x.astype(f32)
        if not first:
            if at % WIDE == 0:
                both = jnp.concatenate(split(state[0, at : at + WIDE, :]), axis=1)
                carried = jnp.dot(both, cc, preferred_element_type=f32)
            y = y + entered[h : h + 1, :] * carried[at % WIDE : at % WIDE + HEAD_DIM, :]
        mixed[0, 0, at : at + HEAD_DIM, :] = y


def block_chunk(chunk, chunks, got, w, xact, bmap, run, dt, cum, state, skip, wholes, dims):
    spg, rows, heads, span, piece_heads = dims
    groups = w.shape[0]

    def whole(*shape):
        return pl.BlockSpec((1, 1) + shape, lambda g: (g, chunk, 0, 0))

    args, specs = chunk_specs(got, chunk, dims)
    args += [w, xact, bmap, run, dt, cum, state, skip]
    specs += [
        per_group(span + 2 * STATE_WIDTH, 4),
        per_group(span, BLOCK),
        per_group(STATE_WIDTH, BLOCK),
        per_group(heads, BLOCK),
        per_group(heads, BLOCK),
        per_group(heads, BLOCK),
        per_group(span, STATE_WIDTH),
        per_group(heads, 1),
    ]
    aliases = {}
    for i, array in enumerate(wholes or ()):
        aliases[len(args)] = i
        args.append(array)
        specs.append(pl.BlockSpec(memory_space=pl.ANY))

    def out(dtype, *shape):
        return jax.ShapeDtypeStruct((groups,) + shape, dtype)

    *wholes, token = pl.pallas_call(
        functools.partial(block_kernel, dims, chunk == 0),
        grid=(groups,),
        in_specs=specs,
        out_specs=[
            whole(span, BLOCK),
            whole(span, BLOCK),
            whole(STATE_WIDTH, BLOCK),
            whole(heads, BLOCK),
            per_group(8, LANES),
        ],
        out_shape=[
            out(f32, chunks, span, BLOCK),
            out(bf16, chunks, span, BLOCK),
            out(bf16, chunks, STATE_WIDTH, BLOCK),
            out(f32, chunks, heads, BLOCK),
            out(f32, 8, LANES),
        ],
        scratch_shapes=[pltpu.VMEM((rows * spg, LANES + BLOCK), f32)],
        input_output_aliases=aliases,
        compiler_params=params(56 if chunk == chunks - 1 else 60),
        cost_estimate=pl.CostEstimate(flops=4 * 10**9, bytes_accessed=10**7, transcendentals=10**6),
        name="block_chunk",
    )(*args)
    return wholes, token


def relay_kernel(src, decays, token, dst, decay):
    for d in range(src.shape[0]):
        both = decays[d].astype(f32)
        decay[d] = both[:8] + both[8:]
    held = jnp.zeros((HEAD_DIM, STATE_WIDTH), f32)
    for d in range(src.shape[0]):
        dst[d] = held.astype(bf16)
        held = decay[d, pl.ds(pl.program_id(0), 1), :] * held + src[d].astype(f32)


def relay(packed, token, piece_heads):
    count = packed.shape[0]
    rows = piece_heads * HEAD_DIM
    return pl.pallas_call(
        relay_kernel,
        grid=(piece_heads,),
        in_specs=[
            pl.BlockSpec((count, HEAD_DIM, STATE_WIDTH), lambda h: (0, h, 0)),
            pl.BlockSpec((count, 16, STATE_WIDTH), lambda h: (0, rows // 16, 0)),
            pl.BlockSpec(memory_space=pl.ANY),
        ],
        out_specs=pl.BlockSpec((count, HEAD_DIM, STATE_WIDTH), lambda h: (0, h, 0)),
        out_shape=jax.ShapeDtypeStruct((count, rows, STATE_WIDTH), bf16),
        scratch_shapes=[pltpu.VMEM((count, 8, STATE_WIDTH), f32)],
        compiler_params=params(16),
        name="relay",
    )(packed, packed, token)


def final_kernel(dims, mixed, gate, c_ref, cum, state, gain, out, kept, gains, carried):
    heads, span = dims

    @pl.when(pl.program_id(1) == 0)
    def _():
        gains[...] = jnp.broadcast_to(gain[0], (span, LANES))

    entered = jnp.exp(cum[0, 0])
    total = jnp.zeros((HEAD_DIM, BLOCK), f32)
    carried[...] = jnp.dot(state[0], c_ref[0, 0], preferred_element_type=f32)
    for h in range(heads):
        at = h * HEAD_DIM
        v = carried[at : at + HEAD_DIM, :] * entered[h : h + 1, :]
        v = mixed[0, 0, at : at + HEAD_DIM, :] + v
        v = v * silu(gate[0, 0, at : at + HEAD_DIM, :].astype(f32))
        kept[at : at + HEAD_DIM, :] = v
        total = total + v * v
    mean = jnp.sum(total, axis=0, keepdims=True) * (1.0 / span)
    factor = lax.rsqrt(mean + EPSILON)
    for at in range(0, span, BLOCK):
        scale = gains[at : at + BLOCK, :]
        scale = jnp.concatenate([scale] * (BLOCK // LANES), axis=1)
        tile = (kept[at : at + BLOCK, :] * factor * scale).astype(bf16)
        out[:, at : at + BLOCK] = tile.T


def finish(mixed, gate, c_all, cum, state, gain):
    groups, chunks, span, _ = mixed.shape
    heads = cum.shape[2]

    def tile(rows):
        return pl.BlockSpec((1, 1, rows, BLOCK), lambda g, c: (g, c, 0, 0))

    return pl.pallas_call(
        functools.partial(final_kernel, (heads, span)),
        grid=(groups, chunks),
        in_specs=[
            tile(span),
            tile(span),
            tile(STATE_WIDTH),
            tile(heads),
            pl.BlockSpec((1, span, STATE_WIDTH), lambda g, c: (g, 0, 0)),
            pl.BlockSpec((1, span, 1), lambda g, c: (g, 0, 0)),
        ],
        out_specs=pl.BlockSpec((BLOCK, span), lambda g, c: (c, g)),
        out_shape=jax.ShapeDtypeStruct((chunks * BLOCK, groups * span), bf16),
        scratch_shapes=[
            pltpu.VMEM((span, BLOCK), f32),
            pltpu.VMEM((span, LANES), f32),
            pltpu.VMEM((span, BLOCK), f32),
        ],
        compiler_params=params(57),
        name="finish",
    )(mixed, gate, c_all, cum, state, gain)


def exchange(array):
    return lax.all_to_all(array, "seq", split_axis=0, concat_axis=0, tiled=True)


def per_device(projected, conv_weight, dt_bias, a_log, d_skip, norm_gain):
    seq_count = lax.axis_size("seq")
    groups = conv_weight.shape[1]
    heads = dt_bias.shape[0] // groups
    span = heads * HEAD_DIM
    rows, all_tokens = projected.shape
    local_tokens = all_tokens // seq_count
    chunks = local_tokens // BLOCK
    spg = seq_count // groups
    piece_heads = groups * heads // seq_count
    dims = (spg, rows, heads, span, piece_heads)

    w = jnp.transpose(conv_weight, (1, 2, 0))
    bias = dt_bias.reshape(groups, heads, 1)
    rate = a_log.reshape(groups, heads, 1)
    skip = d_skip.reshape(groups, heads, 1)
    gain = norm_gain.reshape(groups, span, 1)
    state = jnp.zeros((groups, span, STATE_WIDTH), f32)
    lead = jnp.zeros((groups, heads, LANES), f32)

    split_at = local_tokens - BLOCK
    cut = cut_blocks(projected, seq_count, 0, split_at, [])
    got = [exchange(cut)]
    ready = [cut, w, bias, rate, skip, gain, state, lead]
    got.append(exchange(cut_blocks(projected, seq_count, split_at, local_tokens, ready)))
    wholes = None
    tokens = []
    for c in range(chunks):
        xact, bmap, run, dt, cum, new, lead = state_chunk(
            c, chunks, got, w, bias, rate, state, lead, tokens[c - 2] if c > 1 else None, dims
        )
        wholes, token = block_chunk(
            c, chunks, got, w, xact, bmap, run, dt, cum, state, skip, wholes, dims
        )
        tokens.append(token)
        state = new
    entering = exchange(relay(exchange(state), token, piece_heads))
    mixed, gate_all, c_all, cum_all = wholes
    entering = entering.reshape(groups, span, STATE_WIDTH)
    return finish(mixed, gate_all, c_all, cum_all, entering, gain)


def solution(mesh):
    in_specs = (P(("tp", "seq"), None), P(None, "tp", None), P("tp"), P("tp"), P("tp"), P("tp"))
    return jax.shard_map(
        per_device, mesh=mesh, in_specs=in_specs, out_specs=P("seq", "tp"), check_vma=False
    )
```

```python
import functools

import jax
import jax.numpy as jnp
from jax import lax
from jax.experimental import pallas as pl
from jax.experimental.pallas import tpu as pltpu
from jax.sharding import PartitionSpec as P

HEAD_DIM = 64
STATE_WIDTH = 128
BLOCK = 256
LANES = 128
HALF = BLOCK // 2
WIDE = 256
LOG2E = 1.4426950408889634
CAP = 80.0
EPSILON = 1e-05

f32 = jnp.float32
bf16 = jnp.bfloat16
NT = (((1,), (1,)), ((), ()))


def params(mib=60):
    return pltpu.CompilerParams(vmem_limit_bytes=mib * 2**20)


def silu(v):
    half = 0.5 * v
    return half + half * jnp.tanh(half)


def softplus(v):
    e = jnp.exp(-jnp.abs(v))
    u = 1.0 + e
    gap = u - 1.0
    tiny = gap == 0.0
    log_part = jnp.where(tiny, e, jnp.log(u) * (e / jnp.where(tiny, 1.0, gap)))
    return jnp.maximum(v, 0.0) + log_part


def in_hbm(*arrays):
    return [pltpu.with_memory_space_constraint(array, pltpu.HBM) for array in arrays]


def in_vmem(*arrays):
    return [pltpu.with_memory_space_constraint(array, pltpu.VMEM) for array in arrays]


def per_group(*shape):
    return pl.BlockSpec((1,) + shape, lambda g: (g,) + (0,) * len(shape))


RIM = 4


def rim_rows(rows):
    base = rows // 16 * 16
    height = -(-(rows - base + RIM) // 8) * 8
    assert height <= 16
    return base, height


def cut_kernel(low, count, src, *refs):
    rows, all_tokens = src.shape
    tokens = all_tokens // count
    if low:
        dst, held, in_sems, out_sems = refs[-4:]
        width = dst.shape[2]

        def fetch(d):
            at = d * tokens + low
            return pltpu.make_async_copy(src.at[:, at : at + width], held.at[d], in_sems.at[d])

        def place(d):
            return pltpu.make_async_copy(held.at[d], dst.at[d], out_sems.at[d])

        for d in range(count):
            fetch(d).start()
        for d in range(count):
            fetch(d).wait()
            place(d).start()
        for d in range(count):
            place(d).wait()
        return

    bottom, dst, windows, ends, in_sems, rim_sems, out_sems = refs
    width = dst.shape[2]
    base, height = rim_rows(rows)

    def body(d):
        at = d * tokens
        return pltpu.make_async_copy(
            src.at[:base, at : at + width], dst.at[d, :base, :], in_sems.at[d]
        )

    def window(d):
        at = d * tokens - LANES
        return pltpu.make_async_copy(src.at[:, at : at + LANES], windows.at[d], rim_sems.at[d])

    def place(d):
        return pltpu.make_async_copy(
            ends.at[d], dst.at[d, base : base + height, :], out_sems.at[d]
        )

    for d in range(1, count):
        window(d).start()
    for d in range(count):
        body(d).start()
    row = lax.broadcasted_iota(jnp.int32, (height, LANES), 0) - (rows - base)
    col = lax.broadcasted_iota(jnp.int32, (height, LANES), 1)
    hit = (col == row + LANES - RIM) & (row >= 0) & (row < RIM)
    pick = jnp.where(hit, 1.0, 0.0).astype(bf16)
    own = lax.broadcasted_iota(jnp.int32, (height, width), 0) < rows - base
    for d in range(count):
        end = bottom[:height, d * tokens : d * tokens + width].astype(f32)
        rims = jnp.zeros((height, width), f32)
        if d:
            window(d).wait()
            rims = lax.dot_general(pick, windows[d], NT, preferred_element_type=f32)
            rims = jnp.concatenate([rims, jnp.zeros((height, width - rows), f32)], axis=1)
        ends[d] = jnp.where(own, end, rims).astype(bf16)
        place(d).start()
    for d in range(count):
        place(d).wait()
    for d in range(count):
        body(d).wait()


def cut_blocks(projected, count, low, high, after):
    rows, all_tokens = projected.shape
    width = high - low
    (src,) = in_hbm(projected)
    args, specs = [src], [pl.BlockSpec(memory_space=pl.ANY)]
    sems = pltpu.SemaphoreType.DMA((count,))
    if low:
        out = pltpu.HBM((count, rows, width), bf16)
        scratch = [pltpu.VMEM((count, rows, width), bf16), sems, sems]
    else:
        assert width >= rows
        base, height = rim_rows(rows)
        out = pltpu.VMEM((count, base + height, width), bf16)
        scratch = [
            pltpu.VMEM((count, rows, LANES), bf16),
            pltpu.VMEM((count, height, width), bf16),
            sems,
            sems,
            sems,
        ]
        args.append(src)
        specs.append(pl.BlockSpec((16, all_tokens), lambda i: (base // 16, 0)))
    return pl.pallas_call(
        functools.partial(cut_kernel, low, count),
        grid=(1,),
        in_specs=specs + [pl.BlockSpec(memory_space=pl.ANY)] * len(after),
        out_specs=pl.BlockSpec(memory_space=pl.ANY),
        out_shape=out,
        scratch_shapes=scratch,
        compiler_params=params(40),
        name="cut_blocks",
    )(*args, *after)


def gather_rows(recv, prev, raw, rows, low, high, ahead=True):
    for s in range(recv.shape[0]):
        a = max(low - s * rows, 0) // 16 * 16
        b = min(-(-(high - s * rows) // 16) * 16, rows)
        if b <= a:
            continue
        at = s * rows + a
        raw[at : at + b - a, LANES:] = recv[s, a:b, :BLOCK].astype(f32)
        if not ahead:
            continue
        if prev is not None:
            raw[at : at + b - a, :LANES] = prev[s, a:b, :].astype(f32)
            continue
        base, height = rim_rows(rows)
        wide = -(-rows // LANES) * LANES
        rims = recv[s, base : base + height, :wide].astype(f32)
        shift = height - RIM - (rows - base)
        if shift:
            rims = pltpu.roll(rims, shift, 0)
        tall = jnp.concatenate([jnp.zeros((LANES - height, wide), f32), rims], axis=0).T
        raw[at : at + b - a, :LANES] = tall[a:b]


def band():
    row = lax.broadcasted_iota(jnp.int32, (2 * LANES, 3 * LANES), 0)
    col = lax.broadcasted_iota(jnp.int32, (2 * LANES, 3 * LANES), 1)
    tap = col // LANES
    return jnp.where(row == col - tap * LANES + LANES - 3 + tap, 1.0, 0.0).astype(bf16)


def conv_rows_of(raw, w, picks, span, r, height):
    low = raw[span + r : span + r + height, :].astype(bf16)
    shifted = [
        jnp.dot(low[:, at : at + 2 * LANES], picks, preferred_element_type=f32)
        for at in range(0, BLOCK, LANES)
    ]
    tiles = []
    for q in range(0, height, HEAD_DIM):
        at = r + q
        taps = [
            jnp.broadcast_to(w[0, at : at + HEAD_DIM, k : k + 1], (HEAD_DIM, LANES))
            for k in range(4)
        ]
        parts = []
        for i, three in enumerate(shifted):
            summed = None
            for k in range(3):
                part = taps[k] * three[q : q + HEAD_DIM, k * LANES : (k + 1) * LANES]
                summed = part if summed is None else summed + part
            own = raw[span + at : span + at + HEAD_DIM, (i + 1) * LANES : (i + 2) * LANES]
            parts.append(silu(summed + taps[3] * own).astype(bf16))
        tiles.append(jnp.concatenate(parts, axis=1))
    return tiles


def state_kernel(dims, first, last, recv, *refs):
    spg, rows, heads, span, piece_heads = dims
    prev = None
    if not first:
        prev, refs = refs[0], refs[1:]
    w, bias, a_log, state_in, lead_in = refs[:5]
    xact, bmap, run_out, dt_out, cum_out, state_out, lead_out, raw, xw = refs[-9:]
    steps = 2 * span + 2 * STATE_WIDTH

    gather_rows(recv, prev, raw, rows, steps, steps + heads, False)
    gather_rows(recv, prev, raw, rows, span, 2 * span + STATE_WIDTH)
    dt = softplus(raw[steps : steps + heads, LANES:] + bias[0])
    log_decay = -jnp.exp(a_log[0]) * dt
    lane = lax.broadcasted_iota(jnp.int32, (heads, BLOCK), 1)
    run = log_decay
    shift = 1
    while shift < BLOCK:
        run = run + jnp.where(lane >= shift, pltpu.roll(run, shift, 1), 0.0)
        shift *= 2
    final = run[:, BLOCK - 1 :]
    scale = jnp.exp(final - run) * dt
    cum = run + lead_in[0][:, :1]
    run_out[0] = run
    dt_out[0] = dt
    cum_out[0] = cum
    lead = jnp.broadcast_to(cum[:, BLOCK - 1 :], (heads, LANES))
    lead_out[0] = lead
    keep = jnp.broadcast_to(jnp.exp(final), (heads, LANES))

    picks = band()
    for i, tile in enumerate(conv_rows_of(raw, w, picks, span, span, STATE_WIDTH)):
        bmap[0, i * HEAD_DIM : (i + 1) * HEAD_DIM, :] = tile
    for r in range(0, span, WIDE):
        for i, tile in enumerate(conv_rows_of(raw, w, picks, span, r, WIDE)):
            at = r + i * HEAD_DIM
            h = at // HEAD_DIM
            xact[0, at : at + HEAD_DIM, :] = tile
            xw[at : at + HEAD_DIM, :] = (tile.astype(f32) * scale[h : h + 1, :]).astype(bf16)
    update = lax.dot_general(xw[...], bmap[0], NT, preferred_element_type=f32)
    for h in range(heads):
        r = h * HEAD_DIM
        new = update[r : r + HEAD_DIM, :]
        if not first:
            new = keep[h : h + 1, :] * state_in[0, r : r + HEAD_DIM, :] + new
        if last:
            at = (h % piece_heads) * HEAD_DIM
            state_out[h // piece_heads, at : at + HEAD_DIM, :] = new.astype(bf16)
        else:
            state_out[0, r : r + HEAD_DIM, :] = new
    if last:
        high, low = split(jnp.exp(lead))
        fill = jnp.zeros((8 - piece_heads, LANES), f32)
        for i in range(heads // piece_heads):
            mine = slice(i * piece_heads, (i + 1) * piece_heads)
            parts = [high[mine].astype(f32), fill, low[mine].astype(f32), fill]
            at = piece_heads * HEAD_DIM
            state_out[i, at : at + 16, :] = jnp.concatenate(parts, axis=0).astype(bf16)


def chunk_specs(got, chunk, dims):
    spg, rows = dims[:2]
    first, last = in_hbm(*got)
    ahead = first.shape[2] // BLOCK
    if chunk == 0:
        return [first], [pl.BlockSpec((spg,) + first.shape[1:], lambda g: (g, 0, 0))]
    at = 2 * chunk - 1
    prev = pl.BlockSpec((spg, first.shape[1], LANES), lambda g: (g, 0, at))
    if chunk < ahead:
        block = pl.BlockSpec((spg, first.shape[1], BLOCK), lambda g: (g, 0, chunk))
        return [first, first], [block, prev]
    return [last, first], [pl.BlockSpec((spg, rows, BLOCK), lambda g: (g, 0, 0)), prev]


def state_chunk(chunk, chunks, got, w, bias, a_log, state, lead, token, dims):
    spg, rows, heads, span, piece_heads = dims
    groups = w.shape[0]
    conv_rows = span + 2 * STATE_WIDTH
    last = chunk == chunks - 1
    if last:
        packed = piece_heads * HEAD_DIM + 16
        state_shape = pltpu.HBM((groups * spg, packed, STATE_WIDTH), bf16)
        state_spec = pl.BlockSpec((spg, packed, STATE_WIDTH), lambda g: (g, 0, 0))
    else:
        state_shape = pltpu.HBM((groups, span, STATE_WIDTH), f32)
        state_spec = per_group(span, STATE_WIDTH)

    def out(dtype, *shape):
        return pltpu.HBM((groups,) + shape, dtype)

    args, specs = chunk_specs(got, chunk, dims)
    after = [] if token is None else in_hbm(token)
    return pl.pallas_call(
        functools.partial(state_kernel, dims, chunk == 0, last),
        grid=(groups,),
        in_specs=specs
        + [
            per_group(conv_rows, 4),
            per_group(heads, 1),
            per_group(heads, 1),
            per_group(span, STATE_WIDTH),
            per_group(heads, LANES),
        ]
        + [pl.BlockSpec(memory_space=pl.ANY)] * len(after),
        out_specs=[
            per_group(span, BLOCK),
            per_group(STATE_WIDTH, BLOCK),
            per_group(heads, BLOCK),
            per_group(heads, BLOCK),
            per_group(heads, BLOCK),
            state_spec,
            per_group(heads, LANES),
        ],
        out_shape=[
            out(bf16, span, BLOCK),
            out(bf16, STATE_WIDTH, BLOCK),
            out(f32, heads, BLOCK),
            out(f32, heads, BLOCK),
            out(f32, heads, BLOCK),
            state_shape,
            out(f32, heads, LANES),
        ],
        scratch_shapes=[
            pltpu.VMEM((rows * spg, LANES + BLOCK), f32),
            pltpu.VMEM((span, BLOCK), bf16),
        ],
        compiler_params=params(40),
        cost_estimate=pl.CostEstimate(flops=4 * 10**9, bytes_accessed=10**7, transcendentals=10**6),
        name="state_chunk",
    )(*args, *in_hbm(w, bias, a_log, state, lead), *after)


def split(v):
    high = v.astype(bf16)
    return high, (v - high.astype(f32)).astype(bf16)


def block_kernel(dims, first, recv, *refs):
    spg, rows, heads, span, piece_heads = dims
    prev = None
    if not first:
        prev, refs = refs[0], refs[1:]
    w, xact, bmap, run_ref, dt_ref, cum_ref, state, skip = refs[:8]
    mixed, passed, c_all, token, raw = refs[-5:]
    conv_rows = span + 2 * STATE_WIDTH
    gather_rows(recv, prev, raw, rows, 2 * span + STATE_WIDTH, span + conv_rows)
    gather_rows(recv, prev, raw, rows, 0, span, False)
    token[0] = cum_ref[0, :8, :LANES]
    c = jnp.concatenate(
        conv_rows_of(raw, w, band(), span, span + STATE_WIDTH, STATE_WIDTH), axis=0
    )
    c_all[0, 0] = c.astype(f32).T.astype(bf16)

    b_rows = bmap[0].astype(f32).T.astype(bf16)
    scores = jnp.dot(b_rows, c, preferred_element_type=f32)
    src = lax.broadcasted_iota(jnp.int32, (HALF, HALF), 0)
    dst = lax.broadcasted_iota(jnp.int32, (HALF, HALF), 1)
    causal = src <= dst
    s00 = jnp.where(causal, scores[:HALF, :HALF], 0.0)
    s01 = scores[:HALF, HALF:]
    s11 = jnp.where(causal, scores[HALF:, HALF:], 0.0)
    r = run_ref[0] * LOG2E
    q = (r - jnp.log(dt_ref[0]) * LOG2E).T
    if not first:
        cc = jnp.concatenate([c, c], axis=0)
        entered = jnp.exp2(r)
    reach = jnp.exp(cum_ref[0])
    turned = []
    for h in range(heads):
        at = h * HEAD_DIM
        r0, r1 = r[h : h + 1, :HALF], r[h : h + 1, HALF:]
        q0, q1 = q[:HALF, h : h + 1], q[HALF:, h : h + 1]
        w00 = (s00 * jnp.exp2(jnp.minimum(r0 - q0, CAP))).astype(bf16)
        w01 = (s01 * jnp.exp2(r1 - q0)).astype(bf16)
        w11 = (s11 * jnp.exp2(jnp.minimum(r1 - q1, CAP))).astype(bf16)
        x = xact[0, at : at + HEAD_DIM, :]
        y0 = jnp.dot(x[:, :HALF], w00, preferred_element_type=f32)
        y1 = jnp.dot(x, jnp.concatenate([w01, w11], axis=0), preferred_element_type=f32)
        y = jnp.concatenate([y0, y1], axis=1) + skip[0, h : h + 1, :] * x.astype(f32)
        if not first:
            if at % WIDE == 0:
                both = jnp.concatenate(split(state[0, at : at + WIDE, :]), axis=1)
                carried = jnp.dot(both, cc, preferred_element_type=f32)
            y = y + entered[h : h + 1, :] * carried[at % WIDE : at % WIDE + HEAD_DIM, :]
        gate = silu(raw[at : at + HEAD_DIM, LANES:])
        turned.append((y * gate, gate * reach[h : h + 1, :]))
        if len(turned) * HEAD_DIM == LANES:
            lanes = slice(at + HEAD_DIM - LANES, at + HEAD_DIM)
            mixed[0, 0, :, lanes] = jnp.concatenate([pair[0] for pair in turned], axis=0).T
            passed[0, 0, :, lanes] = jnp.concatenate([pair[1] for pair in turned], axis=0).T
            turned = []


def block_chunk(
    chunk, chunks, got, w, xact, bmap, run, dt, cum, state, skip, wholes, after, dims
):
    spg, rows, heads, span, piece_heads = dims
    groups = w.shape[0]

    def whole(*shape):
        return pl.BlockSpec((1, 1) + shape, lambda g: (g, chunk, 0, 0))

    args, specs = chunk_specs(got, chunk, dims)
    args += in_hbm(w, xact, bmap, run, dt, cum, state, skip)
    specs += [
        per_group(span + 2 * STATE_WIDTH, 4),
        per_group(span, BLOCK),
        per_group(STATE_WIDTH, BLOCK),
        per_group(heads, BLOCK),
        per_group(heads, BLOCK),
        per_group(heads, BLOCK),
        per_group(span, STATE_WIDTH),
        per_group(heads, 1),
    ]
    args += in_vmem(*after)
    specs += [pl.BlockSpec(memory_space=pl.ANY)] * len(after)
    aliases = {}
    for i, array in enumerate(wholes or ()):
        aliases[len(args)] = i
        args.extend(in_vmem(array))
        specs.append(pl.BlockSpec(memory_space=pl.ANY))

    def out(dtype, *shape):
        return pltpu.HBM((groups,) + shape, dtype)

    *wholes, token = pl.pallas_call(
        functools.partial(block_kernel, dims, chunk == 0),
        grid=(groups,),
        in_specs=specs,
        out_specs=[
            whole(BLOCK, span),
            whole(BLOCK, span),
            whole(BLOCK, STATE_WIDTH),
            per_group(8, LANES),
        ],
        out_shape=[
            pltpu.VMEM((groups, chunks, BLOCK, span), f32),
            pltpu.VMEM((groups, chunks, BLOCK, span), f32),
            pltpu.VMEM((groups, chunks, BLOCK, STATE_WIDTH), bf16),
            out(f32, 8, LANES),
        ],
        scratch_shapes=[pltpu.VMEM((rows * spg, LANES + BLOCK), f32)],
        input_output_aliases=aliases,
        compiler_params=params(40),
        cost_estimate=pl.CostEstimate(flops=4 * 10**9, bytes_accessed=10**7, transcendentals=10**6),
        name="block_chunk",
    )(*args)
    return wholes, token


def relay_kernel(piece_heads, src, token, dst):
    rows = piece_heads * HEAD_DIM
    held = jnp.zeros((rows, STATE_WIDTH), f32)
    for d in range(src.shape[0]):
        dst[d] = held.T.astype(bf16)
        both = src[d, rows:, :].astype(f32)
        decay = both[:8] + both[8:]
        spread = [
            jnp.broadcast_to(decay[h : h + 1, :], (HEAD_DIM, STATE_WIDTH))
            for h in range(piece_heads)
        ]
        held = jnp.concatenate(spread, axis=0) * held + src[d, :rows, :].astype(f32)


def relay(packed, token, piece_heads):
    count = packed.shape[0]
    rows = piece_heads * HEAD_DIM
    return pl.pallas_call(
        functools.partial(relay_kernel, piece_heads),
        in_specs=[pl.BlockSpec(memory_space=pltpu.VMEM), pl.BlockSpec(memory_space=pl.ANY)],
        out_shape=pltpu.VMEM((count, STATE_WIDTH, rows), bf16),
        compiler_params=params(16),
        name="relay",
    )(packed, *in_hbm(token))


def final_kernel(mixed, passed, c_ref, state, gain, out, kept, carried):
    span = kept.shape[1]
    piece = state.shape[2]
    for i in range(state.shape[0]):
        carried[:, i * piece : (i + 1) * piece] = jnp.dot(
            c_ref[0, 0], state[i], preferred_element_type=f32
        )
    for q in range(0, BLOCK, HEAD_DIM):
        rows = slice(q, q + HEAD_DIM)
        total = jnp.zeros((HEAD_DIM, LANES), f32)
        for at in range(0, span, LANES):
            lanes = slice(at, at + LANES)
            v = mixed[0, 0, rows, lanes] + passed[0, 0, rows, lanes] * carried[rows, lanes]
            kept[rows, lanes] = v
            total = total + v * v
        mean = jnp.sum(total, axis=1, keepdims=True) * (1.0 / span)
        factor = lax.rsqrt(mean + EPSILON)
        for at in range(0, span, LANES):
            lanes = slice(at, at + LANES)
            out[rows, lanes] = (kept[rows, lanes] * factor * gain[0, :, lanes]).astype(bf16)


def finish(mixed, passed, c_all, state, gain):
    groups, chunks, _, span = mixed.shape
    spg = state.shape[0] // groups

    def tile(width):
        return pl.BlockSpec((1, 1, BLOCK, width), lambda g, c: (g, c, 0, 0))

    return pl.pallas_call(
        final_kernel,
        grid=(groups, chunks),
        in_specs=[
            tile(span),
            tile(span),
            tile(STATE_WIDTH),
            pl.BlockSpec((spg,) + state.shape[1:], lambda g, c: (g, 0, 0)),
            pl.BlockSpec((1, 1, span), lambda g, c: (g, 0, 0)),
        ],
        out_specs=pl.BlockSpec((BLOCK, span), lambda g, c: (c, g)),
        out_shape=jax.ShapeDtypeStruct((chunks * BLOCK, groups * span), bf16),
        scratch_shapes=[pltpu.VMEM((BLOCK, span), f32), pltpu.VMEM((BLOCK, span), f32)],
        compiler_params=params(40),
        name="finish",
    )(*in_vmem(mixed, passed, c_all), state, gain)


def exchange(array):
    return lax.all_to_all(array, "seq", split_axis=0, concat_axis=0, tiled=True)


def per_device(projected, conv_weight, dt_bias, a_log, d_skip, norm_gain):
    seq_count = lax.axis_size("seq")
    groups = conv_weight.shape[1]
    heads = dt_bias.shape[0] // groups
    span = heads * HEAD_DIM
    rows, all_tokens = projected.shape
    local_tokens = all_tokens // seq_count
    chunks = local_tokens // BLOCK
    spg = seq_count // groups
    piece_heads = groups * heads // seq_count
    dims = (spg, rows, heads, span, piece_heads)

    w = jnp.transpose(conv_weight, (1, 2, 0))
    bias = dt_bias.reshape(groups, heads, 1)
    rate = a_log.reshape(groups, heads, 1)
    skip = d_skip.reshape(groups, heads, 1)
    gain = norm_gain.reshape(groups, 1, span)
    state = jnp.zeros((groups, span, STATE_WIDTH), f32)
    lead = jnp.zeros((groups, heads, LANES), f32)

    split_at = local_tokens - BLOCK
    cut = cut_blocks(projected, seq_count, 0, split_at, [])
    got = [exchange(cut)]
    ready = [cut, w, bias, rate, skip, gain, state, lead]
    got.append(exchange(cut_blocks(projected, seq_count, split_at, local_tokens, ready)))
    wholes = None
    tokens = []
    for c in range(chunks):
        xact, bmap, run, dt, cum, new, lead = state_chunk(
            c, chunks, got, w, bias, rate, state, lead, tokens[c - 2] if c > 1 else None, dims
        )
        after = []
        if c == chunks - 1:
            entering = relay(exchange(new), tokens[-1], piece_heads)
            after = [entering]
        wholes, token = block_chunk(
            c, chunks, got, w, xact, bmap, run, dt, cum, state, skip, wholes, after, dims
        )
        tokens.append(token)
        state = new
    return finish(*wholes, exchange(entering), gain)


def solution(mesh):
    in_specs = (P(("tp", "seq"), None), P(None, "tp", None), P("tp"), P("tp"), P("tp"), P("tp"))
    return jax.shard_map(
        per_device, mesh=mesh, in_specs=in_specs, out_specs=P("seq", "tp"), check_vma=False
    )
```

```python
import functools

import jax
import jax.numpy as jnp
from jax import lax
from jax.experimental import pallas as pl
from jax.experimental.pallas import tpu as pltpu
from jax.sharding import PartitionSpec as P

HEAD_DIM = 64
STATE_WIDTH = 128
BLOCK = 256
LANES = 128
HALF = BLOCK // 2
WIDE = 256
LOG2E = 1.4426950408889634
CAP = 80.0
EPSILON = 1e-05

f32 = jnp.float32
bf16 = jnp.bfloat16
NT = (((1,), (1,)), ((), ()))


def params(mib=60):
    return pltpu.CompilerParams(vmem_limit_bytes=mib * 2**20)


def silu(v):
    half = 0.5 * v
    return half + half * jnp.tanh(half)


def softplus(v):
    e = jnp.exp(-jnp.abs(v))
    u = 1.0 + e
    gap = u - 1.0
    tiny = gap == 0.0
    log_part = jnp.where(tiny, e, jnp.log(u) * (e / jnp.where(tiny, 1.0, gap)))
    return jnp.maximum(v, 0.0) + log_part


def in_hbm(*arrays):
    return [pltpu.with_memory_space_constraint(array, pltpu.HBM) for array in arrays]


def in_vmem(*arrays):
    return [pltpu.with_memory_space_constraint(array, pltpu.VMEM) for array in arrays]


def per_group(*shape):
    return pl.BlockSpec((1,) + shape, lambda g: (g,) + (0,) * len(shape))


RIM = 4


def rim_rows(rows):
    base = rows // 16 * 16
    height = -(-(rows - base + RIM) // 8) * 8
    assert height <= 16
    return base, height


def cut_kernel(low, count, src, *refs):
    refs = refs[len(refs) - (4 if low else 7) :]
    dst, held, in_sems, out_sems = refs[:4]
    rows, all_tokens = src.shape
    tokens = all_tokens // count
    width = dst.shape[2]
    sent = held if low else refs[5]

    def fetch(d):
        at = d * tokens + low
        return pltpu.make_async_copy(src.at[:, at : at + width], held.at[d], in_sems.at[d])

    def place(d):
        return pltpu.make_async_copy(sent.at[d], dst.at[d], out_sems.at[d])

    if low:
        for d in range(count):
            fetch(d).start()
        for d in range(count):
            fetch(d).wait()
            place(d).start()
    else:
        windows, rim_sems = refs[4], refs[6]

        def window(d):
            at = d * tokens - LANES
            return pltpu.make_async_copy(src.at[:, at : at + LANES], windows.at[d], rim_sems.at[d])

        for d in range(count):
            if d:
                window(d).start()
            fetch(d).start()
        base, height = rim_rows(rows)
        row = lax.broadcasted_iota(jnp.int32, (height, LANES), 0) - (rows - base)
        col = lax.broadcasted_iota(jnp.int32, (height, LANES), 1)
        hit = (col == row + LANES - RIM) & (row >= 0) & (row < RIM)
        pick = jnp.where(hit, 1.0, 0.0).astype(bf16)
        for d in range(count):
            fetch(d).wait()
            sent[d, :base, :] = held[d, :base, :]
            end = held[d, base:rows, :].astype(f32)
            end = jnp.concatenate([end, jnp.zeros((height - end.shape[0], width), f32)], axis=0)
            if d:
                window(d).wait()
                rims = lax.dot_general(pick, windows[d], NT, preferred_element_type=f32)
                fill = jnp.zeros((height, width - rows), f32)
                end = end + jnp.concatenate([rims, fill], axis=1)
            sent[d, base : base + height, :] = end.astype(bf16)
            place(d).start()
    for d in range(count):
        place(d).wait()


def cut_blocks(projected, count, low, high, after):
    rows = projected.shape[0]
    width = high - low
    args = in_hbm(projected)
    out_rows = rows
    sems = pltpu.SemaphoreType.DMA((count,))
    scratch = [pltpu.VMEM((count, rows, width), bf16), sems, sems]
    if low == 0:
        assert width >= rows
        out_rows = sum(rim_rows(rows))
        scratch += [
            pltpu.VMEM((count, rows, LANES), bf16),
            pltpu.VMEM((count, out_rows, width), bf16),
            sems,
        ]
    args += after
    return pl.pallas_call(
        functools.partial(cut_kernel, low, count),
        in_specs=[pl.BlockSpec(memory_space=pl.ANY)] * len(args),
        out_specs=pl.BlockSpec(memory_space=pl.ANY),
        out_shape=pltpu.HBM((count, out_rows, width), bf16),
        scratch_shapes=scratch,
        compiler_params=params(),
        name="cut_blocks",
    )(*args)


def gather_rows(recv, prev, first, raw, rows, low, high, ahead=True):
    for s in range(recv.shape[0]):
        a = max(low - s * rows, 0) // 16 * 16
        b = min(-(-(high - s * rows) // 16) * 16, rows)
        if b <= a:
            continue
        at = s * rows + a
        raw[at : at + b - a, LANES:] = recv[s, a:b, :].astype(f32)
        if not ahead:
            continue
        if not first:
            raw[at : at + b - a, :LANES] = prev[s, a:b, :].astype(f32)
            continue
        base, height = rim_rows(rows)
        wide = -(-rows // LANES) * LANES
        rims = prev[s, :height, :wide].astype(f32)
        shift = height - RIM - (rows - base)
        if shift:
            rims = pltpu.roll(rims, shift, 0)
        tall = jnp.concatenate([jnp.zeros((LANES - height, wide), f32), rims], axis=0).T
        raw[at : at + b - a, :LANES] = tall[a:b]


def band():
    row = lax.broadcasted_iota(jnp.int32, (2 * LANES, 3 * LANES), 0)
    col = lax.broadcasted_iota(jnp.int32, (2 * LANES, 3 * LANES), 1)
    tap = col // LANES
    return jnp.where(row == col - tap * LANES + LANES - 3 + tap, 1.0, 0.0).astype(bf16)


def conv_rows_of(raw, w, picks, span, r, height):
    low = raw[span + r : span + r + height, :].astype(bf16)
    shifted = [
        jnp.dot(low[:, at : at + 2 * LANES], picks, preferred_element_type=f32)
        for at in range(0, BLOCK, LANES)
    ]
    tiles = []
    for q in range(0, height, HEAD_DIM):
        at = r + q
        taps = [
            jnp.broadcast_to(w[0, at : at + HEAD_DIM, k : k + 1], (HEAD_DIM, LANES))
            for k in range(4)
        ]
        parts = []
        for i, three in enumerate(shifted):
            summed = None
            for k in range(3):
                part = taps[k] * three[q : q + HEAD_DIM, k * LANES : (k + 1) * LANES]
                summed = part if summed is None else summed + part
            own = raw[span + at : span + at + HEAD_DIM, (i + 1) * LANES : (i + 2) * LANES]
            parts.append(silu(summed + taps[3] * own).astype(bf16))
        tiles.append(jnp.concatenate(parts, axis=1))
    return tiles


def state_kernel(dims, first, last, recv, *refs):
    spg, rows, heads, span, piece_heads = dims
    prev, refs = refs[0], refs[1:]
    w, bias, a_log, state_in, lead_in = refs[:5]
    xact, bmap, run_out, dt_out, cum_out, state_out, lead_out, raw, xw = refs[-9:]
    steps = 2 * span + 2 * STATE_WIDTH

    gather_rows(recv, prev, first, raw, rows, steps, steps + heads, False)
    gather_rows(recv, prev, first, raw, rows, span, 2 * span + STATE_WIDTH)
    dt = softplus(raw[steps : steps + heads, LANES:] + bias[0])
    log_decay = -jnp.exp(a_log[0]) * dt
    lane = lax.broadcasted_iota(jnp.int32, (heads, BLOCK), 1)
    run = log_decay
    shift = 1
    while shift < BLOCK:
        run = run + jnp.where(lane >= shift, pltpu.roll(run, shift, 1), 0.0)
        shift *= 2
    final = run[:, BLOCK - 1 :]
    scale = jnp.exp(final - run) * dt
    cum = run + lead_in[0][:, :1]
    run_out[0] = run
    dt_out[0] = dt
    cum_out[0] = cum
    lead = jnp.broadcast_to(cum[:, BLOCK - 1 :], (heads, LANES))
    lead_out[0] = lead
    keep = jnp.broadcast_to(jnp.exp(final), (heads, LANES))

    picks = band()
    for i, tile in enumerate(conv_rows_of(raw, w, picks, span, span, STATE_WIDTH)):
        bmap[0, i * HEAD_DIM : (i + 1) * HEAD_DIM, :] = tile
    for r in range(0, span, WIDE):
        for i, tile in enumerate(conv_rows_of(raw, w, picks, span, r, WIDE)):
            at = r + i * HEAD_DIM
            h = at // HEAD_DIM
            xact[0, at : at + HEAD_DIM, :] = tile
            xw[at : at + HEAD_DIM, :] = (tile.astype(f32) * scale[h : h + 1, :]).astype(bf16)
    update = lax.dot_general(xw[...], bmap[0], NT, preferred_element_type=f32)
    for h in range(heads):
        r = h * HEAD_DIM
        new = update[r : r + HEAD_DIM, :]
        if not first:
            new = keep[h : h + 1, :] * state_in[0, r : r + HEAD_DIM, :] + new
        if last:
            at = (h % piece_heads) * HEAD_DIM
            state_out[h // piece_heads, at : at + HEAD_DIM, :] = new.astype(bf16)
        else:
            state_out[0, r : r + HEAD_DIM, :] = new
    if last:
        high, low = split(jnp.exp(lead))
        fill = jnp.zeros((8 - piece_heads, LANES), f32)
        for i in range(heads // piece_heads):
            mine = slice(i * piece_heads, (i + 1) * piece_heads)
            parts = [high[mine].astype(f32), fill, low[mine].astype(f32), fill]
            at = piece_heads * HEAD_DIM
            state_out[i, at : at + 16, :] = jnp.concatenate(parts, axis=0).astype(bf16)


def chunk_specs(got, chunk, dims):
    spg, rows = dims[:2]
    first, last = got
    held, width = first.shape[1:]
    block = pl.BlockSpec((spg, held, BLOCK), lambda g: (g, 0, chunk))
    if chunk == 0:
        rims = pl.BlockSpec((spg, 16, width), lambda g: (g, rim_rows(rows)[0] // 16, 0))
        return [first, first], [block, rims]
    at = 2 * chunk - 1
    prev = pl.BlockSpec((spg, held, LANES), lambda g: (g, 0, at))
    if chunk < width // BLOCK:
        return [first, first], [block, prev]
    return [last, first], [pl.BlockSpec((spg, rows, BLOCK), lambda g: (g, 0, 0)), prev]


def state_chunk(chunk, chunks, got, w, bias, a_log, state, lead, token, dims):
    spg, rows, heads, span, piece_heads = dims
    groups = w.shape[0]
    conv_rows = span + 2 * STATE_WIDTH
    last = chunk == chunks - 1
    if last:
        packed = piece_heads * HEAD_DIM + 16
        state_shape = pltpu.HBM((groups * spg, packed, STATE_WIDTH), bf16)
        state_spec = pl.BlockSpec((spg, packed, STATE_WIDTH), lambda g: (g, 0, 0))
    else:
        state_shape = pltpu.HBM((groups, span, STATE_WIDTH), f32)
        state_spec = per_group(span, STATE_WIDTH)

    def out(dtype, *shape):
        return pltpu.HBM((groups,) + shape, dtype)

    args, specs = chunk_specs(got, chunk, dims)
    args[1:] = in_hbm(args[1])
    args[:1] = in_vmem(args[0]) if last else in_hbm(args[0])
    after = [] if token is None else in_hbm(token)
    return pl.pallas_call(
        functools.partial(state_kernel, dims, chunk == 0, last),
        grid=(groups,),
        in_specs=specs
        + [
            per_group(conv_rows, 4),
            per_group(heads, 1),
            per_group(heads, 1),
            per_group(span, STATE_WIDTH),
            per_group(heads, LANES),
        ]
        + [pl.BlockSpec(memory_space=pl.ANY)] * len(after),
        out_specs=[
            per_group(span, BLOCK),
            per_group(STATE_WIDTH, BLOCK),
            per_group(heads, BLOCK),
            per_group(heads, BLOCK),
            per_group(heads, BLOCK),
            state_spec,
            per_group(heads, LANES),
        ],
        out_shape=[
            out(bf16, span, BLOCK),
            out(bf16, STATE_WIDTH, BLOCK),
            out(f32, heads, BLOCK),
            out(f32, heads, BLOCK),
            out(f32, heads, BLOCK),
            state_shape,
            out(f32, heads, LANES),
        ],
        scratch_shapes=[
            pltpu.VMEM((rows * spg, LANES + BLOCK), f32),
            pltpu.VMEM((span, BLOCK), bf16),
        ],
        compiler_params=params(48 if last else 60),
        cost_estimate=pl.CostEstimate(flops=4 * 10**9, bytes_accessed=10**7, transcendentals=10**6),
        name="state_chunk",
    )(*args, *in_hbm(w, bias, a_log, state, lead), *after)


def split(v):
    high = v.astype(bf16)
    return high, (v - high.astype(f32)).astype(bf16)


def block_kernel(dims, first, recv, *refs):
    spg, rows, heads, span, piece_heads = dims
    prev, refs = refs[0], refs[1:]
    w, xact, bmap, run_ref, dt_ref, cum_ref, state, skip = refs[:8]
    mixed, gate_out, side, token, raw = refs[-5:]
    conv_rows = span + 2 * STATE_WIDTH
    gather_rows(recv, prev, first, raw, rows, 2 * span + STATE_WIDTH, span + conv_rows)
    gather_rows(recv, prev, first, raw, rows, 0, span, False)
    token[0] = cum_ref[0, :8, :LANES]
    c = jnp.concatenate(
        conv_rows_of(raw, w, band(), span, span + STATE_WIDTH, STATE_WIDTH), axis=0
    )

    b_rows = bmap[0].astype(f32).T.astype(bf16)
    scores = jnp.dot(b_rows, c, preferred_element_type=f32)
    src = lax.broadcasted_iota(jnp.int32, (HALF, HALF), 0)
    dst = lax.broadcasted_iota(jnp.int32, (HALF, HALF), 1)
    causal = src <= dst
    s00 = jnp.where(causal, scores[:HALF, :HALF], 0.0)
    s01 = scores[:HALF, HALF:]
    s11 = jnp.where(causal, scores[HALF:, HALF:], 0.0)
    r = run_ref[0] * LOG2E
    q = (r - jnp.log(dt_ref[0]) * LOG2E).T
    if not first:
        cc = jnp.concatenate([c, c], axis=0)
        entered = jnp.exp2(r)
    reach = [part.astype(f32) for part in split(jnp.exp(cum_ref[0]))]
    reach.append(jnp.zeros((STATE_WIDTH - 2 * heads, BLOCK), f32))
    side[0, :, :STATE_WIDTH] = c.astype(f32).T.astype(bf16)
    side[0, :, STATE_WIDTH:] = jnp.concatenate(reach, axis=0).T.astype(bf16)
    turned = []
    for h in range(heads):
        at = h * HEAD_DIM
        r0, r1 = r[h : h + 1, :HALF], r[h : h + 1, HALF:]
        q0, q1 = q[:HALF, h : h + 1], q[HALF:, h : h + 1]
        w00 = (s00 * jnp.exp2(jnp.minimum(r0 - q0, CAP))).astype(bf16)
        w01 = (s01 * jnp.exp2(r1 - q0)).astype(bf16)
        w11 = (s11 * jnp.exp2(jnp.minimum(r1 - q1, CAP))).astype(bf16)
        x = xact[0, at : at + HEAD_DIM, :]
        y0 = jnp.dot(x[:, :HALF], w00, preferred_element_type=f32)
        y1 = jnp.dot(x, jnp.concatenate([w01, w11], axis=0), preferred_element_type=f32)
        y = jnp.concatenate([y0, y1], axis=1) + skip[0, h : h + 1, :] * x.astype(f32)
        if not first:
            if at % WIDE == 0:
                both = jnp.concatenate(split(state[0, at : at + WIDE, :]), axis=1)
                carried = jnp.dot(both, cc, preferred_element_type=f32)
            y = y + entered[h : h + 1, :] * carried[at % WIDE : at % WIDE + HEAD_DIM, :]
        gate = raw[at : at + HEAD_DIM, LANES:]
        turned.append((y * silu(gate), gate))
        if len(turned) * HEAD_DIM == LANES:
            lanes = slice(at + HEAD_DIM - LANES, at + HEAD_DIM)
            mixed[0, :, lanes] = jnp.concatenate([pair[0] for pair in turned], axis=0).T
            wide = jnp.concatenate([pair[1] for pair in turned], axis=0).T
            gate_out[0, :, lanes] = wide.astype(bf16)
            turned = []


def block_chunk(
    chunk, chunks, got, w, xact, bmap, run, dt, cum, state, skip, after, dims
):
    spg, rows, heads, span, piece_heads = dims
    groups = w.shape[0]

    args, specs = chunk_specs(got, chunk, dims)
    args = in_hbm(*args)
    args += in_hbm(w, xact, bmap, run, dt, cum, state, skip)
    specs += [
        per_group(span + 2 * STATE_WIDTH, 4),
        per_group(span, BLOCK),
        per_group(STATE_WIDTH, BLOCK),
        per_group(heads, BLOCK),
        per_group(heads, BLOCK),
        per_group(heads, BLOCK),
        per_group(span, STATE_WIDTH),
        per_group(heads, 1),
    ]
    args += in_vmem(*after)
    specs += [pl.BlockSpec(memory_space=pl.ANY)] * len(after)

    def out(dtype, *shape):
        return pltpu.HBM((groups,) + shape, dtype)

    return pl.pallas_call(
        functools.partial(block_kernel, dims, chunk == 0),
        grid=(groups,),
        in_specs=specs,
        out_specs=[
            per_group(BLOCK, span),
            per_group(BLOCK, span),
            per_group(BLOCK, 2 * STATE_WIDTH),
            per_group(8, LANES),
        ],
        out_shape=[
            out(f32, BLOCK, span),
            out(bf16, BLOCK, span),
            out(bf16, BLOCK, 2 * STATE_WIDTH),
            out(f32, 8, LANES),
        ],
        scratch_shapes=[pltpu.VMEM((rows * spg, LANES + BLOCK), f32)],
        compiler_params=params(),
        cost_estimate=pl.CostEstimate(flops=4 * 10**9, bytes_accessed=10**7, transcendentals=10**6),
        name="block_chunk",
    )(*args)


def relay_kernel(piece_heads, src, token, dst):
    rows = piece_heads * HEAD_DIM
    held = jnp.zeros((rows, STATE_WIDTH), f32)
    for d in range(src.shape[0]):
        dst[d] = held.T.astype(bf16)
        both = src[d, rows:, :].astype(f32)
        decay = both[:8] + both[8:]
        spread = [
            jnp.broadcast_to(decay[h : h + 1, :], (HEAD_DIM, STATE_WIDTH))
            for h in range(piece_heads)
        ]
        held = jnp.concatenate(spread, axis=0) * held + src[d, :rows, :].astype(f32)


def relay(packed, token, piece_heads):
    count = packed.shape[0]
    rows = piece_heads * HEAD_DIM
    return pl.pallas_call(
        functools.partial(relay_kernel, piece_heads),
        in_specs=[pl.BlockSpec(memory_space=pltpu.VMEM), pl.BlockSpec(memory_space=pl.ANY)],
        out_shape=pltpu.VMEM((count, STATE_WIDTH, rows), bf16),
        compiler_params=params(16),
        name="relay",
    )(packed, *in_hbm(token))


DEEP = 3


def final_kernel(chunks, groups, *refs):
    mixed, gates, sides = (refs[i * chunks : (i + 1) * chunks] for i in range(3))
    state, gain, out = refs[3 * chunks : 3 * chunks + 3]
    held, gate_held, side_held, kept, carried, done, sems, out_sems = refs[3 * chunks + 3 :]
    span = held.shape[2]
    piece = state.shape[2]
    spg = state.shape[0] // groups
    heads = span // HEAD_DIM
    steps = [(g, c) for g in range(groups) for c in range(chunks)]

    def loads(i):
        g, c = steps[i]
        slot = i % DEEP
        moves = []
        half = BLOCK // 2
        for j in range(2):
            rows = slice(j * half, (j + 1) * half)
            moves.append((mixed[c].at[g, rows], held.at[slot, rows]))
            moves.append((gates[c].at[g, rows], gate_held.at[slot, rows]))
        moves.append((sides[c].at[g], side_held.at[slot]))
        return [
            pltpu.make_async_copy(a, b, sems.at[slot, j]) for j, (a, b) in enumerate(moves)
        ]

    def store(i):
        g, c = steps[i]
        return pltpu.make_async_copy(
            done.at[i % 2],
            out.at[c * BLOCK : (c + 1) * BLOCK, g * span : (g + 1) * span],
            out_sems.at[i % 2],
        )

    for i in range(min(DEEP, len(steps))):
        for move in loads(i):
            move.start()
    row = lax.broadcasted_iota(jnp.int32, (STATE_WIDTH, span), 0)
    col = lax.broadcasted_iota(jnp.int32, (STATE_WIDTH, span), 1) // HEAD_DIM
    spread = jnp.where((row == col) | (row == col + heads), 1.0, 0.0).astype(bf16)
    for i, (g, c) in enumerate(steps):
        slot = i % DEEP
        for move in loads(i):
            move.wait()
        if i >= 2:
            store(i - 2).wait()
        side = side_held[slot]
        reach = jnp.dot(side[:, STATE_WIDTH:], spread, preferred_element_type=f32)
        for j in range(spg):
            lanes = slice(j * piece, (j + 1) * piece)
            part = jnp.dot(
                side[:, :STATE_WIDTH], state[g * spg + j], preferred_element_type=f32
            )
            carried[:, lanes] = part * reach[:, lanes]
        for q in range(0, BLOCK, HEAD_DIM):
            rows = slice(q, q + HEAD_DIM)
            total = jnp.zeros((HEAD_DIM, LANES), f32)
            for at in range(0, span, LANES):
                lanes = slice(at, at + LANES)
                gate = silu(gate_held[slot, rows, lanes].astype(f32))
                v = held[slot, rows, lanes] + gate * carried[rows, lanes]
                kept[rows, lanes] = v
                total = total + v * v
            mean = jnp.sum(total, axis=1, keepdims=True) * (1.0 / span)
            factor = lax.rsqrt(mean + EPSILON)
            for at in range(0, span, LANES):
                lanes = slice(at, at + LANES)
                scaled = kept[rows, lanes] * factor * gain[g, :, lanes]
                done[i % 2, rows, lanes] = scaled.astype(bf16)
        store(i).start()
        if i + DEEP < len(steps):
            for move in loads(i + DEEP):
                move.start()
    for i in range(max(len(steps) - 2, 0), len(steps)):
        store(i).wait()


def finish(mixed, gates, sides, state, gain):
    chunks = len(mixed)
    groups, _, span = mixed[0].shape
    anywhere = pl.BlockSpec(memory_space=pl.ANY)
    within = pl.BlockSpec(memory_space=pltpu.VMEM)
    return pl.pallas_call(
        functools.partial(final_kernel, chunks, groups),
        in_specs=[anywhere] * (3 * chunks) + [within] * 2,
        out_specs=anywhere,
        out_shape=jax.ShapeDtypeStruct((chunks * BLOCK, groups * span), bf16),
        scratch_shapes=[
            pltpu.VMEM((DEEP, BLOCK, span), f32),
            pltpu.VMEM((DEEP, BLOCK, span), bf16),
            pltpu.VMEM((DEEP, BLOCK, 2 * STATE_WIDTH), bf16),
            pltpu.VMEM((BLOCK, span), f32),
            pltpu.VMEM((BLOCK, span), f32),
            pltpu.VMEM((2, BLOCK, span), bf16),
            pltpu.SemaphoreType.DMA((DEEP, 5)),
            pltpu.SemaphoreType.DMA((2,)),
        ],
        compiler_params=params(40),
        name="finish",
    )(*in_hbm(*mixed, *gates, *sides), state, gain)


def exchange(array):
    return lax.all_to_all(array, "seq", split_axis=0, concat_axis=0, tiled=True)


def per_device(projected, conv_weight, dt_bias, a_log, d_skip, norm_gain):
    seq_count = lax.axis_size("seq")
    groups = conv_weight.shape[1]
    heads = dt_bias.shape[0] // groups
    span = heads * HEAD_DIM
    rows, all_tokens = projected.shape
    local_tokens = all_tokens // seq_count
    chunks = local_tokens // BLOCK
    spg = seq_count // groups
    piece_heads = groups * heads // seq_count
    dims = (spg, rows, heads, span, piece_heads)

    w = jnp.transpose(conv_weight, (1, 2, 0))
    bias = dt_bias.reshape(groups, heads, 1)
    rate = a_log.reshape(groups, heads, 1)
    skip = d_skip.reshape(groups, heads, 1)
    gain = norm_gain.reshape(groups, 1, span)
    state = jnp.zeros((groups, span, STATE_WIDTH), f32)
    lead = jnp.zeros((groups, heads, LANES), f32)

    split_at = local_tokens - BLOCK
    cut = cut_blocks(projected, seq_count, 0, split_at, [])
    got = [exchange(cut)]
    ready = [cut, w, bias, rate, skip, gain, state, lead]
    got.append(exchange(cut_blocks(projected, seq_count, split_at, local_tokens, ready)))
    results, tokens = [], []
    for c in range(chunks):
        xact, bmap, run, dt, cum, new, lead = state_chunk(
            c, chunks, got, w, bias, rate, state, lead, tokens[c - 2] if c > 1 else None, dims
        )
        after = []
        if c == chunks - 1:
            entering = relay(exchange(new), tokens[-1], piece_heads)
            after = [entering]
        *result, token = block_chunk(
            c, chunks, got, w, xact, bmap, run, dt, cum, state, skip, after, dims
        )
        results.append(result)
        tokens.append(token)
        state = new
    return finish(*zip(*results), exchange(entering), gain)


def solution(mesh):
    in_specs = (P(("tp", "seq"), None), P(None, "tp", None), P("tp"), P("tp"), P("tp"), P("tp"))
    return jax.shard_map(
        per_device, mesh=mesh, in_specs=in_specs, out_specs=P("seq", "tp"), check_vma=False
    )
```

```python
import functools

import jax
import jax.numpy as jnp
from jax import lax
from jax.experimental import pallas as pl
from jax.experimental.pallas import tpu as pltpu
from jax.sharding import PartitionSpec as P

HEAD_DIM = 64
STATE_WIDTH = 128
BLOCK = 256
LANES = 128
HALF = BLOCK // 2
WIDE = 256
LOG2E = 1.4426950408889634
CAP = 80.0
EPSILON = 1e-05

f32 = jnp.float32
bf16 = jnp.bfloat16
NT = (((1,), (1,)), ((), ()))


def params(mib=60):
    return pltpu.CompilerParams(vmem_limit_bytes=mib * 2**20)


def silu(v):
    half = 0.5 * v
    return half + half * jnp.tanh(half)


def softplus(v):
    e = jnp.exp(-jnp.abs(v))
    u = 1.0 + e
    gap = u - 1.0
    tiny = gap == 0.0
    log_part = jnp.where(tiny, e, jnp.log(u) * (e / jnp.where(tiny, 1.0, gap)))
    return jnp.maximum(v, 0.0) + log_part


def in_hbm(*arrays):
    return [pltpu.with_memory_space_constraint(array, pltpu.HBM) for array in arrays]


def in_vmem(*arrays):
    return [pltpu.with_memory_space_constraint(array, pltpu.VMEM) for array in arrays]


def per_group(*shape):
    return pl.BlockSpec((1,) + shape, lambda g: (g,) + (0,) * len(shape))


RIM = 4
AHEAD = 3


def rim_rows(rows):
    base = rows // 16 * 16
    height = -(-(rows - base + RIM) // 8) * 8
    assert height <= 16
    return base, height


def cut_kernel(low, count, src, *refs):
    refs = refs[len(refs) - (4 if low else 8) :]
    dst, held, in_sems, out_sems = refs[:4]
    rows, all_tokens = src.shape
    tokens = all_tokens // count
    width = dst.shape[2]
    base, height = rim_rows(rows)

    def fetch(d):
        at = d * tokens + low
        return pltpu.make_async_copy(src.at[:, at : at + width], held.at[d], in_sems.at[d])

    def place(d):
        if low:
            return pltpu.make_async_copy(held.at[d], dst.at[d], out_sems.at[d])
        return pltpu.make_async_copy(
            held.at[d, :base, :], dst.at[d, :base, :], out_sems.at[d]
        )

    def window(d):
        at = d * tokens - LANES
        return pltpu.make_async_copy(src.at[:, at : at + LANES], windows.at[d], rim_sems.at[d])

    def place_end(d):
        return pltpu.make_async_copy(
            ends.at[d], dst.at[d, base : base + height, :], end_sems.at[d]
        )

    for d in range(min(AHEAD, count)):
        fetch(d).start()
    if not low:
        windows, ends, rim_sems, end_sems = refs[4:]
        for d in range(1, count):
            window(d).start()
        row = lax.broadcasted_iota(jnp.int32, (height, LANES), 0) - (rows - base)
        col = lax.broadcasted_iota(jnp.int32, (height, LANES), 1)
        hit = (col == row + LANES - RIM) & (row >= 0) & (row < RIM)
        pick = jnp.where(hit, 1.0, 0.0).astype(bf16)
    for d in range(count):
        fetch(d).wait()
        place(d).start()
        if d + AHEAD < count:
            fetch(d + AHEAD).start()
        if not low:
            end = held[d, base:rows, :].astype(f32)
            end = jnp.concatenate([end, jnp.zeros((height - end.shape[0], width), f32)], axis=0)
            if d:
                window(d).wait()
                rims = lax.dot_general(pick, windows[d], NT, preferred_element_type=f32)
                fill = jnp.zeros((height, width - rows), f32)
                end = end + jnp.concatenate([rims, fill], axis=1)
            ends[d] = end.astype(bf16)
            place_end(d).start()
    for d in range(count):
        place(d).wait()
        if not low:
            place_end(d).wait()


def cut_blocks(projected, count, low, high, after):
    rows = projected.shape[0]
    width = high - low
    args = in_hbm(projected)
    out_rows = rows
    sems = pltpu.SemaphoreType.DMA((count,))
    scratch = [pltpu.VMEM((count, rows, width), bf16), sems, sems]
    if low == 0:
        assert width >= rows
        base, height = rim_rows(rows)
        out_rows = base + height
        scratch += [
            pltpu.VMEM((count, rows, LANES), bf16),
            pltpu.VMEM((count, height, width), bf16),
            sems,
            sems,
        ]
    args += after
    return pl.pallas_call(
        functools.partial(cut_kernel, low, count),
        in_specs=[pl.BlockSpec(memory_space=pl.ANY)] * len(args),
        out_specs=pl.BlockSpec(memory_space=pl.ANY),
        out_shape=pltpu.HBM((count, out_rows, width), bf16),
        scratch_shapes=scratch,
        compiler_params=params(),
        name="cut_blocks",
    )(*args)


def gather_rows(recv, prev, first, raw, rows, low, high, ahead=True, only=None):
    for s in range(recv.shape[0]):
        a = max(low - s * rows, 0) // 16 * 16
        b = min(-(-(high - s * rows) // 16) * 16, rows)
        if b <= a:
            continue
        at = s * rows + a
        raw[at : at + b - a, LANES:] = recv[s, a:b, :].astype(f32)
        if not ahead:
            continue
        if not first:
            raw[at : at + b - a, :LANES] = prev[s if only is None else 0, a:b, :].astype(f32)
            continue
        base, height = rim_rows(rows)
        wide = -(-rows // LANES) * LANES
        rims = prev[s if only is None else 0, :height, :wide].astype(f32)
        shift = height - RIM - (rows - base)
        if shift:
            rims = pltpu.roll(rims, shift, 0)
        tall = jnp.concatenate([jnp.zeros((LANES - height, wide), f32), rims], axis=0).T
        raw[at : at + b - a, :LANES] = tall[a:b]


def band():
    row = lax.broadcasted_iota(jnp.int32, (2 * LANES, 3 * LANES), 0)
    col = lax.broadcasted_iota(jnp.int32, (2 * LANES, 3 * LANES), 1)
    tap = col // LANES
    return jnp.where(row == col - tap * LANES + LANES - 3 + tap, 1.0, 0.0).astype(bf16)


def shift_rows(raw, low, shifted, at):
    low[...] = raw[at : at + low.shape[0], :].astype(bf16)
    picks = band()
    for i in range(BLOCK // LANES):
        window = low[:, i * LANES : (i + 2) * LANES]
        shifted[i] = jnp.dot(window, picks, preferred_element_type=f32)


def conv_tile(raw, shifted, w, at, r):
    rows = slice(r, r + HEAD_DIM)
    taps = [jnp.broadcast_to(w[0, rows, k : k + 1], (HEAD_DIM, LANES)) for k in range(4)]
    parts = []
    for i in range(BLOCK // LANES):
        summed = None
        for k in range(3):
            part = taps[k] * shifted[i, rows, k * LANES : (k + 1) * LANES]
            summed = part if summed is None else summed + part
        own = raw[at + r : at + r + HEAD_DIM, (i + 1) * LANES : (i + 2) * LANES]
        parts.append(silu(summed + taps[3] * own).astype(bf16))
    return jnp.concatenate(parts, axis=1)


def state_kernel(dims, first, last, recv, *refs):
    spg, rows, heads, span, piece_heads = dims
    prev, refs = refs[0], refs[1:]
    w, bias, a_log, state_in, lead_in = refs[:5]
    xact, bmap, run_out, dt_out, cum_out, state_out, lead_out = refs[-11:-4]
    raw, xw, low, shifted = refs[-4:]
    steps = 2 * span + 2 * STATE_WIDTH

    gather_rows(recv, prev, first, raw, rows, steps, steps + heads, False)
    gather_rows(recv, prev, first, raw, rows, span, 2 * span + STATE_WIDTH)
    dt = softplus(raw[steps : steps + heads, LANES:] + bias[0])
    log_decay = -jnp.exp(a_log[0]) * dt
    lane = lax.broadcasted_iota(jnp.int32, (heads, BLOCK), 1)
    run = log_decay
    shift = 1
    while shift < BLOCK:
        run = run + jnp.where(lane >= shift, pltpu.roll(run, shift, 1), 0.0)
        shift *= 2
    final = run[:, BLOCK - 1 :]
    scale = jnp.exp(final - run) * dt
    cum = run + lead_in[0][:, :1]
    run_out[0] = run
    dt_out[0] = dt
    cum_out[0] = cum
    lead = jnp.broadcast_to(cum[:, BLOCK - 1 :], (heads, LANES))
    lead_out[0] = lead
    keep = jnp.broadcast_to(jnp.exp(final), (heads, LANES))

    shift_rows(raw, low, shifted, span)
    for r in range(0, STATE_WIDTH, HEAD_DIM):
        bmap[0, r : r + HEAD_DIM, :] = conv_tile(raw, shifted, w, span, span + r)
    for h in range(heads):
        r = h * HEAD_DIM
        tile = conv_tile(raw, shifted, w, span, r)
        xact[0, r : r + HEAD_DIM, :] = tile
        xw[r : r + HEAD_DIM, :] = (tile.astype(f32) * scale[h : h + 1, :]).astype(bf16)
    update = lax.dot_general(xw[...], bmap[0], NT, preferred_element_type=f32)
    for h in range(heads):
        r = h * HEAD_DIM
        new = update[r : r + HEAD_DIM, :]
        if not first:
            new = keep[h : h + 1, :] * state_in[0, r : r + HEAD_DIM, :] + new
        if last:
            at = (h % piece_heads) * HEAD_DIM
            state_out[h // piece_heads, at : at + HEAD_DIM, :] = new.astype(bf16)
        else:
            state_out[0, r : r + HEAD_DIM, :] = new
    if last:
        high, low = split(jnp.exp(lead))
        fill = jnp.zeros((8 - piece_heads, LANES), f32)
        for i in range(heads // piece_heads):
            mine = slice(i * piece_heads, (i + 1) * piece_heads)
            parts = [high[mine].astype(f32), fill, low[mine].astype(f32), fill]
            at = piece_heads * HEAD_DIM
            state_out[i, at : at + 16, :] = jnp.concatenate(parts, axis=0).astype(bf16)


def chunk_specs(got, chunk, dims, only=None):
    spg, rows = dims[:2]
    first, last = got
    held, width = first.shape[1:]
    slabs = spg if only is None else 1

    def ahead(shape, row, lane):
        def index(g):
            return (g if only is None else g * spg + only, row, lane)

        return pl.BlockSpec((slabs,) + shape, index)

    block = pl.BlockSpec((spg, held, BLOCK), lambda g: (g, 0, chunk))
    if chunk == 0:
        return [first, first], [block, ahead((16, width), rim_rows(rows)[0] // 16, 0)]
    prev = ahead((held, LANES), 0, 2 * chunk - 1)
    if chunk < width // BLOCK:
        return [first, first], [block, prev]
    return [last, first], [pl.BlockSpec((spg, rows, BLOCK), lambda g: (g, 0, 0)), prev]


def state_chunk(chunk, chunks, got, w, bias, a_log, state, lead, token, dims):
    spg, rows, heads, span, piece_heads = dims
    groups = w.shape[0]
    last = chunk == chunks - 1
    if last:
        packed = piece_heads * HEAD_DIM + 16
        state_shape = pltpu.HBM((groups * spg, packed, STATE_WIDTH), bf16)
        state_spec = pl.BlockSpec((spg, packed, STATE_WIDTH), lambda g: (g, 0, 0))
    else:
        state_shape = pltpu.HBM((groups, span, STATE_WIDTH), f32)
        state_spec = per_group(span, STATE_WIDTH)

    def out(dtype, *shape):
        return pltpu.HBM((groups,) + shape, dtype)

    args, specs = chunk_specs(got, chunk, dims)
    args[1:] = in_hbm(args[1])
    args[:1] = in_vmem(args[0]) if last else in_hbm(args[0])
    after = [] if token is None else in_hbm(token)
    return pl.pallas_call(
        functools.partial(state_kernel, dims, chunk == 0, last),
        grid=(groups,),
        in_specs=specs
        + [
            per_group(span + STATE_WIDTH, 4),
            per_group(heads, 1),
            per_group(heads, 1),
            per_group(span, STATE_WIDTH),
            per_group(heads, LANES),
        ]
        + [pl.BlockSpec(memory_space=pl.ANY)] * len(after),
        out_specs=[
            per_group(span, BLOCK),
            per_group(STATE_WIDTH, BLOCK),
            per_group(heads, BLOCK),
            per_group(heads, BLOCK),
            per_group(heads, BLOCK),
            state_spec,
            per_group(heads, LANES),
        ],
        out_shape=[
            out(bf16, span, BLOCK),
            out(bf16, STATE_WIDTH, BLOCK),
            out(f32, heads, BLOCK),
            out(f32, heads, BLOCK),
            out(f32, heads, BLOCK),
            state_shape,
            out(f32, heads, LANES),
        ],
        scratch_shapes=[
            pltpu.VMEM((rows * spg, LANES + BLOCK), f32),
            pltpu.VMEM((span, BLOCK), bf16),
            pltpu.VMEM((span + STATE_WIDTH, LANES + BLOCK), bf16),
            pltpu.VMEM((BLOCK // LANES, span + STATE_WIDTH, 3 * LANES), f32),
        ],
        compiler_params=params(48 if last else 60),
        cost_estimate=pl.CostEstimate(flops=4 * 10**9, bytes_accessed=10**7, transcendentals=10**6),
        name="state_chunk",
    )(*args, *in_hbm(w, bias, a_log, state, lead), *after)


def split(v):
    high = v.astype(bf16)
    return high, (v - high.astype(f32)).astype(bf16)


def block_kernel(dims, first, recv, *refs):
    spg, rows, heads, span, piece_heads = dims
    prev, refs = refs[0], refs[1:]
    w, xact, bmap, run_ref, dt_ref, cum_ref, state, skip = refs[:8]
    mixed, passed, c_out, token, raw, low, shifted = refs[-7:]
    at_c = 2 * span + STATE_WIDTH
    gather_rows(recv, prev, first, raw, rows, at_c, at_c + STATE_WIDTH, True, at_c // rows)
    gather_rows(recv, prev, first, raw, rows, 0, span, False)
    token[0] = cum_ref[0, :8, :LANES]
    shift_rows(raw, low, shifted, at_c)
    c = [conv_tile(raw, shifted, w, at_c, r) for r in range(0, STATE_WIDTH, HEAD_DIM)]
    c = jnp.concatenate(c, axis=0)
    b_rows = bmap[0].astype(f32).T.astype(bf16)
    scores = jnp.dot(b_rows, c, preferred_element_type=f32)
    src = lax.broadcasted_iota(jnp.int32, (HALF, HALF), 0)
    dst = lax.broadcasted_iota(jnp.int32, (HALF, HALF), 1)
    causal = src <= dst
    s00 = jnp.where(causal, scores[:HALF, :HALF], 0.0)
    s01 = scores[:HALF, HALF:]
    s11 = jnp.where(causal, scores[HALF:, HALF:], 0.0)
    r = run_ref[0] * LOG2E
    q = (r - jnp.log(dt_ref[0]) * LOG2E).T
    if not first:
        cc = jnp.concatenate([c, c], axis=0)
        entered = jnp.exp2(r)
    reach = jnp.exp(cum_ref[0])
    c_out[0] = c.astype(f32).T.astype(bf16)
    turned = []
    for h in range(heads):
        at = h * HEAD_DIM
        r0, r1 = r[h : h + 1, :HALF], r[h : h + 1, HALF:]
        q0, q1 = q[:HALF, h : h + 1], q[HALF:, h : h + 1]
        w00 = (s00 * jnp.exp2(jnp.minimum(r0 - q0, CAP))).astype(bf16)
        w01 = (s01 * jnp.exp2(r1 - q0)).astype(bf16)
        w11 = (s11 * jnp.exp2(jnp.minimum(r1 - q1, CAP))).astype(bf16)
        x = xact[0, at : at + HEAD_DIM, :]
        y0 = jnp.dot(x[:, :HALF], w00, preferred_element_type=f32)
        y1 = jnp.dot(x, jnp.concatenate([w01, w11], axis=0), preferred_element_type=f32)
        y = jnp.concatenate([y0, y1], axis=1) + skip[0, h : h + 1, :] * x.astype(f32)
        if not first:
            if at % WIDE == 0:
                both = jnp.concatenate(split(state[0, at : at + WIDE, :]), axis=1)
                carried = jnp.dot(both, cc, preferred_element_type=f32)
            y = y + entered[h : h + 1, :] * carried[at % WIDE : at % WIDE + HEAD_DIM, :]
        gate = silu(raw[at : at + HEAD_DIM, LANES:])
        turned.append((y * gate, gate * reach[h : h + 1, :]))
        if len(turned) * HEAD_DIM == LANES:
            lanes = slice(at + HEAD_DIM - LANES, at + HEAD_DIM)
            mixed[0, :, lanes] = jnp.concatenate([pair[0] for pair in turned], axis=0).T
            wide = jnp.concatenate([pair[1] for pair in turned], axis=0).T
            passed[0, :, lanes] = wide.astype(bf16)
            turned = []


def block_chunk(
    chunk, chunks, got, w, xact, bmap, run, dt, cum, state, skip, after, dims
):
    spg, rows, heads, span, piece_heads = dims
    groups = w.shape[0]

    at_c = 2 * span + STATE_WIDTH
    one = at_c // rows
    assert (at_c + STATE_WIDTH - 1) // rows == one
    args, specs = chunk_specs(got, chunk, dims, one)
    args = in_hbm(*args)
    args += in_hbm(w, xact, bmap, run, dt, cum, state, skip)
    specs += [
        pl.BlockSpec((1, STATE_WIDTH, 4), lambda g: (g, span // STATE_WIDTH + 1, 0)),
        per_group(span, BLOCK),
        per_group(STATE_WIDTH, BLOCK),
        per_group(heads, BLOCK),
        per_group(heads, BLOCK),
        per_group(heads, BLOCK),
        per_group(span, STATE_WIDTH),
        per_group(heads, 1),
    ]
    args += in_vmem(*after)
    specs += [pl.BlockSpec(memory_space=pl.ANY)] * len(after)

    def out(dtype, *shape):
        return pltpu.HBM((groups,) + shape, dtype)

    return pl.pallas_call(
        functools.partial(block_kernel, dims, chunk == 0),
        grid=(groups,),
        in_specs=specs,
        out_specs=[
            per_group(BLOCK, span),
            per_group(BLOCK, span),
            per_group(BLOCK, STATE_WIDTH),
            per_group(8, LANES),
        ],
        out_shape=[
            out(f32, BLOCK, span),
            out(bf16, BLOCK, span),
            out(bf16, BLOCK, STATE_WIDTH),
            out(f32, 8, LANES),
        ],
        scratch_shapes=[
            pltpu.VMEM((rows * spg, LANES + BLOCK), f32),
            pltpu.VMEM((STATE_WIDTH, LANES + BLOCK), bf16),
            pltpu.VMEM((BLOCK // LANES, STATE_WIDTH, 3 * LANES), f32),
        ],
        compiler_params=params(),
        cost_estimate=pl.CostEstimate(flops=4 * 10**9, bytes_accessed=10**7, transcendentals=10**6),
        name="block_chunk",
    )(*args)


def relay_kernel(piece_heads, src, token, dst):
    rows = piece_heads * HEAD_DIM
    held = jnp.zeros((rows, STATE_WIDTH), f32)
    for d in range(src.shape[0]):
        dst[d] = held.T.astype(bf16)
        both = src[d, rows:, :].astype(f32)
        decay = both[:8] + both[8:]
        spread = [
            jnp.broadcast_to(decay[h : h + 1, :], (HEAD_DIM, STATE_WIDTH))
            for h in range(piece_heads)
        ]
        held = jnp.concatenate(spread, axis=0) * held + src[d, :rows, :].astype(f32)


def relay(packed, token, piece_heads):
    count = packed.shape[0]
    rows = piece_heads * HEAD_DIM
    return pl.pallas_call(
        functools.partial(relay_kernel, piece_heads),
        in_specs=[pl.BlockSpec(memory_space=pltpu.VMEM), pl.BlockSpec(memory_space=pl.ANY)],
        out_shape=pltpu.VMEM((count, STATE_WIDTH, rows), bf16),
        compiler_params=params(16),
        name="relay",
    )(packed, *in_hbm(token))


def final_kernel(chunks, groups, *refs):
    mixed, passed, maps = (refs[i * chunks : (i + 1) * chunks] for i in range(3))
    state, gain, out = refs[3 * chunks : 3 * chunks + 3]
    held, passed_held, map_held, kept, carried, done, sems, out_sems = refs[3 * chunks + 3 :]
    span = kept.shape[1]
    piece = state.shape[2]
    spg = state.shape[0] // groups
    steps = [(g, c) for g in range(groups) for c in range(chunks)]

    def loads(i):
        g, c = steps[i]
        moves = [
            (maps[c].at[g], map_held.at[i]),
            (mixed[c].at[g], held.at[i]),
            (passed[c].at[g], passed_held.at[i]),
        ]
        return [pltpu.make_async_copy(a, b, sems.at[i, j]) for j, (a, b) in enumerate(moves)]

    def store(i):
        g, c = steps[i]
        return pltpu.make_async_copy(
            done.at[i % 2],
            out.at[c * BLOCK : (c + 1) * BLOCK, g * span : (g + 1) * span],
            out_sems.at[i % 2],
        )

    for i in range(len(steps)):
        for move in loads(i):
            move.start()
    for i, (g, c) in enumerate(steps):
        for move in loads(i):
            move.wait()
        if i >= 2:
            store(i - 2).wait()
        for j in range(spg):
            lanes = slice(j * piece, (j + 1) * piece)
            carried[:, lanes] = jnp.dot(
                map_held[i], state[g * spg + j], preferred_element_type=f32
            )
        for q in range(0, BLOCK, HEAD_DIM):
            rows = slice(q, q + HEAD_DIM)
            total = jnp.zeros((HEAD_DIM, LANES), f32)
            for at in range(0, span, LANES):
                lanes = slice(at, at + LANES)
                v = held[i, rows, lanes]
                v = v + passed_held[i, rows, lanes].astype(f32) * carried[rows, lanes]
                kept[rows, lanes] = v
                total = total + v * v
            mean = jnp.sum(total, axis=1, keepdims=True) * (1.0 / span)
            factor = lax.rsqrt(mean + EPSILON)
            for at in range(0, span, LANES):
                lanes = slice(at, at + LANES)
                scaled = kept[rows, lanes] * factor * gain[g, :, lanes]
                done[i % 2, rows, lanes] = scaled.astype(bf16)
        store(i).start()
    for i in range(max(len(steps) - 2, 0), len(steps)):
        store(i).wait()


def finish(mixed, passed, maps, state, gain):
    chunks = len(mixed)
    groups, _, span = mixed[0].shape
    steps = groups * chunks
    anywhere = pl.BlockSpec(memory_space=pl.ANY)
    within = pl.BlockSpec(memory_space=pltpu.VMEM)
    return pl.pallas_call(
        functools.partial(final_kernel, chunks, groups),
        in_specs=[anywhere] * (3 * chunks) + [within] * 2,
        out_specs=anywhere,
        out_shape=jax.ShapeDtypeStruct((chunks * BLOCK, groups * span), bf16),
        scratch_shapes=[
            pltpu.VMEM((steps, BLOCK, span), f32),
            pltpu.VMEM((steps, BLOCK, span), bf16),
            pltpu.VMEM((steps, BLOCK, STATE_WIDTH), bf16),
            pltpu.VMEM((BLOCK, span), f32),
            pltpu.VMEM((BLOCK, span), f32),
            pltpu.VMEM((2, BLOCK, span), bf16),
            pltpu.SemaphoreType.DMA((steps, 3)),
            pltpu.SemaphoreType.DMA((2,)),
        ],
        compiler_params=params(40),
        name="finish",
    )(*in_hbm(*mixed, *passed, *maps), state, gain)


def exchange(array):
    return lax.all_to_all(array, "seq", split_axis=0, concat_axis=0, tiled=True)


def per_device(projected, conv_weight, dt_bias, a_log, d_skip, norm_gain):
    seq_count = lax.axis_size("seq")
    groups = conv_weight.shape[1]
    heads = dt_bias.shape[0] // groups
    span = heads * HEAD_DIM
    rows, all_tokens = projected.shape
    local_tokens = all_tokens // seq_count
    chunks = local_tokens // BLOCK
    spg = seq_count // groups
    piece_heads = groups * heads // seq_count
    dims = (spg, rows, heads, span, piece_heads)

    w = jnp.transpose(conv_weight, (1, 2, 0))
    bias = dt_bias.reshape(groups, heads, 1)
    rate = a_log.reshape(groups, heads, 1)
    skip = d_skip.reshape(groups, heads, 1)
    gain = norm_gain.reshape(groups, 1, span)
    state = jnp.zeros((groups, span, STATE_WIDTH), f32)
    lead = jnp.zeros((groups, heads, LANES), f32)

    split_at = local_tokens - BLOCK
    cut = cut_blocks(projected, seq_count, 0, split_at, [])
    got = [exchange(cut)]
    ready = [cut, w, bias, rate, skip, gain, state, lead]
    got.append(exchange(cut_blocks(projected, seq_count, split_at, local_tokens, ready)))
    results, tokens = [], []
    for c in range(chunks):
        xact, bmap, run, dt, cum, new, lead = state_chunk(
            c, chunks, got, w, bias, rate, state, lead, tokens[c - 2] if c > 1 else None, dims
        )
        after = []
        if c == chunks - 1:
            entering = relay(exchange(new), tokens[-1], piece_heads)
            after = [entering]
        *result, token = block_chunk(
            c, chunks, got, w, xact, bmap, run, dt, cum, state, skip, after, dims
        )
        results.append(result)
        tokens.append(token)
        state = new
    return finish(*zip(*results), exchange(entering), gain)


def solution(mesh):
    in_specs = (P(("tp", "seq"), None), P(None, "tp", None), P("tp"), P("tp"), P("tp"), P("tp"))
    return jax.shard_map(
        per_device, mesh=mesh, in_specs=in_specs, out_specs=P("seq", "tp"), check_vma=False
    )
```

```python
import functools

import jax
import jax.numpy as jnp
from jax import lax
from jax.experimental import pallas as pl
from jax.experimental.pallas import tpu as pltpu
from jax.sharding import PartitionSpec as P

HEAD_DIM = 64
STATE_WIDTH = 128
BLOCK = 256
LANES = 128
HALF = BLOCK // 2
WIDE = 256
LOG2E = 1.4426950408889634
CAP = 80.0
EPSILON = 1e-05

f32 = jnp.float32
bf16 = jnp.bfloat16
NT = (((1,), (1,)), ((), ()))


def params(mib=60):
    return pltpu.CompilerParams(vmem_limit_bytes=mib * 2**20)


def silu(v):
    half = 0.5 * v
    return half + half * jnp.tanh(half)


def softplus(v):
    e = jnp.exp(-jnp.abs(v))
    u = 1.0 + e
    gap = u - 1.0
    tiny = gap == 0.0
    log_part = jnp.where(tiny, e, jnp.log(u) * (e / jnp.where(tiny, 1.0, gap)))
    return jnp.maximum(v, 0.0) + log_part


def in_hbm(*arrays):
    return [pltpu.with_memory_space_constraint(array, pltpu.HBM) for array in arrays]


def in_vmem(*arrays):
    return [pltpu.with_memory_space_constraint(array, pltpu.VMEM) for array in arrays]


def per_group(*shape):
    return pl.BlockSpec((1,) + shape, lambda g: (g,) + (0,) * len(shape))


RIM = 4


def rim_rows(rows):
    base = rows // 16 * 16
    height = -(-(rows - base + RIM * -(-rows // BLOCK)) // 8) * 8
    assert height <= 16
    return base, height


def piece_kernel(count, me_ref, src, *refs):
    dsts, (held, windows, ends, in_sems, rim_sems, out_sems, end_sems) = refs[:count], refs[count:]
    rows, all_tokens = src.shape
    tokens = all_tokens // count
    base, height = rim_rows(rows)
    me = me_ref[0]
    order = list(range(1, count)) + [0]

    def fetch(k):
        at = pl.multiple_of((me ^ k) * tokens, LANES)
        return pltpu.make_async_copy(src.at[:, pl.ds(at, BLOCK)], held.at[k], in_sems.at[k])

    def window(k):
        at = pl.multiple_of(jnp.maximum((me ^ k) * tokens - LANES, 0), LANES)
        return pltpu.make_async_copy(src.at[:, pl.ds(at, LANES)], windows.at[k], rim_sems.at[k])

    def place(k):
        return pltpu.make_async_copy(held.at[k, :base, :], dsts[k].at[:base, :], out_sems.at[k])

    def place_end(k):
        return pltpu.make_async_copy(
            ends.at[k], dsts[k].at[base : base + height, :], end_sems.at[k]
        )

    for k in order:
        fetch(k).start()
        window(k).start()
    row = lax.broadcasted_iota(jnp.int32, (height, LANES), 0) - (rows - base)
    col = lax.broadcasted_iota(jnp.int32, (height, LANES), 1)
    hit = (row >= 0) & (col == lax.rem(row + 16, RIM) + LANES - RIM)
    which = lax.broadcasted_iota(jnp.int32, (height, BLOCK), 0) - (rows - base)
    for k in order:
        fetch(k).wait()
        place(k).start()
        end = held[k, base:rows, :].astype(f32)
        end = jnp.concatenate([end, jnp.zeros((height - end.shape[0], BLOCK), f32)], axis=0)
        window(k).wait()
        pick = jnp.where(hit & ((me ^ k) > 0), 1.0, 0.0).astype(bf16)
        rims = lax.dot_general(pick, windows[k], NT, preferred_element_type=f32)
        for j in range(-(-rows // BLOCK)):
            part = rims[:, j * BLOCK : min((j + 1) * BLOCK, rows)]
            if part.shape[1] < BLOCK:
                fill = jnp.zeros((height, BLOCK - part.shape[1]), f32)
                part = jnp.concatenate([part, fill], axis=1)
            end = jnp.where((which >= RIM * j) & (which < RIM * (j + 1)), part, end)
        ends[k] = end.astype(bf16)
        place_end(k).start()
    for k in order:
        place(k).wait()
        place_end(k).wait()


def cut_pieces(projected, me, count):
    rows = projected.shape[0]
    base, height = rim_rows(rows)
    sems = pltpu.SemaphoreType.DMA((count,))
    anywhere = pl.BlockSpec(memory_space=pl.ANY)
    return pl.pallas_call(
        functools.partial(piece_kernel, count),
        in_specs=[pl.BlockSpec(memory_space=pltpu.SMEM), anywhere],
        out_specs=[anywhere] * count,
        out_shape=[pltpu.HBM((base + height, BLOCK), bf16)] * count,
        scratch_shapes=[
            pltpu.VMEM((count, rows, BLOCK), bf16),
            pltpu.VMEM((count, rows, LANES), bf16),
            pltpu.VMEM((count, height, BLOCK), bf16),
            sems,
            sems,
            sems,
            sems,
        ],
        compiler_params=params(),
        name="cut_pieces",
    )(me, *in_hbm(projected))


def join_kernel(count, me_ref, *refs):
    pieces, (dst, held, in_sems, out_sems) = refs[:count], refs[-4:]
    me = me_ref[0]

    def fetch(k):
        return pltpu.make_async_copy(pieces[k], held.at[k], in_sems.at[k])

    def place(k):
        return pltpu.make_async_copy(held.at[k], dst.at[me ^ k], out_sems.at[k])

    for k in range(count):
        fetch(k).start()
    for k in range(count):
        fetch(k).wait()
        place(k).start()
    for k in range(count):
        place(k).wait()


def join_pieces(pieces, me, token):
    count = len(pieces)
    shape = (count,) + pieces[0].shape
    sems = pltpu.SemaphoreType.DMA((count,))
    anywhere = pl.BlockSpec(memory_space=pl.ANY)
    return pl.pallas_call(
        functools.partial(join_kernel, count),
        in_specs=[pl.BlockSpec(memory_space=pltpu.SMEM)] + [anywhere] * (count + 1),
        out_specs=anywhere,
        out_shape=pltpu.HBM(shape, bf16),
        scratch_shapes=[pltpu.VMEM(shape, bf16), sems, sems],
        compiler_params=params(),
        name="join_pieces",
    )(me, *pieces, *in_hbm(token))


def cut_kernel(low, count, src, *refs):
    dst, held, in_sems, out_sems = refs[-4:]
    tokens = src.shape[1] // count
    width = dst.shape[2]

    def fetch(d):
        at = d * tokens + low
        return pltpu.make_async_copy(src.at[:, at : at + width], held.at[d], in_sems.at[d])

    def place(d):
        return pltpu.make_async_copy(held.at[d], dst.at[d], out_sems.at[d])

    for d in range(count):
        fetch(d).start()
    for d in range(count):
        fetch(d).wait()
        place(d).start()
    for d in range(count):
        place(d).wait()


def cut_blocks(projected, count, low, high, after):
    shape = (count, projected.shape[0], high - low)
    sems = pltpu.SemaphoreType.DMA((count,))
    args = in_hbm(projected, *after)
    return pl.pallas_call(
        functools.partial(cut_kernel, low, count),
        in_specs=[pl.BlockSpec(memory_space=pl.ANY)] * len(args),
        out_specs=pl.BlockSpec(memory_space=pl.ANY),
        out_shape=pltpu.HBM(shape, bf16),
        scratch_shapes=[pltpu.VMEM(shape, bf16), sems, sems],
        compiler_params=params(),
        name="cut_blocks",
    )(*args)


def gather_rows(recv, prev, first, raw, rows, low, high, ahead=True, only=None):
    for s in range(recv.shape[0]):
        a = max(low - s * rows, 0) // 16 * 16
        b = min(-(-(high - s * rows) // 16) * 16, rows)
        if b <= a:
            continue
        at = s * rows + a
        raw[at : at + b - a, LANES:] = recv[s, a:b, :].astype(f32)
        if not ahead:
            continue
        if not first:
            raw[at : at + b - a, :LANES] = prev[s if only is None else 0, a:b, :].astype(f32)
            continue
        base, height = rim_rows(rows)
        rims = prev[s if only is None else 0, :height, :].astype(f32)
        tall = jnp.concatenate([jnp.zeros((LANES - height, BLOCK), f32), rims], axis=0)
        for j in range(-(-rows // BLOCK)):
            c, d = max(a, j * BLOCK), min(b, (j + 1) * BLOCK)
            if d <= c:
                continue
            shift = height - RIM - (rows - base) - RIM * j
            moved = (pltpu.roll(tall, shift, 0) if shift else tall).T
            raw[s * rows + c : s * rows + d, :LANES] = moved[c - j * BLOCK : d - j * BLOCK]


def band():
    row = lax.broadcasted_iota(jnp.int32, (2 * LANES, 3 * LANES), 0)
    col = lax.broadcasted_iota(jnp.int32, (2 * LANES, 3 * LANES), 1)
    tap = col // LANES
    return jnp.where(row == col - tap * LANES + LANES - 3 + tap, 1.0, 0.0).astype(bf16)


def shift_rows(raw, low, shifted, at):
    low[...] = raw[at : at + low.shape[0], :].astype(bf16)
    picks = band()
    for i in range(BLOCK // LANES):
        window = low[:, i * LANES : (i + 2) * LANES]
        shifted[i] = jnp.dot(window, picks, preferred_element_type=f32)


def conv_tile(raw, shifted, w, at, r):
    rows = slice(r, r + HEAD_DIM)
    taps = [jnp.broadcast_to(w[0, rows, k : k + 1], (HEAD_DIM, LANES)) for k in range(4)]
    parts = []
    for i in range(BLOCK // LANES):
        summed = None
        for k in range(3):
            part = taps[k] * shifted[i, rows, k * LANES : (k + 1) * LANES]
            summed = part if summed is None else summed + part
        own = raw[at + r : at + r + HEAD_DIM, (i + 1) * LANES : (i + 2) * LANES]
        parts.append(silu(summed + taps[3] * own).astype(bf16))
    return jnp.concatenate(parts, axis=1)


def state_kernel(dims, first, last, recv, *refs):
    spg, rows, heads, span, piece_heads = dims
    prev, refs = refs[0], refs[1:]
    w, bias, a_log, state_in, lead_in = refs[:5]
    xact, bmap, run_out, dt_out, cum_out, state_out, lead_out = refs[-11:-4]
    raw, xw, low, shifted = refs[-4:]
    steps = 2 * span + 2 * STATE_WIDTH

    gather_rows(recv, prev, first, raw, rows, steps, steps + heads, False)
    gather_rows(recv, prev, first, raw, rows, span, 2 * span + STATE_WIDTH)
    dt = softplus(raw[steps : steps + heads, LANES:] + bias[0])
    log_decay = -jnp.exp(a_log[0]) * dt
    lane = lax.broadcasted_iota(jnp.int32, (heads, BLOCK), 1)
    run = log_decay
    shift = 1
    while shift < BLOCK:
        run = run + jnp.where(lane >= shift, pltpu.roll(run, shift, 1), 0.0)
        shift *= 2
    final = run[:, BLOCK - 1 :]
    scale = jnp.exp(final - run) * dt
    cum = run + lead_in[0][:, :1]
    run_out[0] = run
    dt_out[0] = dt
    cum_out[0] = cum
    lead = jnp.broadcast_to(cum[:, BLOCK - 1 :], (heads, LANES))
    lead_out[0] = lead
    keep = jnp.broadcast_to(jnp.exp(final), (heads, LANES))

    shift_rows(raw, low, shifted, span)
    for r in range(0, STATE_WIDTH, HEAD_DIM):
        bmap[0, r : r + HEAD_DIM, :] = conv_tile(raw, shifted, w, span, span + r)
    for h in range(heads):
        r = h * HEAD_DIM
        tile = conv_tile(raw, shifted, w, span, r)
        xact[0, r : r + HEAD_DIM, :] = tile
        xw[r : r + HEAD_DIM, :] = (tile.astype(f32) * scale[h : h + 1, :]).astype(bf16)
    update = lax.dot_general(xw[...], bmap[0], NT, preferred_element_type=f32)
    for h in range(heads):
        r = h * HEAD_DIM
        new = update[r : r + HEAD_DIM, :]
        if not first:
            new = keep[h : h + 1, :] * state_in[0, r : r + HEAD_DIM, :] + new
        if last:
            at = (h % piece_heads) * HEAD_DIM
            state_out[h // piece_heads, at : at + HEAD_DIM, :] = new.astype(bf16)
        else:
            state_out[0, r : r + HEAD_DIM, :] = new
    if last:
        high, low = split(jnp.exp(lead))
        fill = jnp.zeros((8 - piece_heads, LANES), f32)
        for i in range(heads // piece_heads):
            mine = slice(i * piece_heads, (i + 1) * piece_heads)
            parts = [high[mine].astype(f32), fill, low[mine].astype(f32), fill]
            at = piece_heads * HEAD_DIM
            state_out[i, at : at + 16, :] = jnp.concatenate(parts, axis=0).astype(bf16)


def chunk_specs(got, chunk, dims, only=None):
    spg, rows = dims[:2]
    slabs = spg if only is None else 1

    def ahead(source, shape, row, lane):
        def index(g):
            return (g if only is None else g * spg + only, row, lane)

        return source, pl.BlockSpec((slabs,) + shape, index)

    def lane_of(block):
        first, middle, last = got
        if block == 0:
            return first, 0
        at = block - 1
        return (middle, at) if at < middle.shape[2] // BLOCK else (last, 0)

    source, at = lane_of(chunk)
    block = pl.BlockSpec((spg, source.shape[1], BLOCK), lambda g: (g, 0, at))
    if chunk == 0:
        prev, prev_spec = ahead(source, (16, BLOCK), rim_rows(rows)[0] // 16, 0)
    else:
        prev, place = lane_of(chunk - 1)
        lane = (place + 1) * (BLOCK // LANES) - 1
        prev, prev_spec = ahead(prev, (prev.shape[1], LANES), 0, lane)
    return [source, prev], [block, prev_spec]


def state_chunk(chunk, chunks, got, w, bias, a_log, state, lead, token, dims):
    spg, rows, heads, span, piece_heads = dims
    groups = w.shape[0]
    last = chunk == chunks - 1
    if last:
        packed = piece_heads * HEAD_DIM + 16
        state_shape = pltpu.HBM((groups * spg, packed, STATE_WIDTH), bf16)
        state_spec = pl.BlockSpec((spg, packed, STATE_WIDTH), lambda g: (g, 0, 0))
    else:
        state_shape = pltpu.HBM((groups, span, STATE_WIDTH), f32)
        state_spec = per_group(span, STATE_WIDTH)

    def out(dtype, *shape):
        return pltpu.HBM((groups,) + shape, dtype)

    args, specs = chunk_specs(got, chunk, dims)
    args[1:] = in_hbm(args[1])
    args[:1] = in_vmem(args[0]) if last else in_hbm(args[0])
    after = [] if token is None else in_hbm(token)
    return pl.pallas_call(
        functools.partial(state_kernel, dims, chunk == 0, last),
        grid=(groups,),
        in_specs=specs
        + [
            per_group(span + STATE_WIDTH, 4),
            per_group(heads, 1),
            per_group(heads, 1),
            per_group(span, STATE_WIDTH),
            per_group(heads, LANES),
        ]
        + [pl.BlockSpec(memory_space=pl.ANY)] * len(after),
        out_specs=[
            per_group(span, BLOCK),
            per_group(STATE_WIDTH, BLOCK),
            per_group(heads, BLOCK),
            per_group(heads, BLOCK),
            per_group(heads, BLOCK),
            state_spec,
            per_group(heads, LANES),
        ],
        out_shape=[
            out(bf16, span, BLOCK),
            out(bf16, STATE_WIDTH, BLOCK),
            out(f32, heads, BLOCK),
            out(f32, heads, BLOCK),
            out(f32, heads, BLOCK),
            state_shape,
            out(f32, heads, LANES),
        ],
        scratch_shapes=[
            pltpu.VMEM((rows * spg, LANES + BLOCK), f32),
            pltpu.VMEM((span, BLOCK), bf16),
            pltpu.VMEM((span + STATE_WIDTH, LANES + BLOCK), bf16),
            pltpu.VMEM((BLOCK // LANES, span + STATE_WIDTH, 3 * LANES), f32),
        ],
        compiler_params=params(48 if last else 60),
        cost_estimate=pl.CostEstimate(flops=4 * 10**9, bytes_accessed=10**7, transcendentals=10**6),
        name="state_chunk",
    )(*args, *in_hbm(w, bias, a_log, state, lead), *after)


def split(v):
    high = v.astype(bf16)
    return high, (v - high.astype(f32)).astype(bf16)


def block_kernel(dims, first, recv, *refs):
    spg, rows, heads, span, piece_heads = dims
    prev, refs = refs[0], refs[1:]
    w, xact, bmap, run_ref, dt_ref, cum_ref, state, skip = refs[:8]
    mixed, gate_out, side, token, raw, low, shifted = refs[-7:]
    at_c = 2 * span + STATE_WIDTH
    gather_rows(recv, prev, first, raw, rows, at_c, at_c + STATE_WIDTH, True, at_c // rows)
    gather_rows(recv, prev, first, raw, rows, 0, span, False)
    token[0] = cum_ref[0, :8, :LANES]
    shift_rows(raw, low, shifted, at_c)
    c = [conv_tile(raw, shifted, w, at_c, r) for r in range(0, STATE_WIDTH, HEAD_DIM)]
    c = jnp.concatenate(c, axis=0)
    b_rows = bmap[0].astype(f32).T.astype(bf16)
    scores = jnp.dot(b_rows, c, preferred_element_type=f32)
    src = lax.broadcasted_iota(jnp.int32, (HALF, HALF), 0)
    dst = lax.broadcasted_iota(jnp.int32, (HALF, HALF), 1)
    causal = src <= dst
    s00 = jnp.where(causal, scores[:HALF, :HALF], 0.0)
    s01 = scores[:HALF, HALF:]
    s11 = jnp.where(causal, scores[HALF:, HALF:], 0.0)
    r = run_ref[0] * LOG2E
    q = (r - jnp.log(dt_ref[0]) * LOG2E).T
    if not first:
        cc = jnp.concatenate([c, c], axis=0)
        entered = jnp.exp2(r)
    reach = [part.astype(f32) for part in split(jnp.exp(cum_ref[0]))]
    reach.append(jnp.zeros((STATE_WIDTH - 2 * heads, BLOCK), f32))
    side[0, :, :STATE_WIDTH] = c.astype(f32).T.astype(bf16)
    side[0, :, STATE_WIDTH:] = jnp.concatenate(reach, axis=0).T.astype(bf16)
    turned = []
    for h in range(heads):
        at = h * HEAD_DIM
        r0, r1 = r[h : h + 1, :HALF], r[h : h + 1, HALF:]
        q0, q1 = q[:HALF, h : h + 1], q[HALF:, h : h + 1]
        w00 = (s00 * jnp.exp2(jnp.minimum(r0 - q0, CAP))).astype(bf16)
        w01 = (s01 * jnp.exp2(r1 - q0)).astype(bf16)
        w11 = (s11 * jnp.exp2(jnp.minimum(r1 - q1, CAP))).astype(bf16)
        x = xact[0, at : at + HEAD_DIM, :]
        y0 = jnp.dot(x[:, :HALF], w00, preferred_element_type=f32)
        y1 = jnp.dot(x, jnp.concatenate([w01, w11], axis=0), preferred_element_type=f32)
        y = jnp.concatenate([y0, y1], axis=1) + skip[0, h : h + 1, :] * x.astype(f32)
        if not first:
            if at % WIDE == 0:
                both = jnp.concatenate(split(state[0, at : at + WIDE, :]), axis=1)
                carried = jnp.dot(both, cc, preferred_element_type=f32)
            y = y + entered[h : h + 1, :] * carried[at % WIDE : at % WIDE + HEAD_DIM, :]
        gate = raw[at : at + HEAD_DIM, LANES:]
        turned.append((y * silu(gate), gate))
        if len(turned) * HEAD_DIM == LANES:
            lanes = slice(at + HEAD_DIM - LANES, at + HEAD_DIM)
            mixed[0, :, lanes] = jnp.concatenate([pair[0] for pair in turned], axis=0).T
            wide = jnp.concatenate([pair[1] for pair in turned], axis=0).T
            gate_out[0, :, lanes] = wide.astype(bf16)
            turned = []


def block_chunk(
    chunk, chunks, got, w, xact, bmap, run, dt, cum, state, skip, after, dims
):
    spg, rows, heads, span, piece_heads = dims
    groups = w.shape[0]

    at_c = 2 * span + STATE_WIDTH
    one = at_c // rows
    assert (at_c + STATE_WIDTH - 1) // rows == one
    args, specs = chunk_specs(got, chunk, dims, one)
    args = in_hbm(*args)
    args += in_hbm(w, xact, bmap, run, dt, cum, state, skip)
    specs += [
        pl.BlockSpec((1, STATE_WIDTH, 4), lambda g: (g, span // STATE_WIDTH + 1, 0)),
        per_group(span, BLOCK),
        per_group(STATE_WIDTH, BLOCK),
        per_group(heads, BLOCK),
        per_group(heads, BLOCK),
        per_group(heads, BLOCK),
        per_group(span, STATE_WIDTH),
        per_group(heads, 1),
    ]
    args += in_vmem(*after)
    specs += [pl.BlockSpec(memory_space=pl.ANY)] * len(after)

    def out(dtype, *shape):
        return pltpu.HBM((groups,) + shape, dtype)

    return pl.pallas_call(
        functools.partial(block_kernel, dims, chunk == 0),
        grid=(groups,),
        in_specs=specs,
        out_specs=[
            per_group(BLOCK, span),
            per_group(BLOCK, span),
            per_group(BLOCK, 2 * STATE_WIDTH),
            per_group(8, LANES),
        ],
        out_shape=[
            out(f32, BLOCK, span),
            out(bf16, BLOCK, span),
            out(bf16, BLOCK, 2 * STATE_WIDTH),
            out(f32, 8, LANES),
        ],
        scratch_shapes=[
            pltpu.VMEM((rows * spg, LANES + BLOCK), f32),
            pltpu.VMEM((STATE_WIDTH, LANES + BLOCK), bf16),
            pltpu.VMEM((BLOCK // LANES, STATE_WIDTH, 3 * LANES), f32),
        ],
        compiler_params=params(),
        cost_estimate=pl.CostEstimate(flops=4 * 10**9, bytes_accessed=10**7, transcendentals=10**6),
        name="block_chunk",
    )(*args)


def relay_kernel(piece_heads, src, token, dst):
    rows = piece_heads * HEAD_DIM
    held = jnp.zeros((rows, STATE_WIDTH), f32)
    for d in range(src.shape[0]):
        dst[d] = held.T.astype(bf16)
        both = src[d, rows:, :].astype(f32)
        decay = both[:8] + both[8:]
        spread = [
            jnp.broadcast_to(decay[h : h + 1, :], (HEAD_DIM, STATE_WIDTH))
            for h in range(piece_heads)
        ]
        held = jnp.concatenate(spread, axis=0) * held + src[d, :rows, :].astype(f32)


def relay(packed, token, piece_heads):
    count = packed.shape[0]
    rows = piece_heads * HEAD_DIM
    return pl.pallas_call(
        functools.partial(relay_kernel, piece_heads),
        in_specs=[pl.BlockSpec(memory_space=pltpu.VMEM), pl.BlockSpec(memory_space=pl.ANY)],
        out_shape=pltpu.VMEM((count, STATE_WIDTH, rows), bf16),
        compiler_params=params(16),
        name="relay",
    )(packed, *in_hbm(token))


def final_kernel(chunks, groups, *refs):
    mixed, gates, sides = (refs[i * chunks : (i + 1) * chunks] for i in range(3))
    state, gain, out = refs[3 * chunks : 3 * chunks + 3]
    held, gate_held, side_held, kept, carried, done, sems, out_sems = refs[3 * chunks + 3 :]
    span = held.shape[2]
    piece = state.shape[2]
    spg = state.shape[0] // groups
    heads = span // HEAD_DIM
    steps = [(g, c) for g in range(groups) for c in range(chunks)]

    def loads(i):
        g, c = steps[i]
        slot = i
        moves = []
        moves.append((sides[c].at[g], side_held.at[slot]))
        moves.append((mixed[c].at[g], held.at[slot]))
        moves.append((gates[c].at[g], gate_held.at[slot]))
        return [
            pltpu.make_async_copy(a, b, sems.at[slot, j]) for j, (a, b) in enumerate(moves)
        ]

    def store(i):
        g, c = steps[i]
        return pltpu.make_async_copy(
            done.at[i % 2],
            out.at[c * BLOCK : (c + 1) * BLOCK, g * span : (g + 1) * span],
            out_sems.at[i % 2],
        )

    for i in range(len(steps)):
        for move in loads(i):
            move.start()
    row = lax.broadcasted_iota(jnp.int32, (STATE_WIDTH, span), 0)
    col = lax.broadcasted_iota(jnp.int32, (STATE_WIDTH, span), 1) // HEAD_DIM
    spread = jnp.where((row == col) | (row == col + heads), 1.0, 0.0).astype(bf16)
    for i, (g, c) in enumerate(steps):
        slot = i
        for move in loads(i):
            move.wait()
        if i >= 2:
            store(i - 2).wait()
        side = side_held[slot]
        reach = jnp.dot(side[:, STATE_WIDTH:], spread, preferred_element_type=f32)
        for j in range(spg):
            lanes = slice(j * piece, (j + 1) * piece)
            part = jnp.dot(
                side[:, :STATE_WIDTH], state[g * spg + j], preferred_element_type=f32
            )
            carried[:, lanes] = part * reach[:, lanes]
        for q in range(0, BLOCK, HEAD_DIM):
            rows = slice(q, q + HEAD_DIM)
            total = jnp.zeros((HEAD_DIM, LANES), f32)
            for at in range(0, span, LANES):
                lanes = slice(at, at + LANES)
                gate = silu(gate_held[slot, rows, lanes].astype(f32))
                v = held[slot, rows, lanes] + gate * carried[rows, lanes]
                kept[rows, lanes] = v
                total = total + v * v
            mean = jnp.sum(total, axis=1, keepdims=True) * (1.0 / span)
            factor = lax.rsqrt(mean + EPSILON)
            for at in range(0, span, LANES):
                lanes = slice(at, at + LANES)
                scaled = kept[rows, lanes] * factor * gain[g, :, lanes]
                done[i % 2, rows, lanes] = scaled.astype(bf16)
        store(i).start()
    for i in range(max(len(steps) - 2, 0), len(steps)):
        store(i).wait()


def finish(mixed, gates, sides, state, gain):
    chunks = len(mixed)
    groups, _, span = mixed[0].shape
    steps = groups * chunks
    anywhere = pl.BlockSpec(memory_space=pl.ANY)
    within = pl.BlockSpec(memory_space=pltpu.VMEM)
    return pl.pallas_call(
        functools.partial(final_kernel, chunks, groups),
        in_specs=[anywhere] * (3 * chunks) + [within] * 2,
        out_specs=anywhere,
        out_shape=jax.ShapeDtypeStruct((chunks * BLOCK, groups * span), bf16),
        scratch_shapes=[
            pltpu.VMEM((steps, BLOCK, span), f32),
            pltpu.VMEM((steps, BLOCK, span), bf16),
            pltpu.VMEM((steps, BLOCK, 2 * STATE_WIDTH), bf16),
            pltpu.VMEM((BLOCK, span), f32),
            pltpu.VMEM((BLOCK, span), f32),
            pltpu.VMEM((2, BLOCK, span), bf16),
            pltpu.SemaphoreType.DMA((steps, 3)),
            pltpu.SemaphoreType.DMA((2,)),
        ],
        compiler_params=params(40),
        name="finish",
    )(*in_hbm(*mixed, *gates, *sides), state, gain)


def swap(pieces):
    count = len(pieces)
    return [pieces[0]] + [
        lax.ppermute(pieces[k], "seq", [(i, i ^ k) for i in range(count)])
        for k in range(1, count)
    ]


def exchange(array):
    return lax.all_to_all(array, "seq", split_axis=0, concat_axis=0, tiled=True)


def per_device(projected, conv_weight, dt_bias, a_log, d_skip, norm_gain):
    seq_count = lax.axis_size("seq")
    groups = conv_weight.shape[1]
    heads = dt_bias.shape[0] // groups
    span = heads * HEAD_DIM
    rows, all_tokens = projected.shape
    local_tokens = all_tokens // seq_count
    chunks = local_tokens // BLOCK
    spg = seq_count // groups
    piece_heads = groups * heads // seq_count
    dims = (spg, rows, heads, span, piece_heads)

    w = jnp.transpose(conv_weight, (1, 2, 0))
    bias = dt_bias.reshape(groups, heads, 1)
    rate = a_log.reshape(groups, heads, 1)
    skip = d_skip.reshape(groups, heads, 1)
    gain = norm_gain.reshape(groups, 1, span)
    state = jnp.zeros((groups, span, STATE_WIDTH), f32)
    lead = jnp.zeros((groups, heads, LANES), f32)

    split_at = local_tokens - BLOCK
    me = lax.axis_index("seq").astype(jnp.int32).reshape(1)
    pieces = cut_pieces(projected, me, seq_count)
    cut = cut_blocks(projected, seq_count, BLOCK, split_at, pieces[:1])
    middle = exchange(cut)
    got = [join_pieces(swap(pieces), me, cut), middle, None]
    results, tokens = [], []
    for c in range(chunks):
        xact, bmap, run, dt, cum, new, lead = state_chunk(
            c, chunks, got, w, bias, rate, state, lead, tokens[c - 2] if c > 1 else None, dims
        )
        after = []
        if c == chunks - 1:
            entering = relay(exchange(new), tokens[-1], piece_heads)
            after = [entering]
        *result, token = block_chunk(
            c, chunks, got, w, xact, bmap, run, dt, cum, state, skip, after, dims
        )
        results.append(result)
        tokens.append(token)
        state = new
        if c == 0:
            got[2] = exchange(cut_blocks(projected, seq_count, split_at, local_tokens, tokens))
    return finish(*zip(*results), exchange(entering), gain)


def solution(mesh):
    in_specs = (P(("tp", "seq"), None), P(None, "tp", None), P("tp"), P("tp"), P("tp"), P("tp"))
    return jax.shard_map(
        per_device, mesh=mesh, in_specs=in_specs, out_specs=P("seq", "tp"), check_vma=False
    )
```

```python
import functools

import jax
import jax.numpy as jnp
from jax import lax
from jax.experimental import pallas as pl
from jax.experimental.pallas import tpu as pltpu
from jax.sharding import PartitionSpec as P

HEAD_DIM = 64
STATE_WIDTH = 128
BLOCK = 256
LANES = 128
HALF = BLOCK // 2
WIDE = 256
LOG2E = 1.4426950408889634
CAP = 80.0
EPSILON = 1e-05

f32 = jnp.float32
bf16 = jnp.bfloat16
NT = (((1,), (1,)), ((), ()))


def params(mib=60):
    return pltpu.CompilerParams(vmem_limit_bytes=mib * 2**20)


def silu(v):
    half = 0.5 * v
    return half + half * jnp.tanh(half)


def softplus(v):
    e = jnp.exp(-jnp.abs(v))
    u = 1.0 + e
    gap = u - 1.0
    tiny = gap == 0.0
    log_part = jnp.where(tiny, e, jnp.log(u) * (e / jnp.where(tiny, 1.0, gap)))
    return jnp.maximum(v, 0.0) + log_part


def in_hbm(*arrays):
    return [pltpu.with_memory_space_constraint(array, pltpu.HBM) for array in arrays]


def in_vmem(*arrays):
    return [pltpu.with_memory_space_constraint(array, pltpu.VMEM) for array in arrays]


def per_group(*shape):
    return pl.BlockSpec((1,) + shape, lambda g: (g,) + (0,) * len(shape))


RIM = 4


def rim_rows(rows, width):
    base = rows // 16 * 16
    height = -(-(rows - base + RIM * -(-rows // width)) // 8) * 8
    assert height <= 16
    return base, height


def first_kernel(src, dst, held, windows, ends, in_sems, rim_sems, out_sems, end_sems):
    rows, all_tokens = src.shape
    count, _, width = dst.shape
    tokens = all_tokens // count
    base, height = rim_rows(rows, width)

    def fetch(d):
        at = d * tokens
        return pltpu.make_async_copy(src.at[:, at : at + width], held.at[d], in_sems.at[d])

    def window(d):
        at = d * tokens - LANES
        return pltpu.make_async_copy(src.at[:, at : at + LANES], windows.at[d], rim_sems.at[d])

    def place(d):
        return pltpu.make_async_copy(
            held.at[d, :base, :], dst.at[d, :base, :], out_sems.at[d]
        )

    def place_end(d):
        return pltpu.make_async_copy(
            ends.at[d], dst.at[d, base : base + height, :], end_sems.at[d]
        )

    for d in range(count):
        fetch(d).start()
        if d:
            window(d).start()
    row = lax.broadcasted_iota(jnp.int32, (height, LANES), 0) - (rows - base)
    col = lax.broadcasted_iota(jnp.int32, (height, LANES), 1)
    hit = (row >= 0) & (col == lax.rem(row + 16, RIM) + LANES - RIM)
    pick = jnp.where(hit, 1.0, 0.0).astype(bf16)
    which = lax.broadcasted_iota(jnp.int32, (height, width), 0) - (rows - base)
    for d in range(count):
        fetch(d).wait()
        place(d).start()
        end = held[d, base:rows, :].astype(f32)
        end = jnp.concatenate([end, jnp.zeros((height - end.shape[0], width), f32)], axis=0)
        if d:
            window(d).wait()
            rims = lax.dot_general(pick, windows[d], NT, preferred_element_type=f32)
            for j in range(-(-rows // width)):
                part = rims[:, j * width : min((j + 1) * width, rows)]
                if part.shape[1] < width:
                    fill = jnp.zeros((height, width - part.shape[1]), f32)
                    part = jnp.concatenate([part, fill], axis=1)
                end = jnp.where((which >= RIM * j) & (which < RIM * (j + 1)), part, end)
        ends[d] = end.astype(bf16)
        place_end(d).start()
    for d in range(count):
        place(d).wait()
        place_end(d).wait()


def cut_first(projected, count, width):
    rows = projected.shape[0]
    base, height = rim_rows(rows, width)
    sems = pltpu.SemaphoreType.DMA((count,))
    anywhere = pl.BlockSpec(memory_space=pl.ANY)
    return pl.pallas_call(
        first_kernel,
        in_specs=[anywhere],
        out_specs=anywhere,
        out_shape=pltpu.HBM((count, base + height, width), bf16),
        scratch_shapes=[
            pltpu.VMEM((count, rows, width), bf16),
            pltpu.VMEM((count, rows, LANES), bf16),
            pltpu.VMEM((count, height, width), bf16),
            sems,
            sems,
            sems,
            sems,
        ],
        compiler_params=params(),
        name="cut_first",
    )(*in_hbm(projected))


def staged(moves, held, in_sems, out_sems):
    for i, (source, _) in enumerate(moves):
        pltpu.make_async_copy(source, held.at[i], in_sems.at[i]).start()
    for i, (source, target) in enumerate(moves):
        pltpu.make_async_copy(source, held.at[i], in_sems.at[i]).wait()
        pltpu.make_async_copy(held.at[i], target, out_sems.at[i]).start()
    for i, (_, target) in enumerate(moves):
        pltpu.make_async_copy(held.at[i], target, out_sems.at[i]).wait()


def staging(count, rows):
    sems = pltpu.SemaphoreType.DMA((count,))
    return [pltpu.VMEM((count, rows, BLOCK), bf16), sems, sems]


def cut_kernel(low, count, src, *refs):
    dst = refs[-4]
    tokens = src.shape[1] // count
    moves = []
    for d in range(count):
        at = d * tokens + low
        moves.append((src.at[:, at : at + BLOCK], dst.at[d]))
    staged(moves, *refs[-3:])


def cut_block(projected, count, low, after):
    rows = projected.shape[0]
    args = in_hbm(projected, *after)
    anywhere = pl.BlockSpec(memory_space=pl.ANY)
    return pl.pallas_call(
        functools.partial(cut_kernel, low, count),
        in_specs=[anywhere] * len(args),
        out_specs=anywhere,
        out_shape=pltpu.HBM((count, rows, BLOCK), bf16),
        scratch_shapes=staging(count, rows),
        compiler_params=params(),
        name="cut_block",
    )(*args)


def pairs_kernel(low, count, me_ref, src, *refs):
    own, near, *far = refs[-(count // 2 + 4) : -3]
    tokens = src.shape[1] // count
    me = me_ref[0]
    targets = [own, near]
    for pair in far:
        targets += [pair.at[0], pair.at[1]]
    moves = []
    for k, target in enumerate(targets):
        at = pl.multiple_of((me ^ k) * tokens + low, LANES)
        moves.append((src.at[:, pl.ds(at, BLOCK)], target))
    staged(moves[2:] + moves[:2], *refs[-3:])


def cut_pairs(projected, me, count, low, after):
    rows = projected.shape[0]
    anywhere = pl.BlockSpec(memory_space=pl.ANY)
    one, two = pltpu.HBM((rows, BLOCK), bf16), pltpu.HBM((2, rows, BLOCK), bf16)
    return pl.pallas_call(
        functools.partial(pairs_kernel, low, count),
        in_specs=[pl.BlockSpec(memory_space=pltpu.SMEM)] + [anywhere] * (1 + len(after)),
        out_specs=[anywhere] * (count // 2 + 1),
        out_shape=[one, one] + [two] * (count // 2 - 1),
        scratch_shapes=staging(count, rows),
        compiler_params=params(),
        name="cut_pairs",
    )(me, *in_hbm(projected, *after))


def forward_kernel(count, *refs):
    dst = refs[-4]
    moves = [(refs[j].at[1], dst.at[j]) for j in range(count // 2 - 1)]
    staged(moves, *refs[-3:])


def forward(pairs, after):
    count = 2 * len(pairs) + 2
    rows = pairs[0].shape[1]
    anywhere = pl.BlockSpec(memory_space=pl.ANY)
    return pl.pallas_call(
        functools.partial(forward_kernel, count),
        in_specs=[anywhere] * (len(pairs) + len(after)),
        out_specs=anywhere,
        out_shape=pltpu.HBM((len(pairs), rows, BLOCK), bf16),
        scratch_shapes=staging(len(pairs), rows),
        compiler_params=params(),
        name="forward",
    )(*pairs, *in_hbm(*after))


def join_kernel(count, me_ref, own, near, *refs):
    others = count // 2 - 1
    pairs, passed, dst = refs[:others], refs[others], refs[-4]
    me = me_ref[0]
    sources = [own, near]
    for j in range(others):
        sources += [pairs[j].at[0], passed.at[j]]
    staged([(source, dst.at[me ^ k]) for k, source in enumerate(sources)], *refs[-3:])


def join(me, own, near, pairs, passed, after):
    count = 2 * len(pairs) + 2
    rows = own.shape[0]
    anywhere = pl.BlockSpec(memory_space=pl.ANY)
    args = [own, near, *pairs, passed, *in_hbm(*after)]
    return pl.pallas_call(
        functools.partial(join_kernel, count),
        in_specs=[pl.BlockSpec(memory_space=pltpu.SMEM)] + [anywhere] * len(args),
        out_specs=anywhere,
        out_shape=pltpu.HBM((count, rows, BLOCK), bf16),
        scratch_shapes=staging(count, rows),
        compiler_params=params(),
        name="join",
    )(me, *args)


def gather_rows(recv, prev, first, raw, rows, low, high, ahead=True, only=None):
    for s in range(recv.shape[0]):
        a = max(low - s * rows, 0) // 16 * 16
        b = min(-(-(high - s * rows) // 16) * 16, rows)
        if b <= a:
            continue
        at = s * rows + a
        raw[at : at + b - a, LANES:] = recv[s, a:b, :].astype(f32)
        if not ahead:
            continue
        if not first:
            raw[at : at + b - a, :LANES] = prev[s if only is None else 0, a:b, :].astype(f32)
            continue
        width = prev.shape[2]
        base, height = rim_rows(rows, width)
        rims = prev[s if only is None else 0, :height, :].astype(f32)
        tall = jnp.concatenate([jnp.zeros((LANES - height, width), f32), rims], axis=0)
        for j in range(-(-rows // width)):
            c, d = max(a, j * width), min(b, (j + 1) * width)
            if d <= c:
                continue
            shift = height - RIM - (rows - base) - RIM * j
            moved = (pltpu.roll(tall, shift, 0) if shift else tall).T
            raw[s * rows + c : s * rows + d, :LANES] = moved[c - j * width : d - j * width]


def band():
    row = lax.broadcasted_iota(jnp.int32, (2 * LANES, 3 * LANES), 0)
    col = lax.broadcasted_iota(jnp.int32, (2 * LANES, 3 * LANES), 1)
    tap = col // LANES
    return jnp.where(row == col - tap * LANES + LANES - 3 + tap, 1.0, 0.0).astype(bf16)


def shift_rows(raw, low, shifted, at):
    low[...] = raw[at : at + low.shape[0], :].astype(bf16)
    picks = band()
    for i in range(BLOCK // LANES):
        window = low[:, i * LANES : (i + 2) * LANES]
        shifted[i] = jnp.dot(window, picks, preferred_element_type=f32)


def conv_tile(raw, shifted, w, at, r):
    rows = slice(r, r + HEAD_DIM)
    taps = [jnp.broadcast_to(w[0, rows, k : k + 1], (HEAD_DIM, LANES)) for k in range(4)]
    parts = []
    for i in range(BLOCK // LANES):
        summed = None
        for k in range(3):
            part = taps[k] * shifted[i, rows, k * LANES : (k + 1) * LANES]
            summed = part if summed is None else summed + part
        own = raw[at + r : at + r + HEAD_DIM, (i + 1) * LANES : (i + 2) * LANES]
        parts.append(silu(summed + taps[3] * own).astype(bf16))
    return jnp.concatenate(parts, axis=1)


def state_kernel(dims, first, last, recv, *refs):
    spg, rows, heads, span, piece_heads = dims
    prev, refs = refs[0], refs[1:]
    w, bias, a_log, state_in, lead_in = refs[:5]
    xact, bmap, run_out, dt_out, cum_out, state_out, lead_out = refs[-11:-4]
    raw, xw, low, shifted = refs[-4:]
    steps = 2 * span + 2 * STATE_WIDTH

    gather_rows(recv, prev, first, raw, rows, steps, steps + heads, False)
    gather_rows(recv, prev, first, raw, rows, span, 2 * span + STATE_WIDTH)
    dt = softplus(raw[steps : steps + heads, LANES:] + bias[0])
    log_decay = -jnp.exp(a_log[0]) * dt
    lane = lax.broadcasted_iota(jnp.int32, (heads, BLOCK), 1)
    run = log_decay
    shift = 1
    while shift < BLOCK:
        run = run + jnp.where(lane >= shift, pltpu.roll(run, shift, 1), 0.0)
        shift *= 2
    final = run[:, BLOCK - 1 :]
    scale = jnp.exp(final - run) * dt
    cum = run + lead_in[0][:, :1]
    run_out[0] = run
    dt_out[0] = dt
    cum_out[0] = cum
    lead = jnp.broadcast_to(cum[:, BLOCK - 1 :], (heads, LANES))
    lead_out[0] = lead
    keep = jnp.broadcast_to(jnp.exp(final), (heads, LANES))

    shift_rows(raw, low, shifted, span)
    for r in range(0, STATE_WIDTH, HEAD_DIM):
        bmap[0, r : r + HEAD_DIM, :] = conv_tile(raw, shifted, w, span, span + r)
    for h in range(heads):
        r = h * HEAD_DIM
        tile = conv_tile(raw, shifted, w, span, r)
        xact[0, r : r + HEAD_DIM, :] = tile
        xw[r : r + HEAD_DIM, :] = (tile.astype(f32) * scale[h : h + 1, :]).astype(bf16)
    update = lax.dot_general(xw[...], bmap[0], NT, preferred_element_type=f32)
    for h in range(heads):
        r = h * HEAD_DIM
        new = update[r : r + HEAD_DIM, :]
        if not first:
            new = keep[h : h + 1, :] * state_in[0, r : r + HEAD_DIM, :] + new
        if last:
            at = (h % piece_heads) * HEAD_DIM
            state_out[h // piece_heads, at : at + HEAD_DIM, :] = new.astype(bf16)
        else:
            state_out[0, r : r + HEAD_DIM, :] = new
    if last:
        high, low = split(jnp.exp(lead))
        fill = jnp.zeros((8 - piece_heads, LANES), f32)
        for i in range(heads // piece_heads):
            mine = slice(i * piece_heads, (i + 1) * piece_heads)
            parts = [high[mine].astype(f32), fill, low[mine].astype(f32), fill]
            at = piece_heads * HEAD_DIM
            state_out[i, at : at + 16, :] = jnp.concatenate(parts, axis=0).astype(bf16)


def chunk_specs(got, chunk, dims, only=None):
    spg, rows = dims[:2]
    slabs = spg if only is None else 1

    def ahead(source, shape, row, lane):
        def index(g):
            return (g if only is None else g * spg + only, row, lane)

        return source, pl.BlockSpec((slabs,) + shape, index)

    def lane_of(block):
        first, middle, last = got
        ahead_of = first.shape[2] // BLOCK
        if block < ahead_of:
            return first, block
        return (middle if block == ahead_of else last), 0

    source, at = lane_of(chunk)
    block = pl.BlockSpec((spg, source.shape[1], BLOCK), lambda g: (g, 0, at))
    if chunk == 0:
        width = source.shape[2]
        prev, prev_spec = ahead(source, (16, width), rim_rows(rows, width)[0] // 16, 0)
    else:
        prev, place = lane_of(chunk - 1)
        lane = (place + 1) * (BLOCK // LANES) - 1
        prev, prev_spec = ahead(prev, (prev.shape[1], LANES), 0, lane)
    return [source, prev], [block, prev_spec]


def state_chunk(chunk, chunks, got, w, bias, a_log, state, lead, before, dims):
    spg, rows, heads, span, piece_heads = dims
    groups = w.shape[0]
    last = chunk == chunks - 1
    if last:
        packed = piece_heads * HEAD_DIM + 16
        state_shape = pltpu.HBM((groups * spg, packed, STATE_WIDTH), bf16)
        state_spec = pl.BlockSpec((spg, packed, STATE_WIDTH), lambda g: (g, 0, 0))
    else:
        state_shape = pltpu.HBM((groups, span, STATE_WIDTH), f32)
        state_spec = per_group(span, STATE_WIDTH)

    def out(dtype, *shape):
        return pltpu.HBM((groups,) + shape, dtype)

    args, specs = chunk_specs(got, chunk, dims)
    args[1:] = in_hbm(args[1])
    args[:1] = in_vmem(args[0]) if last else in_hbm(args[0])
    after = in_hbm(*before)
    return pl.pallas_call(
        functools.partial(state_kernel, dims, chunk == 0, last),
        grid=(groups,),
        in_specs=specs
        + [
            per_group(span + STATE_WIDTH, 4),
            per_group(heads, 1),
            per_group(heads, 1),
            per_group(span, STATE_WIDTH),
            per_group(heads, LANES),
        ]
        + [pl.BlockSpec(memory_space=pl.ANY)] * len(after),
        out_specs=[
            per_group(span, BLOCK),
            per_group(STATE_WIDTH, BLOCK),
            per_group(heads, BLOCK),
            per_group(heads, BLOCK),
            per_group(heads, BLOCK),
            state_spec,
            per_group(heads, LANES),
        ],
        out_shape=[
            out(bf16, span, BLOCK),
            out(bf16, STATE_WIDTH, BLOCK),
            out(f32, heads, BLOCK),
            out(f32, heads, BLOCK),
            out(f32, heads, BLOCK),
            state_shape,
            out(f32, heads, LANES),
        ],
        scratch_shapes=[
            pltpu.VMEM((rows * spg, LANES + BLOCK), f32),
            pltpu.VMEM((span, BLOCK), bf16),
            pltpu.VMEM((span + STATE_WIDTH, LANES + BLOCK), bf16),
            pltpu.VMEM((BLOCK // LANES, span + STATE_WIDTH, 3 * LANES), f32),
        ],
        compiler_params=params(48 if last else 60),
        cost_estimate=pl.CostEstimate(flops=4 * 10**9, bytes_accessed=10**7, transcendentals=10**6),
        name="state_chunk",
    )(*args, *in_hbm(w, bias, a_log, state, lead), *after)


def split(v):
    high = v.astype(bf16)
    return high, (v - high.astype(f32)).astype(bf16)


def block_kernel(dims, first, recv, *refs):
    spg, rows, heads, span, piece_heads = dims
    prev, refs = refs[0], refs[1:]
    w, xact, bmap, run_ref, dt_ref, cum_ref, state, skip = refs[:8]
    mixed, gate_out, side, token, raw, low, shifted = refs[-7:]
    at_c = 2 * span + STATE_WIDTH
    gather_rows(recv, prev, first, raw, rows, at_c, at_c + STATE_WIDTH, True, at_c // rows)
    gather_rows(recv, prev, first, raw, rows, 0, span, False)
    token[0] = cum_ref[0, :8, :LANES]
    shift_rows(raw, low, shifted, at_c)
    c = [conv_tile(raw, shifted, w, at_c, r) for r in range(0, STATE_WIDTH, HEAD_DIM)]
    c = jnp.concatenate(c, axis=0)
    b_rows = bmap[0].astype(f32).T.astype(bf16)
    scores = jnp.dot(b_rows, c, preferred_element_type=f32)
    src = lax.broadcasted_iota(jnp.int32, (HALF, HALF), 0)
    dst = lax.broadcasted_iota(jnp.int32, (HALF, HALF), 1)
    causal = src <= dst
    s00 = jnp.where(causal, scores[:HALF, :HALF], 0.0)
    s01 = scores[:HALF, HALF:]
    s11 = jnp.where(causal, scores[HALF:, HALF:], 0.0)
    r = run_ref[0] * LOG2E
    q = (r - jnp.log(dt_ref[0]) * LOG2E).T
    if not first:
        cc = jnp.concatenate([c, c], axis=0)
        entered = jnp.exp2(r)
    reach = [part.astype(f32) for part in split(jnp.exp(cum_ref[0]))]
    reach.append(jnp.zeros((STATE_WIDTH - 2 * heads, BLOCK), f32))
    side[0, :, :STATE_WIDTH] = c.astype(f32).T.astype(bf16)
    side[0, :, STATE_WIDTH:] = jnp.concatenate(reach, axis=0).T.astype(bf16)
    turned = []
    for h in range(heads):
        at = h * HEAD_DIM
        r0, r1 = r[h : h + 1, :HALF], r[h : h + 1, HALF:]
        q0, q1 = q[:HALF, h : h + 1], q[HALF:, h : h + 1]
        w00 = (s00 * jnp.exp2(jnp.minimum(r0 - q0, CAP))).astype(bf16)
        w01 = (s01 * jnp.exp2(r1 - q0)).astype(bf16)
        w11 = (s11 * jnp.exp2(jnp.minimum(r1 - q1, CAP))).astype(bf16)
        x = xact[0, at : at + HEAD_DIM, :]
        y0 = jnp.dot(x[:, :HALF], w00, preferred_element_type=f32)
        y1 = jnp.dot(x, jnp.concatenate([w01, w11], axis=0), preferred_element_type=f32)
        y = jnp.concatenate([y0, y1], axis=1) + skip[0, h : h + 1, :] * x.astype(f32)
        if not first:
            if at % WIDE == 0:
                both = jnp.concatenate(split(state[0, at : at + WIDE, :]), axis=1)
                carried = jnp.dot(both, cc, preferred_element_type=f32)
            y = y + entered[h : h + 1, :] * carried[at % WIDE : at % WIDE + HEAD_DIM, :]
        gate = raw[at : at + HEAD_DIM, LANES:]
        turned.append((y * silu(gate), gate))
        if len(turned) * HEAD_DIM == LANES:
            lanes = slice(at + HEAD_DIM - LANES, at + HEAD_DIM)
            mixed[0, :, lanes] = jnp.concatenate([pair[0] for pair in turned], axis=0).T
            wide = jnp.concatenate([pair[1] for pair in turned], axis=0).T
            gate_out[0, :, lanes] = wide.astype(bf16)
            turned = []


def block_chunk(
    chunk, chunks, got, w, xact, bmap, run, dt, cum, state, skip, after, dims
):
    spg, rows, heads, span, piece_heads = dims
    groups = w.shape[0]

    at_c = 2 * span + STATE_WIDTH
    one = at_c // rows
    assert (at_c + STATE_WIDTH - 1) // rows == one
    args, specs = chunk_specs(got, chunk, dims, one)
    args = in_hbm(*args)
    args += in_hbm(w, xact, bmap, run, dt, cum, state, skip)
    specs += [
        pl.BlockSpec((1, STATE_WIDTH, 4), lambda g: (g, span // STATE_WIDTH + 1, 0)),
        per_group(span, BLOCK),
        per_group(STATE_WIDTH, BLOCK),
        per_group(heads, BLOCK),
        per_group(heads, BLOCK),
        per_group(heads, BLOCK),
        per_group(span, STATE_WIDTH),
        per_group(heads, 1),
    ]
    args += in_vmem(*after)
    specs += [pl.BlockSpec(memory_space=pl.ANY)] * len(after)

    def out(dtype, *shape):
        return pltpu.HBM((groups,) + shape, dtype)

    return pl.pallas_call(
        functools.partial(block_kernel, dims, chunk == 0),
        grid=(groups,),
        in_specs=specs,
        out_specs=[
            per_group(BLOCK, span),
            per_group(BLOCK, span),
            per_group(BLOCK, 2 * STATE_WIDTH),
            per_group(8, LANES),
        ],
        out_shape=[
            out(f32, BLOCK, span),
            out(bf16, BLOCK, span),
            out(bf16, BLOCK, 2 * STATE_WIDTH),
            out(f32, 8, LANES),
        ],
        scratch_shapes=[
            pltpu.VMEM((rows * spg, LANES + BLOCK), f32),
            pltpu.VMEM((STATE_WIDTH, LANES + BLOCK), bf16),
            pltpu.VMEM((BLOCK // LANES, STATE_WIDTH, 3 * LANES), f32),
        ],
        compiler_params=params(),
        cost_estimate=pl.CostEstimate(flops=4 * 10**9, bytes_accessed=10**7, transcendentals=10**6),
        name="block_chunk",
    )(*args)


def relay_kernel(piece_heads, src, token, dst):
    rows = piece_heads * HEAD_DIM
    held = jnp.zeros((rows, STATE_WIDTH), f32)
    for d in range(src.shape[0]):
        dst[d] = held.T.astype(bf16)
        both = src[d, rows:, :].astype(f32)
        decay = both[:8] + both[8:]
        spread = [
            jnp.broadcast_to(decay[h : h + 1, :], (HEAD_DIM, STATE_WIDTH))
            for h in range(piece_heads)
        ]
        held = jnp.concatenate(spread, axis=0) * held + src[d, :rows, :].astype(f32)


def relay(packed, token, piece_heads):
    count = packed.shape[0]
    rows = piece_heads * HEAD_DIM
    return pl.pallas_call(
        functools.partial(relay_kernel, piece_heads),
        in_specs=[pl.BlockSpec(memory_space=pltpu.VMEM), pl.BlockSpec(memory_space=pl.ANY)],
        out_shape=pltpu.VMEM((count, STATE_WIDTH, rows), bf16),
        compiler_params=params(16),
        name="relay",
    )(packed, *in_hbm(token))


def final_kernel(chunks, groups, *refs):
    mixed, gates, sides = (refs[i * chunks : (i + 1) * chunks] for i in range(3))
    state, gain, out = refs[3 * chunks : 3 * chunks + 3]
    held, gate_held, side_held, kept, carried, done, sems, out_sems = refs[3 * chunks + 3 :]
    span = held.shape[2]
    piece = state.shape[2]
    spg = state.shape[0] // groups
    heads = span // HEAD_DIM
    steps = [(g, c) for g in range(groups) for c in range(chunks)]

    def loads(i):
        g, c = steps[i]
        slot = i
        moves = []
        moves.append((sides[c].at[g], side_held.at[slot]))
        moves.append((mixed[c].at[g], held.at[slot]))
        moves.append((gates[c].at[g], gate_held.at[slot]))
        return [
            pltpu.make_async_copy(a, b, sems.at[slot, j]) for j, (a, b) in enumerate(moves)
        ]

    def store(i):
        g, c = steps[i]
        return pltpu.make_async_copy(
            done.at[i % 2],
            out.at[c * BLOCK : (c + 1) * BLOCK, g * span : (g + 1) * span],
            out_sems.at[i % 2],
        )

    for i in range(len(steps)):
        for move in loads(i):
            move.start()
    row = lax.broadcasted_iota(jnp.int32, (STATE_WIDTH, span), 0)
    col = lax.broadcasted_iota(jnp.int32, (STATE_WIDTH, span), 1) // HEAD_DIM
    spread = jnp.where((row == col) | (row == col + heads), 1.0, 0.0).astype(bf16)
    for i, (g, c) in enumerate(steps):
        slot = i
        for move in loads(i):
            move.wait()
        if i >= 2:
            store(i - 2).wait()
        side = side_held[slot]
        reach = jnp.dot(side[:, STATE_WIDTH:], spread, preferred_element_type=f32)
        for j in range(spg):
            lanes = slice(j * piece, (j + 1) * piece)
            part = jnp.dot(
                side[:, :STATE_WIDTH], state[g * spg + j], preferred_element_type=f32
            )
            carried[:, lanes] = part * reach[:, lanes]
        for q in range(0, BLOCK, HEAD_DIM):
            rows = slice(q, q + HEAD_DIM)
            total = jnp.zeros((HEAD_DIM, LANES), f32)
            for at in range(0, span, LANES):
                lanes = slice(at, at + LANES)
                gate = silu(gate_held[slot, rows, lanes].astype(f32))
                v = held[slot, rows, lanes] + gate * carried[rows, lanes]
                kept[rows, lanes] = v
                total = total + v * v
            mean = jnp.sum(total, axis=1, keepdims=True) * (1.0 / span)
            factor = lax.rsqrt(mean + EPSILON)
            for at in range(0, span, LANES):
                lanes = slice(at, at + LANES)
                scaled = kept[rows, lanes] * factor * gain[g, :, lanes]
                done[i % 2, rows, lanes] = scaled.astype(bf16)
        store(i).start()
    for i in range(max(len(steps) - 2, 0), len(steps)):
        store(i).wait()


def finish(mixed, gates, sides, state, gain):
    chunks = len(mixed)
    groups, _, span = mixed[0].shape
    steps = groups * chunks
    anywhere = pl.BlockSpec(memory_space=pl.ANY)
    within = pl.BlockSpec(memory_space=pltpu.VMEM)
    return pl.pallas_call(
        functools.partial(final_kernel, chunks, groups),
        in_specs=[anywhere] * (3 * chunks) + [within] * 2,
        out_specs=anywhere,
        out_shape=jax.ShapeDtypeStruct((chunks * BLOCK, groups * span), bf16),
        scratch_shapes=[
            pltpu.VMEM((steps, BLOCK, span), f32),
            pltpu.VMEM((steps, BLOCK, span), bf16),
            pltpu.VMEM((steps, BLOCK, 2 * STATE_WIDTH), bf16),
            pltpu.VMEM((BLOCK, span), f32),
            pltpu.VMEM((BLOCK, span), f32),
            pltpu.VMEM((2, BLOCK, span), bf16),
            pltpu.SemaphoreType.DMA((steps, 3)),
            pltpu.SemaphoreType.DMA((2,)),
        ],
        compiler_params=params(40),
        name="finish",
    )(*in_hbm(*mixed, *gates, *sides), state, gain)


def swap(array, k):
    count = lax.axis_size("seq")
    return lax.ppermute(array, "seq", [(i, i ^ k) for i in range(count)])


def exchange(array):
    return lax.all_to_all(array, "seq", split_axis=0, concat_axis=0, tiled=True)


def per_device(projected, conv_weight, dt_bias, a_log, d_skip, norm_gain):
    seq_count = lax.axis_size("seq")
    groups = conv_weight.shape[1]
    heads = dt_bias.shape[0] // groups
    span = heads * HEAD_DIM
    rows, all_tokens = projected.shape
    local_tokens = all_tokens // seq_count
    chunks = local_tokens // BLOCK
    spg = seq_count // groups
    piece_heads = groups * heads // seq_count
    dims = (spg, rows, heads, span, piece_heads)

    w = jnp.transpose(conv_weight, (1, 2, 0))
    bias = dt_bias.reshape(groups, heads, 1)
    rate = a_log.reshape(groups, heads, 1)
    skip = d_skip.reshape(groups, heads, 1)
    gain = norm_gain.reshape(groups, 1, span)
    state = jnp.zeros((groups, span, STATE_WIDTH), f32)
    lead = jnp.zeros((groups, heads, LANES), f32)

    me = lax.axis_index("seq").astype(jnp.int32).reshape(1)
    assert chunks > 2 and seq_count & (seq_count - 1) == 0
    cut = cut_first(projected, seq_count, local_tokens - 2 * BLOCK)
    got = [exchange(cut)]
    own, near, *pairs = cut_pairs(projected, me, seq_count, local_tokens - 2 * BLOCK, [cut])
    near = swap(near, 1)
    pairs = [swap(pair, 2 * j + 2) for j, pair in enumerate(pairs)]
    ready = [own, w, bias, rate, skip, gain, state, lead]
    cut = cut_block(projected, seq_count, local_tokens - BLOCK, ready)
    got += [None, exchange(cut)]

    results, tokens = [], []
    for c in range(chunks):
        before = []
        if c == chunks - 2:
            passed = swap(forward(pairs, [lead]), 1)
            got[1] = join(me, own, near, pairs, passed, tokens)
        if c == chunks - 1:
            before = tokens[-2:-1]
        xact, bmap, run, dt, cum, new, lead = state_chunk(
            c, chunks, got, w, bias, rate, state, lead, before, dims
        )
        after = []
        if c == chunks - 1:
            entering = relay(exchange(new), tokens[-1], piece_heads)
            after = [entering]
        *result, token = block_chunk(
            c, chunks, got, w, xact, bmap, run, dt, cum, state, skip, after, dims
        )
        results.append(result)
        tokens.append(token)
        state = new
    return finish(*zip(*results), exchange(entering), gain)


def solution(mesh):
    in_specs = (P(("tp", "seq"), None), P(None, "tp", None), P("tp"), P("tp"), P("tp"), P("tp"))
    return jax.shard_map(
        per_device, mesh=mesh, in_specs=in_specs, out_specs=P("seq", "tp"), check_vma=False
    )
```

```python
import functools

import jax
import jax.numpy as jnp
from jax import lax
from jax.experimental import pallas as pl
from jax.experimental.pallas import tpu as pltpu
from jax.sharding import PartitionSpec as P

HEAD_DIM = 64
STATE_WIDTH = 128
BLOCK = 256
LANES = 128
HALF = BLOCK // 2
WIDE = 256
LOG2E = 1.4426950408889634
CAP = 80.0
EPSILON = 1e-05

f32 = jnp.float32
bf16 = jnp.bfloat16
NT = (((1,), (1,)), ((), ()))


def params(mib=60):
    return pltpu.CompilerParams(vmem_limit_bytes=mib * 2**20)


def silu(v):
    half = 0.5 * v
    return half + half * jnp.tanh(half)


def softplus(v):
    e = jnp.exp(-jnp.abs(v))
    u = 1.0 + e
    gap = u - 1.0
    tiny = gap == 0.0
    log_part = jnp.where(tiny, e, jnp.log(u) * (e / jnp.where(tiny, 1.0, gap)))
    return jnp.maximum(v, 0.0) + log_part


def in_hbm(*arrays):
    return [pltpu.with_memory_space_constraint(array, pltpu.HBM) for array in arrays]


def in_vmem(*arrays):
    return [pltpu.with_memory_space_constraint(array, pltpu.VMEM) for array in arrays]


def per_group(*shape):
    return pl.BlockSpec((1,) + shape, lambda g: (g,) + (0,) * len(shape))


RIM = 4


def rim_rows(rows, width):
    base = rows // 16 * 16
    height = -(-(rows - base + RIM * -(-rows // width)) // 8) * 8
    assert height <= 16
    return base, height


def first_kernel(src, dst, held, windows, ends, in_sems, rim_sems, out_sems, end_sems):
    rows, all_tokens = src.shape
    count, _, width = dst.shape
    tokens = all_tokens // count
    base, height = rim_rows(rows, width)

    def fetch(d):
        at = d * tokens
        return pltpu.make_async_copy(src.at[:, at : at + width], held.at[d], in_sems.at[d])

    def window(d):
        at = d * tokens - LANES
        return pltpu.make_async_copy(src.at[:, at : at + LANES], windows.at[d], rim_sems.at[d])

    def place(d):
        return pltpu.make_async_copy(
            held.at[d, :base, :], dst.at[d, :base, :], out_sems.at[d]
        )

    def place_end(d):
        return pltpu.make_async_copy(
            ends.at[d], dst.at[d, base : base + height, :], end_sems.at[d]
        )

    for d in range(count):
        fetch(d).start()
        if d:
            window(d).start()
    row = lax.broadcasted_iota(jnp.int32, (height, LANES), 0) - (rows - base)
    col = lax.broadcasted_iota(jnp.int32, (height, LANES), 1)
    hit = (row >= 0) & (col == lax.rem(row + 16, RIM) + LANES - RIM)
    pick = jnp.where(hit, 1.0, 0.0).astype(bf16)
    which = lax.broadcasted_iota(jnp.int32, (height, width), 0) - (rows - base)
    for d in range(count):
        fetch(d).wait()
        place(d).start()
        end = held[d, base:rows, :].astype(f32)
        end = jnp.concatenate([end, jnp.zeros((height - end.shape[0], width), f32)], axis=0)
        if d:
            window(d).wait()
            rims = lax.dot_general(pick, windows[d], NT, preferred_element_type=f32)
            for j in range(-(-rows // width)):
                part = rims[:, j * width : min((j + 1) * width, rows)]
                if part.shape[1] < width:
                    fill = jnp.zeros((height, width - part.shape[1]), f32)
                    part = jnp.concatenate([part, fill], axis=1)
                end = jnp.where((which >= RIM * j) & (which < RIM * (j + 1)), part, end)
        ends[d] = end.astype(bf16)
        place_end(d).start()
    for d in range(count):
        place(d).wait()
        place_end(d).wait()


def cut_first(projected, count, width):
    rows = projected.shape[0]
    base, height = rim_rows(rows, width)
    sems = pltpu.SemaphoreType.DMA((count,))
    anywhere = pl.BlockSpec(memory_space=pl.ANY)
    return pl.pallas_call(
        first_kernel,
        in_specs=[anywhere],
        out_specs=anywhere,
        out_shape=pltpu.HBM((count, base + height, width), bf16),
        scratch_shapes=[
            pltpu.VMEM((count, rows, width), bf16),
            pltpu.VMEM((count, rows, LANES), bf16),
            pltpu.VMEM((count, height, width), bf16),
            sems,
            sems,
            sems,
            sems,
        ],
        compiler_params=params(),
        name="cut_first",
    )(*in_hbm(projected))


def staged(moves, held, in_sems, out_sems):
    for i, (source, _) in enumerate(moves):
        pltpu.make_async_copy(source, held.at[i], in_sems.at[i]).start()
    for i, (source, target) in enumerate(moves):
        pltpu.make_async_copy(source, held.at[i], in_sems.at[i]).wait()
        pltpu.make_async_copy(held.at[i], target, out_sems.at[i]).start()
    for i, (_, target) in enumerate(moves):
        pltpu.make_async_copy(held.at[i], target, out_sems.at[i]).wait()


def staging(count, rows):
    sems = pltpu.SemaphoreType.DMA((count,))
    return [pltpu.VMEM((count, rows, BLOCK), bf16), sems, sems]


def cut_kernel(low, count, src, *refs):
    dst = refs[-4]
    tokens = src.shape[1] // count
    moves = []
    for d in range(count):
        at = d * tokens + low
        moves.append((src.at[:, at : at + BLOCK], dst.at[d]))
    staged(moves, *refs[-3:])


def cut_block(projected, count, low, after):
    rows = projected.shape[0]
    args = in_hbm(projected, *after)
    anywhere = pl.BlockSpec(memory_space=pl.ANY)
    return pl.pallas_call(
        functools.partial(cut_kernel, low, count),
        in_specs=[anywhere] * len(args),
        out_specs=anywhere,
        out_shape=pltpu.HBM((count, rows, BLOCK), bf16),
        scratch_shapes=staging(count, rows),
        compiler_params=params(),
        name="cut_block",
    )(*args)


def pairs_kernel(low, count, me_ref, src, *refs):
    own, near, *far = refs[-(count // 2 + 4) : -3]
    tokens = src.shape[1] // count
    me = me_ref[0]
    targets = [own, near]
    for pair in far:
        targets += [pair.at[:, :BLOCK], pair.at[:, BLOCK:]]
    moves = []
    for k, target in enumerate(targets):
        at = pl.multiple_of((me ^ k) * tokens + low, LANES)
        moves.append((src.at[:, pl.ds(at, BLOCK)], target))
    staged(moves[2:] + moves[:2], *refs[-3:])


def cut_pairs(projected, me, count, low, after):
    rows = projected.shape[0]
    anywhere = pl.BlockSpec(memory_space=pl.ANY)
    one, two = pltpu.HBM((rows, BLOCK), bf16), pltpu.HBM((rows, 2 * BLOCK), bf16)
    return pl.pallas_call(
        functools.partial(pairs_kernel, low, count),
        in_specs=[pl.BlockSpec(memory_space=pltpu.SMEM)] + [anywhere] * (1 + len(after)),
        out_specs=[anywhere] * (count // 2 + 1),
        out_shape=[one, one] + [two] * (count // 2 - 1),
        scratch_shapes=staging(count, rows),
        compiler_params=params(),
        name="cut_pairs",
    )(me, *in_hbm(projected, *after))


def forward_kernel(count, *refs):
    dst = refs[-4]
    moves = [
        (refs[j].at[:, BLOCK:], dst.at[:, j * BLOCK : (j + 1) * BLOCK])
        for j in range(count // 2 - 1)
    ]
    staged(moves, *refs[-3:])


def forward(pairs, after):
    count = 2 * len(pairs) + 2
    rows = pairs[0].shape[0]
    anywhere = pl.BlockSpec(memory_space=pl.ANY)
    return pl.pallas_call(
        functools.partial(forward_kernel, count),
        in_specs=[anywhere] * (len(pairs) + len(after)),
        out_specs=anywhere,
        out_shape=pltpu.HBM((rows, len(pairs) * BLOCK), bf16),
        scratch_shapes=staging(len(pairs), rows),
        compiler_params=params(),
        name="forward",
    )(*pairs, *in_hbm(*after))


def join_kernel(count, me_ref, own, near, *refs):
    others = count // 2 - 1
    pairs, passed, dst = refs[:others], refs[others], refs[-4]
    me = me_ref[0]
    sources = [own, near]
    for j in range(others):
        sources += [pairs[j].at[:, :BLOCK], passed.at[:, j * BLOCK : (j + 1) * BLOCK]]
    staged([(source, dst.at[me ^ k]) for k, source in enumerate(sources)], *refs[-3:])


def join(me, own, near, pairs, passed, after):
    count = 2 * len(pairs) + 2
    rows = own.shape[0]
    anywhere = pl.BlockSpec(memory_space=pl.ANY)
    args = [own, near, *pairs, passed, *in_hbm(*after)]
    return pl.pallas_call(
        functools.partial(join_kernel, count),
        in_specs=[pl.BlockSpec(memory_space=pltpu.SMEM)] + [anywhere] * len(args),
        out_specs=anywhere,
        out_shape=pltpu.HBM((count, rows, BLOCK), bf16),
        scratch_shapes=staging(count, rows),
        compiler_params=params(),
        name="join",
    )(me, *args)


def gather_rows(recv, prev, first, raw, rows, low, high, ahead=True, only=None):
    for s in range(recv.shape[0]):
        a = max(low - s * rows, 0) // 16 * 16
        b = min(-(-(high - s * rows) // 16) * 16, rows)
        if b <= a:
            continue
        at = s * rows + a
        raw[at : at + b - a, LANES:] = recv[s, a:b, :].astype(f32)
        if not ahead:
            continue
        if not first:
            raw[at : at + b - a, :LANES] = prev[s if only is None else 0, a:b, :].astype(f32)
            continue
        width = prev.shape[2]
        base, height = rim_rows(rows, width)
        rims = prev[s if only is None else 0, :height, :].astype(f32)
        tall = jnp.concatenate([jnp.zeros((LANES - height, width), f32), rims], axis=0)
        for j in range(-(-rows // width)):
            c, d = max(a, j * width), min(b, (j + 1) * width)
            if d <= c:
                continue
            shift = height - RIM - (rows - base) - RIM * j
            moved = (pltpu.roll(tall, shift, 0) if shift else tall).T
            raw[s * rows + c : s * rows + d, :LANES] = moved[c - j * width : d - j * width]


def band():
    row = lax.broadcasted_iota(jnp.int32, (2 * LANES, 3 * LANES), 0)
    col = lax.broadcasted_iota(jnp.int32, (2 * LANES, 3 * LANES), 1)
    tap = col // LANES
    return jnp.where(row == col - tap * LANES + LANES - 3 + tap, 1.0, 0.0).astype(bf16)


def shift_rows(raw, low, shifted, at):
    low[...] = raw[at : at + low.shape[0], :].astype(bf16)
    picks = band()
    for i in range(BLOCK // LANES):
        window = low[:, i * LANES : (i + 2) * LANES]
        shifted[i] = jnp.dot(window, picks, preferred_element_type=f32)


def conv_tile(raw, shifted, w, at, r):
    rows = slice(r, r + HEAD_DIM)
    taps = [jnp.broadcast_to(w[0, rows, k : k + 1], (HEAD_DIM, LANES)) for k in range(4)]
    parts = []
    for i in range(BLOCK // LANES):
        summed = None
        for k in range(3):
            part = taps[k] * shifted[i, rows, k * LANES : (k + 1) * LANES]
            summed = part if summed is None else summed + part
        own = raw[at + r : at + r + HEAD_DIM, (i + 1) * LANES : (i + 2) * LANES]
        parts.append(silu(summed + taps[3] * own).astype(bf16))
    return jnp.concatenate(parts, axis=1)


def state_kernel(dims, first, last, recv, *refs):
    spg, rows, heads, span, piece_heads = dims
    prev, refs = refs[0], refs[1:]
    w, bias, a_log, state_in, lead_in = refs[:5]
    xact, bmap, run_out, dt_out, cum_out, state_out, lead_out = refs[-11:-4]
    raw, xw, low, shifted = refs[-4:]
    steps = 2 * span + 2 * STATE_WIDTH

    gather_rows(recv, prev, first, raw, rows, steps, steps + heads, False)
    gather_rows(recv, prev, first, raw, rows, span, 2 * span + STATE_WIDTH)
    dt = softplus(raw[steps : steps + heads, LANES:] + bias[0])
    log_decay = -jnp.exp(a_log[0]) * dt
    lane = lax.broadcasted_iota(jnp.int32, (heads, BLOCK), 1)
    run = log_decay
    shift = 1
    while shift < BLOCK:
        run = run + jnp.where(lane >= shift, pltpu.roll(run, shift, 1), 0.0)
        shift *= 2
    final = run[:, BLOCK - 1 :]
    scale = jnp.exp(final - run) * dt
    cum = run + lead_in[0][:, :1]
    run_out[0] = run
    dt_out[0] = dt
    cum_out[0] = cum
    lead = jnp.broadcast_to(cum[:, BLOCK - 1 :], (heads, LANES))
    lead_out[0] = lead
    keep = jnp.broadcast_to(jnp.exp(final), (heads, LANES))

    shift_rows(raw, low, shifted, span)
    for r in range(0, STATE_WIDTH, HEAD_DIM):
        bmap[0, r : r + HEAD_DIM, :] = conv_tile(raw, shifted, w, span, span + r)
    for h in range(heads):
        r = h * HEAD_DIM
        tile = conv_tile(raw, shifted, w, span, r)
        xact[0, r : r + HEAD_DIM, :] = tile
        xw[r : r + HEAD_DIM, :] = (tile.astype(f32) * scale[h : h + 1, :]).astype(bf16)
    update = lax.dot_general(xw[...], bmap[0], NT, preferred_element_type=f32)
    for h in range(heads):
        r = h * HEAD_DIM
        new = update[r : r + HEAD_DIM, :]
        if not first:
            new = keep[h : h + 1, :] * state_in[0, r : r + HEAD_DIM, :] + new
        if last:
            at = (h % piece_heads) * HEAD_DIM
            state_out[h // piece_heads, at : at + HEAD_DIM, :] = new.astype(bf16)
        else:
            state_out[0, r : r + HEAD_DIM, :] = new
    if last:
        high, low = split(jnp.exp(lead))
        fill = jnp.zeros((8 - piece_heads, LANES), f32)
        for i in range(heads // piece_heads):
            mine = slice(i * piece_heads, (i + 1) * piece_heads)
            parts = [high[mine].astype(f32), fill, low[mine].astype(f32), fill]
            at = piece_heads * HEAD_DIM
            state_out[i, at : at + 16, :] = jnp.concatenate(parts, axis=0).astype(bf16)


def chunk_specs(got, chunk, dims, only=None):
    spg, rows = dims[:2]
    slabs = spg if only is None else 1

    def ahead(source, shape, row, lane):
        def index(g):
            return (g if only is None else g * spg + only, row, lane)

        return source, pl.BlockSpec((slabs,) + shape, index)

    def lane_of(block):
        first, middle, last = got
        ahead_of = first.shape[2] // BLOCK
        if block < ahead_of:
            return first, block
        return (middle if block == ahead_of else last), 0

    source, at = lane_of(chunk)
    block = pl.BlockSpec((spg, source.shape[1], BLOCK), lambda g: (g, 0, at))
    if chunk == 0:
        width = source.shape[2]
        prev, prev_spec = ahead(source, (16, width), rim_rows(rows, width)[0] // 16, 0)
    else:
        prev, place = lane_of(chunk - 1)
        lane = (place + 1) * (BLOCK // LANES) - 1
        prev, prev_spec = ahead(prev, (prev.shape[1], LANES), 0, lane)
    return [source, prev], [block, prev_spec]


def state_chunk(chunk, chunks, got, w, bias, a_log, state, lead, before, dims):
    spg, rows, heads, span, piece_heads = dims
    groups = w.shape[0]
    last = chunk == chunks - 1
    if last:
        packed = piece_heads * HEAD_DIM + 16
        state_shape = pltpu.HBM((groups * spg, packed, STATE_WIDTH), bf16)
        state_spec = pl.BlockSpec((spg, packed, STATE_WIDTH), lambda g: (g, 0, 0))
    else:
        state_shape = pltpu.HBM((groups, span, STATE_WIDTH), f32)
        state_spec = per_group(span, STATE_WIDTH)

    def out(dtype, *shape):
        return pltpu.HBM((groups,) + shape, dtype)

    args, specs = chunk_specs(got, chunk, dims)
    args[1:] = in_hbm(args[1])
    args[:1] = in_vmem(args[0]) if last else in_hbm(args[0])
    after = in_hbm(*before)
    return pl.pallas_call(
        functools.partial(state_kernel, dims, chunk == 0, last),
        grid=(groups,),
        in_specs=specs
        + [
            per_group(span + STATE_WIDTH, 4),
            per_group(heads, 1),
            per_group(heads, 1),
            per_group(span, STATE_WIDTH),
            per_group(heads, LANES),
        ]
        + [pl.BlockSpec(memory_space=pl.ANY)] * len(after),
        out_specs=[
            per_group(span, BLOCK),
            per_group(STATE_WIDTH, BLOCK),
            per_group(heads, BLOCK),
            per_group(heads, BLOCK),
            per_group(heads, BLOCK),
            state_spec,
            per_group(heads, LANES),
        ],
        out_shape=[
            out(bf16, span, BLOCK),
            out(bf16, STATE_WIDTH, BLOCK),
            out(f32, heads, BLOCK),
            out(f32, heads, BLOCK),
            out(f32, heads, BLOCK),
            state_shape,
            out(f32, heads, LANES),
        ],
        scratch_shapes=[
            pltpu.VMEM((rows * spg, LANES + BLOCK), f32),
            pltpu.VMEM((span, BLOCK), bf16),
            pltpu.VMEM((span + STATE_WIDTH, LANES + BLOCK), bf16),
            pltpu.VMEM((BLOCK // LANES, span + STATE_WIDTH, 3 * LANES), f32),
        ],
        compiler_params=params(48 if last else 60),
        cost_estimate=pl.CostEstimate(flops=4 * 10**9, bytes_accessed=10**7, transcendentals=10**6),
        name="state_chunk",
    )(*args, *in_hbm(w, bias, a_log, state, lead), *after)


def split(v):
    high = v.astype(bf16)
    return high, (v - high.astype(f32)).astype(bf16)


def block_kernel(dims, first, recv, *refs):
    spg, rows, heads, span, piece_heads = dims
    prev, refs = refs[0], refs[1:]
    w, xact, bmap, run_ref, dt_ref, cum_ref, state, skip = refs[:8]
    mixed, gate_out, side, token, raw, low, shifted = refs[-7:]
    at_c = 2 * span + STATE_WIDTH
    gather_rows(recv, prev, first, raw, rows, at_c, at_c + STATE_WIDTH, True, at_c // rows)
    gather_rows(recv, prev, first, raw, rows, 0, span, False)
    token[0] = cum_ref[0, :8, :LANES]
    shift_rows(raw, low, shifted, at_c)
    c = [conv_tile(raw, shifted, w, at_c, r) for r in range(0, STATE_WIDTH, HEAD_DIM)]
    c = jnp.concatenate(c, axis=0)
    b_rows = bmap[0].astype(f32).T.astype(bf16)
    scores = jnp.dot(b_rows, c, preferred_element_type=f32)
    src = lax.broadcasted_iota(jnp.int32, (HALF, HALF), 0)
    dst = lax.broadcasted_iota(jnp.int32, (HALF, HALF), 1)
    causal = src <= dst
    s00 = jnp.where(causal, scores[:HALF, :HALF], 0.0)
    s01 = scores[:HALF, HALF:]
    s11 = jnp.where(causal, scores[HALF:, HALF:], 0.0)
    r = run_ref[0] * LOG2E
    q = (r - jnp.log(dt_ref[0]) * LOG2E).T
    if not first:
        cc = jnp.concatenate([c, c], axis=0)
        entered = jnp.exp2(r)
    reach = [part.astype(f32) for part in split(jnp.exp(cum_ref[0]))]
    reach.append(jnp.zeros((STATE_WIDTH - 2 * heads, BLOCK), f32))
    side[0, :, :STATE_WIDTH] = c.astype(f32).T.astype(bf16)
    side[0, :, STATE_WIDTH:] = jnp.concatenate(reach, axis=0).T.astype(bf16)
    turned = []
    for h in range(heads):
        at = h * HEAD_DIM
        r0, r1 = r[h : h + 1, :HALF], r[h : h + 1, HALF:]
        q0, q1 = q[:HALF, h : h + 1], q[HALF:, h : h + 1]
        w00 = (s00 * jnp.exp2(jnp.minimum(r0 - q0, CAP))).astype(bf16)
        w01 = (s01 * jnp.exp2(r1 - q0)).astype(bf16)
        w11 = (s11 * jnp.exp2(jnp.minimum(r1 - q1, CAP))).astype(bf16)
        x = xact[0, at : at + HEAD_DIM, :]
        y0 = jnp.dot(x[:, :HALF], w00, preferred_element_type=f32)
        y1 = jnp.dot(x, jnp.concatenate([w01, w11], axis=0), preferred_element_type=f32)
        y = jnp.concatenate([y0, y1], axis=1) + skip[0, h : h + 1, :] * x.astype(f32)
        if not first:
            if at % WIDE == 0:
                both = jnp.concatenate(split(state[0, at : at + WIDE, :]), axis=1)
                carried = jnp.dot(both, cc, preferred_element_type=f32)
            y = y + entered[h : h + 1, :] * carried[at % WIDE : at % WIDE + HEAD_DIM, :]
        gate = raw[at : at + HEAD_DIM, LANES:]
        turned.append((y * silu(gate), gate))
        if len(turned) * HEAD_DIM == LANES:
            lanes = slice(at + HEAD_DIM - LANES, at + HEAD_DIM)
            mixed[0, :, lanes] = jnp.concatenate([pair[0] for pair in turned], axis=0).T
            wide = jnp.concatenate([pair[1] for pair in turned], axis=0).T
            gate_out[0, :, lanes] = wide.astype(bf16)
            turned = []


def block_chunk(
    chunk, chunks, got, w, xact, bmap, run, dt, cum, state, skip, after, dims
):
    spg, rows, heads, span, piece_heads = dims
    groups = w.shape[0]

    at_c = 2 * span + STATE_WIDTH
    one = at_c // rows
    assert (at_c + STATE_WIDTH - 1) // rows == one
    args, specs = chunk_specs(got, chunk, dims, one)
    args = in_hbm(*args)
    args += in_hbm(w, xact, bmap, run, dt, cum, state, skip)
    specs += [
        pl.BlockSpec((1, STATE_WIDTH, 4), lambda g: (g, span // STATE_WIDTH + 1, 0)),
        per_group(span, BLOCK),
        per_group(STATE_WIDTH, BLOCK),
        per_group(heads, BLOCK),
        per_group(heads, BLOCK),
        per_group(heads, BLOCK),
        per_group(span, STATE_WIDTH),
        per_group(heads, 1),
    ]
    args += in_vmem(*after)
    specs += [pl.BlockSpec(memory_space=pl.ANY)] * len(after)

    def out(dtype, *shape):
        return pltpu.HBM((groups,) + shape, dtype)

    return pl.pallas_call(
        functools.partial(block_kernel, dims, chunk == 0),
        grid=(groups,),
        in_specs=specs,
        out_specs=[
            per_group(BLOCK, span),
            per_group(BLOCK, span),
            per_group(BLOCK, 2 * STATE_WIDTH),
            per_group(8, LANES),
        ],
        out_shape=[
            out(f32, BLOCK, span),
            out(bf16, BLOCK, span),
            out(bf16, BLOCK, 2 * STATE_WIDTH),
            out(f32, 8, LANES),
        ],
        scratch_shapes=[
            pltpu.VMEM((rows * spg, LANES + BLOCK), f32),
            pltpu.VMEM((STATE_WIDTH, LANES + BLOCK), bf16),
            pltpu.VMEM((BLOCK // LANES, STATE_WIDTH, 3 * LANES), f32),
        ],
        compiler_params=params(),
        cost_estimate=pl.CostEstimate(flops=4 * 10**9, bytes_accessed=10**7, transcendentals=10**6),
        name="block_chunk",
    )(*args)


def relay_kernel(piece_heads, src, token, dst):
    rows = piece_heads * HEAD_DIM
    held = jnp.zeros((rows, STATE_WIDTH), f32)
    for d in range(src.shape[0]):
        dst[d] = held.T.astype(bf16)
        both = src[d, rows:, :].astype(f32)
        decay = both[:8] + both[8:]
        spread = [
            jnp.broadcast_to(decay[h : h + 1, :], (HEAD_DIM, STATE_WIDTH))
            for h in range(piece_heads)
        ]
        held = jnp.concatenate(spread, axis=0) * held + src[d, :rows, :].astype(f32)


def relay(packed, token, piece_heads):
    count = packed.shape[0]
    rows = piece_heads * HEAD_DIM
    return pl.pallas_call(
        functools.partial(relay_kernel, piece_heads),
        in_specs=[pl.BlockSpec(memory_space=pltpu.VMEM), pl.BlockSpec(memory_space=pl.ANY)],
        out_shape=pltpu.VMEM((count, STATE_WIDTH, rows), bf16),
        compiler_params=params(16),
        name="relay",
    )(packed, *in_hbm(token))


def final_kernel(chunks, groups, *refs):
    mixed, gates, sides = (refs[i * chunks : (i + 1) * chunks] for i in range(3))
    state, gain, out = refs[3 * chunks : 3 * chunks + 3]
    held, gate_held, side_held, kept, carried, done, sems, out_sems = refs[3 * chunks + 3 :]
    span = held.shape[2]
    piece = state.shape[2]
    spg = state.shape[0] // groups
    heads = span // HEAD_DIM
    steps = [(g, c) for g in range(groups) for c in range(chunks)]

    def loads(i):
        g, c = steps[i]
        slot = i
        moves = []
        moves.append((sides[c].at[g], side_held.at[slot]))
        moves.append((mixed[c].at[g], held.at[slot]))
        moves.append((gates[c].at[g], gate_held.at[slot]))
        return [
            pltpu.make_async_copy(a, b, sems.at[slot, j]) for j, (a, b) in enumerate(moves)
        ]

    def store(i):
        g, c = steps[i]
        return pltpu.make_async_copy(
            done.at[i % 2],
            out.at[c * BLOCK : (c + 1) * BLOCK, g * span : (g + 1) * span],
            out_sems.at[i % 2],
        )

    for i in range(len(steps)):
        for move in loads(i):
            move.start()
    row = lax.broadcasted_iota(jnp.int32, (STATE_WIDTH, span), 0)
    col = lax.broadcasted_iota(jnp.int32, (STATE_WIDTH, span), 1) // HEAD_DIM
    spread = jnp.where((row == col) | (row == col + heads), 1.0, 0.0).astype(bf16)
    for i, (g, c) in enumerate(steps):
        slot = i
        for move in loads(i):
            move.wait()
        if i >= 2:
            store(i - 2).wait()
        side = side_held[slot]
        reach = jnp.dot(side[:, STATE_WIDTH:], spread, preferred_element_type=f32)
        for j in range(spg):
            lanes = slice(j * piece, (j + 1) * piece)
            part = jnp.dot(
                side[:, :STATE_WIDTH], state[g * spg + j], preferred_element_type=f32
            )
            carried[:, lanes] = part * reach[:, lanes]
        for q in range(0, BLOCK, HEAD_DIM):
            rows = slice(q, q + HEAD_DIM)
            total = jnp.zeros((HEAD_DIM, LANES), f32)
            for at in range(0, span, LANES):
                lanes = slice(at, at + LANES)
                gate = silu(gate_held[slot, rows, lanes].astype(f32))
                v = held[slot, rows, lanes] + gate * carried[rows, lanes]
                kept[rows, lanes] = v
                total = total + v * v
            mean = jnp.sum(total, axis=1, keepdims=True) * (1.0 / span)
            factor = lax.rsqrt(mean + EPSILON)
            for at in range(0, span, LANES):
                lanes = slice(at, at + LANES)
                scaled = kept[rows, lanes] * factor * gain[g, :, lanes]
                done[i % 2, rows, lanes] = scaled.astype(bf16)
        store(i).start()
    for i in range(max(len(steps) - 2, 0), len(steps)):
        store(i).wait()


def finish(mixed, gates, sides, state, gain):
    chunks = len(mixed)
    groups, _, span = mixed[0].shape
    steps = groups * chunks
    anywhere = pl.BlockSpec(memory_space=pl.ANY)
    within = pl.BlockSpec(memory_space=pltpu.VMEM)
    return pl.pallas_call(
        functools.partial(final_kernel, chunks, groups),
        in_specs=[anywhere] * (3 * chunks) + [within] * 2,
        out_specs=anywhere,
        out_shape=jax.ShapeDtypeStruct((chunks * BLOCK, groups * span), bf16),
        scratch_shapes=[
            pltpu.VMEM((steps, BLOCK, span), f32),
            pltpu.VMEM((steps, BLOCK, span), bf16),
            pltpu.VMEM((steps, BLOCK, 2 * STATE_WIDTH), bf16),
            pltpu.VMEM((BLOCK, span), f32),
            pltpu.VMEM((BLOCK, span), f32),
            pltpu.VMEM((2, BLOCK, span), bf16),
            pltpu.SemaphoreType.DMA((steps, 3)),
            pltpu.SemaphoreType.DMA((2,)),
        ],
        compiler_params=params(40),
        name="finish",
    )(*in_hbm(*mixed, *gates, *sides), state, gain)


def swap(array, k):
    count = lax.axis_size("seq")
    return lax.ppermute(array, "seq", [(i, i ^ k) for i in range(count)])


def exchange(array):
    return lax.all_to_all(array, "seq", split_axis=0, concat_axis=0, tiled=True)


def per_device(projected, conv_weight, dt_bias, a_log, d_skip, norm_gain):
    seq_count = lax.axis_size("seq")
    groups = conv_weight.shape[1]
    heads = dt_bias.shape[0] // groups
    span = heads * HEAD_DIM
    rows, all_tokens = projected.shape
    local_tokens = all_tokens // seq_count
    chunks = local_tokens // BLOCK
    spg = seq_count // groups
    piece_heads = groups * heads // seq_count
    dims = (spg, rows, heads, span, piece_heads)

    w = jnp.transpose(conv_weight, (1, 2, 0))
    bias = dt_bias.reshape(groups, heads, 1)
    rate = a_log.reshape(groups, heads, 1)
    skip = d_skip.reshape(groups, heads, 1)
    gain = norm_gain.reshape(groups, 1, span)
    state = jnp.zeros((groups, span, STATE_WIDTH), f32)
    lead = jnp.zeros((groups, heads, LANES), f32)

    me = lax.axis_index("seq").astype(jnp.int32).reshape(1)
    assert chunks > 2 and seq_count & (seq_count - 1) == 0
    cut = cut_first(projected, seq_count, local_tokens - 2 * BLOCK)
    got = [exchange(cut)]
    own, near, *pairs = cut_pairs(projected, me, seq_count, local_tokens - 2 * BLOCK, [cut])
    near = swap(near, 1)
    pairs = [swap(pair, 2 * j + 2) for j, pair in enumerate(pairs)]
    ready = [own, w, bias, rate, skip, gain, state, lead]
    cut = cut_block(projected, seq_count, local_tokens - BLOCK, ready)
    got += [None, exchange(cut)]

    results, tokens = [], []
    for c in range(chunks):
        before = []
        if c == chunks - 2:
            passed = swap(forward(pairs, [lead, tokens[0]]), 1)
            got[1] = join(me, own, near, pairs, passed, tokens)
        if c == chunks - 1:
            before = tokens[-2:-1]
        xact, bmap, run, dt, cum, new, lead = state_chunk(
            c, chunks, got, w, bias, rate, state, lead, before, dims
        )
        after = []
        if c == chunks - 1:
            entering = relay(exchange(new), tokens[-1], piece_heads)
            after = [entering]
        *result, token = block_chunk(
            c, chunks, got, w, xact, bmap, run, dt, cum, state, skip, after, dims
        )
        results.append(result)
        tokens.append(token)
        state = new
    return finish(*zip(*results), exchange(entering), gain)


def solution(mesh):
    in_specs = (P(("tp", "seq"), None), P(None, "tp", None), P("tp"), P("tp"), P("tp"), P("tp"))
    return jax.shard_map(
        per_device, mesh=mesh, in_specs=in_specs, out_specs=P("seq", "tp"), check_vma=False
    )
```

```python
import functools

import jax
import jax.numpy as jnp
from jax import lax
from jax.experimental import pallas as pl
from jax.experimental.pallas import tpu as pltpu
from jax.sharding import PartitionSpec as P

HEAD_DIM = 64
STATE_WIDTH = 128
BLOCK = 256
LANES = 128
HALF = BLOCK // 2
WIDE = 256
LOG2E = 1.4426950408889634
CAP = 80.0
EPSILON = 1e-05

f32 = jnp.float32
bf16 = jnp.bfloat16
NT = (((1,), (1,)), ((), ()))


def params(mib=60):
    return pltpu.CompilerParams(vmem_limit_bytes=mib * 2**20)


def silu(v):
    half = 0.5 * v
    return half + half * jnp.tanh(half)


def softplus(v):
    e = jnp.exp(-jnp.abs(v))
    u = 1.0 + e
    gap = u - 1.0
    tiny = gap == 0.0
    log_part = jnp.where(tiny, e, jnp.log(u) * (e / jnp.where(tiny, 1.0, gap)))
    return jnp.maximum(v, 0.0) + log_part


def in_hbm(*arrays):
    return [pltpu.with_memory_space_constraint(array, pltpu.HBM) for array in arrays]


def in_vmem(*arrays):
    return [pltpu.with_memory_space_constraint(array, pltpu.VMEM) for array in arrays]


def per_group(*shape):
    return pl.BlockSpec((1,) + shape, lambda g: (g,) + (0,) * len(shape))


RIM = 4


def rim_rows(rows, width):
    base = rows // 16 * 16
    height = -(-(rows - base + RIM * -(-rows // width)) // 8) * 8
    assert height <= 16
    return base, height


def first_kernel(src, dst, held, windows, ends, in_sems, rim_sems, out_sems, end_sems):
    rows, all_tokens = src.shape
    count, _, width = dst.shape
    tokens = all_tokens // count
    base, height = rim_rows(rows, width)

    def fetch(d):
        at = d * tokens
        return pltpu.make_async_copy(src.at[:, at : at + width], held.at[d], in_sems.at[d])

    def window(d):
        at = d * tokens - LANES
        return pltpu.make_async_copy(src.at[:, at : at + LANES], windows.at[d], rim_sems.at[d])

    def place(d):
        return pltpu.make_async_copy(
            held.at[d, :base, :], dst.at[d, :base, :], out_sems.at[d]
        )

    def place_end(d):
        return pltpu.make_async_copy(
            ends.at[d], dst.at[d, base : base + height, :], end_sems.at[d]
        )

    for d in range(count):
        fetch(d).start()
        if d:
            window(d).start()
    row = lax.broadcasted_iota(jnp.int32, (height, LANES), 0) - (rows - base)
    col = lax.broadcasted_iota(jnp.int32, (height, LANES), 1)
    hit = (row >= 0) & (col == lax.rem(row + 16, RIM) + LANES - RIM)
    pick = jnp.where(hit, 1.0, 0.0).astype(bf16)
    which = lax.broadcasted_iota(jnp.int32, (height, width), 0) - (rows - base)
    for d in range(count):
        fetch(d).wait()
        place(d).start()
        end = held[d, base:rows, :].astype(f32)
        end = jnp.concatenate([end, jnp.zeros((height - end.shape[0], width), f32)], axis=0)
        if d:
            window(d).wait()
            rims = lax.dot_general(pick, windows[d], NT, preferred_element_type=f32)
            for j in range(-(-rows // width)):
                part = rims[:, j * width : min((j + 1) * width, rows)]
                if part.shape[1] < width:
                    fill = jnp.zeros((height, width - part.shape[1]), f32)
                    part = jnp.concatenate([part, fill], axis=1)
                end = jnp.where((which >= RIM * j) & (which < RIM * (j + 1)), part, end)
        ends[d] = end.astype(bf16)
        place_end(d).start()
    for d in range(count):
        place(d).wait()
        place_end(d).wait()


def cut_first(projected, count, width):
    rows = projected.shape[0]
    base, height = rim_rows(rows, width)
    sems = pltpu.SemaphoreType.DMA((count,))
    anywhere = pl.BlockSpec(memory_space=pl.ANY)
    return pl.pallas_call(
        first_kernel,
        in_specs=[anywhere],
        out_specs=anywhere,
        out_shape=pltpu.HBM((count, base + height, width), bf16),
        scratch_shapes=[
            pltpu.VMEM((count, rows, width), bf16),
            pltpu.VMEM((count, rows, LANES), bf16),
            pltpu.VMEM((count, height, width), bf16),
            sems,
            sems,
            sems,
            sems,
        ],
        compiler_params=params(),
        name="cut_first",
    )(*in_hbm(projected))


def staged(moves, held, in_sems, out_sems):
    for i, (source, _) in enumerate(moves):
        pltpu.make_async_copy(source, held.at[i], in_sems.at[i]).start()
    for i, (source, target) in enumerate(moves):
        pltpu.make_async_copy(source, held.at[i], in_sems.at[i]).wait()
        pltpu.make_async_copy(held.at[i], target, out_sems.at[i]).start()
    for i, (_, target) in enumerate(moves):
        pltpu.make_async_copy(held.at[i], target, out_sems.at[i]).wait()


def staging(count, rows, width):
    sems = pltpu.SemaphoreType.DMA((count,))
    return [pltpu.VMEM((count, rows, width), bf16), sems, sems]


def cut_kernel(low, count, src, *refs):
    dst = refs[-4]
    tokens = src.shape[1] // count
    moves = []
    for d in range(count):
        at = d * tokens + low
        moves.append((src.at[:, at : at + BLOCK], dst.at[d]))
    staged(moves, *refs[-3:])


def cut_block(projected, count, low, after):
    rows = projected.shape[0]
    args = in_hbm(projected, *after)
    anywhere = pl.BlockSpec(memory_space=pl.ANY)
    return pl.pallas_call(
        functools.partial(cut_kernel, low, count),
        in_specs=[anywhere] * len(args),
        out_specs=anywhere,
        out_shape=pltpu.HBM((count, rows, BLOCK), bf16),
        scratch_shapes=staging(count, rows, BLOCK),
        compiler_params=params(),
        name="cut_block",
    )(*args)


def pairs_kernel(low, count, me_ref, src, *refs):
    own, near, *far = refs[-(count // 2 + 4) : -3]
    tokens = src.shape[1] // count
    width = own.shape[1]
    me = me_ref[0]
    targets = [own, near]
    for pair in far:
        targets += [pair.at[:, :width], pair.at[:, width:]]
    moves = []
    for k, target in enumerate(targets):
        at = pl.multiple_of((me ^ k) * tokens + low, LANES)
        moves.append((src.at[:, pl.ds(at, width)], target))
    staged(moves[2:] + moves[:2], *refs[-3:])


def cut_pairs(projected, me, count, low, high, after):
    rows = projected.shape[0]
    anywhere = pl.BlockSpec(memory_space=pl.ANY)
    width = high - low
    one, two = pltpu.HBM((rows, width), bf16), pltpu.HBM((rows, 2 * width), bf16)
    return pl.pallas_call(
        functools.partial(pairs_kernel, low, count),
        in_specs=[pl.BlockSpec(memory_space=pltpu.SMEM)] + [anywhere] * (1 + len(after)),
        out_specs=[anywhere] * (count // 2 + 1),
        out_shape=[one, one] + [two] * (count // 2 - 1),
        scratch_shapes=staging(count, rows, width),
        compiler_params=params(),
        name="cut_pairs",
    )(me, *in_hbm(projected, *after))


def forward_kernel(count, *refs):
    dst = refs[-4]
    others = count // 2 - 1
    width = dst.shape[1] // others
    moves = [
        (refs[j].at[:, width:], dst.at[:, j * width : (j + 1) * width]) for j in range(others)
    ]
    staged(moves, *refs[-3:])


def forward(pairs, after):
    count = 2 * len(pairs) + 2
    rows, width = pairs[0].shape
    anywhere = pl.BlockSpec(memory_space=pl.ANY)
    return pl.pallas_call(
        functools.partial(forward_kernel, count),
        in_specs=[anywhere] * (len(pairs) + len(after)),
        out_specs=anywhere,
        out_shape=pltpu.HBM((rows, len(pairs) * width // 2), bf16),
        scratch_shapes=staging(len(pairs), rows, width // 2),
        compiler_params=params(),
        name="forward",
    )(*pairs, *in_hbm(*after))


def join_kernel(count, me_ref, own, near, *refs):
    others = count // 2 - 1
    pairs, passed, dst = refs[:others], refs[others], refs[-4]
    me = me_ref[0]
    width = own.shape[1]
    sources = [own, near]
    for j in range(others):
        sources += [pairs[j].at[:, :width], passed.at[:, j * width : (j + 1) * width]]
    staged([(source, dst.at[me ^ k]) for k, source in enumerate(sources)], *refs[-3:])


def join(me, own, near, pairs, passed, after):
    count = 2 * len(pairs) + 2
    rows, width = own.shape
    anywhere = pl.BlockSpec(memory_space=pl.ANY)
    args = [own, near, *pairs, passed, *in_hbm(*after)]
    return pl.pallas_call(
        functools.partial(join_kernel, count),
        in_specs=[pl.BlockSpec(memory_space=pltpu.SMEM)] + [anywhere] * len(args),
        out_specs=anywhere,
        out_shape=pltpu.HBM((count, rows, width), bf16),
        scratch_shapes=staging(count, rows, width),
        compiler_params=params(),
        name="join",
    )(me, *args)


def gather_rows(recv, prev, first, raw, rows, low, high, ahead=True, only=None):
    for s in range(recv.shape[0]):
        a = max(low - s * rows, 0) // 16 * 16
        b = min(-(-(high - s * rows) // 16) * 16, rows)
        if b <= a:
            continue
        at = s * rows + a
        raw[at : at + b - a, LANES:] = recv[s, a:b, :].astype(f32)
        if not ahead:
            continue
        if not first:
            raw[at : at + b - a, :LANES] = prev[s if only is None else 0, a:b, :].astype(f32)
            continue
        width = prev.shape[2]
        base, height = rim_rows(rows, width)
        rims = prev[s if only is None else 0, :height, :].astype(f32)
        tall = jnp.concatenate([jnp.zeros((LANES - height, width), f32), rims], axis=0)
        for j in range(-(-rows // width)):
            c, d = max(a, j * width), min(b, (j + 1) * width)
            if d <= c:
                continue
            shift = height - RIM - (rows - base) - RIM * j
            moved = (pltpu.roll(tall, shift, 0) if shift else tall).T
            raw[s * rows + c : s * rows + d, :LANES] = moved[c - j * width : d - j * width]


def band():
    row = lax.broadcasted_iota(jnp.int32, (2 * LANES, 3 * LANES), 0)
    col = lax.broadcasted_iota(jnp.int32, (2 * LANES, 3 * LANES), 1)
    tap = col // LANES
    return jnp.where(row == col - tap * LANES + LANES - 3 + tap, 1.0, 0.0).astype(bf16)


def shift_rows(raw, low, shifted, at):
    low[...] = raw[at : at + low.shape[0], :].astype(bf16)
    picks = band()
    for i in range(BLOCK // LANES):
        window = low[:, i * LANES : (i + 2) * LANES]
        shifted[i] = jnp.dot(window, picks, preferred_element_type=f32)


def conv_tile(raw, shifted, w, at, r):
    rows = slice(r, r + HEAD_DIM)
    taps = [jnp.broadcast_to(w[0, rows, k : k + 1], (HEAD_DIM, LANES)) for k in range(4)]
    parts = []
    for i in range(BLOCK // LANES):
        summed = None
        for k in range(3):
            part = taps[k] * shifted[i, rows, k * LANES : (k + 1) * LANES]
            summed = part if summed is None else summed + part
        own = raw[at + r : at + r + HEAD_DIM, (i + 1) * LANES : (i + 2) * LANES]
        parts.append(silu(summed + taps[3] * own).astype(bf16))
    return jnp.concatenate(parts, axis=1)


def state_kernel(dims, first, last, recv, *refs):
    spg, rows, heads, span, piece_heads = dims
    prev, refs = refs[0], refs[1:]
    w, bias, a_log, state_in, lead_in = refs[:5]
    xact, bmap, run_out, dt_out, cum_out, state_out, lead_out = refs[-11:-4]
    raw, xw, low, shifted = refs[-4:]
    steps = 2 * span + 2 * STATE_WIDTH

    gather_rows(recv, prev, first, raw, rows, steps, steps + heads, False)
    gather_rows(recv, prev, first, raw, rows, span, 2 * span + STATE_WIDTH)
    dt = softplus(raw[steps : steps + heads, LANES:] + bias[0])
    log_decay = -jnp.exp(a_log[0]) * dt
    lane = lax.broadcasted_iota(jnp.int32, (heads, BLOCK), 1)
    run = log_decay
    shift = 1
    while shift < BLOCK:
        run = run + jnp.where(lane >= shift, pltpu.roll(run, shift, 1), 0.0)
        shift *= 2
    final = run[:, BLOCK - 1 :]
    scale = jnp.exp(final - run) * dt
    cum = run + lead_in[0][:, :1]
    run_out[0] = run
    dt_out[0] = dt
    cum_out[0] = cum
    lead = jnp.broadcast_to(cum[:, BLOCK - 1 :], (heads, LANES))
    lead_out[0] = lead
    keep = jnp.broadcast_to(jnp.exp(final), (heads, LANES))

    shift_rows(raw, low, shifted, span)
    for r in range(0, STATE_WIDTH, HEAD_DIM):
        bmap[0, r : r + HEAD_DIM, :] = conv_tile(raw, shifted, w, span, span + r)
    for h in range(heads):
        r = h * HEAD_DIM
        tile = conv_tile(raw, shifted, w, span, r)
        xact[0, r : r + HEAD_DIM, :] = tile
        xw[r : r + HEAD_DIM, :] = (tile.astype(f32) * scale[h : h + 1, :]).astype(bf16)
    update = lax.dot_general(xw[...], bmap[0], NT, preferred_element_type=f32)
    for h in range(heads):
        r = h * HEAD_DIM
        new = update[r : r + HEAD_DIM, :]
        if not first:
            new = keep[h : h + 1, :] * state_in[0, r : r + HEAD_DIM, :] + new
        if last:
            at = (h % piece_heads) * HEAD_DIM
            state_out[h // piece_heads, at : at + HEAD_DIM, :] = new.astype(bf16)
        else:
            state_out[0, r : r + HEAD_DIM, :] = new
    if last:
        high, low = split(jnp.exp(lead))
        fill = jnp.zeros((8 - piece_heads, LANES), f32)
        for i in range(heads // piece_heads):
            mine = slice(i * piece_heads, (i + 1) * piece_heads)
            parts = [high[mine].astype(f32), fill, low[mine].astype(f32), fill]
            at = piece_heads * HEAD_DIM
            state_out[i, at : at + 16, :] = jnp.concatenate(parts, axis=0).astype(bf16)


def chunk_specs(got, chunk, dims, only=None):
    spg, rows = dims[:2]
    slabs = spg if only is None else 1

    def ahead(source, shape, row, lane):
        def index(g):
            return (g if only is None else g * spg + only, row, lane)

        return source, pl.BlockSpec((slabs,) + shape, index)

    def lane_of(block):
        for array in got:
            here = array.shape[2] // BLOCK
            if block < here:
                return array, block
            block -= here

    source, at = lane_of(chunk)
    block = pl.BlockSpec((spg, source.shape[1], BLOCK), lambda g: (g, 0, at))
    if chunk == 0:
        width = source.shape[2]
        prev, prev_spec = ahead(source, (16, width), rim_rows(rows, width)[0] // 16, 0)
    else:
        prev, place = lane_of(chunk - 1)
        lane = (place + 1) * (BLOCK // LANES) - 1
        prev, prev_spec = ahead(prev, (prev.shape[1], LANES), 0, lane)
    return [source, prev], [block, prev_spec]


def state_chunk(chunk, chunks, got, w, bias, a_log, state, lead, before, dims):
    spg, rows, heads, span, piece_heads = dims
    groups = w.shape[0]
    last = chunk == chunks - 1
    if last:
        packed = piece_heads * HEAD_DIM + 16
        state_shape = pltpu.HBM((groups * spg, packed, STATE_WIDTH), bf16)
        state_spec = pl.BlockSpec((spg, packed, STATE_WIDTH), lambda g: (g, 0, 0))
    else:
        state_shape = pltpu.HBM((groups, span, STATE_WIDTH), f32)
        state_spec = per_group(span, STATE_WIDTH)

    def out(dtype, *shape):
        return pltpu.HBM((groups,) + shape, dtype)

    args, specs = chunk_specs(got, chunk, dims)
    args[1:] = in_hbm(args[1])
    args[:1] = in_vmem(args[0]) if last else in_hbm(args[0])
    after = in_hbm(*before)
    return pl.pallas_call(
        functools.partial(state_kernel, dims, chunk == 0, last),
        grid=(groups,),
        in_specs=specs
        + [
            per_group(span + STATE_WIDTH, 4),
            per_group(heads, 1),
            per_group(heads, 1),
            per_group(span, STATE_WIDTH),
            per_group(heads, LANES),
        ]
        + [pl.BlockSpec(memory_space=pl.ANY)] * len(after),
        out_specs=[
            per_group(span, BLOCK),
            per_group(STATE_WIDTH, BLOCK),
            per_group(heads, BLOCK),
            per_group(heads, BLOCK),
            per_group(heads, BLOCK),
            state_spec,
            per_group(heads, LANES),
        ],
        out_shape=[
            out(bf16, span, BLOCK),
            out(bf16, STATE_WIDTH, BLOCK),
            out(f32, heads, BLOCK),
            out(f32, heads, BLOCK),
            out(f32, heads, BLOCK),
            state_shape,
            out(f32, heads, LANES),
        ],
        scratch_shapes=[
            pltpu.VMEM((rows * spg, LANES + BLOCK), f32),
            pltpu.VMEM((span, BLOCK), bf16),
            pltpu.VMEM((span + STATE_WIDTH, LANES + BLOCK), bf16),
            pltpu.VMEM((BLOCK // LANES, span + STATE_WIDTH, 3 * LANES), f32),
        ],
        compiler_params=params(48 if last else 60),
        cost_estimate=pl.CostEstimate(flops=4 * 10**9, bytes_accessed=10**7, transcendentals=10**6),
        name="state_chunk",
    )(*args, *in_hbm(w, bias, a_log, state, lead), *after)


def split(v):
    high = v.astype(bf16)
    return high, (v - high.astype(f32)).astype(bf16)


def block_kernel(dims, first, recv, *refs):
    spg, rows, heads, span, piece_heads = dims
    prev, refs = refs[0], refs[1:]
    w, xact, bmap, run_ref, dt_ref, cum_ref, state, skip = refs[:8]
    mixed, gate_out, side, token, raw, low, shifted = refs[-7:]
    at_c = 2 * span + STATE_WIDTH
    gather_rows(recv, prev, first, raw, rows, at_c, at_c + STATE_WIDTH, True, at_c // rows)
    gather_rows(recv, prev, first, raw, rows, 0, span, False)
    token[0] = cum_ref[0, :8, :LANES]
    shift_rows(raw, low, shifted, at_c)
    c = [conv_tile(raw, shifted, w, at_c, r) for r in range(0, STATE_WIDTH, HEAD_DIM)]
    c = jnp.concatenate(c, axis=0)
    b_rows = bmap[0].astype(f32).T.astype(bf16)
    scores = jnp.dot(b_rows, c, preferred_element_type=f32)
    src = lax.broadcasted_iota(jnp.int32, (HALF, HALF), 0)
    dst = lax.broadcasted_iota(jnp.int32, (HALF, HALF), 1)
    causal = src <= dst
    s00 = jnp.where(causal, scores[:HALF, :HALF], 0.0)
    s01 = scores[:HALF, HALF:]
    s11 = jnp.where(causal, scores[HALF:, HALF:], 0.0)
    r = run_ref[0] * LOG2E
    q = (r - jnp.log(dt_ref[0]) * LOG2E).T
    if not first:
        cc = jnp.concatenate([c, c], axis=0)
        entered = jnp.exp2(r)
    reach = [part.astype(f32) for part in split(jnp.exp(cum_ref[0]))]
    reach.append(jnp.zeros((STATE_WIDTH - 2 * heads, BLOCK), f32))
    side[0, :, :STATE_WIDTH] = c.astype(f32).T.astype(bf16)
    side[0, :, STATE_WIDTH:] = jnp.concatenate(reach, axis=0).T.astype(bf16)
    turned = []
    for h in range(heads):
        at = h * HEAD_DIM
        r0, r1 = r[h : h + 1, :HALF], r[h : h + 1, HALF:]
        q0, q1 = q[:HALF, h : h + 1], q[HALF:, h : h + 1]
        w00 = (s00 * jnp.exp2(jnp.minimum(r0 - q0, CAP))).astype(bf16)
        w01 = (s01 * jnp.exp2(r1 - q0)).astype(bf16)
        w11 = (s11 * jnp.exp2(jnp.minimum(r1 - q1, CAP))).astype(bf16)
        x = xact[0, at : at + HEAD_DIM, :]
        y0 = jnp.dot(x[:, :HALF], w00, preferred_element_type=f32)
        y1 = jnp.dot(x, jnp.concatenate([w01, w11], axis=0), preferred_element_type=f32)
        y = jnp.concatenate([y0, y1], axis=1) + skip[0, h : h + 1, :] * x.astype(f32)
        if not first:
            if at % WIDE == 0:
                both = jnp.concatenate(split(state[0, at : at + WIDE, :]), axis=1)
                carried = jnp.dot(both, cc, preferred_element_type=f32)
            y = y + entered[h : h + 1, :] * carried[at % WIDE : at % WIDE + HEAD_DIM, :]
        gate = raw[at : at + HEAD_DIM, LANES:]
        turned.append((y * silu(gate), gate))
        if len(turned) * HEAD_DIM == LANES:
            lanes = slice(at + HEAD_DIM - LANES, at + HEAD_DIM)
            mixed[0, :, lanes] = jnp.concatenate([pair[0] for pair in turned], axis=0).T
            wide = jnp.concatenate([pair[1] for pair in turned], axis=0).T
            gate_out[0, :, lanes] = wide.astype(bf16)
            turned = []


def block_chunk(
    chunk, chunks, got, w, xact, bmap, run, dt, cum, state, skip, after, dims
):
    spg, rows, heads, span, piece_heads = dims
    groups = w.shape[0]

    at_c = 2 * span + STATE_WIDTH
    one = at_c // rows
    assert (at_c + STATE_WIDTH - 1) // rows == one
    args, specs = chunk_specs(got, chunk, dims, one)
    args = in_hbm(*args)
    args += in_hbm(w, xact, bmap, run, dt, cum, state, skip)
    specs += [
        pl.BlockSpec((1, STATE_WIDTH, 4), lambda g: (g, span // STATE_WIDTH + 1, 0)),
        per_group(span, BLOCK),
        per_group(STATE_WIDTH, BLOCK),
        per_group(heads, BLOCK),
        per_group(heads, BLOCK),
        per_group(heads, BLOCK),
        per_group(span, STATE_WIDTH),
        per_group(heads, 1),
    ]
    args += in_vmem(*after)
    specs += [pl.BlockSpec(memory_space=pl.ANY)] * len(after)

    def out(dtype, *shape):
        return pltpu.HBM((groups,) + shape, dtype)

    return pl.pallas_call(
        functools.partial(block_kernel, dims, chunk == 0),
        grid=(groups,),
        in_specs=specs,
        out_specs=[
            per_group(BLOCK, span),
            per_group(BLOCK, span),
            per_group(BLOCK, 2 * STATE_WIDTH),
            per_group(8, LANES),
        ],
        out_shape=[
            out(f32, BLOCK, span),
            out(bf16, BLOCK, span),
            out(bf16, BLOCK, 2 * STATE_WIDTH),
            out(f32, 8, LANES),
        ],
        scratch_shapes=[
            pltpu.VMEM((rows * spg, LANES + BLOCK), f32),
            pltpu.VMEM((STATE_WIDTH, LANES + BLOCK), bf16),
            pltpu.VMEM((BLOCK // LANES, STATE_WIDTH, 3 * LANES), f32),
        ],
        compiler_params=params(),
        cost_estimate=pl.CostEstimate(flops=4 * 10**9, bytes_accessed=10**7, transcendentals=10**6),
        name="block_chunk",
    )(*args)


def relay_kernel(piece_heads, src, token, dst):
    rows = piece_heads * HEAD_DIM
    held = jnp.zeros((rows, STATE_WIDTH), f32)
    for d in range(src.shape[0]):
        dst[d] = held.T.astype(bf16)
        both = src[d, rows:, :].astype(f32)
        decay = both[:8] + both[8:]
        spread = [
            jnp.broadcast_to(decay[h : h + 1, :], (HEAD_DIM, STATE_WIDTH))
            for h in range(piece_heads)
        ]
        held = jnp.concatenate(spread, axis=0) * held + src[d, :rows, :].astype(f32)


def relay(packed, token, piece_heads):
    count = packed.shape[0]
    rows = piece_heads * HEAD_DIM
    return pl.pallas_call(
        functools.partial(relay_kernel, piece_heads),
        in_specs=[pl.BlockSpec(memory_space=pltpu.VMEM), pl.BlockSpec(memory_space=pl.ANY)],
        out_shape=pltpu.VMEM((count, STATE_WIDTH, rows), bf16),
        compiler_params=params(16),
        name="relay",
    )(packed, *in_hbm(token))


def final_kernel(chunks, groups, *refs):
    mixed, gates, sides = (refs[i * chunks : (i + 1) * chunks] for i in range(3))
    state, gain, out = refs[3 * chunks : 3 * chunks + 3]
    held, gate_held, side_held, kept, carried, done, sems, out_sems = refs[3 * chunks + 3 :]
    span = held.shape[2]
    piece = state.shape[2]
    spg = state.shape[0] // groups
    heads = span // HEAD_DIM
    steps = [(g, c) for g in range(groups) for c in range(chunks)]

    def loads(i):
        g, c = steps[i]
        slot = i
        moves = []
        moves.append((sides[c].at[g], side_held.at[slot]))
        moves.append((mixed[c].at[g], held.at[slot]))
        moves.append((gates[c].at[g], gate_held.at[slot]))
        return [
            pltpu.make_async_copy(a, b, sems.at[slot, j]) for j, (a, b) in enumerate(moves)
        ]

    def store(i):
        g, c = steps[i]
        return pltpu.make_async_copy(
            done.at[i % 2],
            out.at[c * BLOCK : (c + 1) * BLOCK, g * span : (g + 1) * span],
            out_sems.at[i % 2],
        )

    for i in range(len(steps)):
        for move in loads(i):
            move.start()
    row = lax.broadcasted_iota(jnp.int32, (STATE_WIDTH, span), 0)
    col = lax.broadcasted_iota(jnp.int32, (STATE_WIDTH, span), 1) // HEAD_DIM
    spread = jnp.where((row == col) | (row == col + heads), 1.0, 0.0).astype(bf16)
    for i, (g, c) in enumerate(steps):
        slot = i
        for move in loads(i):
            move.wait()
        if i >= 2:
            store(i - 2).wait()
        side = side_held[slot]
        reach = jnp.dot(side[:, STATE_WIDTH:], spread, preferred_element_type=f32)
        for j in range(spg):
            lanes = slice(j * piece, (j + 1) * piece)
            part = jnp.dot(
                side[:, :STATE_WIDTH], state[g * spg + j], preferred_element_type=f32
            )
            carried[:, lanes] = part * reach[:, lanes]
        for q in range(0, BLOCK, HEAD_DIM):
            rows = slice(q, q + HEAD_DIM)
            total = jnp.zeros((HEAD_DIM, LANES), f32)
            for at in range(0, span, LANES):
                lanes = slice(at, at + LANES)
                gate = silu(gate_held[slot, rows, lanes].astype(f32))
                v = held[slot, rows, lanes] + gate * carried[rows, lanes]
                kept[rows, lanes] = v
                total = total + v * v
            mean = jnp.sum(total, axis=1, keepdims=True) * (1.0 / span)
            factor = lax.rsqrt(mean + EPSILON)
            for at in range(0, span, LANES):
                lanes = slice(at, at + LANES)
                scaled = kept[rows, lanes] * factor * gain[g, :, lanes]
                done[i % 2, rows, lanes] = scaled.astype(bf16)
        store(i).start()
    for i in range(max(len(steps) - 2, 0), len(steps)):
        store(i).wait()


def finish(mixed, gates, sides, state, gain):
    chunks = len(mixed)
    groups, _, span = mixed[0].shape
    steps = groups * chunks
    anywhere = pl.BlockSpec(memory_space=pl.ANY)
    within = pl.BlockSpec(memory_space=pltpu.VMEM)
    return pl.pallas_call(
        functools.partial(final_kernel, chunks, groups),
        in_specs=[anywhere] * (3 * chunks) + [within] * 2,
        out_specs=anywhere,
        out_shape=jax.ShapeDtypeStruct((chunks * BLOCK, groups * span), bf16),
        scratch_shapes=[
            pltpu.VMEM((steps, BLOCK, span), f32),
            pltpu.VMEM((steps, BLOCK, span), bf16),
            pltpu.VMEM((steps, BLOCK, 2 * STATE_WIDTH), bf16),
            pltpu.VMEM((BLOCK, span), f32),
            pltpu.VMEM((BLOCK, span), f32),
            pltpu.VMEM((2, BLOCK, span), bf16),
            pltpu.SemaphoreType.DMA((steps, 3)),
            pltpu.SemaphoreType.DMA((2,)),
        ],
        compiler_params=params(40),
        name="finish",
    )(*in_hbm(*mixed, *gates, *sides), state, gain)


def swap(array, k):
    count = lax.axis_size("seq")
    return lax.ppermute(array, "seq", [(i, i ^ k) for i in range(count)])


def exchange(array):
    return lax.all_to_all(array, "seq", split_axis=0, concat_axis=0, tiled=True)


def per_device(projected, conv_weight, dt_bias, a_log, d_skip, norm_gain):
    seq_count = lax.axis_size("seq")
    groups = conv_weight.shape[1]
    heads = dt_bias.shape[0] // groups
    span = heads * HEAD_DIM
    rows, all_tokens = projected.shape
    local_tokens = all_tokens // seq_count
    chunks = local_tokens // BLOCK
    spg = seq_count // groups
    piece_heads = groups * heads // seq_count
    dims = (spg, rows, heads, span, piece_heads)

    w = jnp.transpose(conv_weight, (1, 2, 0))
    bias = dt_bias.reshape(groups, heads, 1)
    rate = a_log.reshape(groups, heads, 1)
    skip = d_skip.reshape(groups, heads, 1)
    gain = norm_gain.reshape(groups, 1, span)
    state = jnp.zeros((groups, span, STATE_WIDTH), f32)
    lead = jnp.zeros((groups, heads, LANES), f32)

    me = lax.axis_index("seq").astype(jnp.int32).reshape(1)
    assert chunks > 2 and seq_count & (seq_count - 1) == 0
    split_at = local_tokens - BLOCK
    cut = cut_first(projected, seq_count, BLOCK)
    got = [exchange(cut)]
    own, near, *pairs = cut_pairs(projected, me, seq_count, BLOCK, split_at, [cut])
    near = swap(near, 1)
    pairs = [swap(pair, 2 * j + 2) for j, pair in enumerate(pairs)]
    ready = [own, w, bias, rate, skip, gain, state, lead]
    cut = cut_block(projected, seq_count, split_at, ready)
    got += [None, exchange(cut)]

    results, tokens = [], []
    for c in range(chunks):
        before = []
        if c == 1:
            passed = swap(forward(pairs, [lead]), 1)
            got[1] = join(me, own, near, pairs, passed, tokens)
        if c == chunks - 1:
            before = tokens[-2:-1]
        xact, bmap, run, dt, cum, new, lead = state_chunk(
            c, chunks, got, w, bias, rate, state, lead, before, dims
        )
        after = []
        if c == chunks - 1:
            entering = relay(exchange(new), tokens[-1], piece_heads)
            after = [entering]
        *result, token = block_chunk(
            c, chunks, got, w, xact, bmap, run, dt, cum, state, skip, after, dims
        )
        results.append(result)
        tokens.append(token)
        state = new
    return finish(*zip(*results), exchange(entering), gain)


def solution(mesh):
    in_specs = (P(("tp", "seq"), None), P(None, "tp", None), P("tp"), P("tp"), P("tp"), P("tp"))
    return jax.shard_map(
        per_device, mesh=mesh, in_specs=in_specs, out_specs=P("seq", "tp"), check_vma=False
    )
```

```python
import functools

import jax
import jax.numpy as jnp
from jax import lax
from jax.experimental import pallas as pl
from jax.experimental.pallas import tpu as pltpu
from jax.sharding import PartitionSpec as P

HEAD_DIM = 64
STATE_WIDTH = 128
BLOCK = 256
LANES = 128
HALF = BLOCK // 2
WIDE = 256
LOG2E = 1.4426950408889634
CAP = 80.0
EPSILON = 1e-05

f32 = jnp.float32
bf16 = jnp.bfloat16
NT = (((1,), (1,)), ((), ()))


def params(mib=60):
    return pltpu.CompilerParams(vmem_limit_bytes=mib * 2**20)


def silu(v):
    half = 0.5 * v
    return half + half * jnp.tanh(half)


def softplus(v):
    e = jnp.exp(-jnp.abs(v))
    u = 1.0 + e
    gap = u - 1.0
    tiny = gap == 0.0
    log_part = jnp.where(tiny, e, jnp.log(u) * (e / jnp.where(tiny, 1.0, gap)))
    return jnp.maximum(v, 0.0) + log_part


def in_hbm(*arrays):
    return [pltpu.with_memory_space_constraint(array, pltpu.HBM) for array in arrays]


def in_vmem(*arrays):
    return [pltpu.with_memory_space_constraint(array, pltpu.VMEM) for array in arrays]


def per_group(*shape):
    return pl.BlockSpec((1,) + shape, lambda g: (g,) + (0,) * len(shape))


RIM = 4


def rim_rows(rows, width):
    base = rows // 16 * 16
    height = -(-(rows - base + RIM * -(-rows // width)) // 8) * 8
    assert height <= 16
    return base, height


def first_kernel(src, dst, held, windows, ends, in_sems, rim_sems, out_sems, end_sems):
    rows, all_tokens = src.shape
    count, _, width = dst.shape
    tokens = all_tokens // count
    base, height = rim_rows(rows, width)

    def fetch(d):
        at = d * tokens
        return pltpu.make_async_copy(src.at[:, at : at + width], held.at[d], in_sems.at[d])

    def window(d):
        at = d * tokens - LANES
        return pltpu.make_async_copy(src.at[:, at : at + LANES], windows.at[d], rim_sems.at[d])

    def place(d):
        return pltpu.make_async_copy(
            held.at[d, :base, :], dst.at[d, :base, :], out_sems.at[d]
        )

    def place_end(d):
        return pltpu.make_async_copy(
            ends.at[d], dst.at[d, base : base + height, :], end_sems.at[d]
        )

    for d in range(count):
        fetch(d).start()
        if d:
            window(d).start()
    row = lax.broadcasted_iota(jnp.int32, (height, LANES), 0) - (rows - base)
    col = lax.broadcasted_iota(jnp.int32, (height, LANES), 1)
    hit = (row >= 0) & (col == lax.rem(row + 16, RIM) + LANES - RIM)
    pick = jnp.where(hit, 1.0, 0.0).astype(bf16)
    which = lax.broadcasted_iota(jnp.int32, (height, width), 0) - (rows - base)
    for d in range(count):
        fetch(d).wait()
        place(d).start()
        end = held[d, base:rows, :].astype(f32)
        end = jnp.concatenate([end, jnp.zeros((height - end.shape[0], width), f32)], axis=0)
        if d:
            window(d).wait()
            rims = lax.dot_general(pick, windows[d], NT, preferred_element_type=f32)
            for j in range(-(-rows // width)):
                part = rims[:, j * width : min((j + 1) * width, rows)]
                if part.shape[1] < width:
                    fill = jnp.zeros((height, width - part.shape[1]), f32)
                    part = jnp.concatenate([part, fill], axis=1)
                end = jnp.where((which >= RIM * j) & (which < RIM * (j + 1)), part, end)
        ends[d] = end.astype(bf16)
        place_end(d).start()
    for d in range(count):
        place(d).wait()
        place_end(d).wait()


def cut_first(projected, count, width):
    rows = projected.shape[0]
    base, height = rim_rows(rows, width)
    sems = pltpu.SemaphoreType.DMA((count,))
    anywhere = pl.BlockSpec(memory_space=pl.ANY)
    return pl.pallas_call(
        first_kernel,
        in_specs=[anywhere],
        out_specs=anywhere,
        out_shape=pltpu.HBM((count, base + height, width), bf16),
        scratch_shapes=[
            pltpu.VMEM((count, rows, width), bf16),
            pltpu.VMEM((count, rows, LANES), bf16),
            pltpu.VMEM((count, height, width), bf16),
            sems,
            sems,
            sems,
            sems,
        ],
        compiler_params=params(),
        name="cut_first",
    )(*in_hbm(projected))


def staged(moves, held, in_sems, out_sems):
    for i, (source, _) in enumerate(moves):
        pltpu.make_async_copy(source, held.at[i], in_sems.at[i]).start()
    for i, (source, target) in enumerate(moves):
        pltpu.make_async_copy(source, held.at[i], in_sems.at[i]).wait()
        pltpu.make_async_copy(held.at[i], target, out_sems.at[i]).start()
    for i, (_, target) in enumerate(moves):
        pltpu.make_async_copy(held.at[i], target, out_sems.at[i]).wait()


def staging(count, rows):
    sems = pltpu.SemaphoreType.DMA((count,))
    return [pltpu.VMEM((count, rows, BLOCK), bf16), sems, sems]


def cut_kernel(low, count, src, *refs):
    dst = refs[-4]
    tokens = src.shape[1] // count
    moves = []
    for d in range(count):
        at = d * tokens + low
        moves.append((src.at[:, at : at + BLOCK], dst.at[d]))
    staged(moves, *refs[-3:])


def cut_block(projected, count, low, after):
    rows = projected.shape[0]
    args = in_hbm(projected, *after)
    anywhere = pl.BlockSpec(memory_space=pl.ANY)
    return pl.pallas_call(
        functools.partial(cut_kernel, low, count),
        in_specs=[anywhere] * len(args),
        out_specs=anywhere,
        out_shape=pltpu.HBM((count, rows, BLOCK), bf16),
        scratch_shapes=staging(count, rows),
        compiler_params=params(),
        name="cut_block",
    )(*args)


def pairs_kernel(low, count, me_ref, src, *refs):
    own, near, *far = refs[-(count // 2 + 4) : -3]
    tokens = src.shape[1] // count
    me = me_ref[0]
    targets = [own, near]
    for pair in far:
        targets += [pair.at[:, :BLOCK], pair.at[:, BLOCK:]]
    moves = []
    for k, target in enumerate(targets):
        at = pl.multiple_of((me ^ k) * tokens + low, LANES)
        moves.append((src.at[:, pl.ds(at, BLOCK)], target))
    staged(moves[2:] + moves[:2], *refs[-3:])


def cut_pairs(projected, me, count, low, after):
    rows = projected.shape[0]
    anywhere = pl.BlockSpec(memory_space=pl.ANY)
    one, two = pltpu.HBM((rows, BLOCK), bf16), pltpu.HBM((rows, 2 * BLOCK), bf16)
    return pl.pallas_call(
        functools.partial(pairs_kernel, low, count),
        in_specs=[pl.BlockSpec(memory_space=pltpu.SMEM)] + [anywhere] * (1 + len(after)),
        out_specs=[anywhere] * (count // 2 + 1),
        out_shape=[one, one] + [two] * (count // 2 - 1),
        scratch_shapes=staging(count, rows),
        compiler_params=params(),
        name="cut_pairs",
    )(me, *in_hbm(projected, *after))


def forward_kernel(count, *refs):
    dst = refs[-4]
    moves = [
        (refs[j].at[:, BLOCK:], dst.at[:, j * BLOCK : (j + 1) * BLOCK])
        for j in range(count // 2 - 1)
    ]
    staged(moves, *refs[-3:])


def forward(pairs, after):
    count = 2 * len(pairs) + 2
    rows = pairs[0].shape[0]
    anywhere = pl.BlockSpec(memory_space=pl.ANY)
    return pl.pallas_call(
        functools.partial(forward_kernel, count),
        in_specs=[anywhere] * (len(pairs) + len(after)),
        out_specs=anywhere,
        out_shape=pltpu.HBM((rows, len(pairs) * BLOCK), bf16),
        scratch_shapes=staging(len(pairs), rows),
        compiler_params=params(),
        name="forward",
    )(*pairs, *in_hbm(*after))


def join_kernel(count, me_ref, own, near, *refs):
    others = count // 2 - 1
    pairs, passed, dst = refs[:others], refs[others], refs[-4]
    me = me_ref[0]
    sources = [own, near]
    for j in range(others):
        sources += [pairs[j].at[:, :BLOCK], passed.at[:, j * BLOCK : (j + 1) * BLOCK]]
    staged([(source, dst.at[me ^ k]) for k, source in enumerate(sources)], *refs[-3:])


def join(me, own, near, pairs, passed, after):
    count = 2 * len(pairs) + 2
    rows = own.shape[0]
    anywhere = pl.BlockSpec(memory_space=pl.ANY)
    args = [own, near, *pairs, passed, *in_hbm(*after)]
    return pl.pallas_call(
        functools.partial(join_kernel, count),
        in_specs=[pl.BlockSpec(memory_space=pltpu.SMEM)] + [anywhere] * len(args),
        out_specs=anywhere,
        out_shape=pltpu.HBM((count, rows, BLOCK), bf16),
        scratch_shapes=staging(count, rows),
        compiler_params=params(),
        name="join",
    )(me, *args)


def gather_rows(take, ahead, first, raw, rows, low, high, with_ahead=True):
    for s in range(raw.shape[0] // rows):
        a = max(low - s * rows, 0) // 16 * 16
        b = min(-(-(high - s * rows) // 16) * 16, rows)
        if b <= a:
            continue
        at = s * rows + a
        raw[at : at + b - a, LANES:] = take(s)[a:b, :].astype(f32)
        if not with_ahead:
            continue
        prev = ahead(s)
        if not first:
            raw[at : at + b - a, :LANES] = prev[a:b, :].astype(f32)
            continue
        width = prev.shape[1]
        base, height = rim_rows(rows, width)
        rims = prev[:height, :].astype(f32)
        tall = jnp.concatenate([jnp.zeros((LANES - height, width), f32), rims], axis=0)
        for j in range(-(-rows // width)):
            c, d = max(a, j * width), min(b, (j + 1) * width)
            if d <= c:
                continue
            shift = height - RIM - (rows - base) - RIM * j
            moved = (pltpu.roll(tall, shift, 0) if shift else tall).T
            raw[s * rows + c : s * rows + d, :LANES] = moved[c - j * width : d - j * width]


def band():
    row = lax.broadcasted_iota(jnp.int32, (2 * LANES, 3 * LANES), 0)
    col = lax.broadcasted_iota(jnp.int32, (2 * LANES, 3 * LANES), 1)
    tap = col // LANES
    return jnp.where(row == col - tap * LANES + LANES - 3 + tap, 1.0, 0.0).astype(bf16)


def shift_rows(raw, low, shifted, at, picks):
    low[...] = raw[at : at + low.shape[0], :].astype(bf16)
    for i in range(BLOCK // LANES):
        window = low[:, i * LANES : (i + 2) * LANES]
        shifted[i] = jnp.dot(window, picks, preferred_element_type=f32)


def conv_tile(raw, shifted, w, at, r, known):
    rows = slice(r, r + HEAD_DIM)
    wide = r // LANES * LANES
    if wide not in known:
        fill = jnp.zeros((LANES - 8, LANES), f32)
        known[wide] = jnp.concatenate([w[:, wide : wide + LANES], fill], axis=0).T
    turned = known[wide][r - wide : r - wide + HEAD_DIM]
    taps = [jnp.broadcast_to(turned[:, k : k + 1], (HEAD_DIM, LANES)) for k in range(4)]
    parts = []
    for i in range(BLOCK // LANES):
        summed = None
        for k in range(3):
            part = taps[k] * shifted[i, rows, k * LANES : (k + 1) * LANES]
            summed = part if summed is None else summed + part
        own = raw[at + r : at + r + HEAD_DIM, (i + 1) * LANES : (i + 2) * LANES]
        parts.append(silu(summed + taps[3] * own).astype(bf16))
    return jnp.concatenate(parts, axis=1)


def state_kernel(dims, first, last, places, recv, prev, state_in, *refs):
    spg, rows, heads, span, piece_heads = dims
    w, bias, a_log, lead_in = refs[:4]
    xact, bmap, run_out, dt_out, cum_out, state_out, lead_out = refs[-20:-13]
    raw, xw, low, shifted, slabs, heads_of, held, values, news = refs[-13:-4]
    slab_sems, ahead_sems, state_sems, out_sems = refs[-4:]
    steps = 2 * span + 2 * STATE_WIDTH
    groups = w.shape[0]
    skipped = span // rows

    def load_slab(g, s):
        at = places[0] * BLOCK
        source = recv.at[g * spg + s, :, at : at + BLOCK]
        return pltpu.make_async_copy(source, slabs.at[g, s - skipped], slab_sems.at[g, s - skipped])

    def load_ahead(g, s):
        if first:
            width = recv.shape[2]
            base, height = rim_rows(rows, width)
            source = prev.at[g * spg + s, base : base + height, :]
        else:
            at = places[1] * LANES
            source = prev.at[g * spg + s, :, at : at + LANES]
        return pltpu.make_async_copy(
            source, heads_of.at[g, s - skipped], ahead_sems.at[g, s - skipped]
        )

    def load_state(g):
        return pltpu.make_async_copy(state_in.at[g], held.at[g], state_sems.at[g])

    def leave(g, i):
        if i == 0:
            return pltpu.make_async_copy(values.at[g], xact.at[g], out_sems.at[g, 0])
        target = state_out.at[g * spg : (g + 1) * spg] if last else state_out.at[g]
        return pltpu.make_async_copy(news.at[g], target, out_sems.at[g, 1])

    for g in range(groups):
        for s in range(skipped, spg):
            load_slab(g, s).start()
            load_ahead(g, s).start()
        if not first:
            load_state(g).start()
    picked = band()
    for g in range(groups):

        def take(s):
            return slabs.at[g, s - skipped]

        def ahead(s):
            return heads_of.at[g, s - skipped]

        for s in range(skipped, spg):
            load_slab(g, s).wait()
            load_ahead(g, s).wait()
        gather_rows(take, ahead, first, raw, rows, steps, steps + heads, False)
        gather_rows(take, ahead, first, raw, rows, span, 2 * span + STATE_WIDTH)
        dt = softplus(raw[steps : steps + heads, LANES:] + bias[g])
        log_decay = -jnp.exp(a_log[g]) * dt
        lane = lax.broadcasted_iota(jnp.int32, (heads, BLOCK), 1)
        run = log_decay
        shift = 1
        while shift < BLOCK:
            run = run + jnp.where(lane >= shift, pltpu.roll(run, shift, 1), 0.0)
            shift *= 2
        final = run[:, BLOCK - 1 :]
        scale = jnp.exp(final - run) * dt
        cum = run + lead_in[g][:, :1]
        run_out[g] = run
        dt_out[g] = dt
        cum_out[g] = cum
        lead = jnp.broadcast_to(cum[:, BLOCK - 1 :], (heads, LANES))
        lead_out[g] = lead
        keep = jnp.broadcast_to(jnp.exp(final), (heads, LANES))

        shift_rows(raw, low, shifted, span, picked)
        known = {}
        for r in range(0, STATE_WIDTH, HEAD_DIM):
            bmap[g, r : r + HEAD_DIM, :] = conv_tile(raw, shifted, w[g], span, span + r, known)
        for h in range(heads):
            r = h * HEAD_DIM
            tile = conv_tile(raw, shifted, w[g], span, r, known)
            values[g, r : r + HEAD_DIM, :] = tile
            xw[r : r + HEAD_DIM, :] = (tile.astype(f32) * scale[h : h + 1, :]).astype(bf16)
        leave(g, 0).start()
        update = lax.dot_general(xw[...], bmap[g], NT, preferred_element_type=f32)
        if not first:
            load_state(g).wait()
        for h in range(heads):
            r = h * HEAD_DIM
            new = update[r : r + HEAD_DIM, :]
            if not first:
                new = keep[h : h + 1, :] * held[g, r : r + HEAD_DIM, :] + new
            if last:
                at = (h % piece_heads) * HEAD_DIM
                news[g, h // piece_heads, at : at + HEAD_DIM, :] = new.astype(bf16)
            else:
                news[g, r : r + HEAD_DIM, :] = new
        if last:
            high, low_part = split(jnp.exp(lead))
            fill = jnp.zeros((8 - piece_heads, LANES), f32)
            for i in range(heads // piece_heads):
                mine = slice(i * piece_heads, (i + 1) * piece_heads)
                parts = [high[mine].astype(f32), fill, low_part[mine].astype(f32), fill]
                at = piece_heads * HEAD_DIM
                news[g, i, at : at + 16, :] = jnp.concatenate(parts, axis=0).astype(bf16)
        leave(g, 1).start()
    for g in range(groups):
        leave(g, 0).wait()
        leave(g, 1).wait()


def lane_of(got, block):
    for array in got:
        here = array.shape[2] // BLOCK
        if block < here:
            return array, block
        block -= here


def sources(got, chunk):
    source, at = lane_of(got, chunk)
    if chunk == 0:
        return source, source, (at, 0)
    prev, place = lane_of(got, chunk - 1)
    return source, prev, (at, (place + 1) * (BLOCK // LANES) - 1)


def state_chunk(chunk, chunks, got, w, bias, a_log, state, lead, before, dims):
    spg, rows, heads, span, piece_heads = dims
    groups = w.shape[0]
    first, last = chunk == 0, chunk == chunks - 1
    if last:
        packed = (spg, piece_heads * HEAD_DIM + 16, STATE_WIDTH)
        state_shape = pltpu.HBM((groups * spg,) + packed[1:], bf16)
        news = pltpu.VMEM((groups,) + packed, bf16)
    else:
        state_shape = pltpu.HBM((groups, span, STATE_WIDTH), f32)
        news = pltpu.VMEM((groups, span, STATE_WIDTH), f32)

    def out(dtype, *shape):
        return pltpu.HBM((groups,) + shape, dtype)

    source, prev, places = sources(got, chunk)
    needed = spg - span // rows
    if first:
        ahead = (rim_rows(rows, source.shape[2])[1], source.shape[2])
    else:
        ahead = (prev.shape[1], LANES)
    args = (in_vmem if last else in_hbm)(source) + in_hbm(prev, state)
    anywhere = pl.BlockSpec(memory_space=pl.ANY)
    within = pl.BlockSpec(memory_space=pltpu.VMEM)
    conv_rows = span + STATE_WIDTH
    return pl.pallas_call(
        functools.partial(state_kernel, dims, first, last, places),
        in_specs=[anywhere] * 3 + [within] * 4 + [anywhere] * len(before),
        out_specs=[anywhere] + [within] * 4 + [anywhere, within],
        out_shape=[
            out(bf16, span, BLOCK),
            out(bf16, STATE_WIDTH, BLOCK),
            out(f32, heads, BLOCK),
            out(f32, heads, BLOCK),
            out(f32, heads, BLOCK),
            state_shape,
            out(f32, heads, LANES),
        ],
        scratch_shapes=[
            pltpu.VMEM((rows * spg, LANES + BLOCK), f32),
            pltpu.VMEM((span, BLOCK), bf16),
            pltpu.VMEM((conv_rows, LANES + BLOCK), bf16),
            pltpu.VMEM((BLOCK // LANES, conv_rows, 3 * LANES), f32),
            pltpu.VMEM((groups, needed, source.shape[1], BLOCK), bf16),
            pltpu.VMEM((groups, needed) + ahead, bf16),
            pltpu.VMEM((groups, span, STATE_WIDTH), f32),
            pltpu.VMEM((groups, span, BLOCK), bf16),
            news,
            pltpu.SemaphoreType.DMA((groups, needed)),
            pltpu.SemaphoreType.DMA((groups, needed)),
            pltpu.SemaphoreType.DMA((groups,)),
            pltpu.SemaphoreType.DMA((groups, 2)),
        ],
        compiler_params=params(48 if last else 60),
        cost_estimate=pl.CostEstimate(flops=4 * 10**9, bytes_accessed=10**7, transcendentals=10**6),
        name="state_chunk",
    )(*args, *in_hbm(w, bias, a_log, lead, *before))


def split(v):
    high = v.astype(bf16)
    return high, (v - high.astype(f32)).astype(bf16)


def block_kernel(dims, first, recv, *refs):
    spg, rows, heads, span, piece_heads = dims
    prev, refs = refs[0], refs[1:]
    w, xact, bmap, run_ref, dt_ref, cum_ref, state, skip = refs[:8]
    mixed, gate_out, side, token, raw, low, shifted = refs[-7:]
    at_c = 2 * span + STATE_WIDTH

    def take(slab):
        return recv.at[slab]

    def ahead(slab):
        return prev.at[0]

    gather_rows(take, ahead, first, raw, rows, at_c, at_c + STATE_WIDTH)
    gather_rows(take, ahead, first, raw, rows, 0, span, False)
    token[0] = cum_ref[0, :8, :LANES]
    shift_rows(raw, low, shifted, at_c, band())
    known = {}
    c = [conv_tile(raw, shifted, w[0], at_c, r, known) for r in range(0, STATE_WIDTH, HEAD_DIM)]
    c = jnp.concatenate(c, axis=0)
    b_rows = bmap[0].astype(f32).T.astype(bf16)
    scores = jnp.dot(b_rows, c, preferred_element_type=f32)
    src = lax.broadcasted_iota(jnp.int32, (HALF, HALF), 0)
    dst = lax.broadcasted_iota(jnp.int32, (HALF, HALF), 1)
    causal = src <= dst
    s00 = jnp.where(causal, scores[:HALF, :HALF], 0.0)
    s01 = scores[:HALF, HALF:]
    s11 = jnp.where(causal, scores[HALF:, HALF:], 0.0)
    r = run_ref[0] * LOG2E
    q = (r - jnp.log(dt_ref[0]) * LOG2E).T
    if not first:
        cc = jnp.concatenate([c, c], axis=0)
        entered = jnp.exp2(r)
    reach = [part.astype(f32) for part in split(jnp.exp(cum_ref[0]))]
    reach.append(jnp.zeros((STATE_WIDTH - 2 * heads, BLOCK), f32))
    side[0, :, :STATE_WIDTH] = c.astype(f32).T.astype(bf16)
    side[0, :, STATE_WIDTH:] = jnp.concatenate(reach, axis=0).T.astype(bf16)
    turned = []
    for h in range(heads):
        at = h * HEAD_DIM
        r0, r1 = r[h : h + 1, :HALF], r[h : h + 1, HALF:]
        q0, q1 = q[:HALF, h : h + 1], q[HALF:, h : h + 1]
        w00 = (s00 * jnp.exp2(jnp.minimum(r0 - q0, CAP))).astype(bf16)
        w01 = (s01 * jnp.exp2(r1 - q0)).astype(bf16)
        w11 = (s11 * jnp.exp2(jnp.minimum(r1 - q1, CAP))).astype(bf16)
        x = xact[0, at : at + HEAD_DIM, :]
        y0 = jnp.dot(x[:, :HALF], w00, preferred_element_type=f32)
        y1 = jnp.dot(x, jnp.concatenate([w01, w11], axis=0), preferred_element_type=f32)
        y = jnp.concatenate([y0, y1], axis=1) + skip[0, h : h + 1, :] * x.astype(f32)
        if not first:
            if at % WIDE == 0:
                both = jnp.concatenate(split(state[0, at : at + WIDE, :]), axis=1)
                carried = jnp.dot(both, cc, preferred_element_type=f32)
            y = y + entered[h : h + 1, :] * carried[at % WIDE : at % WIDE + HEAD_DIM, :]
        gate = raw[at : at + HEAD_DIM, LANES:]
        turned.append((y * silu(gate), gate))
        if len(turned) * HEAD_DIM == LANES:
            lanes = slice(at + HEAD_DIM - LANES, at + HEAD_DIM)
            mixed[0, :, lanes] = jnp.concatenate([pair[0] for pair in turned], axis=0).T
            wide = jnp.concatenate([pair[1] for pair in turned], axis=0).T
            gate_out[0, :, lanes] = wide.astype(bf16)
            turned = []


def block_chunk(
    chunk, chunks, got, w, xact, bmap, run, dt, cum, state, skip, after, dims
):
    spg, rows, heads, span, piece_heads = dims
    groups = w.shape[0]

    at_c = 2 * span + STATE_WIDTH
    one = at_c // rows
    assert (at_c + STATE_WIDTH - 1) // rows == one
    source, prev, (at, ahead) = sources(got, chunk)
    args = in_hbm(source, prev)
    specs = [pl.BlockSpec((spg, source.shape[1], BLOCK), lambda g: (g, 0, at))]
    if chunk == 0:
        width = source.shape[2]
        base = rim_rows(rows, width)[0] // 16
        specs.append(pl.BlockSpec((1, 16, width), lambda g: (g * spg + one, base, 0)))
    else:
        shape = (1, prev.shape[1], LANES)
        specs.append(pl.BlockSpec(shape, lambda g: (g * spg + one, 0, ahead)))
    args += in_hbm(w, xact, bmap, run, dt, cum, state, skip)
    specs += [
        pl.BlockSpec((1, 8, STATE_WIDTH), lambda g: (g, 0, span // STATE_WIDTH + 1)),
        per_group(span, BLOCK),
        per_group(STATE_WIDTH, BLOCK),
        per_group(heads, BLOCK),
        per_group(heads, BLOCK),
        per_group(heads, BLOCK),
        per_group(span, STATE_WIDTH),
        per_group(heads, 1),
    ]
    args += in_vmem(*after)
    specs += [pl.BlockSpec(memory_space=pl.ANY)] * len(after)

    def out(dtype, *shape):
        return pltpu.HBM((groups,) + shape, dtype)

    return pl.pallas_call(
        functools.partial(block_kernel, dims, chunk == 0),
        grid=(groups,),
        in_specs=specs,
        out_specs=[
            per_group(BLOCK, span),
            per_group(BLOCK, span),
            per_group(BLOCK, 2 * STATE_WIDTH),
            per_group(8, LANES),
        ],
        out_shape=[
            out(f32, BLOCK, span),
            out(bf16, BLOCK, span),
            out(bf16, BLOCK, 2 * STATE_WIDTH),
            out(f32, 8, LANES),
        ],
        scratch_shapes=[
            pltpu.VMEM((rows * spg, LANES + BLOCK), f32),
            pltpu.VMEM((STATE_WIDTH, LANES + BLOCK), bf16),
            pltpu.VMEM((BLOCK // LANES, STATE_WIDTH, 3 * LANES), f32),
        ],
        compiler_params=params(),
        cost_estimate=pl.CostEstimate(flops=4 * 10**9, bytes_accessed=10**7, transcendentals=10**6),
        name="block_chunk",
    )(*args)


def relay_kernel(piece_heads, src, token, dst):
    rows = piece_heads * HEAD_DIM
    held = jnp.zeros((rows, STATE_WIDTH), f32)
    for d in range(src.shape[0]):
        dst[d] = held.T.astype(bf16)
        both = src[d, rows:, :].astype(f32)
        decay = both[:8] + both[8:]
        spread = [
            jnp.broadcast_to(decay[h : h + 1, :], (HEAD_DIM, STATE_WIDTH))
            for h in range(piece_heads)
        ]
        held = jnp.concatenate(spread, axis=0) * held + src[d, :rows, :].astype(f32)


def relay(packed, token, piece_heads):
    count = packed.shape[0]
    rows = piece_heads * HEAD_DIM
    return pl.pallas_call(
        functools.partial(relay_kernel, piece_heads),
        in_specs=[pl.BlockSpec(memory_space=pltpu.VMEM), pl.BlockSpec(memory_space=pl.ANY)],
        out_shape=pltpu.VMEM((count, STATE_WIDTH, rows), bf16),
        compiler_params=params(16),
        name="relay",
    )(packed, *in_hbm(token))


def final_kernel(chunks, groups, *refs):
    mixed, gates, sides = (refs[i * chunks : (i + 1) * chunks] for i in range(3))
    state, gain, out = refs[3 * chunks : 3 * chunks + 3]
    held, gate_held, side_held, kept, done, sems, out_sems = refs[3 * chunks + 3 :]
    span = held.shape[2]
    piece = state.shape[2]
    spg = state.shape[0] // groups
    heads = span // HEAD_DIM
    steps = [(g, c) for g in range(groups) for c in range(chunks)]

    def loads(i):
        g, c = steps[i]
        slot = i
        moves = []
        moves.append((sides[c].at[g], side_held.at[slot]))
        moves.append((mixed[c].at[g], held.at[slot]))
        moves.append((gates[c].at[g], gate_held.at[slot]))
        return [
            pltpu.make_async_copy(a, b, sems.at[slot, j]) for j, (a, b) in enumerate(moves)
        ]

    def store(i):
        g, c = steps[i]
        return pltpu.make_async_copy(
            done.at[i % 2],
            out.at[c * BLOCK : (c + 1) * BLOCK, g * span : (g + 1) * span],
            out_sems.at[i % 2],
        )

    for i in range(len(steps)):
        for move in loads(i):
            move.start()
    row = lax.broadcasted_iota(jnp.int32, (STATE_WIDTH, span), 0)
    col = lax.broadcasted_iota(jnp.int32, (STATE_WIDTH, span), 1) // HEAD_DIM
    spread = jnp.where((row == col) | (row == col + heads), 1.0, 0.0).astype(bf16)
    for i, (g, c) in enumerate(steps):
        slot = i
        for move in loads(i):
            move.wait()
        if i >= 2:
            store(i - 2).wait()
        side = side_held[slot]
        half = BLOCK // 2
        for q in range(0, BLOCK, half):
            rows = slice(q, q + half)
            total = jnp.zeros((half, LANES), f32)
            for j in range(spg):
                piece_lanes = slice(j * piece, (j + 1) * piece)
                part = jnp.dot(
                    side[rows, :STATE_WIDTH], state[g * spg + j], preferred_element_type=f32
                )
                reach = jnp.dot(
                    side[rows, STATE_WIDTH:], spread[:, piece_lanes], preferred_element_type=f32
                )
                gate = silu(gate_held[slot, rows, piece_lanes].astype(f32))
                v = held[slot, rows, piece_lanes] + gate * (part * reach)
                kept[rows, piece_lanes] = v
                for at in range(0, piece, LANES):
                    t = v[:, at : at + LANES]
                    if piece < LANES:
                        t = jnp.concatenate([t, jnp.zeros((half, LANES - piece), f32)], axis=1)
                    total = total + t * t
            mean = jnp.sum(total, axis=1, keepdims=True) * (1.0 / span)
            factor = lax.rsqrt(mean + EPSILON)
            for at in range(0, span, LANES):
                lanes = slice(at, at + LANES)
                scaled = kept[rows, lanes] * factor * gain[g, :, lanes]
                done[i % 2, rows, lanes] = scaled.astype(bf16)
        store(i).start()
    for i in range(max(len(steps) - 2, 0), len(steps)):
        store(i).wait()


def finish(mixed, gates, sides, state, gain):
    chunks = len(mixed)
    groups, _, span = mixed[0].shape
    steps = groups * chunks
    anywhere = pl.BlockSpec(memory_space=pl.ANY)
    within = pl.BlockSpec(memory_space=pltpu.VMEM)
    return pl.pallas_call(
        functools.partial(final_kernel, chunks, groups),
        in_specs=[anywhere] * (3 * chunks) + [within] * 2,
        out_specs=anywhere,
        out_shape=jax.ShapeDtypeStruct((chunks * BLOCK, groups * span), bf16),
        scratch_shapes=[
            pltpu.VMEM((steps, BLOCK, span), f32),
            pltpu.VMEM((steps, BLOCK, span), bf16),
            pltpu.VMEM((steps, BLOCK, 2 * STATE_WIDTH), bf16),
            pltpu.VMEM((BLOCK, span), f32),
            pltpu.VMEM((2, BLOCK, span), bf16),
            pltpu.SemaphoreType.DMA((steps, 3)),
            pltpu.SemaphoreType.DMA((2,)),
        ],
        compiler_params=params(40),
        name="finish",
    )(*in_hbm(*mixed, *gates, *sides), state, gain)


def swap(array, k):
    count = lax.axis_size("seq")
    return lax.ppermute(array, "seq", [(i, i ^ k) for i in range(count)])


def exchange(array):
    return lax.all_to_all(array, "seq", split_axis=0, concat_axis=0, tiled=True)


def per_device(projected, conv_weight, dt_bias, a_log, d_skip, norm_gain):
    seq_count = lax.axis_size("seq")
    groups = conv_weight.shape[1]
    heads = dt_bias.shape[0] // groups
    span = heads * HEAD_DIM
    rows, all_tokens = projected.shape
    local_tokens = all_tokens // seq_count
    chunks = local_tokens // BLOCK
    spg = seq_count // groups
    piece_heads = groups * heads // seq_count
    dims = (spg, rows, heads, span, piece_heads)

    w = jnp.pad(jnp.transpose(conv_weight, (1, 0, 2)), ((0, 0), (0, 4), (0, 0)))
    bias = dt_bias.reshape(groups, heads, 1)
    rate = a_log.reshape(groups, heads, 1)
    skip = d_skip.reshape(groups, heads, 1)
    gain = norm_gain.reshape(groups, 1, span)
    state = jnp.zeros((groups, span, STATE_WIDTH), f32)
    lead = jnp.zeros((groups, heads, LANES), f32)

    me = lax.axis_index("seq").astype(jnp.int32).reshape(1)
    assert chunks > 2 and seq_count & (seq_count - 1) == 0
    cut = cut_first(projected, seq_count, local_tokens - 2 * BLOCK)
    got = [exchange(cut)]
    own, near, *pairs = cut_pairs(projected, me, seq_count, local_tokens - 2 * BLOCK, [cut])
    near = swap(near, 1)
    pairs = [swap(pair, 2 * j + 2) for j, pair in enumerate(pairs)]
    ready = [own, w, bias, rate, skip, gain, state, lead]
    cut = cut_block(projected, seq_count, local_tokens - BLOCK, ready)
    got += [None, exchange(cut)]

    results, tokens = [], []
    for c in range(chunks):
        before = []
        if c == chunks - 2:
            passed = swap(forward(pairs, [lead, tokens[0]]), 1)
            got[1] = join(me, own, near, pairs, passed, tokens)
        if c == chunks - 1:
            before = tokens[-2:-1]
        xact, bmap, run, dt, cum, new, lead = state_chunk(
            c, chunks, got, w, bias, rate, state, lead, before, dims
        )
        after = []
        if c == chunks - 1:
            entering = relay(exchange(new), tokens[-1], piece_heads)
            after = [entering]
        *result, token = block_chunk(
            c, chunks, got, w, xact, bmap, run, dt, cum, state, skip, after, dims
        )
        results.append(result)
        tokens.append(token)
        state = new
    return finish(*zip(*results), exchange(entering), gain)


def solution(mesh):
    in_specs = (P(("tp", "seq"), None), P(None, "tp", None), P("tp"), P("tp"), P("tp"), P("tp"))
    return jax.shard_map(
        per_device, mesh=mesh, in_specs=in_specs, out_specs=P("seq", "tp"), check_vma=False
    )
```

```python
import functools

import jax
import jax.numpy as jnp
from jax import lax
from jax.experimental import pallas as pl
from jax.experimental.pallas import tpu as pltpu
from jax.sharding import PartitionSpec as P

HEAD_DIM = 64
STATE_WIDTH = 128
BLOCK = 256
LANES = 128
HALF = BLOCK // 2
WIDE = 256
LOG2E = 1.4426950408889634
CAP = 80.0
EPSILON = 1e-05

f32 = jnp.float32
bf16 = jnp.bfloat16
NT = (((1,), (1,)), ((), ()))


def params(mib=60):
    return pltpu.CompilerParams(vmem_limit_bytes=mib * 2**20)


def silu(v):
    half = 0.5 * v
    return half + half * jnp.tanh(half)


def softplus(v):
    e = jnp.exp(-jnp.abs(v))
    u = 1.0 + e
    gap = u - 1.0
    tiny = gap == 0.0
    log_part = jnp.where(tiny, e, jnp.log(u) * (e / jnp.where(tiny, 1.0, gap)))
    return jnp.maximum(v, 0.0) + log_part


def in_hbm(*arrays):
    return [pltpu.with_memory_space_constraint(array, pltpu.HBM) for array in arrays]


def in_vmem(*arrays):
    return [pltpu.with_memory_space_constraint(array, pltpu.VMEM) for array in arrays]


def per_group(*shape):
    return pl.BlockSpec((1,) + shape, lambda g: (g,) + (0,) * len(shape))


RIM = 4


def rim_rows(rows, width):
    base = rows // 16 * 16
    height = -(-(rows - base + RIM * -(-rows // width)) // 8) * 8
    assert height <= 16
    return base, height


def first_kernel(src, token, dst, held, windows, ends, in_sems, rim_sems, out_sems, end_sems):
    rows, all_tokens = src.shape
    count, _, width = dst.shape
    tokens = all_tokens // count
    base, height = rim_rows(rows, width)

    def fetch(d):
        at = d * tokens
        return pltpu.make_async_copy(src.at[:, at : at + width], held.at[d], in_sems.at[d])

    def window(d):
        at = d * tokens - LANES
        return pltpu.make_async_copy(src.at[:, at : at + LANES], windows.at[d], rim_sems.at[d])

    def place(d):
        return pltpu.make_async_copy(
            held.at[d, :base, :], dst.at[d, :base, :], out_sems.at[d]
        )

    def place_end(d):
        return pltpu.make_async_copy(
            ends.at[d], dst.at[d, base : base + height, :], end_sems.at[d]
        )

    for d in range(count):
        fetch(d).start()
        if d:
            window(d).start()
    row = lax.broadcasted_iota(jnp.int32, (height, LANES), 0) - (rows - base)
    col = lax.broadcasted_iota(jnp.int32, (height, LANES), 1)
    hit = (row >= 0) & (col == lax.rem(row + 16, RIM) + LANES - RIM)
    pick = jnp.where(hit, 1.0, 0.0).astype(bf16)
    which = lax.broadcasted_iota(jnp.int32, (height, width), 0) - (rows - base)
    for d in range(count):
        fetch(d).wait()
        place(d).start()
        end = held[d, base:rows, :].astype(f32)
        end = jnp.concatenate([end, jnp.zeros((height - end.shape[0], width), f32)], axis=0)
        if d:
            window(d).wait()
            rims = lax.dot_general(pick, windows[d], NT, preferred_element_type=f32)
            for j in range(-(-rows // width)):
                part = rims[:, j * width : min((j + 1) * width, rows)]
                if part.shape[1] < width:
                    fill = jnp.zeros((height, width - part.shape[1]), f32)
                    part = jnp.concatenate([part, fill], axis=1)
                end = jnp.where((which >= RIM * j) & (which < RIM * (j + 1)), part, end)
        ends[d] = end.astype(bf16)
        place_end(d).start()
    for d in range(count):
        place(d).wait()
        place_end(d).wait()


def cut_first(projected, count, width, token):
    rows = projected.shape[0]
    base, height = rim_rows(rows, width)
    sems = pltpu.SemaphoreType.DMA((count,))
    anywhere = pl.BlockSpec(memory_space=pl.ANY)
    return pl.pallas_call(
        first_kernel,
        in_specs=[anywhere] * 2,
        out_specs=anywhere,
        out_shape=pltpu.HBM((count, base + height, width), bf16),
        scratch_shapes=[
            pltpu.VMEM((count, rows, width), bf16),
            pltpu.VMEM((count, rows, LANES), bf16),
            pltpu.VMEM((count, height, width), bf16),
            sems,
            sems,
            sems,
            sems,
        ],
        compiler_params=params(),
        name="cut_first",
    )(*in_hbm(projected), token)


def staged(moves, held, in_sems, out_sems):
    for i, (source, _) in enumerate(moves):
        pltpu.make_async_copy(source, held.at[i], in_sems.at[i]).start()
    for i, (source, target) in enumerate(moves):
        pltpu.make_async_copy(source, held.at[i], in_sems.at[i]).wait()
        pltpu.make_async_copy(held.at[i], target, out_sems.at[i]).start()
    for i, (_, target) in enumerate(moves):
        pltpu.make_async_copy(held.at[i], target, out_sems.at[i]).wait()


def staging(count, rows, width):
    sems = pltpu.SemaphoreType.DMA((count,))
    return [pltpu.VMEM((count, rows, width), bf16), sems, sems]


def cut_kernel(low, count, src, *refs):
    dst = refs[-4]
    tokens = src.shape[1] // count
    moves = []
    for d in range(count):
        at = d * tokens + low
        moves.append((src.at[:, at : at + BLOCK], dst.at[d]))
    staged(moves, *refs[-3:])


def cut_block(projected, count, low, after):
    rows = projected.shape[0]
    args = in_hbm(projected, *after)
    anywhere = pl.BlockSpec(memory_space=pl.ANY)
    return pl.pallas_call(
        functools.partial(cut_kernel, low, count),
        in_specs=[anywhere] * len(args),
        out_specs=anywhere,
        out_shape=pltpu.HBM((count, rows, BLOCK), bf16),
        scratch_shapes=staging(count, rows, BLOCK),
        compiler_params=params(),
        name="cut_block",
    )(*args)


def pairs_kernel(low, count, me_ref, src, *refs):
    own, near, *far = refs[-(count // 2 + 4) : -3]
    tokens = src.shape[1] // count
    width = own.shape[1]
    me = me_ref[0]
    targets = [own, near]
    for pair in far:
        targets += [pair.at[:, :width], pair.at[:, width:]]
    moves = []
    for k, target in enumerate(targets):
        at = pl.multiple_of((me ^ k) * tokens + low, LANES)
        moves.append((src.at[:, pl.ds(at, width)], target))
    staged(moves[2:] + moves[:2], *refs[-3:])


def cut_pairs(projected, me, count, low, high, after):
    rows = projected.shape[0]
    anywhere = pl.BlockSpec(memory_space=pl.ANY)
    width = high - low
    one, two = pltpu.HBM((rows, width), bf16), pltpu.HBM((rows, 2 * width), bf16)
    return pl.pallas_call(
        functools.partial(pairs_kernel, low, count),
        in_specs=[pl.BlockSpec(memory_space=pltpu.SMEM)] + [anywhere] * (1 + len(after)),
        out_specs=[anywhere] * (count // 2 + 1),
        out_shape=[one, one] + [two] * (count // 2 - 1),
        scratch_shapes=staging(count, rows, width),
        compiler_params=params(),
        name="cut_pairs",
    )(me, *in_hbm(projected, *after))


def forward_kernel(parts, *refs):
    dst = refs[-4]
    moves = []
    for pair in refs[:parts]:
        width = pair.shape[1] // 2
        at = len(moves) * width
        moves.append((pair.at[:, width:], dst.at[:, at : at + width]))
    staged(moves, *refs[-3:])


def forward(pairs, after):
    rows, width = pairs[0].shape
    anywhere = pl.BlockSpec(memory_space=pl.ANY)
    return pl.pallas_call(
        functools.partial(forward_kernel, len(pairs)),
        in_specs=[anywhere] * (len(pairs) + len(after)),
        out_specs=anywhere,
        out_shape=pltpu.HBM((rows, len(pairs) * width // 2), bf16),
        scratch_shapes=staging(len(pairs), rows, width // 2),
        compiler_params=params(),
        name="forward",
    )(*pairs, *in_hbm(*after))


def join_kernel(count, parts, me_ref, passed, *refs):
    each = count // 2 + 1
    dst = refs[-4]
    me = me_ref[0]
    moves = []
    for p in range(parts):
        own, near, *pairs = refs[p * each : (p + 1) * each]
        width = own.shape[1]
        sources = [own, near]
        for j, pair in enumerate(pairs):
            at = (p * len(pairs) + j) * width
            sources += [pair.at[:, :width], passed.at[:, at : at + width]]
        lanes = slice(p * width, (p + 1) * width)
        moves += [(source, dst.at[me ^ k, :, lanes]) for k, source in enumerate(sources)]
    staged(moves, *refs[-3:])


def join(me, passed, parts, after):
    count = 2 * len(parts[0]) - 2
    rows, width = parts[0][0].shape
    anywhere = pl.BlockSpec(memory_space=pl.ANY)
    args = [passed, *(array for part in parts for array in part), *in_hbm(*after)]
    return pl.pallas_call(
        functools.partial(join_kernel, count, len(parts)),
        in_specs=[pl.BlockSpec(memory_space=pltpu.SMEM)] + [anywhere] * len(args),
        out_specs=anywhere,
        out_shape=pltpu.HBM((count, rows, len(parts) * width), bf16),
        scratch_shapes=staging(count * len(parts), rows, width),
        compiler_params=params(),
        name="join",
    )(me, *args)


def gather_rows(recv, prev, first, raw, rows, low, high, ahead=True, only=None):
    for s in range(recv.shape[0]):
        a = max(low - s * rows, 0) // 16 * 16
        b = min(-(-(high - s * rows) // 16) * 16, rows)
        if b <= a:
            continue
        at = s * rows + a
        raw[at : at + b - a, LANES:] = recv[s, a:b, :].astype(f32)
        if not ahead:
            continue
        if not first:
            raw[at : at + b - a, :LANES] = prev[s if only is None else 0, a:b, :].astype(f32)
            continue
        width = prev.shape[2]
        base, height = rim_rows(rows, width)
        rims = prev[s if only is None else 0, :height, :].astype(f32)
        tall = jnp.concatenate([jnp.zeros((LANES - height, width), f32), rims], axis=0)
        for j in range(-(-rows // width)):
            c, d = max(a, j * width), min(b, (j + 1) * width)
            if d <= c:
                continue
            shift = height - RIM - (rows - base) - RIM * j
            moved = (pltpu.roll(tall, shift, 0) if shift else tall).T
            raw[s * rows + c : s * rows + d, :LANES] = moved[c - j * width : d - j * width]


def band():
    row = lax.broadcasted_iota(jnp.int32, (2 * LANES, 3 * LANES), 0)
    col = lax.broadcasted_iota(jnp.int32, (2 * LANES, 3 * LANES), 1)
    tap = col // LANES
    return jnp.where(row == col - tap * LANES + LANES - 3 + tap, 1.0, 0.0).astype(bf16)


def shift_rows(raw, low, shifted, at):
    low[...] = raw[at : at + low.shape[0], :].astype(bf16)
    picks = band()
    for i in range(BLOCK // LANES):
        window = low[:, i * LANES : (i + 2) * LANES]
        shifted[i] = jnp.dot(window, picks, preferred_element_type=f32)


def conv_tile(raw, shifted, w, at, r):
    rows = slice(r, r + HEAD_DIM)
    taps = [jnp.broadcast_to(w[0, rows, k : k + 1], (HEAD_DIM, LANES)) for k in range(4)]
    parts = []
    for i in range(BLOCK // LANES):
        summed = None
        for k in range(3):
            part = taps[k] * shifted[i, rows, k * LANES : (k + 1) * LANES]
            summed = part if summed is None else summed + part
        own = raw[at + r : at + r + HEAD_DIM, (i + 1) * LANES : (i + 2) * LANES]
        parts.append(silu(summed + taps[3] * own).astype(bf16))
    return jnp.concatenate(parts, axis=1)


def state_kernel(dims, first, last, recv, *refs):
    spg, rows, heads, span, piece_heads = dims
    prev, refs = refs[0], refs[1:]
    w, bias, a_log, state_in, lead_in = refs[:5]
    xact, bmap, run_out, dt_out, cum_out, state_out, lead_out = refs[-11:-4]
    raw, xw, low, shifted = refs[-4:]
    steps = 2 * span + 2 * STATE_WIDTH

    gather_rows(recv, prev, first, raw, rows, steps, steps + heads, False)
    gather_rows(recv, prev, first, raw, rows, span, 2 * span + STATE_WIDTH)
    dt = softplus(raw[steps : steps + heads, LANES:] + bias[0])
    log_decay = -jnp.exp(a_log[0]) * dt
    lane = lax.broadcasted_iota(jnp.int32, (heads, BLOCK), 1)
    run = log_decay
    shift = 1
    while shift < BLOCK:
        run = run + jnp.where(lane >= shift, pltpu.roll(run, shift, 1), 0.0)
        shift *= 2
    final = run[:, BLOCK - 1 :]
    scale = jnp.exp(final - run) * dt
    cum = run + lead_in[0][:, :1]
    run_out[0] = run
    dt_out[0] = dt
    cum_out[0] = cum
    lead = jnp.broadcast_to(cum[:, BLOCK - 1 :], (heads, LANES))
    lead_out[0] = lead
    keep = jnp.broadcast_to(jnp.exp(final), (heads, LANES))

    shift_rows(raw, low, shifted, span)
    for r in range(0, STATE_WIDTH, HEAD_DIM):
        bmap[0, r : r + HEAD_DIM, :] = conv_tile(raw, shifted, w, span, span + r)
    for h in range(heads):
        r = h * HEAD_DIM
        tile = conv_tile(raw, shifted, w, span, r)
        xact[0, r : r + HEAD_DIM, :] = tile
        xw[r : r + HEAD_DIM, :] = (tile.astype(f32) * scale[h : h + 1, :]).astype(bf16)
    update = lax.dot_general(xw[...], bmap[0], NT, preferred_element_type=f32)
    for h in range(heads):
        r = h * HEAD_DIM
        new = update[r : r + HEAD_DIM, :]
        if not first:
            new = keep[h : h + 1, :] * state_in[0, r : r + HEAD_DIM, :] + new
        if last:
            at = (h % piece_heads) * HEAD_DIM
            state_out[h // piece_heads, at : at + HEAD_DIM, :] = new.astype(bf16)
        else:
            state_out[0, r : r + HEAD_DIM, :] = new
    if last:
        high, low = split(jnp.exp(lead))
        fill = jnp.zeros((8 - piece_heads, LANES), f32)
        for i in range(heads // piece_heads):
            mine = slice(i * piece_heads, (i + 1) * piece_heads)
            parts = [high[mine].astype(f32), fill, low[mine].astype(f32), fill]
            at = piece_heads * HEAD_DIM
            state_out[i, at : at + 16, :] = jnp.concatenate(parts, axis=0).astype(bf16)


def chunk_specs(got, chunk, dims, only=None):
    spg, rows = dims[:2]
    slabs = spg if only is None else 1

    def ahead(source, shape, row, lane):
        def index(g):
            return (g if only is None else g * spg + only, row, lane)

        return source, pl.BlockSpec((slabs,) + shape, index)

    def lane_of(block):
        first, middle, last = got
        ahead_of = first.shape[2] // BLOCK
        if block < ahead_of:
            return first, block
        return (middle if block == ahead_of else last), 0

    source, at = lane_of(chunk)
    block = pl.BlockSpec((spg, source.shape[1], BLOCK), lambda g: (g, 0, at))
    if chunk == 0:
        width = source.shape[2]
        prev, prev_spec = ahead(source, (16, width), rim_rows(rows, width)[0] // 16, 0)
    else:
        prev, place = lane_of(chunk - 1)
        lane = (place + 1) * (BLOCK // LANES) - 1
        prev, prev_spec = ahead(prev, (prev.shape[1], LANES), 0, lane)
    return [source, prev], [block, prev_spec]


def state_chunk(chunk, chunks, got, w, bias, a_log, state, lead, before, dims):
    spg, rows, heads, span, piece_heads = dims
    groups = w.shape[0]
    last = chunk == chunks - 1
    if last:
        packed = piece_heads * HEAD_DIM + 16
        state_shape = pltpu.HBM((groups * spg, packed, STATE_WIDTH), bf16)
        state_spec = pl.BlockSpec((spg, packed, STATE_WIDTH), lambda g: (g, 0, 0))
    else:
        state_shape = pltpu.HBM((groups, span, STATE_WIDTH), f32)
        state_spec = per_group(span, STATE_WIDTH)

    def out(dtype, *shape):
        return pltpu.HBM((groups,) + shape, dtype)

    args, specs = chunk_specs(got, chunk, dims)
    args[1:] = in_hbm(args[1])
    args[:1] = in_vmem(args[0]) if last else in_hbm(args[0])
    after = in_hbm(*before)
    return pl.pallas_call(
        functools.partial(state_kernel, dims, chunk == 0, last),
        grid=(groups,),
        in_specs=specs
        + [
            per_group(span + STATE_WIDTH, 4),
            per_group(heads, 1),
            per_group(heads, 1),
            per_group(span, STATE_WIDTH),
            per_group(heads, LANES),
        ]
        + [pl.BlockSpec(memory_space=pl.ANY)] * len(after),
        out_specs=[
            per_group(span, BLOCK),
            per_group(STATE_WIDTH, BLOCK),
            per_group(heads, BLOCK),
            per_group(heads, BLOCK),
            per_group(heads, BLOCK),
            state_spec,
            per_group(heads, LANES),
        ],
        out_shape=[
            out(bf16, span, BLOCK),
            out(bf16, STATE_WIDTH, BLOCK),
            out(f32, heads, BLOCK),
            out(f32, heads, BLOCK),
            out(f32, heads, BLOCK),
            state_shape,
            out(f32, heads, LANES),
        ],
        scratch_shapes=[
            pltpu.VMEM((rows * spg, LANES + BLOCK), f32),
            pltpu.VMEM((span, BLOCK), bf16),
            pltpu.VMEM((span + STATE_WIDTH, LANES + BLOCK), bf16),
            pltpu.VMEM((BLOCK // LANES, span + STATE_WIDTH, 3 * LANES), f32),
        ],
        compiler_params=params(48 if last else 60),
        cost_estimate=pl.CostEstimate(flops=4 * 10**9, bytes_accessed=10**7, transcendentals=10**6),
        name="state_chunk",
    )(*args, *in_hbm(w, bias, a_log, state, lead), *after)


def split(v):
    high = v.astype(bf16)
    return high, (v - high.astype(f32)).astype(bf16)


def block_kernel(dims, first, recv, *refs):
    spg, rows, heads, span, piece_heads = dims
    prev, refs = refs[0], refs[1:]
    w, xact, bmap, run_ref, dt_ref, cum_ref, state, skip = refs[:8]
    mixed, gate_out, side, token, raw, low, shifted = refs[-7:]
    at_c = 2 * span + STATE_WIDTH
    gather_rows(recv, prev, first, raw, rows, at_c, at_c + STATE_WIDTH, True, at_c // rows)
    gather_rows(recv, prev, first, raw, rows, 0, span, False)
    token[0] = cum_ref[0, :8, :LANES]
    shift_rows(raw, low, shifted, at_c)
    c = [conv_tile(raw, shifted, w, at_c, r) for r in range(0, STATE_WIDTH, HEAD_DIM)]
    c = jnp.concatenate(c, axis=0)
    b_rows = bmap[0].astype(f32).T.astype(bf16)
    scores = jnp.dot(b_rows, c, preferred_element_type=f32)
    src = lax.broadcasted_iota(jnp.int32, (HALF, HALF), 0)
    dst = lax.broadcasted_iota(jnp.int32, (HALF, HALF), 1)
    causal = src <= dst
    s00 = jnp.where(causal, scores[:HALF, :HALF], 0.0)
    s01 = scores[:HALF, HALF:]
    s11 = jnp.where(causal, scores[HALF:, HALF:], 0.0)
    r = run_ref[0] * LOG2E
    q = (r - jnp.log(dt_ref[0]) * LOG2E).T
    if not first:
        cc = jnp.concatenate([c, c], axis=0)
        entered = jnp.exp2(r)
    reach = [part.astype(f32) for part in split(jnp.exp(cum_ref[0]))]
    reach.append(jnp.zeros((STATE_WIDTH - 2 * heads, BLOCK), f32))
    side[0, :, :STATE_WIDTH] = c.astype(f32).T.astype(bf16)
    side[0, :, STATE_WIDTH:] = jnp.concatenate(reach, axis=0).T.astype(bf16)
    turned = []
    for h in range(heads):
        at = h * HEAD_DIM
        r0, r1 = r[h : h + 1, :HALF], r[h : h + 1, HALF:]
        q0, q1 = q[:HALF, h : h + 1], q[HALF:, h : h + 1]
        w00 = (s00 * jnp.exp2(jnp.minimum(r0 - q0, CAP))).astype(bf16)
        w01 = (s01 * jnp.exp2(r1 - q0)).astype(bf16)
        w11 = (s11 * jnp.exp2(jnp.minimum(r1 - q1, CAP))).astype(bf16)
        x = xact[0, at : at + HEAD_DIM, :]
        y0 = jnp.dot(x[:, :HALF], w00, preferred_element_type=f32)
        y1 = jnp.dot(x, jnp.concatenate([w01, w11], axis=0), preferred_element_type=f32)
        y = jnp.concatenate([y0, y1], axis=1) + skip[0, h : h + 1, :] * x.astype(f32)
        if not first:
            if at % WIDE == 0:
                both = jnp.concatenate(split(state[0, at : at + WIDE, :]), axis=1)
                carried = jnp.dot(both, cc, preferred_element_type=f32)
            y = y + entered[h : h + 1, :] * carried[at % WIDE : at % WIDE + HEAD_DIM, :]
        gate = raw[at : at + HEAD_DIM, LANES:]
        turned.append((y * silu(gate), gate))
        if len(turned) * HEAD_DIM == LANES:
            lanes = slice(at + HEAD_DIM - LANES, at + HEAD_DIM)
            mixed[0, :, lanes] = jnp.concatenate([pair[0] for pair in turned], axis=0).T
            wide = jnp.concatenate([pair[1] for pair in turned], axis=0).T
            gate_out[0, :, lanes] = wide.astype(bf16)
            turned = []


def block_chunk(
    chunk, chunks, got, w, xact, bmap, run, dt, cum, state, skip, after, dims
):
    spg, rows, heads, span, piece_heads = dims
    groups = w.shape[0]

    at_c = 2 * span + STATE_WIDTH
    one = at_c // rows
    assert (at_c + STATE_WIDTH - 1) // rows == one
    args, specs = chunk_specs(got, chunk, dims, one)
    args = in_hbm(*args)
    args += in_hbm(w, xact, bmap, run, dt, cum, state, skip)
    specs += [
        pl.BlockSpec((1, STATE_WIDTH, 4), lambda g: (g, span // STATE_WIDTH + 1, 0)),
        per_group(span, BLOCK),
        per_group(STATE_WIDTH, BLOCK),
        per_group(heads, BLOCK),
        per_group(heads, BLOCK),
        per_group(heads, BLOCK),
        per_group(span, STATE_WIDTH),
        per_group(heads, 1),
    ]
    args += in_vmem(*after)
    specs += [pl.BlockSpec(memory_space=pl.ANY)] * len(after)

    def out(dtype, *shape):
        return pltpu.HBM((groups,) + shape, dtype)

    return pl.pallas_call(
        functools.partial(block_kernel, dims, chunk == 0),
        grid=(groups,),
        in_specs=specs,
        out_specs=[
            per_group(BLOCK, span),
            per_group(BLOCK, span),
            per_group(BLOCK, 2 * STATE_WIDTH),
            per_group(8, LANES),
        ],
        out_shape=[
            out(f32, BLOCK, span),
            out(bf16, BLOCK, span),
            out(bf16, BLOCK, 2 * STATE_WIDTH),
            out(f32, 8, LANES),
        ],
        scratch_shapes=[
            pltpu.VMEM((rows * spg, LANES + BLOCK), f32),
            pltpu.VMEM((STATE_WIDTH, LANES + BLOCK), bf16),
            pltpu.VMEM((BLOCK // LANES, STATE_WIDTH, 3 * LANES), f32),
        ],
        compiler_params=params(),
        cost_estimate=pl.CostEstimate(flops=4 * 10**9, bytes_accessed=10**7, transcendentals=10**6),
        name="block_chunk",
    )(*args)


def relay_kernel(piece_heads, src, token, dst):
    rows = piece_heads * HEAD_DIM
    held = jnp.zeros((rows, STATE_WIDTH), f32)
    for d in range(src.shape[0]):
        dst[d] = held.T.astype(bf16)
        both = src[d, rows:, :].astype(f32)
        decay = both[:8] + both[8:]
        spread = [
            jnp.broadcast_to(decay[h : h + 1, :], (HEAD_DIM, STATE_WIDTH))
            for h in range(piece_heads)
        ]
        held = jnp.concatenate(spread, axis=0) * held + src[d, :rows, :].astype(f32)


def relay(packed, token, piece_heads):
    count = packed.shape[0]
    rows = piece_heads * HEAD_DIM
    return pl.pallas_call(
        functools.partial(relay_kernel, piece_heads),
        in_specs=[pl.BlockSpec(memory_space=pltpu.VMEM), pl.BlockSpec(memory_space=pl.ANY)],
        out_shape=pltpu.VMEM((count, STATE_WIDTH, rows), bf16),
        compiler_params=params(16),
        name="relay",
    )(packed, *in_hbm(token))


def final_kernel(chunks, groups, *refs):
    mixed, gates, sides = (refs[i * chunks : (i + 1) * chunks] for i in range(3))
    state, gain, out = refs[3 * chunks : 3 * chunks + 3]
    held, gate_held, side_held, kept, done, sems, out_sems = refs[3 * chunks + 3 :]
    span = held.shape[2]
    piece = state.shape[2]
    spg = state.shape[0] // groups
    heads = span // HEAD_DIM
    steps = [(g, c) for g in range(groups) for c in range(chunks)]

    def loads(i):
        g, c = steps[i]
        slot = i
        moves = []
        moves.append((sides[c].at[g], side_held.at[slot]))
        moves.append((mixed[c].at[g], held.at[slot]))
        moves.append((gates[c].at[g], gate_held.at[slot]))
        return [
            pltpu.make_async_copy(a, b, sems.at[slot, j]) for j, (a, b) in enumerate(moves)
        ]

    def store(i):
        g, c = steps[i]
        return pltpu.make_async_copy(
            done.at[i % 2],
            out.at[c * BLOCK : (c + 1) * BLOCK, g * span : (g + 1) * span],
            out_sems.at[i % 2],
        )

    for i in range(len(steps)):
        for move in loads(i):
            move.start()
    row = lax.broadcasted_iota(jnp.int32, (STATE_WIDTH, span), 0)
    col = lax.broadcasted_iota(jnp.int32, (STATE_WIDTH, span), 1) // HEAD_DIM
    spread = jnp.where((row == col) | (row == col + heads), 1.0, 0.0).astype(bf16)
    for i, (g, c) in enumerate(steps):
        slot = i
        for move in loads(i):
            move.wait()
        if i >= 2:
            store(i - 2).wait()
        side = side_held[slot]
        half = BLOCK // 2
        for q in range(0, BLOCK, half):
            rows = slice(q, q + half)
            total = jnp.zeros((half, LANES), f32)
            for j in range(spg):
                piece_lanes = slice(j * piece, (j + 1) * piece)
                part = jnp.dot(
                    side[rows, :STATE_WIDTH], state[g * spg + j], preferred_element_type=f32
                )
                reach = jnp.dot(
                    side[rows, STATE_WIDTH:], spread[:, piece_lanes], preferred_element_type=f32
                )
                gate = silu(gate_held[slot, rows, piece_lanes].astype(f32))
                v = held[slot, rows, piece_lanes] + gate * (part * reach)
                kept[rows, piece_lanes] = v
                for at in range(0, piece, LANES):
                    t = v[:, at : at + LANES]
                    if piece < LANES:
                        t = jnp.concatenate([t, jnp.zeros((half, LANES - piece), f32)], axis=1)
                    total = total + t * t
            mean = jnp.sum(total, axis=1, keepdims=True) * (1.0 / span)
            factor = lax.rsqrt(mean + EPSILON)
            for at in range(0, span, LANES):
                lanes = slice(at, at + LANES)
                scaled = kept[rows, lanes] * factor * gain[g, :, lanes]
                done[i % 2, rows, lanes] = scaled.astype(bf16)
        store(i).start()
    for i in range(max(len(steps) - 2, 0), len(steps)):
        store(i).wait()


def finish(mixed, gates, sides, state, gain):
    chunks = len(mixed)
    groups, _, span = mixed[0].shape
    steps = groups * chunks
    anywhere = pl.BlockSpec(memory_space=pl.ANY)
    within = pl.BlockSpec(memory_space=pltpu.VMEM)
    return pl.pallas_call(
        functools.partial(final_kernel, chunks, groups),
        in_specs=[anywhere] * (3 * chunks) + [within] * 2,
        out_specs=anywhere,
        out_shape=jax.ShapeDtypeStruct((chunks * BLOCK, groups * span), bf16),
        scratch_shapes=[
            pltpu.VMEM((steps, BLOCK, span), f32),
            pltpu.VMEM((steps, BLOCK, span), bf16),
            pltpu.VMEM((steps, BLOCK, 2 * STATE_WIDTH), bf16),
            pltpu.VMEM((BLOCK, span), f32),
            pltpu.VMEM((2, BLOCK, span), bf16),
            pltpu.SemaphoreType.DMA((steps, 3)),
            pltpu.SemaphoreType.DMA((2,)),
        ],
        compiler_params=params(40),
        name="finish",
    )(*in_hbm(*mixed, *gates, *sides), state, gain)


def swap(array, k):
    count = lax.axis_size("seq")
    return lax.ppermute(array, "seq", [(i, i ^ k) for i in range(count)])


def exchange(array):
    return lax.all_to_all(array, "seq", split_axis=0, concat_axis=0, tiled=True)


def per_device(projected, conv_weight, dt_bias, a_log, d_skip, norm_gain):
    seq_count = lax.axis_size("seq")
    groups = conv_weight.shape[1]
    heads = dt_bias.shape[0] // groups
    span = heads * HEAD_DIM
    rows, all_tokens = projected.shape
    local_tokens = all_tokens // seq_count
    chunks = local_tokens // BLOCK
    spg = seq_count // groups
    piece_heads = groups * heads // seq_count
    dims = (spg, rows, heads, span, piece_heads)

    w = jnp.transpose(conv_weight, (1, 2, 0))
    bias = dt_bias.reshape(groups, heads, 1)
    rate = a_log.reshape(groups, heads, 1)
    skip = d_skip.reshape(groups, heads, 1)
    gain = norm_gain.reshape(groups, 1, span)
    state = jnp.zeros((groups, span, STATE_WIDTH), f32)
    lead = jnp.zeros((groups, heads, LANES), f32)

    me = lax.axis_index("seq").astype(jnp.int32).reshape(1)
    assert chunks > 2 and seq_count & (seq_count - 1) == 0
    middle, split_at = local_tokens - 2 * BLOCK, local_tokens - BLOCK

    def send(low, after):
        own, near, *pairs = cut_pairs(projected, me, seq_count, low, low + HALF, after)
        pairs = [swap(pair, 2 * j + 2) for j, pair in enumerate(pairs)]
        return [own, swap(near, 1), *pairs]

    parts = [send(middle, [])]
    cut = cut_first(projected, seq_count, middle, parts[0][1])
    got = [exchange(cut)]
    parts.append(send(middle + HALF, [cut]))
    ready = [parts[1][0], w, bias, rate, skip, gain, state, lead]
    cut = cut_block(projected, seq_count, split_at, ready)
    got += [None, exchange(cut)]

    results, tokens = [], []
    for c in range(chunks):
        before = []
        if c == chunks - 2:
            pairs = [pair for part in parts for pair in part[2:]]
            passed = swap(forward(pairs, [lead, tokens[0], cut]), 1)
            got[1] = join(me, passed, parts, tokens)
        if c == chunks - 1:
            before = tokens[-2:-1]
        xact, bmap, run, dt, cum, new, lead = state_chunk(
            c, chunks, got, w, bias, rate, state, lead, before, dims
        )
        after = []
        if c == chunks - 1:
            entering = relay(exchange(new), tokens[-1], piece_heads)
            after = [entering]
        *result, token = block_chunk(
            c, chunks, got, w, xact, bmap, run, dt, cum, state, skip, after, dims
        )
        results.append(result)
        tokens.append(token)
        state = new
    return finish(*zip(*results), exchange(entering), gain)


def solution(mesh):
    in_specs = (P(("tp", "seq"), None), P(None, "tp", None), P("tp"), P("tp"), P("tp"), P("tp"))
    return jax.shard_map(
        per_device, mesh=mesh, in_specs=in_specs, out_specs=P("seq", "tp"), check_vma=False
    )
```

```python
import functools

import jax
import jax.numpy as jnp
from jax import lax
from jax.experimental import pallas as pl
from jax.experimental.pallas import tpu as pltpu
from jax.sharding import PartitionSpec as P

HEAD_DIM = 64
STATE_WIDTH = 128
BLOCK = 256
LANES = 128
HALF = BLOCK // 2
WIDE = 256
LOG2E = 1.4426950408889634
CAP = 80.0
EPSILON = 1e-05

f32 = jnp.float32
bf16 = jnp.bfloat16
NT = (((1,), (1,)), ((), ()))


def params(mib=60):
    return pltpu.CompilerParams(vmem_limit_bytes=mib * 2**20)


def silu(v):
    half = 0.5 * v
    return half + half * jnp.tanh(half)


def softplus(v):
    e = jnp.exp(-jnp.abs(v))
    u = 1.0 + e
    gap = u - 1.0
    tiny = gap == 0.0
    log_part = jnp.where(tiny, e, jnp.log(u) * (e / jnp.where(tiny, 1.0, gap)))
    return jnp.maximum(v, 0.0) + log_part


def in_hbm(*arrays):
    return [pltpu.with_memory_space_constraint(array, pltpu.HBM) for array in arrays]


def in_vmem(*arrays):
    return [pltpu.with_memory_space_constraint(array, pltpu.VMEM) for array in arrays]


def per_group(*shape):
    return pl.BlockSpec((1,) + shape, lambda g: (g,) + (0,) * len(shape))


RIM = 4


def rim_rows(rows, width):
    base = rows // 16 * 16
    height = -(-(rows - base + RIM * -(-rows // width)) // 8) * 8
    assert height <= 16
    return base, height


def first_kernel(src, dst, held, windows, ends, rims, in_sems, rim_sems, out_sems, end_sems):
    rows, all_tokens = src.shape
    count, _, width = dst.shape
    tokens = all_tokens // count
    base, height = rim_rows(rows, width)

    def fetch(d):
        at = d * tokens
        return pltpu.make_async_copy(src.at[:, at : at + width], held.at[d], in_sems.at[d])

    def window(d):
        at = d * tokens - LANES
        return pltpu.make_async_copy(src.at[:, at : at + LANES], windows.at[d], rim_sems.at[d])

    def place(d):
        return pltpu.make_async_copy(
            held.at[d, :base, :], dst.at[d, :base, :], out_sems.at[d]
        )

    def place_end(d):
        return pltpu.make_async_copy(
            ends.at[d], dst.at[d, base : base + height, :], end_sems.at[d]
        )

    for d in range(1, count):
        window(d).start()
    for d in range(count):
        fetch(d).start()
    row = lax.broadcasted_iota(jnp.int32, (height, LANES), 0) - (rows - base)
    col = lax.broadcasted_iota(jnp.int32, (height, LANES), 1)
    hit = (row >= 0) & (col == lax.rem(row + 16, RIM) + LANES - RIM)
    pick = jnp.where(hit, 1.0, 0.0).astype(bf16)
    which = lax.broadcasted_iota(jnp.int32, (height, width), 0) - (rows - base)
    for d in range(count):
        merged = jnp.zeros((height, width), f32)
        if d:
            window(d).wait()
            every = lax.dot_general(pick, windows[d], NT, preferred_element_type=f32)
            for j in range(-(-rows // width)):
                part = every[:, j * width : min((j + 1) * width, rows)]
                if part.shape[1] < width:
                    fill = jnp.zeros((height, width - part.shape[1]), f32)
                    part = jnp.concatenate([part, fill], axis=1)
                merged = jnp.where((which >= RIM * j) & (which < RIM * (j + 1)), part, merged)
        rims[d] = merged
    for d in range(count):
        fetch(d).wait()
        place(d).start()
    for d in range(count):
        end = held[d, base:rows, :].astype(f32)
        end = jnp.concatenate([end, jnp.zeros((height - end.shape[0], width), f32)], axis=0)
        ends[d] = (end + rims[d]).astype(bf16)
        place_end(d).start()
    for d in range(count):
        place(d).wait()
        place_end(d).wait()


def cut_first(projected, count, width):
    rows = projected.shape[0]
    base, height = rim_rows(rows, width)
    sems = pltpu.SemaphoreType.DMA((count,))
    anywhere = pl.BlockSpec(memory_space=pl.ANY)
    return pl.pallas_call(
        first_kernel,
        in_specs=[anywhere],
        out_specs=anywhere,
        out_shape=pltpu.HBM((count, base + height, width), bf16),
        scratch_shapes=[
            pltpu.VMEM((count, rows, width), bf16),
            pltpu.VMEM((count, rows, LANES), bf16),
            pltpu.VMEM((count, height, width), bf16),
            pltpu.VMEM((count, height, width), f32),
            sems,
            sems,
            sems,
            sems,
        ],
        compiler_params=params(),
        name="cut_first",
    )(*in_hbm(projected))


def staged(moves, held, in_sems, out_sems):
    for i, (source, _) in enumerate(moves):
        pltpu.make_async_copy(source, held.at[i], in_sems.at[i]).start()
    for i, (source, target) in enumerate(moves):
        pltpu.make_async_copy(source, held.at[i], in_sems.at[i]).wait()
        pltpu.make_async_copy(held.at[i], target, out_sems.at[i]).start()
    for i, (_, target) in enumerate(moves):
        pltpu.make_async_copy(held.at[i], target, out_sems.at[i]).wait()


def staging(count, rows, width):
    sems = pltpu.SemaphoreType.DMA((count,))
    return [pltpu.VMEM((count, rows, width), bf16), sems, sems]


def cut_kernel(low, count, src, *refs):
    dst = refs[-4]
    tokens = src.shape[1] // count
    moves = []
    for d in range(count):
        at = d * tokens + low
        moves.append((src.at[:, at : at + BLOCK], dst.at[d]))
    staged(moves, *refs[-3:])


def cut_block(projected, count, low, after):
    rows = projected.shape[0]
    args = in_hbm(projected, *after)
    anywhere = pl.BlockSpec(memory_space=pl.ANY)
    return pl.pallas_call(
        functools.partial(cut_kernel, low, count),
        in_specs=[anywhere] * len(args),
        out_specs=anywhere,
        out_shape=pltpu.HBM((count, rows, BLOCK), bf16),
        scratch_shapes=staging(count, rows, BLOCK),
        compiler_params=params(),
        name="cut_block",
    )(*args)


def pairs_kernel(low, count, me_ref, src, *refs):
    own, near, *far = refs[-(count // 2 + 4) : -3]
    tokens = src.shape[1] // count
    width = own.shape[1]
    me = me_ref[0]
    targets = [own, near]
    for pair in far:
        targets += [pair.at[:, :width], pair.at[:, width:]]
    moves = []
    for k, target in enumerate(targets):
        at = pl.multiple_of((me ^ k) * tokens + low, LANES)
        moves.append((src.at[:, pl.ds(at, width)], target))
    staged(moves[2:] + moves[:2], *refs[-3:])


def cut_pairs(projected, me, count, low, high, after):
    rows = projected.shape[0]
    anywhere = pl.BlockSpec(memory_space=pl.ANY)
    width = high - low
    one, two = pltpu.HBM((rows, width), bf16), pltpu.HBM((rows, 2 * width), bf16)
    return pl.pallas_call(
        functools.partial(pairs_kernel, low, count),
        in_specs=[pl.BlockSpec(memory_space=pltpu.SMEM)] + [anywhere] * (1 + len(after)),
        out_specs=[anywhere] * (count // 2 + 1),
        out_shape=[one, one] + [two] * (count // 2 - 1),
        scratch_shapes=staging(count, rows, width),
        compiler_params=params(),
        name="cut_pairs",
    )(me, *in_hbm(projected, *after))


def forward_kernel(parts, *refs):
    dst = refs[-4]
    moves = []
    for pair in refs[:parts]:
        width = pair.shape[1] // 2
        at = len(moves) * width
        moves.append((pair.at[:, width:], dst.at[:, at : at + width]))
    staged(moves, *refs[-3:])


def forward(pairs, after):
    rows, width = pairs[0].shape
    anywhere = pl.BlockSpec(memory_space=pl.ANY)
    return pl.pallas_call(
        functools.partial(forward_kernel, len(pairs)),
        in_specs=[anywhere] * (len(pairs) + len(after)),
        out_specs=anywhere,
        out_shape=pltpu.HBM((rows, len(pairs) * width // 2), bf16),
        scratch_shapes=staging(len(pairs), rows, width // 2),
        compiler_params=params(),
        name="forward",
    )(*pairs, *in_hbm(*after))


def join_kernel(count, parts, me_ref, passed, *refs):
    each = count // 2 + 1
    dst = refs[-4]
    me = me_ref[0]
    moves = []
    for p in range(parts):
        own, near, *pairs = refs[p * each : (p + 1) * each]
        width = own.shape[1]
        sources = [own, near]
        for j, pair in enumerate(pairs):
            at = (p * len(pairs) + j) * width
            sources += [pair.at[:, :width], passed.at[:, at : at + width]]
        lanes = slice(p * width, (p + 1) * width)
        moves += [(source, dst.at[me ^ k, :, lanes]) for k, source in enumerate(sources)]
    staged(moves, *refs[-3:])


def join(me, passed, parts, after):
    count = 2 * len(parts[0]) - 2
    rows, width = parts[0][0].shape
    anywhere = pl.BlockSpec(memory_space=pl.ANY)
    args = [passed, *(array for part in parts for array in part), *in_hbm(*after)]
    return pl.pallas_call(
        functools.partial(join_kernel, count, len(parts)),
        in_specs=[pl.BlockSpec(memory_space=pltpu.SMEM)] + [anywhere] * len(args),
        out_specs=anywhere,
        out_shape=pltpu.HBM((count, rows, len(parts) * width), bf16),
        scratch_shapes=staging(count * len(parts), rows, width),
        compiler_params=params(),
        name="join",
    )(me, *args)


def gather_rows(recv, prev, first, raw, rows, low, high, ahead=True, only=None):
    for s in range(recv.shape[0]):
        a = max(low - s * rows, 0) // 16 * 16
        b = min(-(-(high - s * rows) // 16) * 16, rows)
        if b <= a:
            continue
        at = s * rows + a
        raw[at : at + b - a, LANES:] = recv[s, a:b, :].astype(f32)
        if not ahead:
            continue
        if not first:
            raw[at : at + b - a, :LANES] = prev[s if only is None else 0, a:b, :].astype(f32)
            continue
        width = prev.shape[2]
        base, height = rim_rows(rows, width)
        rims = prev[s if only is None else 0, :height, :].astype(f32)
        tall = jnp.concatenate([jnp.zeros((LANES - height, width), f32), rims], axis=0)
        for j in range(-(-rows // width)):
            c, d = max(a, j * width), min(b, (j + 1) * width)
            if d <= c:
                continue
            shift = height - RIM - (rows - base) - RIM * j
            moved = (pltpu.roll(tall, shift, 0) if shift else tall).T
            raw[s * rows + c : s * rows + d, :LANES] = moved[c - j * width : d - j * width]


def band():
    row = lax.broadcasted_iota(jnp.int32, (2 * LANES, 3 * LANES), 0)
    col = lax.broadcasted_iota(jnp.int32, (2 * LANES, 3 * LANES), 1)
    tap = col // LANES
    return jnp.where(row == col - tap * LANES + LANES - 3 + tap, 1.0, 0.0).astype(bf16)


def shift_rows(raw, low, shifted, at):
    low[...] = raw[at : at + low.shape[0], :].astype(bf16)
    picks = band()
    for i in range(BLOCK // LANES):
        window = low[:, i * LANES : (i + 2) * LANES]
        shifted[i] = jnp.dot(window, picks, preferred_element_type=f32)


def conv_tile(raw, shifted, w, at, r):
    rows = slice(r, r + HEAD_DIM)
    taps = [jnp.broadcast_to(w[0, rows, k : k + 1], (HEAD_DIM, LANES)) for k in range(4)]
    parts = []
    for i in range(BLOCK // LANES):
        summed = None
        for k in range(3):
            part = taps[k] * shifted[i, rows, k * LANES : (k + 1) * LANES]
            summed = part if summed is None else summed + part
        own = raw[at + r : at + r + HEAD_DIM, (i + 1) * LANES : (i + 2) * LANES]
        parts.append(silu(summed + taps[3] * own).astype(bf16))
    return jnp.concatenate(parts, axis=1)


def state_kernel(dims, first, last, recv, *refs):
    spg, rows, heads, span, piece_heads = dims
    prev, refs = refs[0], refs[1:]
    w, bias, a_log, state_in, lead_in = refs[:5]
    xact, bmap, run_out, dt_out, cum_out, state_out, lead_out = refs[-11:-4]
    raw, xw, low, shifted = refs[-4:]
    steps = 2 * span + 2 * STATE_WIDTH

    gather_rows(recv, prev, first, raw, rows, steps, steps + heads, False)
    gather_rows(recv, prev, first, raw, rows, span, 2 * span + STATE_WIDTH)
    dt = softplus(raw[steps : steps + heads, LANES:] + bias[0])
    log_decay = -jnp.exp(a_log[0]) * dt
    lane = lax.broadcasted_iota(jnp.int32, (heads, BLOCK), 1)
    run = log_decay
    shift = 1
    while shift < BLOCK:
        run = run + jnp.where(lane >= shift, pltpu.roll(run, shift, 1), 0.0)
        shift *= 2
    final = run[:, BLOCK - 1 :]
    scale = jnp.exp(final - run) * dt
    cum = run + lead_in[0][:, :1]
    run_out[0] = run
    dt_out[0] = dt
    cum_out[0] = cum
    lead = jnp.broadcast_to(cum[:, BLOCK - 1 :], (heads, LANES))
    lead_out[0] = lead
    keep = jnp.broadcast_to(jnp.exp(final), (heads, LANES))

    shift_rows(raw, low, shifted, span)
    for r in range(0, STATE_WIDTH, HEAD_DIM):
        bmap[0, r : r + HEAD_DIM, :] = conv_tile(raw, shifted, w, span, span + r)
    for h in range(heads):
        r = h * HEAD_DIM
        tile = conv_tile(raw, shifted, w, span, r)
        xact[0, r : r + HEAD_DIM, :] = tile
        xw[r : r + HEAD_DIM, :] = (tile.astype(f32) * scale[h : h + 1, :]).astype(bf16)
    update = lax.dot_general(xw[...], bmap[0], NT, preferred_element_type=f32)
    for h in range(heads):
        r = h * HEAD_DIM
        new = update[r : r + HEAD_DIM, :]
        if not first:
            new = keep[h : h + 1, :] * state_in[0, r : r + HEAD_DIM, :] + new
        if last:
            at = (h % piece_heads) * HEAD_DIM
            state_out[h // piece_heads, at : at + HEAD_DIM, :] = new.astype(bf16)
        else:
            state_out[0, r : r + HEAD_DIM, :] = new
    if last:
        high, low = split(jnp.exp(lead))
        fill = jnp.zeros((8 - piece_heads, LANES), f32)
        for i in range(heads // piece_heads):
            mine = slice(i * piece_heads, (i + 1) * piece_heads)
            parts = [high[mine].astype(f32), fill, low[mine].astype(f32), fill]
            at = piece_heads * HEAD_DIM
            state_out[i, at : at + 16, :] = jnp.concatenate(parts, axis=0).astype(bf16)


def chunk_specs(got, chunk, dims, only=None):
    spg, rows = dims[:2]
    slabs = spg if only is None else 1

    def ahead(source, shape, row, lane):
        def index(g):
            return (g if only is None else g * spg + only, row, lane)

        return source, pl.BlockSpec((slabs,) + shape, index)

    def lane_of(block):
        first, middle, last = got
        ahead_of = first.shape[2] // BLOCK
        if block < ahead_of:
            return first, block
        return (middle if block == ahead_of else last), 0

    source, at = lane_of(chunk)
    block = pl.BlockSpec((spg, source.shape[1], BLOCK), lambda g: (g, 0, at))
    if chunk == 0:
        width = source.shape[2]
        prev, prev_spec = ahead(source, (16, width), rim_rows(rows, width)[0] // 16, 0)
    else:
        prev, place = lane_of(chunk - 1)
        lane = (place + 1) * (BLOCK // LANES) - 1
        prev, prev_spec = ahead(prev, (prev.shape[1], LANES), 0, lane)
    return [source, prev], [block, prev_spec]


def state_chunk(chunk, chunks, got, w, bias, a_log, state, lead, before, dims):
    spg, rows, heads, span, piece_heads = dims
    groups = w.shape[0]
    last = chunk == chunks - 1
    if last:
        packed = piece_heads * HEAD_DIM + 16
        state_shape = pltpu.HBM((groups * spg, packed, STATE_WIDTH), bf16)
        state_spec = pl.BlockSpec((spg, packed, STATE_WIDTH), lambda g: (g, 0, 0))
    else:
        state_shape = pltpu.HBM((groups, span, STATE_WIDTH), f32)
        state_spec = per_group(span, STATE_WIDTH)

    def out(dtype, *shape):
        return pltpu.HBM((groups,) + shape, dtype)

    args, specs = chunk_specs(got, chunk, dims)
    args[1:] = in_hbm(args[1])
    args[:1] = in_vmem(args[0]) if last else in_hbm(args[0])
    after = in_hbm(*before)
    return pl.pallas_call(
        functools.partial(state_kernel, dims, chunk == 0, last),
        grid=(groups,),
        in_specs=specs
        + [
            per_group(span + STATE_WIDTH, 4),
            per_group(heads, 1),
            per_group(heads, 1),
            per_group(span, STATE_WIDTH),
            per_group(heads, LANES),
        ]
        + [pl.BlockSpec(memory_space=pl.ANY)] * len(after),
        out_specs=[
            per_group(span, BLOCK),
            per_group(STATE_WIDTH, BLOCK),
            per_group(heads, BLOCK),
            per_group(heads, BLOCK),
            per_group(heads, BLOCK),
            state_spec,
            per_group(heads, LANES),
        ],
        out_shape=[
            out(bf16, span, BLOCK),
            out(bf16, STATE_WIDTH, BLOCK),
            out(f32, heads, BLOCK),
            out(f32, heads, BLOCK),
            out(f32, heads, BLOCK),
            state_shape,
            out(f32, heads, LANES),
        ],
        scratch_shapes=[
            pltpu.VMEM((rows * spg, LANES + BLOCK), f32),
            pltpu.VMEM((span, BLOCK), bf16),
            pltpu.VMEM((span + STATE_WIDTH, LANES + BLOCK), bf16),
            pltpu.VMEM((BLOCK // LANES, span + STATE_WIDTH, 3 * LANES), f32),
        ],
        compiler_params=params(48 if last else 60),
        cost_estimate=pl.CostEstimate(flops=4 * 10**9, bytes_accessed=10**7, transcendentals=10**6),
        name="state_chunk",
    )(*args, *in_hbm(w, bias, a_log, state, lead), *after)


def split(v):
    high = v.astype(bf16)
    return high, (v - high.astype(f32)).astype(bf16)


def block_kernel(dims, first, recv, *refs):
    spg, rows, heads, span, piece_heads = dims
    prev, refs = refs[0], refs[1:]
    w, xact, bmap, run_ref, dt_ref, cum_ref, state, skip = refs[:8]
    mixed, gate_out, side, token, raw, low, shifted = refs[-7:]
    at_c = 2 * span + STATE_WIDTH
    gather_rows(recv, prev, first, raw, rows, at_c, at_c + STATE_WIDTH, True, at_c // rows)
    gather_rows(recv, prev, first, raw, rows, 0, span, False)
    token[0] = cum_ref[0, :8, :LANES]
    shift_rows(raw, low, shifted, at_c)
    c = [conv_tile(raw, shifted, w, at_c, r) for r in range(0, STATE_WIDTH, HEAD_DIM)]
    c = jnp.concatenate(c, axis=0)
    b_rows = bmap[0].astype(f32).T.astype(bf16)
    scores = jnp.dot(b_rows, c, preferred_element_type=f32)
    src = lax.broadcasted_iota(jnp.int32, (HALF, HALF), 0)
    dst = lax.broadcasted_iota(jnp.int32, (HALF, HALF), 1)
    causal = src <= dst
    s00 = jnp.where(causal, scores[:HALF, :HALF], 0.0)
    s01 = scores[:HALF, HALF:]
    s11 = jnp.where(causal, scores[HALF:, HALF:], 0.0)
    r = run_ref[0] * LOG2E
    q = (r - jnp.log(dt_ref[0]) * LOG2E).T
    if not first:
        cc = jnp.concatenate([c, c], axis=0)
        entered = jnp.exp2(r)
    reach = [part.astype(f32) for part in split(jnp.exp(cum_ref[0]))]
    reach.append(jnp.zeros((STATE_WIDTH - 2 * heads, BLOCK), f32))
    side[0, :, :STATE_WIDTH] = c.astype(f32).T.astype(bf16)
    side[0, :, STATE_WIDTH:] = jnp.concatenate(reach, axis=0).T.astype(bf16)
    turned = []
    for h in range(heads):
        at = h * HEAD_DIM
        r0, r1 = r[h : h + 1, :HALF], r[h : h + 1, HALF:]
        q0, q1 = q[:HALF, h : h + 1], q[HALF:, h : h + 1]
        w00 = (s00 * jnp.exp2(jnp.minimum(r0 - q0, CAP))).astype(bf16)
        w01 = (s01 * jnp.exp2(r1 - q0)).astype(bf16)
        w11 = (s11 * jnp.exp2(jnp.minimum(r1 - q1, CAP))).astype(bf16)
        x = xact[0, at : at + HEAD_DIM, :]
        y0 = jnp.dot(x[:, :HALF], w00, preferred_element_type=f32)
        y1 = jnp.dot(x, jnp.concatenate([w01, w11], axis=0), preferred_element_type=f32)
        y = jnp.concatenate([y0, y1], axis=1) + skip[0, h : h + 1, :] * x.astype(f32)
        if not first:
            if at % WIDE == 0:
                both = jnp.concatenate(split(state[0, at : at + WIDE, :]), axis=1)
                carried = jnp.dot(both, cc, preferred_element_type=f32)
            y = y + entered[h : h + 1, :] * carried[at % WIDE : at % WIDE + HEAD_DIM, :]
        gate = raw[at : at + HEAD_DIM, LANES:]
        turned.append((y * silu(gate), gate))
        if len(turned) * HEAD_DIM == LANES:
            lanes = slice(at + HEAD_DIM - LANES, at + HEAD_DIM)
            mixed[0, :, lanes] = jnp.concatenate([pair[0] for pair in turned], axis=0).T
            wide = jnp.concatenate([pair[1] for pair in turned], axis=0).T
            gate_out[0, :, lanes] = wide.astype(bf16)
            turned = []


def block_chunk(
    chunk, chunks, got, w, xact, bmap, run, dt, cum, state, skip, after, dims
):
    spg, rows, heads, span, piece_heads = dims
    groups = w.shape[0]

    at_c = 2 * span + STATE_WIDTH
    one = at_c // rows
    assert (at_c + STATE_WIDTH - 1) // rows == one
    args, specs = chunk_specs(got, chunk, dims, one)
    args = in_hbm(*args)
    args += in_hbm(w, xact, bmap, run, dt, cum, state, skip)
    specs += [
        pl.BlockSpec((1, STATE_WIDTH, 4), lambda g: (g, span // STATE_WIDTH + 1, 0)),
        per_group(span, BLOCK),
        per_group(STATE_WIDTH, BLOCK),
        per_group(heads, BLOCK),
        per_group(heads, BLOCK),
        per_group(heads, BLOCK),
        per_group(span, STATE_WIDTH),
        per_group(heads, 1),
    ]
    args += in_vmem(*after)
    specs += [pl.BlockSpec(memory_space=pl.ANY)] * len(after)

    def out(dtype, *shape):
        return pltpu.HBM((groups,) + shape, dtype)

    return pl.pallas_call(
        functools.partial(block_kernel, dims, chunk == 0),
        grid=(groups,),
        in_specs=specs,
        out_specs=[
            per_group(BLOCK, span),
            per_group(BLOCK, span),
            per_group(BLOCK, 2 * STATE_WIDTH),
            per_group(8, LANES),
        ],
        out_shape=[
            out(f32, BLOCK, span),
            out(bf16, BLOCK, span),
            out(bf16, BLOCK, 2 * STATE_WIDTH),
            out(f32, 8, LANES),
        ],
        scratch_shapes=[
            pltpu.VMEM((rows * spg, LANES + BLOCK), f32),
            pltpu.VMEM((STATE_WIDTH, LANES + BLOCK), bf16),
            pltpu.VMEM((BLOCK // LANES, STATE_WIDTH, 3 * LANES), f32),
        ],
        compiler_params=params(),
        cost_estimate=pl.CostEstimate(flops=4 * 10**9, bytes_accessed=10**7, transcendentals=10**6),
        name="block_chunk",
    )(*args)


def relay_kernel(piece_heads, src, token, dst):
    rows = piece_heads * HEAD_DIM
    held = jnp.zeros((rows, STATE_WIDTH), f32)
    for d in range(src.shape[0]):
        dst[d] = held.T.astype(bf16)
        both = src[d, rows:, :].astype(f32)
        decay = both[:8] + both[8:]
        spread = [
            jnp.broadcast_to(decay[h : h + 1, :], (HEAD_DIM, STATE_WIDTH))
            for h in range(piece_heads)
        ]
        held = jnp.concatenate(spread, axis=0) * held + src[d, :rows, :].astype(f32)


def relay(packed, token, piece_heads):
    count = packed.shape[0]
    rows = piece_heads * HEAD_DIM
    return pl.pallas_call(
        functools.partial(relay_kernel, piece_heads),
        in_specs=[pl.BlockSpec(memory_space=pltpu.VMEM), pl.BlockSpec(memory_space=pl.ANY)],
        out_shape=pltpu.VMEM((count, STATE_WIDTH, rows), bf16),
        compiler_params=params(16),
        name="relay",
    )(packed, *in_hbm(token))


def final_kernel(chunks, groups, *refs):
    mixed, gates, sides = (refs[i * chunks : (i + 1) * chunks] for i in range(3))
    state, gain, out = refs[3 * chunks : 3 * chunks + 3]
    held, gate_held, side_held, kept, done, sems, out_sems = refs[3 * chunks + 3 :]
    span = held.shape[2]
    piece = state.shape[2]
    spg = state.shape[0] // groups
    heads = span // HEAD_DIM
    steps = [(g, c) for g in range(groups) for c in range(chunks)]

    def loads(i):
        g, c = steps[i]
        slot = i
        moves = []
        moves.append((sides[c].at[g], side_held.at[slot]))
        moves.append((mixed[c].at[g], held.at[slot]))
        moves.append((gates[c].at[g], gate_held.at[slot]))
        return [
            pltpu.make_async_copy(a, b, sems.at[slot, j]) for j, (a, b) in enumerate(moves)
        ]

    def store(i):
        g, c = steps[i]
        return pltpu.make_async_copy(
            done.at[i % 2],
            out.at[c * BLOCK : (c + 1) * BLOCK, g * span : (g + 1) * span],
            out_sems.at[i % 2],
        )

    for i in range(len(steps)):
        for move in loads(i):
            move.start()
    row = lax.broadcasted_iota(jnp.int32, (STATE_WIDTH, span), 0)
    col = lax.broadcasted_iota(jnp.int32, (STATE_WIDTH, span), 1) // HEAD_DIM
    spread = jnp.where((row == col) | (row == col + heads), 1.0, 0.0).astype(bf16)
    for i, (g, c) in enumerate(steps):
        slot = i
        for move in loads(i):
            move.wait()
        if i >= 2:
            store(i - 2).wait()
        side = side_held[slot]
        half = BLOCK // 2
        for q in range(0, BLOCK, half):
            rows = slice(q, q + half)
            total = jnp.zeros((half, LANES), f32)
            for j in range(spg):
                piece_lanes = slice(j * piece, (j + 1) * piece)
                part = jnp.dot(
                    side[rows, :STATE_WIDTH], state[g * spg + j], preferred_element_type=f32
                )
                reach = jnp.dot(
                    side[rows, STATE_WIDTH:], spread[:, piece_lanes], preferred_element_type=f32
                )
                gate = silu(gate_held[slot, rows, piece_lanes].astype(f32))
                v = held[slot, rows, piece_lanes] + gate * (part * reach)
                kept[rows, piece_lanes] = v
                for at in range(0, piece, LANES):
                    t = v[:, at : at + LANES]
                    if piece < LANES:
                        t = jnp.concatenate([t, jnp.zeros((half, LANES - piece), f32)], axis=1)
                    total = total + t * t
            mean = jnp.sum(total, axis=1, keepdims=True) * (1.0 / span)
            factor = lax.rsqrt(mean + EPSILON)
            for at in range(0, span, LANES):
                lanes = slice(at, at + LANES)
                scaled = kept[rows, lanes] * factor * gain[g, :, lanes]
                done[i % 2, rows, lanes] = scaled.astype(bf16)
        store(i).start()
    for i in range(max(len(steps) - 2, 0), len(steps)):
        store(i).wait()


def finish(mixed, gates, sides, state, gain):
    chunks = len(mixed)
    groups, _, span = mixed[0].shape
    steps = groups * chunks
    anywhere = pl.BlockSpec(memory_space=pl.ANY)
    within = pl.BlockSpec(memory_space=pltpu.VMEM)
    return pl.pallas_call(
        functools.partial(final_kernel, chunks, groups),
        in_specs=[anywhere] * (3 * chunks) + [within] * 2,
        out_specs=anywhere,
        out_shape=jax.ShapeDtypeStruct((chunks * BLOCK, groups * span), bf16),
        scratch_shapes=[
            pltpu.VMEM((steps, BLOCK, span), f32),
            pltpu.VMEM((steps, BLOCK, span), bf16),
            pltpu.VMEM((steps, BLOCK, 2 * STATE_WIDTH), bf16),
            pltpu.VMEM((BLOCK, span), f32),
            pltpu.VMEM((2, BLOCK, span), bf16),
            pltpu.SemaphoreType.DMA((steps, 3)),
            pltpu.SemaphoreType.DMA((2,)),
        ],
        compiler_params=params(40),
        name="finish",
    )(*in_hbm(*mixed, *gates, *sides), state, gain)


def swap(array, k):
    count = lax.axis_size("seq")
    return lax.ppermute(array, "seq", [(i, i ^ k) for i in range(count)])


def exchange(array):
    return lax.all_to_all(array, "seq", split_axis=0, concat_axis=0, tiled=True)


def per_device(projected, conv_weight, dt_bias, a_log, d_skip, norm_gain):
    seq_count = lax.axis_size("seq")
    groups = conv_weight.shape[1]
    heads = dt_bias.shape[0] // groups
    span = heads * HEAD_DIM
    rows, all_tokens = projected.shape
    local_tokens = all_tokens // seq_count
    chunks = local_tokens // BLOCK
    spg = seq_count // groups
    piece_heads = groups * heads // seq_count
    dims = (spg, rows, heads, span, piece_heads)

    w = jnp.transpose(conv_weight, (1, 2, 0))
    bias = dt_bias.reshape(groups, heads, 1)
    rate = a_log.reshape(groups, heads, 1)
    skip = d_skip.reshape(groups, heads, 1)
    gain = norm_gain.reshape(groups, 1, span)
    state = jnp.zeros((groups, span, STATE_WIDTH), f32)
    lead = jnp.zeros((groups, heads, LANES), f32)

    me = lax.axis_index("seq").astype(jnp.int32).reshape(1)
    assert chunks > 2 and seq_count & (seq_count - 1) == 0
    middle, split_at = local_tokens - 2 * BLOCK, local_tokens - BLOCK

    def send(low, after):
        own, near, *pairs = cut_pairs(projected, me, seq_count, low, low + HALF, after)
        pairs = [swap(pair, 2 * j + 2) for j, pair in enumerate(pairs)]
        return [own, swap(near, 1), *pairs]

    parts = [send(middle, [])]
    cut = cut_first(projected, seq_count, middle)
    got = [exchange(cut)]
    parts.append(send(middle + HALF, [cut, *parts[0][1:]]))
    ready = [parts[1][0], w, bias, rate, skip, gain, state, lead]
    cut = cut_block(projected, seq_count, split_at, ready)
    got += [None, exchange(cut)]

    results, tokens = [], []
    for c in range(chunks):
        before = []
        if c == chunks - 2:
            pairs = [pair for part in parts for pair in part[2:]]
            passed = swap(forward(pairs, [lead, tokens[0], cut]), 1)
            got[1] = join(me, passed, parts, tokens)
        if c == chunks - 1:
            before = tokens[-2:-1]
        xact, bmap, run, dt, cum, new, lead = state_chunk(
            c, chunks, got, w, bias, rate, state, lead, before, dims
        )
        after = []
        if c == chunks - 1:
            entering = relay(exchange(new), tokens[-1], piece_heads)
            after = [entering]
        *result, token = block_chunk(
            c, chunks, got, w, xact, bmap, run, dt, cum, state, skip, after, dims
        )
        results.append(result)
        tokens.append(token)
        state = new
    return finish(*zip(*results), exchange(entering), gain)


def solution(mesh):
    in_specs = (P(("tp", "seq"), None), P(None, "tp", None), P("tp"), P("tp"), P("tp"), P("tp"))
    return jax.shard_map(
        per_device, mesh=mesh, in_specs=in_specs, out_specs=P("seq", "tp"), check_vma=False
    )
```

```python
import functools

import jax
import jax.numpy as jnp
from jax import lax
from jax.experimental import pallas as pl
from jax.experimental.pallas import tpu as pltpu
from jax.sharding import PartitionSpec as P

HEAD_DIM = 64
STATE_WIDTH = 128
BLOCK = 256
LANES = 128
HALF = BLOCK // 2
WIDE = 256
LOG2E = 1.4426950408889634
CAP = 80.0
EPSILON = 1e-05

f32 = jnp.float32
bf16 = jnp.bfloat16
NT = (((1,), (1,)), ((), ()))


def params(mib=60):
    return pltpu.CompilerParams(vmem_limit_bytes=mib * 2**20)


def silu(v):
    half = 0.5 * v
    return half + half * jnp.tanh(half)


def softplus(v):
    e = jnp.exp(-jnp.abs(v))
    u = 1.0 + e
    gap = u - 1.0
    tiny = gap == 0.0
    log_part = jnp.where(tiny, e, jnp.log(u) * (e / jnp.where(tiny, 1.0, gap)))
    return jnp.maximum(v, 0.0) + log_part


def in_hbm(*arrays):
    return [pltpu.with_memory_space_constraint(array, pltpu.HBM) for array in arrays]


def in_vmem(*arrays):
    return [pltpu.with_memory_space_constraint(array, pltpu.VMEM) for array in arrays]


def per_group(*shape):
    return pl.BlockSpec((1,) + shape, lambda g: (g,) + (0,) * len(shape))


RIM = 4


def rim_rows(rows, width):
    base = rows // 16 * 16
    height = -(-(rows - base + RIM * -(-rows // width)) // 8) * 8
    assert height <= 16
    return base, height


def first_kernel(src, token, dst, held, windows, ends, rims, in_sems, rim_sems, out_sems, end_sems):
    rows, all_tokens = src.shape
    count, _, width = dst.shape
    tokens = all_tokens // count
    base, height = rim_rows(rows, width)

    def fetch(d):
        at = d * tokens
        return pltpu.make_async_copy(src.at[:, at : at + width], held.at[d], in_sems.at[d])

    def window(d):
        at = d * tokens - LANES
        return pltpu.make_async_copy(src.at[:, at : at + LANES], windows.at[d], rim_sems.at[d])

    def place(d):
        return pltpu.make_async_copy(
            held.at[d, :base, :], dst.at[d, :base, :], out_sems.at[d]
        )

    def place_end(d):
        return pltpu.make_async_copy(
            ends.at[d], dst.at[d, base : base + height, :], end_sems.at[d]
        )

    for d in range(1, count):
        window(d).start()
    for d in range(count):
        fetch(d).start()
    row = lax.broadcasted_iota(jnp.int32, (height, LANES), 0) - (rows - base)
    col = lax.broadcasted_iota(jnp.int32, (height, LANES), 1)
    hit = (row >= 0) & (col == lax.rem(row + 16, RIM) + LANES - RIM)
    pick = jnp.where(hit, 1.0, 0.0).astype(bf16)
    which = lax.broadcasted_iota(jnp.int32, (height, width), 0) - (rows - base)
    for d in range(count):
        merged = jnp.zeros((height, width), f32)
        if d:
            window(d).wait()
            every = lax.dot_general(pick, windows[d], NT, preferred_element_type=f32)
            for j in range(-(-rows // width)):
                part = every[:, j * width : min((j + 1) * width, rows)]
                if part.shape[1] < width:
                    fill = jnp.zeros((height, width - part.shape[1]), f32)
                    part = jnp.concatenate([part, fill], axis=1)
                merged = jnp.where((which >= RIM * j) & (which < RIM * (j + 1)), part, merged)
        rims[d] = merged
    for d in range(count):
        fetch(d).wait()
        place(d).start()
    for d in range(count):
        end = held[d, base:rows, :].astype(f32)
        end = jnp.concatenate([end, jnp.zeros((height - end.shape[0], width), f32)], axis=0)
        ends[d] = (end + rims[d]).astype(bf16)
        place_end(d).start()
    for d in range(count):
        place(d).wait()
        place_end(d).wait()


def cut_first(projected, count, width, token):
    rows = projected.shape[0]
    base, height = rim_rows(rows, width)
    sems = pltpu.SemaphoreType.DMA((count,))
    anywhere = pl.BlockSpec(memory_space=pl.ANY)
    return pl.pallas_call(
        first_kernel,
        in_specs=[anywhere] * 2,
        out_specs=anywhere,
        out_shape=pltpu.HBM((count, base + height, width), bf16),
        scratch_shapes=[
            pltpu.VMEM((count, rows, width), bf16),
            pltpu.VMEM((count, rows, LANES), bf16),
            pltpu.VMEM((count, height, width), bf16),
            pltpu.VMEM((count, height, width), f32),
            sems,
            sems,
            sems,
            sems,
        ],
        compiler_params=params(),
        name="cut_first",
    )(*in_hbm(projected, token))


def staged(moves, held, in_sems, out_sems):
    for i, (source, _) in enumerate(moves):
        pltpu.make_async_copy(source, held.at[i], in_sems.at[i]).start()
    for i, (source, target) in enumerate(moves):
        pltpu.make_async_copy(source, held.at[i], in_sems.at[i]).wait()
        pltpu.make_async_copy(held.at[i], target, out_sems.at[i]).start()
    for i, (_, target) in enumerate(moves):
        pltpu.make_async_copy(held.at[i], target, out_sems.at[i]).wait()


def staging(count, rows, width):
    sems = pltpu.SemaphoreType.DMA((count,))
    return [pltpu.VMEM((count, rows, width), bf16), sems, sems]


def cut_kernel(low, count, src, *refs):
    dst = refs[-4]
    tokens = src.shape[1] // count
    moves = []
    for d in range(count):
        at = d * tokens + low
        moves.append((src.at[:, at : at + BLOCK], dst.at[d]))
    staged(moves, *refs[-3:])


def cut_block(projected, count, low, after):
    rows = projected.shape[0]
    args = in_hbm(projected, *after)
    anywhere = pl.BlockSpec(memory_space=pl.ANY)
    return pl.pallas_call(
        functools.partial(cut_kernel, low, count),
        in_specs=[anywhere] * len(args),
        out_specs=anywhere,
        out_shape=pltpu.HBM((count, rows, BLOCK), bf16),
        scratch_shapes=staging(count, rows, BLOCK),
        compiler_params=params(),
        name="cut_block",
    )(*args)


def pairs_kernel(low, count, me_ref, src, *refs):
    own, near, *far = refs[-(count // 2 + 4) : -3]
    tokens = src.shape[1] // count
    width = own.shape[1]
    me = me_ref[0]
    targets = [own, near]
    for pair in far:
        targets += [pair.at[:, :width], pair.at[:, width:]]
    moves = []
    for k, target in enumerate(targets):
        at = pl.multiple_of((me ^ k) * tokens + low, LANES)
        moves.append((src.at[:, pl.ds(at, width)], target))
    staged(moves[2:] + moves[:2], *refs[-3:])


def cut_pairs(projected, me, count, low, high, after):
    rows = projected.shape[0]
    anywhere = pl.BlockSpec(memory_space=pl.ANY)
    width = high - low
    one, two = pltpu.HBM((rows, width), bf16), pltpu.HBM((rows, 2 * width), bf16)
    return pl.pallas_call(
        functools.partial(pairs_kernel, low, count),
        in_specs=[pl.BlockSpec(memory_space=pltpu.SMEM)] + [anywhere] * (1 + len(after)),
        out_specs=[anywhere] * (count // 2 + 1),
        out_shape=[one, one] + [two] * (count // 2 - 1),
        scratch_shapes=staging(count, rows, width),
        compiler_params=params(),
        name="cut_pairs",
    )(me, *in_hbm(projected, *after))


def forward_kernel(parts, *refs):
    dst = refs[-4]
    moves = []
    for pair in refs[:parts]:
        width = pair.shape[1] // 2
        at = len(moves) * width
        moves.append((pair.at[:, width:], dst.at[:, at : at + width]))
    staged(moves, *refs[-3:])


def forward(pairs, after):
    rows, width = pairs[0].shape
    anywhere = pl.BlockSpec(memory_space=pl.ANY)
    return pl.pallas_call(
        functools.partial(forward_kernel, len(pairs)),
        in_specs=[anywhere] * (len(pairs) + len(after)),
        out_specs=anywhere,
        out_shape=pltpu.HBM((rows, len(pairs) * width // 2), bf16),
        scratch_shapes=staging(len(pairs), rows, width // 2),
        compiler_params=params(),
        name="forward",
    )(*pairs, *in_hbm(*after))


def join_kernel(count, parts, me_ref, passed, *refs):
    each = count // 2 + 1
    dst = refs[-4]
    me = me_ref[0]
    moves = []
    for p in range(parts):
        own, near, *pairs = refs[p * each : (p + 1) * each]
        width = own.shape[1]
        sources = [own, near]
        for j, pair in enumerate(pairs):
            at = (p * len(pairs) + j) * width
            sources += [pair.at[:, :width], passed.at[:, at : at + width]]
        lanes = slice(p * width, (p + 1) * width)
        moves += [(source, dst.at[me ^ k, :, lanes]) for k, source in enumerate(sources)]
    staged(moves, *refs[-3:])


def join(me, passed, parts, after):
    count = 2 * len(parts[0]) - 2
    rows, width = parts[0][0].shape
    anywhere = pl.BlockSpec(memory_space=pl.ANY)
    args = [passed, *(array for part in parts for array in part), *in_hbm(*after)]
    return pl.pallas_call(
        functools.partial(join_kernel, count, len(parts)),
        in_specs=[pl.BlockSpec(memory_space=pltpu.SMEM)] + [anywhere] * len(args),
        out_specs=anywhere,
        out_shape=pltpu.HBM((count, rows, len(parts) * width), bf16),
        scratch_shapes=staging(count * len(parts), rows, width),
        compiler_params=params(),
        name="join",
    )(me, *args)


def gather_rows(recv, prev, first, raw, rows, low, high, ahead=True, only=None):
    for s in range(recv.shape[0]):
        a = max(low - s * rows, 0) // 16 * 16
        b = min(-(-(high - s * rows) // 16) * 16, rows)
        if b <= a:
            continue
        at = s * rows + a
        raw[at : at + b - a, LANES:] = recv[s, a:b, :].astype(f32)
        if not ahead:
            continue
        if not first:
            raw[at : at + b - a, :LANES] = prev[s if only is None else 0, a:b, :].astype(f32)
            continue
        width = prev.shape[2]
        base, height = rim_rows(rows, width)
        rims = prev[s if only is None else 0, :height, :].astype(f32)
        tall = jnp.concatenate([jnp.zeros((LANES - height, width), f32), rims], axis=0)
        for j in range(-(-rows // width)):
            c, d = max(a, j * width), min(b, (j + 1) * width)
            if d <= c:
                continue
            shift = height - RIM - (rows - base) - RIM * j
            moved = (pltpu.roll(tall, shift, 0) if shift else tall).T
            raw[s * rows + c : s * rows + d, :LANES] = moved[c - j * width : d - j * width]


def band():
    row = lax.broadcasted_iota(jnp.int32, (2 * LANES, 3 * LANES), 0)
    col = lax.broadcasted_iota(jnp.int32, (2 * LANES, 3 * LANES), 1)
    tap = col // LANES
    return jnp.where(row == col - tap * LANES + LANES - 3 + tap, 1.0, 0.0).astype(bf16)


def shift_rows(raw, low, shifted, at):
    low[...] = raw[at : at + low.shape[0], :].astype(bf16)
    picks = band()
    for i in range(BLOCK // LANES):
        window = low[:, i * LANES : (i + 2) * LANES]
        shifted[i] = jnp.dot(window, picks, preferred_element_type=f32)


def conv_tile(raw, shifted, w, at, r):
    rows = slice(r, r + HEAD_DIM)
    taps = [jnp.broadcast_to(w[0, rows, k : k + 1], (HEAD_DIM, LANES)) for k in range(4)]
    parts = []
    for i in range(BLOCK // LANES):
        summed = None
        for k in range(3):
            part = taps[k] * shifted[i, rows, k * LANES : (k + 1) * LANES]
            summed = part if summed is None else summed + part
        own = raw[at + r : at + r + HEAD_DIM, (i + 1) * LANES : (i + 2) * LANES]
        parts.append(silu(summed + taps[3] * own).astype(bf16))
    return jnp.concatenate(parts, axis=1)


def state_kernel(dims, first, last, recv, *refs):
    spg, rows, heads, span, piece_heads = dims
    prev, refs = refs[0], refs[1:]
    w, bias, a_log, state_in, lead_in = refs[:5]
    xact, bmap, run_out, dt_out, cum_out, state_out, lead_out = refs[-11:-4]
    raw, xw, low, shifted = refs[-4:]
    steps = 2 * span + 2 * STATE_WIDTH

    gather_rows(recv, prev, first, raw, rows, steps, steps + heads, False)
    gather_rows(recv, prev, first, raw, rows, span, 2 * span + STATE_WIDTH)
    dt = softplus(raw[steps : steps + heads, LANES:] + bias[0])
    log_decay = -jnp.exp(a_log[0]) * dt
    lane = lax.broadcasted_iota(jnp.int32, (heads, BLOCK), 1)
    run = log_decay
    shift = 1
    while shift < BLOCK:
        run = run + jnp.where(lane >= shift, pltpu.roll(run, shift, 1), 0.0)
        shift *= 2
    final = run[:, BLOCK - 1 :]
    scale = jnp.exp(final - run) * dt
    cum = run + lead_in[0][:, :1]
    run_out[0] = run
    dt_out[0] = dt
    cum_out[0] = cum
    lead = jnp.broadcast_to(cum[:, BLOCK - 1 :], (heads, LANES))
    lead_out[0] = lead
    keep = jnp.broadcast_to(jnp.exp(final), (heads, LANES))

    shift_rows(raw, low, shifted, span)
    for r in range(0, STATE_WIDTH, HEAD_DIM):
        bmap[0, r : r + HEAD_DIM, :] = conv_tile(raw, shifted, w, span, span + r)
    for h in range(heads):
        r = h * HEAD_DIM
        tile = conv_tile(raw, shifted, w, span, r)
        xact[0, r : r + HEAD_DIM, :] = tile
        xw[r : r + HEAD_DIM, :] = (tile.astype(f32) * scale[h : h + 1, :]).astype(bf16)
    update = lax.dot_general(xw[...], bmap[0], NT, preferred_element_type=f32)
    for h in range(heads):
        r = h * HEAD_DIM
        new = update[r : r + HEAD_DIM, :]
        if not first:
            new = keep[h : h + 1, :] * state_in[0, r : r + HEAD_DIM, :] + new
        if last:
            at = (h % piece_heads) * HEAD_DIM
            state_out[h // piece_heads, at : at + HEAD_DIM, :] = new.astype(bf16)
        else:
            state_out[0, r : r + HEAD_DIM, :] = new
    if last:
        high, low = split(jnp.exp(lead))
        fill = jnp.zeros((8 - piece_heads, LANES), f32)
        for i in range(heads // piece_heads):
            mine = slice(i * piece_heads, (i + 1) * piece_heads)
            parts = [high[mine].astype(f32), fill, low[mine].astype(f32), fill]
            at = piece_heads * HEAD_DIM
            state_out[i, at : at + 16, :] = jnp.concatenate(parts, axis=0).astype(bf16)


def chunk_specs(got, chunk, dims, only=None):
    spg, rows = dims[:2]
    slabs = spg if only is None else 1

    def ahead(source, shape, row, lane):
        def index(g):
            return (g if only is None else g * spg + only, row, lane)

        return source, pl.BlockSpec((slabs,) + shape, index)

    def lane_of(block):
        first, middle, last = got
        ahead_of = first.shape[2] // BLOCK
        if block < ahead_of:
            return first, block
        return (middle if block == ahead_of else last), 0

    source, at = lane_of(chunk)
    block = pl.BlockSpec((spg, source.shape[1], BLOCK), lambda g: (g, 0, at))
    if chunk == 0:
        width = source.shape[2]
        prev, prev_spec = ahead(source, (16, width), rim_rows(rows, width)[0] // 16, 0)
    else:
        prev, place = lane_of(chunk - 1)
        lane = (place + 1) * (BLOCK // LANES) - 1
        prev, prev_spec = ahead(prev, (prev.shape[1], LANES), 0, lane)
    return [source, prev], [block, prev_spec]


def state_chunk(chunk, chunks, got, w, bias, a_log, state, lead, before, dims):
    spg, rows, heads, span, piece_heads = dims
    groups = w.shape[0]
    last = chunk == chunks - 1
    if last:
        packed = piece_heads * HEAD_DIM + 16
        state_shape = pltpu.HBM((groups * spg, packed, STATE_WIDTH), bf16)
        state_spec = pl.BlockSpec((spg, packed, STATE_WIDTH), lambda g: (g, 0, 0))
    else:
        state_shape = pltpu.HBM((groups, span, STATE_WIDTH), f32)
        state_spec = per_group(span, STATE_WIDTH)

    def out(dtype, *shape):
        return pltpu.HBM((groups,) + shape, dtype)

    args, specs = chunk_specs(got, chunk, dims)
    args[1:] = in_hbm(args[1])
    args[:1] = in_vmem(args[0]) if last else in_hbm(args[0])
    after = in_hbm(*before)
    return pl.pallas_call(
        functools.partial(state_kernel, dims, chunk == 0, last),
        grid=(groups,),
        in_specs=specs
        + [
            per_group(span + STATE_WIDTH, 4),
            per_group(heads, 1),
            per_group(heads, 1),
            per_group(span, STATE_WIDTH),
            per_group(heads, LANES),
        ]
        + [pl.BlockSpec(memory_space=pl.ANY)] * len(after),
        out_specs=[
            per_group(span, BLOCK),
            per_group(STATE_WIDTH, BLOCK),
            per_group(heads, BLOCK),
            per_group(heads, BLOCK),
            per_group(heads, BLOCK),
            state_spec,
            per_group(heads, LANES),
        ],
        out_shape=[
            out(bf16, span, BLOCK),
            out(bf16, STATE_WIDTH, BLOCK),
            out(f32, heads, BLOCK),
            out(f32, heads, BLOCK),
            out(f32, heads, BLOCK),
            state_shape,
            out(f32, heads, LANES),
        ],
        scratch_shapes=[
            pltpu.VMEM((rows * spg, LANES + BLOCK), f32),
            pltpu.VMEM((span, BLOCK), bf16),
            pltpu.VMEM((span + STATE_WIDTH, LANES + BLOCK), bf16),
            pltpu.VMEM((BLOCK // LANES, span + STATE_WIDTH, 3 * LANES), f32),
        ],
        compiler_params=params(48 if last else 60),
        cost_estimate=pl.CostEstimate(flops=4 * 10**9, bytes_accessed=10**7, transcendentals=10**6),
        name="state_chunk",
    )(*args, *in_hbm(w, bias, a_log, state, lead), *after)


def split(v):
    high = v.astype(bf16)
    return high, (v - high.astype(f32)).astype(bf16)


def block_kernel(dims, first, recv, *refs):
    spg, rows, heads, span, piece_heads = dims
    prev, refs = refs[0], refs[1:]
    w, xact, bmap, run_ref, dt_ref, cum_ref, state, skip = refs[:8]
    mixed, gate_out, side, token, raw, low, shifted = refs[-7:]
    at_c = 2 * span + STATE_WIDTH
    gather_rows(recv, prev, first, raw, rows, at_c, at_c + STATE_WIDTH, True, at_c // rows)
    gather_rows(recv, prev, first, raw, rows, 0, span, False)
    token[0] = cum_ref[0, :8, :LANES]
    shift_rows(raw, low, shifted, at_c)
    c = [conv_tile(raw, shifted, w, at_c, r) for r in range(0, STATE_WIDTH, HEAD_DIM)]
    c = jnp.concatenate(c, axis=0)
    b_rows = bmap[0].astype(f32).T.astype(bf16)
    scores = jnp.dot(b_rows, c, preferred_element_type=f32)
    src = lax.broadcasted_iota(jnp.int32, (HALF, HALF), 0)
    dst = lax.broadcasted_iota(jnp.int32, (HALF, HALF), 1)
    causal = src <= dst
    s00 = jnp.where(causal, scores[:HALF, :HALF], 0.0)
    s01 = scores[:HALF, HALF:]
    s11 = jnp.where(causal, scores[HALF:, HALF:], 0.0)
    r = run_ref[0] * LOG2E
    q = (r - jnp.log(dt_ref[0]) * LOG2E).T
    if not first:
        cc = jnp.concatenate([c, c], axis=0)
        entered = jnp.exp2(r)
    reach = [part.astype(f32) for part in split(jnp.exp(cum_ref[0]))]
    reach.append(jnp.zeros((STATE_WIDTH - 2 * heads, BLOCK), f32))
    side[0, :, :STATE_WIDTH] = c.astype(f32).T.astype(bf16)
    side[0, :, STATE_WIDTH:] = jnp.concatenate(reach, axis=0).T.astype(bf16)
    turned = []
    for h in range(heads):
        at = h * HEAD_DIM
        r0, r1 = r[h : h + 1, :HALF], r[h : h + 1, HALF:]
        q0, q1 = q[:HALF, h : h + 1], q[HALF:, h : h + 1]
        w00 = (s00 * jnp.exp2(jnp.minimum(r0 - q0, CAP))).astype(bf16)
        w01 = (s01 * jnp.exp2(r1 - q0)).astype(bf16)
        w11 = (s11 * jnp.exp2(jnp.minimum(r1 - q1, CAP))).astype(bf16)
        x = xact[0, at : at + HEAD_DIM, :]
        y0 = jnp.dot(x[:, :HALF], w00, preferred_element_type=f32)
        y1 = jnp.dot(x, jnp.concatenate([w01, w11], axis=0), preferred_element_type=f32)
        y = jnp.concatenate([y0, y1], axis=1) + skip[0, h : h + 1, :] * x.astype(f32)
        if not first:
            if at % WIDE == 0:
                both = jnp.concatenate(split(state[0, at : at + WIDE, :]), axis=1)
                carried = jnp.dot(both, cc, preferred_element_type=f32)
            y = y + entered[h : h + 1, :] * carried[at % WIDE : at % WIDE + HEAD_DIM, :]
        gate = raw[at : at + HEAD_DIM, LANES:]
        turned.append((y * silu(gate), gate))
        if len(turned) * HEAD_DIM == LANES:
            lanes = slice(at + HEAD_DIM - LANES, at + HEAD_DIM)
            mixed[0, :, lanes] = jnp.concatenate([pair[0] for pair in turned], axis=0).T
            wide = jnp.concatenate([pair[1] for pair in turned], axis=0).T
            gate_out[0, :, lanes] = wide.astype(bf16)
            turned = []


def block_chunk(
    chunk, chunks, got, w, xact, bmap, run, dt, cum, state, skip, after, dims
):
    spg, rows, heads, span, piece_heads = dims
    groups = w.shape[0]

    at_c = 2 * span + STATE_WIDTH
    one = at_c // rows
    assert (at_c + STATE_WIDTH - 1) // rows == one
    args, specs = chunk_specs(got, chunk, dims, one)
    args = in_hbm(*args)
    args += in_hbm(w, xact, bmap, run, dt, cum, state, skip)
    specs += [
        pl.BlockSpec((1, STATE_WIDTH, 4), lambda g: (g, span // STATE_WIDTH + 1, 0)),
        per_group(span, BLOCK),
        per_group(STATE_WIDTH, BLOCK),
        per_group(heads, BLOCK),
        per_group(heads, BLOCK),
        per_group(heads, BLOCK),
        per_group(span, STATE_WIDTH),
        per_group(heads, 1),
    ]
    args += in_vmem(*after)
    specs += [pl.BlockSpec(memory_space=pl.ANY)] * len(after)

    def out(dtype, *shape):
        return pltpu.HBM((groups,) + shape, dtype)

    return pl.pallas_call(
        functools.partial(block_kernel, dims, chunk == 0),
        grid=(groups,),
        in_specs=specs,
        out_specs=[
            per_group(BLOCK, span),
            per_group(BLOCK, span),
            per_group(BLOCK, 2 * STATE_WIDTH),
            per_group(8, LANES),
        ],
        out_shape=[
            out(f32, BLOCK, span),
            out(bf16, BLOCK, span),
            out(bf16, BLOCK, 2 * STATE_WIDTH),
            out(f32, 8, LANES),
        ],
        scratch_shapes=[
            pltpu.VMEM((rows * spg, LANES + BLOCK), f32),
            pltpu.VMEM((STATE_WIDTH, LANES + BLOCK), bf16),
            pltpu.VMEM((BLOCK // LANES, STATE_WIDTH, 3 * LANES), f32),
        ],
        compiler_params=params(),
        cost_estimate=pl.CostEstimate(flops=4 * 10**9, bytes_accessed=10**7, transcendentals=10**6),
        name="block_chunk",
    )(*args)


def relay_kernel(piece_heads, src, token, dst):
    rows = piece_heads * HEAD_DIM
    held = jnp.zeros((rows, STATE_WIDTH), f32)
    for d in range(src.shape[0]):
        dst[d] = held.T.astype(bf16)
        both = src[d, rows:, :].astype(f32)
        decay = both[:8] + both[8:]
        spread = [
            jnp.broadcast_to(decay[h : h + 1, :], (HEAD_DIM, STATE_WIDTH))
            for h in range(piece_heads)
        ]
        held = jnp.concatenate(spread, axis=0) * held + src[d, :rows, :].astype(f32)


def relay(packed, token, piece_heads):
    count = packed.shape[0]
    rows = piece_heads * HEAD_DIM
    return pl.pallas_call(
        functools.partial(relay_kernel, piece_heads),
        in_specs=[pl.BlockSpec(memory_space=pltpu.VMEM), pl.BlockSpec(memory_space=pl.ANY)],
        out_shape=pltpu.VMEM((count, STATE_WIDTH, rows), bf16),
        compiler_params=params(16),
        name="relay",
    )(packed, *in_hbm(token))


def final_kernel(chunks, groups, *refs):
    mixed, gates, sides = (refs[i * chunks : (i + 1) * chunks] for i in range(3))
    state, gain, out = refs[3 * chunks : 3 * chunks + 3]
    held, gate_held, side_held, kept, done, sems, out_sems = refs[3 * chunks + 3 :]
    span = held.shape[2]
    piece = state.shape[2]
    spg = state.shape[0] // groups
    heads = span // HEAD_DIM
    steps = [(g, c) for g in range(groups) for c in range(chunks)]

    def loads(i):
        g, c = steps[i]
        slot = i
        moves = []
        moves.append((sides[c].at[g], side_held.at[slot]))
        moves.append((mixed[c].at[g], held.at[slot]))
        moves.append((gates[c].at[g], gate_held.at[slot]))
        return [
            pltpu.make_async_copy(a, b, sems.at[slot, j]) for j, (a, b) in enumerate(moves)
        ]

    def store(i):
        g, c = steps[i]
        return pltpu.make_async_copy(
            done.at[i % 2],
            out.at[c * BLOCK : (c + 1) * BLOCK, g * span : (g + 1) * span],
            out_sems.at[i % 2],
        )

    for i in range(len(steps)):
        for move in loads(i):
            move.start()
    row = lax.broadcasted_iota(jnp.int32, (STATE_WIDTH, span), 0)
    col = lax.broadcasted_iota(jnp.int32, (STATE_WIDTH, span), 1) // HEAD_DIM
    spread = jnp.where((row == col) | (row == col + heads), 1.0, 0.0).astype(bf16)
    for i, (g, c) in enumerate(steps):
        slot = i
        for move in loads(i):
            move.wait()
        if i >= 2:
            store(i - 2).wait()
        side = side_held[slot]
        half = BLOCK // 2
        for q in range(0, BLOCK, half):
            rows = slice(q, q + half)
            total = jnp.zeros((half, LANES), f32)
            for j in range(spg):
                piece_lanes = slice(j * piece, (j + 1) * piece)
                part = jnp.dot(
                    side[rows, :STATE_WIDTH], state[g * spg + j], preferred_element_type=f32
                )
                reach = jnp.dot(
                    side[rows, STATE_WIDTH:], spread[:, piece_lanes], preferred_element_type=f32
                )
                gate = silu(gate_held[slot, rows, piece_lanes].astype(f32))
                v = held[slot, rows, piece_lanes] + gate * (part * reach)
                kept[rows, piece_lanes] = v
                for at in range(0, piece, LANES):
                    t = v[:, at : at + LANES]
                    if piece < LANES:
                        t = jnp.concatenate([t, jnp.zeros((half, LANES - piece), f32)], axis=1)
                    total = total + t * t
            mean = jnp.sum(total, axis=1, keepdims=True) * (1.0 / span)
            factor = lax.rsqrt(mean + EPSILON)
            for at in range(0, span, LANES):
                lanes = slice(at, at + LANES)
                scaled = kept[rows, lanes] * factor * gain[g, :, lanes]
                done[i % 2, rows, lanes] = scaled.astype(bf16)
        store(i).start()
    for i in range(max(len(steps) - 2, 0), len(steps)):
        store(i).wait()


def finish(mixed, gates, sides, state, gain):
    chunks = len(mixed)
    groups, _, span = mixed[0].shape
    steps = groups * chunks
    anywhere = pl.BlockSpec(memory_space=pl.ANY)
    within = pl.BlockSpec(memory_space=pltpu.VMEM)
    return pl.pallas_call(
        functools.partial(final_kernel, chunks, groups),
        in_specs=[anywhere] * (3 * chunks) + [within] * 2,
        out_specs=anywhere,
        out_shape=jax.ShapeDtypeStruct((chunks * BLOCK, groups * span), bf16),
        scratch_shapes=[
            pltpu.VMEM((steps, BLOCK, span), f32),
            pltpu.VMEM((steps, BLOCK, span), bf16),
            pltpu.VMEM((steps, BLOCK, 2 * STATE_WIDTH), bf16),
            pltpu.VMEM((BLOCK, span), f32),
            pltpu.VMEM((2, BLOCK, span), bf16),
            pltpu.SemaphoreType.DMA((steps, 3)),
            pltpu.SemaphoreType.DMA((2,)),
        ],
        compiler_params=params(40),
        name="finish",
    )(*in_hbm(*mixed, *gates, *sides), state, gain)


def swap(array, k):
    count = lax.axis_size("seq")
    return lax.ppermute(array, "seq", [(i, i ^ k) for i in range(count)])


def exchange(array):
    return lax.all_to_all(array, "seq", split_axis=0, concat_axis=0, tiled=True)


def per_device(projected, conv_weight, dt_bias, a_log, d_skip, norm_gain):
    seq_count = lax.axis_size("seq")
    groups = conv_weight.shape[1]
    heads = dt_bias.shape[0] // groups
    span = heads * HEAD_DIM
    rows, all_tokens = projected.shape
    local_tokens = all_tokens // seq_count
    chunks = local_tokens // BLOCK
    spg = seq_count // groups
    piece_heads = groups * heads // seq_count
    dims = (spg, rows, heads, span, piece_heads)

    me = lax.axis_index("seq").astype(jnp.int32).reshape(1)
    assert chunks > 2 and seq_count & (seq_count - 1) == 0
    middle, split_at = local_tokens - 2 * BLOCK, local_tokens - BLOCK

    def send(low, after):
        own, near, *pairs = cut_pairs(projected, me, seq_count, low, low + HALF, after)
        pairs = [swap(pair, 2 * j + 2) for j, pair in enumerate(pairs)]
        return [own, swap(near, 1), *pairs]

    parts = [send(middle, [])]
    cut = cut_first(projected, seq_count, middle, parts[0][0])
    got = [exchange(cut)]
    parts.append(send(middle + HALF, [cut, *parts[0][1:]]))

    conv_weight, dt_bias, a_log, d_skip, norm_gain, parts[1][0] = lax.optimization_barrier(
        (conv_weight, dt_bias, a_log, d_skip, norm_gain, parts[1][0])
    )
    w = jnp.transpose(conv_weight, (1, 2, 0))
    bias = dt_bias.reshape(groups, heads, 1)
    rate = a_log.reshape(groups, heads, 1)
    skip = d_skip.reshape(groups, heads, 1)
    gain = norm_gain.reshape(groups, 1, span)
    lead = jnp.broadcast_to(bias * 0.0, (groups, heads, LANES))
    state = jnp.broadcast_to(bias[:, :1] * 0.0, (groups, span, STATE_WIDTH))
    ready = [parts[1][0], w, bias, rate, skip, gain, state, lead]
    cut = cut_block(projected, seq_count, split_at, ready)
    got += [None, exchange(cut)]

    results, tokens = [], []
    for c in range(chunks):
        before = [] if c else [cut]
        if c == chunks - 2:
            pairs = [pair for part in parts for pair in part[2:]]
            passed = swap(forward(pairs, [lead, tokens[0], cut]), 1)
            got[1] = join(me, passed, parts, tokens)
        if c == chunks - 1:
            before = tokens[-2:-1]
        xact, bmap, run, dt, cum, new, lead = state_chunk(
            c, chunks, got, w, bias, rate, state, lead, before, dims
        )
        after = []
        if c == chunks - 1:
            entering = relay(exchange(new), tokens[-1], piece_heads)
            after = [entering]
        *result, token = block_chunk(
            c, chunks, got, w, xact, bmap, run, dt, cum, state, skip, after, dims
        )
        results.append(result)
        tokens.append(token)
        state = new
    return finish(*zip(*results), exchange(entering), gain)


def solution(mesh):
    in_specs = (P(("tp", "seq"), None), P(None, "tp", None), P("tp"), P("tp"), P("tp"), P("tp"))
    return jax.shard_map(
        per_device, mesh=mesh, in_specs=in_specs, out_specs=P("seq", "tp"), check_vma=False
    )
```

```python
import functools

import jax
import jax.numpy as jnp
from jax import lax
from jax.experimental import pallas as pl
from jax.experimental.pallas import tpu as pltpu
from jax.sharding import PartitionSpec as P

HEAD_DIM = 64
STATE_WIDTH = 128
BLOCK = 256
LANES = 128
HALF = BLOCK // 2
WIDE = 256
LOG2E = 1.4426950408889634
CAP = 80.0
EPSILON = 1e-05

f32 = jnp.float32
bf16 = jnp.bfloat16
NT = (((1,), (1,)), ((), ()))


def params(mib=60):
    return pltpu.CompilerParams(vmem_limit_bytes=mib * 2**20)


def silu(v):
    half = 0.5 * v
    return half + half * jnp.tanh(half)


def softplus(v):
    e = jnp.exp(-jnp.abs(v))
    u = 1.0 + e
    gap = u - 1.0
    tiny = gap == 0.0
    log_part = jnp.where(tiny, e, jnp.log(u) * (e / jnp.where(tiny, 1.0, gap)))
    return jnp.maximum(v, 0.0) + log_part


def in_hbm(*arrays):
    return [pltpu.with_memory_space_constraint(array, pltpu.HBM) for array in arrays]


def in_vmem(*arrays):
    return [pltpu.with_memory_space_constraint(array, pltpu.VMEM) for array in arrays]


def per_group(*shape):
    return pl.BlockSpec((1,) + shape, lambda g: (g,) + (0,) * len(shape))


RIM = 4


def rim_rows(rows, width):
    base = rows // 16 * 16
    height = -(-(rows - base + RIM * -(-rows // width)) // 8) * 8
    assert height <= 16
    return base, height


def first_kernel(src, dst, held, windows, ends, in_sems, rim_sems, out_sems, end_sems):
    rows, all_tokens = src.shape
    count, _, width = dst.shape
    tokens = all_tokens // count
    base, height = rim_rows(rows, width)

    def fetch(d):
        at = d * tokens
        return pltpu.make_async_copy(src.at[:, at : at + width], held.at[d], in_sems.at[d])

    def window(d):
        at = d * tokens - LANES
        return pltpu.make_async_copy(src.at[:, at : at + LANES], windows.at[d], rim_sems.at[d])

    def place(d):
        return pltpu.make_async_copy(
            held.at[d, :base, :], dst.at[d, :base, :], out_sems.at[d]
        )

    def place_end(d):
        return pltpu.make_async_copy(
            ends.at[d], dst.at[d, base : base + height, :], end_sems.at[d]
        )

    for d in range(count):
        fetch(d).start()
    for d in range(1, count):
        window(d).start()
    row = lax.broadcasted_iota(jnp.int32, (height, LANES), 0) - (rows - base)
    col = lax.broadcasted_iota(jnp.int32, (height, LANES), 1)
    hit = (row >= 0) & (col == lax.rem(row + 16, RIM) + LANES - RIM)
    pick = jnp.where(hit, 1.0, 0.0).astype(bf16)
    which = lax.broadcasted_iota(jnp.int32, (height, width), 0) - (rows - base)
    for d in range(count):
        fetch(d).wait()
        place(d).start()
    for d in range(count):
        end = held[d, base:rows, :].astype(f32)
        end = jnp.concatenate([end, jnp.zeros((height - end.shape[0], width), f32)], axis=0)
        if d:
            window(d).wait()
            rims = lax.dot_general(pick, windows[d], NT, preferred_element_type=f32)
            for j in range(-(-rows // width)):
                part = rims[:, j * width : min((j + 1) * width, rows)]
                if part.shape[1] < width:
                    fill = jnp.zeros((height, width - part.shape[1]), f32)
                    part = jnp.concatenate([part, fill], axis=1)
                end = jnp.where((which >= RIM * j) & (which < RIM * (j + 1)), part, end)
        ends[d] = end.astype(bf16)
        place_end(d).start()
    for d in range(count):
        place(d).wait()
        place_end(d).wait()


def cut_first(projected, count, width):
    rows = projected.shape[0]
    base, height = rim_rows(rows, width)
    sems = pltpu.SemaphoreType.DMA((count,))
    anywhere = pl.BlockSpec(memory_space=pl.ANY)
    return pl.pallas_call(
        first_kernel,
        in_specs=[anywhere],
        out_specs=anywhere,
        out_shape=pltpu.HBM((count, base + height, width), bf16),
        scratch_shapes=[
            pltpu.VMEM((count, rows, width), bf16),
            pltpu.VMEM((count, rows, LANES), bf16),
            pltpu.VMEM((count, height, width), bf16),
            sems,
            sems,
            sems,
            sems,
        ],
        compiler_params=params(),
        name="cut_first",
    )(*in_hbm(projected))


def staged(moves, held, in_sems, out_sems):
    for i, (source, _) in enumerate(moves):
        pltpu.make_async_copy(source, held.at[i], in_sems.at[i]).start()
    for i, (source, target) in enumerate(moves):
        pltpu.make_async_copy(source, held.at[i], in_sems.at[i]).wait()
        pltpu.make_async_copy(held.at[i], target, out_sems.at[i]).start()
    for i, (_, target) in enumerate(moves):
        pltpu.make_async_copy(held.at[i], target, out_sems.at[i]).wait()


def staging(count, rows):
    sems = pltpu.SemaphoreType.DMA((count,))
    return [pltpu.VMEM((count, rows, BLOCK), bf16), sems, sems]


def cut_kernel(low, count, src, *refs):
    dst = refs[-4]
    tokens = src.shape[1] // count
    moves = []
    for d in range(count):
        at = d * tokens + low
        moves.append((src.at[:, at : at + BLOCK], dst.at[d]))
    staged(moves, *refs[-3:])


def cut_block(projected, count, low, after):
    rows = projected.shape[0]
    args = in_hbm(projected, *after)
    anywhere = pl.BlockSpec(memory_space=pl.ANY)
    return pl.pallas_call(
        functools.partial(cut_kernel, low, count),
        in_specs=[anywhere] * len(args),
        out_specs=anywhere,
        out_shape=pltpu.HBM((count, rows, BLOCK), bf16),
        scratch_shapes=staging(count, rows),
        compiler_params=params(),
        name="cut_block",
    )(*args)


def pairs_kernel(low, count, me_ref, src, *refs):
    own, near, *far = refs[-(count // 2 + 4) : -3]
    tokens = src.shape[1] // count
    me = me_ref[0]
    targets = [own, near]
    for pair in far:
        targets += [pair.at[:, :BLOCK], pair.at[:, BLOCK:]]
    moves = []
    for k, target in enumerate(targets):
        at = pl.multiple_of((me ^ k) * tokens + low, LANES)
        moves.append((src.at[:, pl.ds(at, BLOCK)], target))
    staged(moves[2:] + moves[:2], *refs[-3:])


def cut_pairs(projected, me, count, low, after):
    rows = projected.shape[0]
    anywhere = pl.BlockSpec(memory_space=pl.ANY)
    one, two = pltpu.HBM((rows, BLOCK), bf16), pltpu.HBM((rows, 2 * BLOCK), bf16)
    return pl.pallas_call(
        functools.partial(pairs_kernel, low, count),
        in_specs=[pl.BlockSpec(memory_space=pltpu.SMEM)] + [anywhere] * (1 + len(after)),
        out_specs=[anywhere] * (count // 2 + 1),
        out_shape=[one, one] + [two] * (count // 2 - 1),
        scratch_shapes=staging(count, rows),
        compiler_params=params(),
        name="cut_pairs",
    )(me, *in_hbm(projected, *after))


def forward_kernel(count, *refs):
    dst = refs[-4]
    moves = [
        (refs[j].at[:, BLOCK:], dst.at[:, j * BLOCK : (j + 1) * BLOCK])
        for j in range(count // 2 - 1)
    ]
    staged(moves, *refs[-3:])


def forward(pairs, after):
    count = 2 * len(pairs) + 2
    rows = pairs[0].shape[0]
    anywhere = pl.BlockSpec(memory_space=pl.ANY)
    return pl.pallas_call(
        functools.partial(forward_kernel, count),
        in_specs=[anywhere] * (len(pairs) + len(after)),
        out_specs=anywhere,
        out_shape=pltpu.HBM((rows, len(pairs) * BLOCK), bf16),
        scratch_shapes=staging(len(pairs), rows),
        compiler_params=params(),
        name="forward",
    )(*pairs, *in_hbm(*after))


def join_kernel(count, me_ref, own, near, *refs):
    others = count // 2 - 1
    pairs, passed, dst = refs[:others], refs[others], refs[-4]
    me = me_ref[0]
    sources = [own, near]
    for j in range(others):
        sources += [pairs[j].at[:, :BLOCK], passed.at[:, j * BLOCK : (j + 1) * BLOCK]]
    staged([(source, dst.at[me ^ k]) for k, source in enumerate(sources)], *refs[-3:])


def join(me, own, near, pairs, passed, after):
    count = 2 * len(pairs) + 2
    rows = own.shape[0]
    anywhere = pl.BlockSpec(memory_space=pl.ANY)
    args = [own, near, *pairs, passed, *in_hbm(*after)]
    return pl.pallas_call(
        functools.partial(join_kernel, count),
        in_specs=[pl.BlockSpec(memory_space=pltpu.SMEM)] + [anywhere] * len(args),
        out_specs=anywhere,
        out_shape=pltpu.HBM((count, rows, BLOCK), bf16),
        scratch_shapes=staging(count, rows),
        compiler_params=params(),
        name="join",
    )(me, *args)


def gather_rows(recv, prev, first, raw, rows, low, high, ahead=True, only=None):
    for s in range(recv.shape[0]):
        a = max(low - s * rows, 0) // 16 * 16
        b = min(-(-(high - s * rows) // 16) * 16, rows)
        if b <= a:
            continue
        at = s * rows + a
        raw[at : at + b - a, LANES:] = recv[s, a:b, :].astype(f32)
        if not ahead:
            continue
        if not first:
            raw[at : at + b - a, :LANES] = prev[s if only is None else 0, a:b, :].astype(f32)
            continue
        width = prev.shape[2]
        base, height = rim_rows(rows, width)
        rims = prev[s if only is None else 0, :height, :].astype(f32)
        tall = jnp.concatenate([jnp.zeros((LANES - height, width), f32), rims], axis=0)
        for j in range(-(-rows // width)):
            c, d = max(a, j * width), min(b, (j + 1) * width)
            if d <= c:
                continue
            shift = height - RIM - (rows - base) - RIM * j
            moved = (pltpu.roll(tall, shift, 0) if shift else tall).T
            raw[s * rows + c : s * rows + d, :LANES] = moved[c - j * width : d - j * width]


def band():
    row = lax.broadcasted_iota(jnp.int32, (2 * LANES, 3 * LANES), 0)
    col = lax.broadcasted_iota(jnp.int32, (2 * LANES, 3 * LANES), 1)
    tap = col // LANES
    return jnp.where(row == col - tap * LANES + LANES - 3 + tap, 1.0, 0.0).astype(bf16)


def shift_rows(raw, low, shifted, at):
    low[...] = raw[at : at + low.shape[0], :].astype(bf16)
    picks = band()
    for i in range(BLOCK // LANES):
        window = low[:, i * LANES : (i + 2) * LANES]
        shifted[i] = jnp.dot(window, picks, preferred_element_type=f32)


def conv_tile(raw, shifted, w, at, r):
    rows = slice(r, r + HEAD_DIM)
    taps = [jnp.broadcast_to(w[0, rows, k : k + 1], (HEAD_DIM, LANES)) for k in range(4)]
    parts = []
    for i in range(BLOCK // LANES):
        summed = None
        for k in range(3):
            part = taps[k] * shifted[i, rows, k * LANES : (k + 1) * LANES]
            summed = part if summed is None else summed + part
        own = raw[at + r : at + r + HEAD_DIM, (i + 1) * LANES : (i + 2) * LANES]
        parts.append(silu(summed + taps[3] * own).astype(bf16))
    return jnp.concatenate(parts, axis=1)


def state_kernel(dims, first, last, recv, *refs):
    spg, rows, heads, span, piece_heads = dims
    prev, refs = refs[0], refs[1:]
    w, bias, a_log, state_in, lead_in = refs[:5]
    xact, bmap, run_out, dt_out, cum_out, state_out, lead_out = refs[-11:-4]
    raw, xw, low, shifted = refs[-4:]
    steps = 2 * span + 2 * STATE_WIDTH

    gather_rows(recv, prev, first, raw, rows, steps, steps + heads, False)
    gather_rows(recv, prev, first, raw, rows, span, 2 * span + STATE_WIDTH)
    dt = softplus(raw[steps : steps + heads, LANES:] + bias[0])
    log_decay = -jnp.exp(a_log[0]) * dt
    lane = lax.broadcasted_iota(jnp.int32, (heads, BLOCK), 1)
    run = log_decay
    shift = 1
    while shift < BLOCK:
        run = run + jnp.where(lane >= shift, pltpu.roll(run, shift, 1), 0.0)
        shift *= 2
    final = run[:, BLOCK - 1 :]
    scale = jnp.exp(final - run) * dt
    cum = run + lead_in[0][:, :1]
    run_out[0] = run
    dt_out[0] = dt
    cum_out[0] = cum
    lead = jnp.broadcast_to(cum[:, BLOCK - 1 :], (heads, LANES))
    lead_out[0] = lead
    keep = jnp.broadcast_to(jnp.exp(final), (heads, LANES))

    shift_rows(raw, low, shifted, span)
    for r in range(0, STATE_WIDTH, HEAD_DIM):
        bmap[0, r : r + HEAD_DIM, :] = conv_tile(raw, shifted, w, span, span + r)
    for h in range(heads):
        r = h * HEAD_DIM
        tile = conv_tile(raw, shifted, w, span, r)
        xact[0, r : r + HEAD_DIM, :] = tile
        xw[r : r + HEAD_DIM, :] = (tile.astype(f32) * scale[h : h + 1, :]).astype(bf16)
    update = lax.dot_general(xw[...], bmap[0], NT, preferred_element_type=f32)
    for h in range(heads):
        r = h * HEAD_DIM
        new = update[r : r + HEAD_DIM, :]
        if not first:
            new = keep[h : h + 1, :] * state_in[0, r : r + HEAD_DIM, :] + new
        if last:
            at = (h % piece_heads) * HEAD_DIM
            state_out[h // piece_heads, at : at + HEAD_DIM, :] = new.astype(bf16)
        else:
            state_out[0, r : r + HEAD_DIM, :] = new
    if last:
        high, low = split(jnp.exp(lead))
        fill = jnp.zeros((8 - piece_heads, LANES), f32)
        for i in range(heads // piece_heads):
            mine = slice(i * piece_heads, (i + 1) * piece_heads)
            parts = [high[mine].astype(f32), fill, low[mine].astype(f32), fill]
            at = piece_heads * HEAD_DIM
            state_out[i, at : at + 16, :] = jnp.concatenate(parts, axis=0).astype(bf16)


def chunk_specs(got, chunk, dims, only=None):
    spg, rows = dims[:2]
    slabs = spg if only is None else 1

    def ahead(source, shape, row, lane):
        def index(g):
            return (g if only is None else g * spg + only, row, lane)

        return source, pl.BlockSpec((slabs,) + shape, index)

    def lane_of(block):
        first, middle, last = got
        ahead_of = first.shape[2] // BLOCK
        if block < ahead_of:
            return first, block
        return (middle if block == ahead_of else last), 0

    source, at = lane_of(chunk)
    block = pl.BlockSpec((spg, source.shape[1], BLOCK), lambda g: (g, 0, at))
    if chunk == 0:
        width = source.shape[2]
        prev, prev_spec = ahead(source, (16, width), rim_rows(rows, width)[0] // 16, 0)
    else:
        prev, place = lane_of(chunk - 1)
        lane = (place + 1) * (BLOCK // LANES) - 1
        prev, prev_spec = ahead(prev, (prev.shape[1], LANES), 0, lane)
    return [source, prev], [block, prev_spec]


def state_chunk(chunk, chunks, got, w, bias, a_log, state, lead, before, dims):
    spg, rows, heads, span, piece_heads = dims
    groups = w.shape[0]
    last = chunk == chunks - 1
    if last:
        packed = piece_heads * HEAD_DIM + 16
        state_shape = pltpu.HBM((groups * spg, packed, STATE_WIDTH), bf16)
        state_spec = pl.BlockSpec((spg, packed, STATE_WIDTH), lambda g: (g, 0, 0))
    else:
        state_shape = pltpu.HBM((groups, span, STATE_WIDTH), f32)
        state_spec = per_group(span, STATE_WIDTH)

    def out(dtype, *shape):
        return pltpu.HBM((groups,) + shape, dtype)

    args, specs = chunk_specs(got, chunk, dims)
    args[1:] = in_hbm(args[1])
    args[:1] = in_vmem(args[0]) if last else in_hbm(args[0])
    after = in_hbm(*before)
    return pl.pallas_call(
        functools.partial(state_kernel, dims, chunk == 0, last),
        grid=(groups,),
        in_specs=specs
        + [
            per_group(span + STATE_WIDTH, 4),
            per_group(heads, 1),
            per_group(heads, 1),
            per_group(span, STATE_WIDTH),
            per_group(heads, LANES),
        ]
        + [pl.BlockSpec(memory_space=pl.ANY)] * len(after),
        out_specs=[
            per_group(span, BLOCK),
            per_group(STATE_WIDTH, BLOCK),
            per_group(heads, BLOCK),
            per_group(heads, BLOCK),
            per_group(heads, BLOCK),
            state_spec,
            per_group(heads, LANES),
        ],
        out_shape=[
            out(bf16, span, BLOCK),
            out(bf16, STATE_WIDTH, BLOCK),
            out(f32, heads, BLOCK),
            out(f32, heads, BLOCK),
            out(f32, heads, BLOCK),
            state_shape,
            out(f32, heads, LANES),
        ],
        scratch_shapes=[
            pltpu.VMEM((rows * spg, LANES + BLOCK), f32),
            pltpu.VMEM((span, BLOCK), bf16),
            pltpu.VMEM((span + STATE_WIDTH, LANES + BLOCK), bf16),
            pltpu.VMEM((BLOCK // LANES, span + STATE_WIDTH, 3 * LANES), f32),
        ],
        compiler_params=params(48 if last else 60),
        cost_estimate=pl.CostEstimate(flops=4 * 10**9, bytes_accessed=10**7, transcendentals=10**6),
        name="state_chunk",
    )(*args, *in_hbm(w, bias, a_log, state, lead), *after)


def split(v):
    high = v.astype(bf16)
    return high, (v - high.astype(f32)).astype(bf16)


def block_kernel(dims, first, recv, *refs):
    spg, rows, heads, span, piece_heads = dims
    prev, refs = refs[0], refs[1:]
    w, xact, bmap, run_ref, dt_ref, cum_ref, state, skip = refs[:8]
    mixed, gate_out, side, token, raw, low, shifted = refs[-7:]
    at_c = 2 * span + STATE_WIDTH
    gather_rows(recv, prev, first, raw, rows, at_c, at_c + STATE_WIDTH, True, at_c // rows)
    gather_rows(recv, prev, first, raw, rows, 0, span, False)
    token[0] = cum_ref[0, :8, :LANES]
    shift_rows(raw, low, shifted, at_c)
    c = [conv_tile(raw, shifted, w, at_c, r) for r in range(0, STATE_WIDTH, HEAD_DIM)]
    c = jnp.concatenate(c, axis=0)
    b_rows = bmap[0].astype(f32).T.astype(bf16)
    scores = jnp.dot(b_rows, c, preferred_element_type=f32)
    src = lax.broadcasted_iota(jnp.int32, (HALF, HALF), 0)
    dst = lax.broadcasted_iota(jnp.int32, (HALF, HALF), 1)
    causal = src <= dst
    s00 = jnp.where(causal, scores[:HALF, :HALF], 0.0)
    s01 = scores[:HALF, HALF:]
    s11 = jnp.where(causal, scores[HALF:, HALF:], 0.0)
    r = run_ref[0] * LOG2E
    q = (r - jnp.log(dt_ref[0]) * LOG2E).T
    if not first:
        cc = jnp.concatenate([c, c], axis=0)
        entered = jnp.exp2(r)
    reach = [part.astype(f32) for part in split(jnp.exp(cum_ref[0]))]
    reach.append(jnp.zeros((STATE_WIDTH - 2 * heads, BLOCK), f32))
    side[0, :, :STATE_WIDTH] = c.astype(f32).T.astype(bf16)
    side[0, :, STATE_WIDTH:] = jnp.concatenate(reach, axis=0).T.astype(bf16)
    turned = []
    for h in range(heads):
        at = h * HEAD_DIM
        r0, r1 = r[h : h + 1, :HALF], r[h : h + 1, HALF:]
        q0, q1 = q[:HALF, h : h + 1], q[HALF:, h : h + 1]
        w00 = (s00 * jnp.exp2(jnp.minimum(r0 - q0, CAP))).astype(bf16)
        w01 = (s01 * jnp.exp2(r1 - q0)).astype(bf16)
        w11 = (s11 * jnp.exp2(jnp.minimum(r1 - q1, CAP))).astype(bf16)
        x = xact[0, at : at + HEAD_DIM, :]
        y0 = jnp.dot(x[:, :HALF], w00, preferred_element_type=f32)
        y1 = jnp.dot(x, jnp.concatenate([w01, w11], axis=0), preferred_element_type=f32)
        y = jnp.concatenate([y0, y1], axis=1) + skip[0, h : h + 1, :] * x.astype(f32)
        if not first:
            if at % WIDE == 0:
                both = jnp.concatenate(split(state[0, at : at + WIDE, :]), axis=1)
                carried = jnp.dot(both, cc, preferred_element_type=f32)
            y = y + entered[h : h + 1, :] * carried[at % WIDE : at % WIDE + HEAD_DIM, :]
        gate = raw[at : at + HEAD_DIM, LANES:]
        turned.append((y * silu(gate), gate))
        if len(turned) * HEAD_DIM == LANES:
            lanes = slice(at + HEAD_DIM - LANES, at + HEAD_DIM)
            mixed[0, :, lanes] = jnp.concatenate([pair[0] for pair in turned], axis=0).T
            wide = jnp.concatenate([pair[1] for pair in turned], axis=0).T
            gate_out[0, :, lanes] = wide.astype(bf16)
            turned = []


def block_chunk(
    chunk, chunks, got, w, xact, bmap, run, dt, cum, state, skip, after, dims
):
    spg, rows, heads, span, piece_heads = dims
    groups = w.shape[0]

    at_c = 2 * span + STATE_WIDTH
    one = at_c // rows
    assert (at_c + STATE_WIDTH - 1) // rows == one
    args, specs = chunk_specs(got, chunk, dims, one)
    args = in_hbm(*args)
    args += in_hbm(w, xact, bmap, run, dt, cum, state, skip)
    specs += [
        pl.BlockSpec((1, STATE_WIDTH, 4), lambda g: (g, span // STATE_WIDTH + 1, 0)),
        per_group(span, BLOCK),
        per_group(STATE_WIDTH, BLOCK),
        per_group(heads, BLOCK),
        per_group(heads, BLOCK),
        per_group(heads, BLOCK),
        per_group(span, STATE_WIDTH),
        per_group(heads, 1),
    ]
    args += in_vmem(*after)
    specs += [pl.BlockSpec(memory_space=pl.ANY)] * len(after)

    def out(dtype, *shape):
        return pltpu.HBM((groups,) + shape, dtype)

    return pl.pallas_call(
        functools.partial(block_kernel, dims, chunk == 0),
        grid=(groups,),
        in_specs=specs,
        out_specs=[
            per_group(BLOCK, span),
            per_group(BLOCK, span),
            per_group(BLOCK, 2 * STATE_WIDTH),
            per_group(8, LANES),
        ],
        out_shape=[
            out(f32, BLOCK, span),
            out(bf16, BLOCK, span),
            out(bf16, BLOCK, 2 * STATE_WIDTH),
            out(f32, 8, LANES),
        ],
        scratch_shapes=[
            pltpu.VMEM((rows * spg, LANES + BLOCK), f32),
            pltpu.VMEM((STATE_WIDTH, LANES + BLOCK), bf16),
            pltpu.VMEM((BLOCK // LANES, STATE_WIDTH, 3 * LANES), f32),
        ],
        compiler_params=params(),
        cost_estimate=pl.CostEstimate(flops=4 * 10**9, bytes_accessed=10**7, transcendentals=10**6),
        name="block_chunk",
    )(*args)


def relay_kernel(piece_heads, src, token, dst):
    rows = piece_heads * HEAD_DIM
    held = jnp.zeros((rows, STATE_WIDTH), f32)
    for d in range(src.shape[0]):
        dst[d] = held.T.astype(bf16)
        both = src[d, rows:, :].astype(f32)
        decay = both[:8] + both[8:]
        spread = [
            jnp.broadcast_to(decay[h : h + 1, :], (HEAD_DIM, STATE_WIDTH))
            for h in range(piece_heads)
        ]
        held = jnp.concatenate(spread, axis=0) * held + src[d, :rows, :].astype(f32)


def relay(packed, token, piece_heads):
    count = packed.shape[0]
    rows = piece_heads * HEAD_DIM
    return pl.pallas_call(
        functools.partial(relay_kernel, piece_heads),
        in_specs=[pl.BlockSpec(memory_space=pltpu.VMEM), pl.BlockSpec(memory_space=pl.ANY)],
        out_shape=pltpu.VMEM((count, STATE_WIDTH, rows), bf16),
        compiler_params=params(16),
        name="relay",
    )(packed, *in_hbm(token))


def final_kernel(chunks, groups, *refs):
    mixed, gates, sides = (refs[i * chunks : (i + 1) * chunks] for i in range(3))
    state, gain, out = refs[3 * chunks : 3 * chunks + 3]
    held, gate_held, side_held, kept, done, sems, out_sems = refs[3 * chunks + 3 :]
    span = held.shape[2]
    piece = state.shape[2]
    spg = state.shape[0] // groups
    heads = span // HEAD_DIM
    steps = [(g, c) for g in range(groups) for c in range(chunks)]

    def loads(i):
        g, c = steps[i]
        slot = i
        moves = []
        moves.append((sides[c].at[g], side_held.at[slot]))
        moves.append((mixed[c].at[g], held.at[slot]))
        moves.append((gates[c].at[g], gate_held.at[slot]))
        return [
            pltpu.make_async_copy(a, b, sems.at[slot, j]) for j, (a, b) in enumerate(moves)
        ]

    def store(i):
        g, c = steps[i]
        return pltpu.make_async_copy(
            done.at[i % 2],
            out.at[c * BLOCK : (c + 1) * BLOCK, g * span : (g + 1) * span],
            out_sems.at[i % 2],
        )

    for i in range(len(steps)):
        for move in loads(i):
            move.start()
    row = lax.broadcasted_iota(jnp.int32, (STATE_WIDTH, span), 0)
    col = lax.broadcasted_iota(jnp.int32, (STATE_WIDTH, span), 1) // HEAD_DIM
    spread = jnp.where((row == col) | (row == col + heads), 1.0, 0.0).astype(bf16)
    for i, (g, c) in enumerate(steps):
        slot = i
        for move in loads(i):
            move.wait()
        if i >= 2:
            store(i - 2).wait()
        side = side_held[slot]
        half = BLOCK // 2
        for q in range(0, BLOCK, half):
            rows = slice(q, q + half)
            total = jnp.zeros((half, LANES), f32)
            for j in range(spg):
                piece_lanes = slice(j * piece, (j + 1) * piece)
                part = jnp.dot(
                    side[rows, :STATE_WIDTH], state[g * spg + j], preferred_element_type=f32
                )
                reach = jnp.dot(
                    side[rows, STATE_WIDTH:], spread[:, piece_lanes], preferred_element_type=f32
                )
                gate = silu(gate_held[slot, rows, piece_lanes].astype(f32))
                v = held[slot, rows, piece_lanes] + gate * (part * reach)
                kept[rows, piece_lanes] = v
                for at in range(0, piece, LANES):
                    t = v[:, at : at + LANES]
                    if piece < LANES:
                        t = jnp.concatenate([t, jnp.zeros((half, LANES - piece), f32)], axis=1)
                    total = total + t * t
            mean = jnp.sum(total, axis=1, keepdims=True) * (1.0 / span)
            factor = lax.rsqrt(mean + EPSILON)
            for at in range(0, span, LANES):
                lanes = slice(at, at + LANES)
                scaled = kept[rows, lanes] * factor * gain[g, :, lanes]
                done[i % 2, rows, lanes] = scaled.astype(bf16)
        store(i).start()
    for i in range(max(len(steps) - 2, 0), len(steps)):
        store(i).wait()


def finish(mixed, gates, sides, state, gain):
    chunks = len(mixed)
    groups, _, span = mixed[0].shape
    steps = groups * chunks
    anywhere = pl.BlockSpec(memory_space=pl.ANY)
    within = pl.BlockSpec(memory_space=pltpu.VMEM)
    return pl.pallas_call(
        functools.partial(final_kernel, chunks, groups),
        in_specs=[anywhere] * (3 * chunks) + [within] * 2,
        out_specs=anywhere,
        out_shape=jax.ShapeDtypeStruct((chunks * BLOCK, groups * span), bf16),
        scratch_shapes=[
            pltpu.VMEM((steps, BLOCK, span), f32),
            pltpu.VMEM((steps, BLOCK, span), bf16),
            pltpu.VMEM((steps, BLOCK, 2 * STATE_WIDTH), bf16),
            pltpu.VMEM((BLOCK, span), f32),
            pltpu.VMEM((2, BLOCK, span), bf16),
            pltpu.SemaphoreType.DMA((steps, 3)),
            pltpu.SemaphoreType.DMA((2,)),
        ],
        compiler_params=params(40),
        name="finish",
    )(*in_hbm(*mixed, *gates, *sides), state, gain)


def swap(array, k):
    count = lax.axis_size("seq")
    return lax.ppermute(array, "seq", [(i, i ^ k) for i in range(count)])


def exchange(array):
    return lax.all_to_all(array, "seq", split_axis=0, concat_axis=0, tiled=True)


def per_device(projected, conv_weight, dt_bias, a_log, d_skip, norm_gain):
    seq_count = lax.axis_size("seq")
    groups = conv_weight.shape[1]
    heads = dt_bias.shape[0] // groups
    span = heads * HEAD_DIM
    rows, all_tokens = projected.shape
    local_tokens = all_tokens // seq_count
    chunks = local_tokens // BLOCK
    spg = seq_count // groups
    piece_heads = groups * heads // seq_count
    dims = (spg, rows, heads, span, piece_heads)

    w = jnp.transpose(conv_weight, (1, 2, 0))
    bias = dt_bias.reshape(groups, heads, 1)
    rate = a_log.reshape(groups, heads, 1)
    skip = d_skip.reshape(groups, heads, 1)
    gain = norm_gain.reshape(groups, 1, span)
    state = jnp.zeros((groups, span, STATE_WIDTH), f32)
    lead = jnp.zeros((groups, heads, LANES), f32)

    me = lax.axis_index("seq").astype(jnp.int32).reshape(1)
    assert chunks > 2 and seq_count & (seq_count - 1) == 0
    cut = cut_first(projected, seq_count, local_tokens - 2 * BLOCK)
    got = [exchange(cut)]
    own, near, *pairs = cut_pairs(projected, me, seq_count, local_tokens - 2 * BLOCK, [cut])
    near = swap(near, 1)
    pairs = [swap(pair, 2 * j + 2) for j, pair in enumerate(pairs)]
    ready = [own, w, bias, rate, skip, gain, state, lead]
    cut = cut_block(projected, seq_count, local_tokens - BLOCK, ready)
    got += [None, exchange(cut)]

    results, tokens = [], []
    for c in range(chunks):
        before = []
        if c == chunks - 2:
            passed = swap(forward(pairs, [lead, tokens[0]]), 1)
            got[1] = join(me, own, near, pairs, passed, tokens)
        if c == chunks - 1:
            before = tokens[-2:-1]
        xact, bmap, run, dt, cum, new, lead = state_chunk(
            c, chunks, got, w, bias, rate, state, lead, before, dims
        )
        after = []
        if c == chunks - 1:
            entering = relay(exchange(new), tokens[-1], piece_heads)
            after = [entering]
        *result, token = block_chunk(
            c, chunks, got, w, xact, bmap, run, dt, cum, state, skip, after, dims
        )
        results.append(result)
        tokens.append(token)
        state = new
    return finish(*zip(*results), exchange(entering), gain)


def solution(mesh):
    in_specs = (P(("tp", "seq"), None), P(None, "tp", None), P("tp"), P("tp"), P("tp"), P("tp"))
    return jax.shard_map(
        per_device, mesh=mesh, in_specs=in_specs, out_specs=P("seq", "tp"), check_vma=False
    )
```

```python
import functools

import jax
import jax.numpy as jnp
from jax import lax
from jax.experimental import pallas as pl
from jax.experimental.pallas import tpu as pltpu
from jax.sharding import PartitionSpec as P

HEAD_DIM = 64
STATE_WIDTH = 128
BLOCK = 256
LANES = 128
HALF = BLOCK // 2
WIDE = 256
LOG2E = 1.4426950408889634
CAP = 80.0
EPSILON = 1e-05

f32 = jnp.float32
bf16 = jnp.bfloat16
NT = (((1,), (1,)), ((), ()))


def params(mib=60):
    return pltpu.CompilerParams(vmem_limit_bytes=mib * 2**20)


def silu(v):
    half = 0.5 * v
    return half + half * jnp.tanh(half)


def softplus(v):
    e = jnp.exp(-jnp.abs(v))
    u = 1.0 + e
    gap = u - 1.0
    tiny = gap == 0.0
    log_part = jnp.where(tiny, e, jnp.log(u) * (e / jnp.where(tiny, 1.0, gap)))
    return jnp.maximum(v, 0.0) + log_part


def in_hbm(*arrays):
    return [pltpu.with_memory_space_constraint(array, pltpu.HBM) for array in arrays]


def in_vmem(*arrays):
    return [pltpu.with_memory_space_constraint(array, pltpu.VMEM) for array in arrays]


def per_group(*shape):
    return pl.BlockSpec((1,) + shape, lambda g: (g,) + (0,) * len(shape))


RIM = 4


def rim_rows(rows, width):
    base = rows // 16 * 16
    height = -(-(rows - base + RIM * -(-rows // width)) // 8) * 8
    assert height <= 16
    return base, height


def first_kernel(src, dst, held, windows, ends, in_sems, rim_sems, out_sems, end_sems):
    rows, all_tokens = src.shape
    count, _, width = dst.shape
    tokens = all_tokens // count
    base, height = rim_rows(rows, width)

    def fetch(d):
        at = d * tokens
        return pltpu.make_async_copy(src.at[:, at : at + width], held.at[d], in_sems.at[d])

    def window(d):
        at = d * tokens - LANES
        return pltpu.make_async_copy(src.at[:, at : at + LANES], windows.at[d], rim_sems.at[d])

    def place(d):
        return pltpu.make_async_copy(
            held.at[d, :base, :], dst.at[d, :base, :], out_sems.at[d]
        )

    def place_end(d):
        return pltpu.make_async_copy(
            ends.at[d], dst.at[d, base : base + height, :], end_sems.at[d]
        )

    for d in range(count):
        fetch(d).start()
        if d:
            window(d).start()
    row = lax.broadcasted_iota(jnp.int32, (height, LANES), 0) - (rows - base)
    col = lax.broadcasted_iota(jnp.int32, (height, LANES), 1)
    hit = (row >= 0) & (col == lax.rem(row + 16, RIM) + LANES - RIM)
    pick = jnp.where(hit, 1.0, 0.0).astype(bf16)
    which = lax.broadcasted_iota(jnp.int32, (height, width), 0) - (rows - base)
    for d in range(count):
        fetch(d).wait()
        place(d).start()
        end = held[d, base:rows, :].astype(f32)
        end = jnp.concatenate([end, jnp.zeros((height - end.shape[0], width), f32)], axis=0)
        if d:
            window(d).wait()
            rims = lax.dot_general(pick, windows[d], NT, preferred_element_type=f32)
            for j in range(-(-rows // width)):
                part = rims[:, j * width : min((j + 1) * width, rows)]
                if part.shape[1] < width:
                    fill = jnp.zeros((height, width - part.shape[1]), f32)
                    part = jnp.concatenate([part, fill], axis=1)
                end = jnp.where((which >= RIM * j) & (which < RIM * (j + 1)), part, end)
        ends[d] = end.astype(bf16)
        place_end(d).start()
    for d in range(count):
        place(d).wait()
        place_end(d).wait()


def cut_first(projected, count, width):
    rows = projected.shape[0]
    base, height = rim_rows(rows, width)
    sems = pltpu.SemaphoreType.DMA((count,))
    anywhere = pl.BlockSpec(memory_space=pl.ANY)
    return pl.pallas_call(
        first_kernel,
        in_specs=[anywhere],
        out_specs=anywhere,
        out_shape=pltpu.HBM((count, base + height, width), bf16),
        scratch_shapes=[
            pltpu.VMEM((count, rows, width), bf16),
            pltpu.VMEM((count, rows, LANES), bf16),
            pltpu.VMEM((count, height, width), bf16),
            sems,
            sems,
            sems,
            sems,
        ],
        compiler_params=params(),
        name="cut_first",
    )(*in_hbm(projected))


def staged(moves, held, in_sems, out_sems):
    for i, (source, _) in enumerate(moves):
        pltpu.make_async_copy(source, held.at[i], in_sems.at[i]).start()
    for i, (source, target) in enumerate(moves):
        pltpu.make_async_copy(source, held.at[i], in_sems.at[i]).wait()
        pltpu.make_async_copy(held.at[i], target, out_sems.at[i]).start()
    for i, (_, target) in enumerate(moves):
        pltpu.make_async_copy(held.at[i], target, out_sems.at[i]).wait()


def staging(count, rows):
    sems = pltpu.SemaphoreType.DMA((count,))
    return [pltpu.VMEM((count, rows, BLOCK), bf16), sems, sems]


def cut_kernel(low, count, src, *refs):
    dst = refs[-4]
    tokens = src.shape[1] // count
    moves = []
    for d in range(count):
        at = d * tokens + low
        moves.append((src.at[:, at : at + BLOCK], dst.at[d]))
    staged(moves, *refs[-3:])


def cut_block(projected, count, low, after):
    rows = projected.shape[0]
    args = in_hbm(projected, *after)
    anywhere = pl.BlockSpec(memory_space=pl.ANY)
    return pl.pallas_call(
        functools.partial(cut_kernel, low, count),
        in_specs=[anywhere] * len(args),
        out_specs=anywhere,
        out_shape=pltpu.HBM((count, rows, BLOCK), bf16),
        scratch_shapes=staging(count, rows),
        compiler_params=params(),
        name="cut_block",
    )(*args)


def pairs_kernel(low, count, me_ref, src, *refs):
    own, near, *far = refs[-(count // 2 + 4) : -3]
    tokens = src.shape[1] // count
    me = me_ref[0]
    targets = [own, near]
    for pair in far:
        targets += [pair.at[:, :BLOCK], pair.at[:, BLOCK:]]
    moves = []
    for k, target in enumerate(targets):
        at = pl.multiple_of((me ^ k) * tokens + low, LANES)
        moves.append((src.at[:, pl.ds(at, BLOCK)], target))
    staged(moves[2:] + moves[:2], *refs[-3:])


def cut_pairs(projected, me, count, low, after):
    rows = projected.shape[0]
    anywhere = pl.BlockSpec(memory_space=pl.ANY)
    one, two = pltpu.HBM((rows, BLOCK), bf16), pltpu.HBM((rows, 2 * BLOCK), bf16)
    return pl.pallas_call(
        functools.partial(pairs_kernel, low, count),
        in_specs=[pl.BlockSpec(memory_space=pltpu.SMEM)] + [anywhere] * (1 + len(after)),
        out_specs=[anywhere] * (count // 2 + 1),
        out_shape=[one, one] + [two] * (count // 2 - 1),
        scratch_shapes=staging(count, rows),
        compiler_params=params(),
        name="cut_pairs",
    )(me, *in_hbm(projected, *after))


def forward_kernel(count, *refs):
    dst = refs[-4]
    moves = [
        (refs[j].at[:, BLOCK:], dst.at[:, j * BLOCK : (j + 1) * BLOCK])
        for j in range(count // 2 - 1)
    ]
    staged(moves, *refs[-3:])


def forward(pairs, after):
    count = 2 * len(pairs) + 2
    rows = pairs[0].shape[0]
    anywhere = pl.BlockSpec(memory_space=pl.ANY)
    return pl.pallas_call(
        functools.partial(forward_kernel, count),
        in_specs=[anywhere] * (len(pairs) + len(after)),
        out_specs=anywhere,
        out_shape=pltpu.HBM((rows, len(pairs) * BLOCK), bf16),
        scratch_shapes=staging(len(pairs), rows),
        compiler_params=params(),
        name="forward",
    )(*pairs, *in_hbm(*after))


def join_kernel(count, me_ref, own, near, *refs):
    others = count // 2 - 1
    pairs, passed, dst = refs[:others], refs[others], refs[-4]
    me = me_ref[0]
    sources = [own, near]
    for j in range(others):
        sources += [pairs[j].at[:, :BLOCK], passed.at[:, j * BLOCK : (j + 1) * BLOCK]]
    staged([(source, dst.at[me ^ k]) for k, source in enumerate(sources)], *refs[-3:])


def join(me, own, near, pairs, passed, after):
    count = 2 * len(pairs) + 2
    rows = own.shape[0]
    anywhere = pl.BlockSpec(memory_space=pl.ANY)
    args = [own, near, *pairs, passed, *in_hbm(*after)]
    return pl.pallas_call(
        functools.partial(join_kernel, count),
        in_specs=[pl.BlockSpec(memory_space=pltpu.SMEM)] + [anywhere] * len(args),
        out_specs=anywhere,
        out_shape=pltpu.HBM((count, rows, BLOCK), bf16),
        scratch_shapes=staging(count, rows),
        compiler_params=params(),
        name="join",
    )(me, *args)


def gather_rows(recv, prev, first, raw, rows, low, high, ahead=True, only=None):
    for s in range(recv.shape[0]):
        a = max(low - s * rows, 0) // 16 * 16
        b = min(-(-(high - s * rows) // 16) * 16, rows)
        if b <= a:
            continue
        at = s * rows + a
        raw[at : at + b - a, LANES:] = recv[s, a:b, :].astype(f32)
        if not ahead:
            continue
        if not first:
            raw[at : at + b - a, :LANES] = prev[s if only is None else 0, a:b, :].astype(f32)
            continue
        width = prev.shape[2]
        base, height = rim_rows(rows, width)
        rims = prev[s if only is None else 0, :height, :].astype(f32)
        tall = jnp.concatenate([jnp.zeros((LANES - height, width), f32), rims], axis=0)
        for j in range(-(-rows // width)):
            c, d = max(a, j * width), min(b, (j + 1) * width)
            if d <= c:
                continue
            shift = height - RIM - (rows - base) - RIM * j
            moved = (pltpu.roll(tall, shift, 0) if shift else tall).T
            raw[s * rows + c : s * rows + d, :LANES] = moved[c - j * width : d - j * width]


def band():
    row = lax.broadcasted_iota(jnp.int32, (2 * LANES, 3 * LANES), 0)
    col = lax.broadcasted_iota(jnp.int32, (2 * LANES, 3 * LANES), 1)
    tap = col // LANES
    return jnp.where(row == col - tap * LANES + LANES - 3 + tap, 1.0, 0.0).astype(bf16)


def shift_rows(raw, low, shifted, at):
    low[...] = raw[at : at + low.shape[0], :].astype(bf16)
    picks = band()
    for i in range(BLOCK // LANES):
        window = low[:, i * LANES : (i + 2) * LANES]
        shifted[i] = jnp.dot(window, picks, preferred_element_type=f32)


def conv_tile(raw, shifted, w, at, r):
    rows = slice(r, r + HEAD_DIM)
    taps = [jnp.broadcast_to(w[0, rows, k : k + 1], (HEAD_DIM, LANES)) for k in range(4)]
    parts = []
    for i in range(BLOCK // LANES):
        summed = None
        for k in range(3):
            part = taps[k] * shifted[i, rows, k * LANES : (k + 1) * LANES]
            summed = part if summed is None else summed + part
        own = raw[at + r : at + r + HEAD_DIM, (i + 1) * LANES : (i + 2) * LANES]
        parts.append(silu(summed + taps[3] * own).astype(bf16))
    return jnp.concatenate(parts, axis=1)


def state_kernel(dims, first, last, recv, *refs):
    spg, rows, heads, span, piece_heads = dims
    prev, refs = refs[0], refs[1:]
    w, bias, a_log, state_in, lead_in = refs[:5]
    xact, bmap, run_out, dt_out, cum_out, state_out, lead_out = refs[-11:-4]
    raw, xw, low, shifted = refs[-4:]
    steps = 2 * span + 2 * STATE_WIDTH

    gather_rows(recv, prev, first, raw, rows, steps, steps + heads, False)
    gather_rows(recv, prev, first, raw, rows, span, 2 * span + STATE_WIDTH)
    dt = softplus(raw[steps : steps + heads, LANES:] + bias[0])
    log_decay = -jnp.exp(a_log[0]) * dt
    lane = lax.broadcasted_iota(jnp.int32, (heads, BLOCK), 1)
    run = log_decay
    shift = 1
    while shift < BLOCK:
        run = run + jnp.where(lane >= shift, pltpu.roll(run, shift, 1), 0.0)
        shift *= 2
    final = run[:, BLOCK - 1 :]
    scale = jnp.exp(final - run) * dt
    cum = run + lead_in[0][:, :1]
    run_out[0] = run
    dt_out[0] = dt
    cum_out[0] = cum
    lead = jnp.broadcast_to(cum[:, BLOCK - 1 :], (heads, LANES))
    lead_out[0] = lead
    keep = jnp.broadcast_to(jnp.exp(final), (heads, LANES))

    shift_rows(raw, low, shifted, span)
    for r in range(0, STATE_WIDTH, HEAD_DIM):
        bmap[0, r : r + HEAD_DIM, :] = conv_tile(raw, shifted, w, span, span + r)
    for h in range(heads):
        r = h * HEAD_DIM
        tile = conv_tile(raw, shifted, w, span, r)
        xact[0, r : r + HEAD_DIM, :] = tile
        xw[r : r + HEAD_DIM, :] = (tile.astype(f32) * scale[h : h + 1, :]).astype(bf16)
    update = lax.dot_general(xw[...], bmap[0], NT, preferred_element_type=f32)
    for h in range(heads):
        r = h * HEAD_DIM
        new = update[r : r + HEAD_DIM, :]
        if not first:
            new = keep[h : h + 1, :] * state_in[0, r : r + HEAD_DIM, :] + new
        if last:
            at = (h % piece_heads) * HEAD_DIM
            state_out[h // piece_heads, at : at + HEAD_DIM, :] = new.astype(bf16)
        else:
            state_out[0, r : r + HEAD_DIM, :] = new
    if last:
        high, low = split(jnp.exp(lead))
        fill = jnp.zeros((8 - piece_heads, LANES), f32)
        for i in range(heads // piece_heads):
            mine = slice(i * piece_heads, (i + 1) * piece_heads)
            parts = [high[mine].astype(f32), fill, low[mine].astype(f32), fill]
            at = piece_heads * HEAD_DIM
            state_out[i, at : at + 16, :] = jnp.concatenate(parts, axis=0).astype(bf16)


def chunk_specs(got, chunk, dims, only=None):
    spg, rows = dims[:2]
    slabs = spg if only is None else 1

    def ahead(source, shape, row, lane):
        def index(g):
            return (g if only is None else g * spg + only, row, lane)

        return source, pl.BlockSpec((slabs,) + shape, index)

    def lane_of(block):
        first, middle, last = got
        ahead_of = first.shape[2] // BLOCK
        if block < ahead_of:
            return first, block
        return (middle if block == ahead_of else last), 0

    source, at = lane_of(chunk)
    block = pl.BlockSpec((spg, source.shape[1], BLOCK), lambda g: (g, 0, at))
    if chunk == 0:
        width = source.shape[2]
        prev, prev_spec = ahead(source, (16, width), rim_rows(rows, width)[0] // 16, 0)
    else:
        prev, place = lane_of(chunk - 1)
        lane = (place + 1) * (BLOCK // LANES) - 1
        prev, prev_spec = ahead(prev, (prev.shape[1], LANES), 0, lane)
    return [source, prev], [block, prev_spec]


def state_chunk(chunk, chunks, got, w, bias, a_log, state, lead, before, dims):
    spg, rows, heads, span, piece_heads = dims
    groups = w.shape[0]
    last = chunk == chunks - 1
    if last:
        packed = piece_heads * HEAD_DIM + 16
        state_shape = pltpu.HBM((groups * spg, packed, STATE_WIDTH), bf16)
        state_spec = pl.BlockSpec((spg, packed, STATE_WIDTH), lambda g: (g, 0, 0))
    else:
        state_shape = pltpu.HBM((groups, span, STATE_WIDTH), f32)
        state_spec = per_group(span, STATE_WIDTH)

    def out(dtype, *shape):
        return pltpu.HBM((groups,) + shape, dtype)

    args, specs = chunk_specs(got, chunk, dims)
    args[1:] = in_hbm(args[1])
    args[:1] = in_vmem(args[0]) if last else in_hbm(args[0])
    after = in_hbm(*before)
    return pl.pallas_call(
        functools.partial(state_kernel, dims, chunk == 0, last),
        grid=(groups,),
        in_specs=specs
        + [
            per_group(span + STATE_WIDTH, 4),
            per_group(heads, 1),
            per_group(heads, 1),
            per_group(span, STATE_WIDTH),
            per_group(heads, LANES),
        ]
        + [pl.BlockSpec(memory_space=pl.ANY)] * len(after),
        out_specs=[
            per_group(span, BLOCK),
            per_group(STATE_WIDTH, BLOCK),
            per_group(heads, BLOCK),
            per_group(heads, BLOCK),
            per_group(heads, BLOCK),
            state_spec,
            per_group(heads, LANES),
        ],
        out_shape=[
            out(bf16, span, BLOCK),
            out(bf16, STATE_WIDTH, BLOCK),
            out(f32, heads, BLOCK),
            out(f32, heads, BLOCK),
            out(f32, heads, BLOCK),
            state_shape,
            out(f32, heads, LANES),
        ],
        scratch_shapes=[
            pltpu.VMEM((rows * spg, LANES + BLOCK), f32),
            pltpu.VMEM((span, BLOCK), bf16),
            pltpu.VMEM((span + STATE_WIDTH, LANES + BLOCK), bf16),
            pltpu.VMEM((BLOCK // LANES, span + STATE_WIDTH, 3 * LANES), f32),
        ],
        compiler_params=params(48 if last else 60),
        cost_estimate=pl.CostEstimate(flops=4 * 10**9, bytes_accessed=10**7, transcendentals=10**6),
        name="state_chunk",
    )(*args, *in_hbm(w, bias, a_log, state, lead), *after)


def split(v):
    high = v.astype(bf16)
    return high, (v - high.astype(f32)).astype(bf16)


def block_kernel(dims, first, recv, *refs):
    spg, rows, heads, span, piece_heads = dims
    prev, refs = refs[0], refs[1:]
    w, xact, bmap, run_ref, dt_ref, cum_ref, state, skip = refs[:8]
    mixed, passed, c_out, token, raw, low, shifted = refs[-7:]
    at_c = 2 * span + STATE_WIDTH
    gather_rows(recv, prev, first, raw, rows, at_c, at_c + STATE_WIDTH, True, at_c // rows)
    gather_rows(recv, prev, first, raw, rows, 0, span, False)
    token[0] = cum_ref[0, :8, :LANES]
    shift_rows(raw, low, shifted, at_c)
    c = [conv_tile(raw, shifted, w, at_c, r) for r in range(0, STATE_WIDTH, HEAD_DIM)]
    c = jnp.concatenate(c, axis=0)
    b_rows = bmap[0].astype(f32).T.astype(bf16)
    scores = jnp.dot(b_rows, c, preferred_element_type=f32)
    src = lax.broadcasted_iota(jnp.int32, (HALF, HALF), 0)
    dst = lax.broadcasted_iota(jnp.int32, (HALF, HALF), 1)
    causal = src <= dst
    s00 = jnp.where(causal, scores[:HALF, :HALF], 0.0)
    s01 = scores[:HALF, HALF:]
    s11 = jnp.where(causal, scores[HALF:, HALF:], 0.0)
    r = run_ref[0] * LOG2E
    q = (r - jnp.log(dt_ref[0]) * LOG2E).T
    if not first:
        cc = jnp.concatenate([c, c], axis=0)
        entered = jnp.exp2(r)
    reach = jnp.exp(cum_ref[0])
    c_out[0] = c.astype(f32).T.astype(bf16)
    turned = []
    for h in range(heads):
        at = h * HEAD_DIM
        r0, r1 = r[h : h + 1, :HALF], r[h : h + 1, HALF:]
        q0, q1 = q[:HALF, h : h + 1], q[HALF:, h : h + 1]
        w00 = (s00 * jnp.exp2(jnp.minimum(r0 - q0, CAP))).astype(bf16)
        w01 = (s01 * jnp.exp2(r1 - q0)).astype(bf16)
        w11 = (s11 * jnp.exp2(jnp.minimum(r1 - q1, CAP))).astype(bf16)
        x = xact[0, at : at + HEAD_DIM, :]
        y0 = jnp.dot(x[:, :HALF], w00, preferred_element_type=f32)
        y1 = jnp.dot(x, jnp.concatenate([w01, w11], axis=0), preferred_element_type=f32)
        y = jnp.concatenate([y0, y1], axis=1) + skip[0, h : h + 1, :] * x.astype(f32)
        if not first:
            if at % WIDE == 0:
                both = jnp.concatenate(split(state[0, at : at + WIDE, :]), axis=1)
                carried = jnp.dot(both, cc, preferred_element_type=f32)
            y = y + entered[h : h + 1, :] * carried[at % WIDE : at % WIDE + HEAD_DIM, :]
        gate = silu(raw[at : at + HEAD_DIM, LANES:])
        turned.append((y * gate, gate * reach[h : h + 1, :]))
        if len(turned) * HEAD_DIM == LANES:
            lanes = slice(at + HEAD_DIM - LANES, at + HEAD_DIM)
            mixed[0, :, lanes] = jnp.concatenate([pair[0] for pair in turned], axis=0).T
            wide = jnp.concatenate([pair[1] for pair in turned], axis=0).T
            passed[0, :, lanes] = wide.astype(bf16)
            turned = []


def block_chunk(
    chunk, chunks, got, w, xact, bmap, run, dt, cum, state, skip, after, dims
):
    spg, rows, heads, span, piece_heads = dims
    groups = w.shape[0]

    at_c = 2 * span + STATE_WIDTH
    one = at_c // rows
    assert (at_c + STATE_WIDTH - 1) // rows == one
    args, specs = chunk_specs(got, chunk, dims, one)
    args = in_hbm(*args)
    args += in_hbm(w, xact, bmap, run, dt, cum, state, skip)
    specs += [
        pl.BlockSpec((1, STATE_WIDTH, 4), lambda g: (g, span // STATE_WIDTH + 1, 0)),
        per_group(span, BLOCK),
        per_group(STATE_WIDTH, BLOCK),
        per_group(heads, BLOCK),
        per_group(heads, BLOCK),
        per_group(heads, BLOCK),
        per_group(span, STATE_WIDTH),
        per_group(heads, 1),
    ]
    args += in_vmem(*after)
    specs += [pl.BlockSpec(memory_space=pl.ANY)] * len(after)

    def out(dtype, *shape):
        return pltpu.HBM((groups,) + shape, dtype)

    return pl.pallas_call(
        functools.partial(block_kernel, dims, chunk == 0),
        grid=(groups,),
        in_specs=specs,
        out_specs=[
            per_group(BLOCK, span),
            per_group(BLOCK, span),
            per_group(BLOCK, STATE_WIDTH),
            per_group(8, LANES),
        ],
        out_shape=[
            out(f32, BLOCK, span),
            out(bf16, BLOCK, span),
            out(bf16, BLOCK, STATE_WIDTH),
            out(f32, 8, LANES),
        ],
        scratch_shapes=[
            pltpu.VMEM((rows * spg, LANES + BLOCK), f32),
            pltpu.VMEM((STATE_WIDTH, LANES + BLOCK), bf16),
            pltpu.VMEM((BLOCK // LANES, STATE_WIDTH, 3 * LANES), f32),
        ],
        compiler_params=params(),
        cost_estimate=pl.CostEstimate(flops=4 * 10**9, bytes_accessed=10**7, transcendentals=10**6),
        name="block_chunk",
    )(*args)


def relay_kernel(piece_heads, src, token, dst):
    rows = piece_heads * HEAD_DIM
    held = jnp.zeros((rows, STATE_WIDTH), f32)
    for d in range(src.shape[0]):
        dst[d] = held.T.astype(bf16)
        both = src[d, rows:, :].astype(f32)
        decay = both[:8] + both[8:]
        spread = [
            jnp.broadcast_to(decay[h : h + 1, :], (HEAD_DIM, STATE_WIDTH))
            for h in range(piece_heads)
        ]
        held = jnp.concatenate(spread, axis=0) * held + src[d, :rows, :].astype(f32)


def relay(packed, token, piece_heads):
    count = packed.shape[0]
    rows = piece_heads * HEAD_DIM
    return pl.pallas_call(
        functools.partial(relay_kernel, piece_heads),
        in_specs=[pl.BlockSpec(memory_space=pltpu.VMEM), pl.BlockSpec(memory_space=pl.ANY)],
        out_shape=pltpu.VMEM((count, STATE_WIDTH, rows), bf16),
        compiler_params=params(16),
        name="relay",
    )(packed, *in_hbm(token))


def final_kernel(chunks, groups, *refs):
    mixed, passed, maps = (refs[i * chunks : (i + 1) * chunks] for i in range(3))
    state_src, gain_src, out = refs[3 * chunks : 3 * chunks + 3]
    held, passed_held, map_held, state, gain, kept, done = refs[3 * chunks + 3 : -3]
    sems, few_sems, out_sems = refs[-3:]
    span = kept.shape[1]
    piece = state.shape[2]
    spg = state.shape[0] // groups
    half = BLOCK // 2
    steps = [(g, c) for g in range(groups) for c in range(chunks)]

    def loads(i):
        g, c = steps[i]
        moves = [
            (maps[c].at[g], map_held.at[i]),
            (mixed[c].at[g], held.at[i]),
            (passed[c].at[g], passed_held.at[i]),
        ]
        return [pltpu.make_async_copy(a, b, sems.at[i, j]) for j, (a, b) in enumerate(moves)]

    def store(i):
        g, c = steps[i]
        return pltpu.make_async_copy(
            done.at[i % 2],
            out.at[c * BLOCK : (c + 1) * BLOCK, g * span : (g + 1) * span],
            out_sems.at[i % 2],
        )

    few = [
        pltpu.make_async_copy(state_src, state, few_sems.at[0]),
        pltpu.make_async_copy(gain_src, gain, few_sems.at[1]),
    ]
    for move in few:
        move.start()
    for i in range(len(steps)):
        for move in loads(i):
            move.start()
    for move in few:
        move.wait()
    for i, (g, c) in enumerate(steps):
        for move in loads(i):
            move.wait()
        if i >= 2:
            store(i - 2).wait()
        for q in range(0, BLOCK, half):
            rows = slice(q, q + half)
            total = jnp.zeros((half, LANES), f32)
            for j in range(spg):
                piece_lanes = slice(j * piece, (j + 1) * piece)
                carried = jnp.dot(
                    map_held[i, rows, :], state[g * spg + j], preferred_element_type=f32
                )
                scale = passed_held[i, rows, piece_lanes].astype(f32)
                v = held[i, rows, piece_lanes] + scale * carried
                kept[rows, piece_lanes] = v
                for at in range(0, piece, LANES):
                    t = v[:, at : at + LANES]
                    if piece < LANES:
                        t = jnp.concatenate([t, jnp.zeros((half, LANES - piece), f32)], axis=1)
                    total = total + t * t
            mean = jnp.sum(total, axis=1, keepdims=True) * (1.0 / span)
            factor = lax.rsqrt(mean + EPSILON)
            for at in range(0, span, LANES):
                lanes = slice(at, at + LANES)
                scaled = kept[rows, lanes] * factor * gain[g, :, lanes]
                done[i % 2, rows, lanes] = scaled.astype(bf16)
        store(i).start()
    for i in range(max(len(steps) - 2, 0), len(steps)):
        store(i).wait()


def finish(mixed, passed, maps, state, gain):
    chunks = len(mixed)
    groups, _, span = mixed[0].shape
    steps = groups * chunks
    anywhere = pl.BlockSpec(memory_space=pl.ANY)
    return pl.pallas_call(
        functools.partial(final_kernel, chunks, groups),
        in_specs=[anywhere] * (3 * chunks + 2),
        out_specs=anywhere,
        out_shape=jax.ShapeDtypeStruct((chunks * BLOCK, groups * span), bf16),
        scratch_shapes=[
            pltpu.VMEM((steps, BLOCK, span), f32),
            pltpu.VMEM((steps, BLOCK, span), bf16),
            pltpu.VMEM((steps, BLOCK, STATE_WIDTH), bf16),
            pltpu.VMEM(state.shape, bf16),
            pltpu.VMEM(gain.shape, f32),
            pltpu.VMEM((BLOCK, span), f32),
            pltpu.VMEM((2, BLOCK, span), bf16),
            pltpu.SemaphoreType.DMA((steps, 3)),
            pltpu.SemaphoreType.DMA((2,)),
            pltpu.SemaphoreType.DMA((2,)),
        ],
        compiler_params=params(40),
        name="finish",
    )(*in_hbm(*mixed, *passed, *maps), state, gain)


def swap(array, k):
    count = lax.axis_size("seq")
    return lax.ppermute(array, "seq", [(i, i ^ k) for i in range(count)])


def exchange(array):
    return lax.all_to_all(array, "seq", split_axis=0, concat_axis=0, tiled=True)


def per_device(projected, conv_weight, dt_bias, a_log, d_skip, norm_gain):
    seq_count = lax.axis_size("seq")
    groups = conv_weight.shape[1]
    heads = dt_bias.shape[0] // groups
    span = heads * HEAD_DIM
    rows, all_tokens = projected.shape
    local_tokens = all_tokens // seq_count
    chunks = local_tokens // BLOCK
    spg = seq_count // groups
    piece_heads = groups * heads // seq_count
    dims = (spg, rows, heads, span, piece_heads)

    w = jnp.transpose(conv_weight, (1, 2, 0))
    bias = dt_bias.reshape(groups, heads, 1)
    rate = a_log.reshape(groups, heads, 1)
    skip = d_skip.reshape(groups, heads, 1)
    gain = norm_gain.reshape(groups, 1, span)
    state = jnp.zeros((groups, span, STATE_WIDTH), f32)
    lead = jnp.zeros((groups, heads, LANES), f32)

    me = lax.axis_index("seq").astype(jnp.int32).reshape(1)
    assert chunks > 2 and seq_count & (seq_count - 1) == 0
    cut = cut_first(projected, seq_count, local_tokens - 2 * BLOCK)
    got = [exchange(cut)]
    own, near, *pairs = cut_pairs(projected, me, seq_count, local_tokens - 2 * BLOCK, [cut])
    near = swap(near, 1)
    pairs = [swap(pair, 2 * j + 2) for j, pair in enumerate(pairs)]
    ready = [own, w, bias, rate, skip, gain, state, lead]
    cut = cut_block(projected, seq_count, local_tokens - BLOCK, ready)
    got += [None, exchange(cut)]

    results, tokens = [], []
    for c in range(chunks):
        before = []
        if c == chunks - 2:
            passed = swap(forward(pairs, [lead, tokens[0]]), 1)
            got[1] = join(me, own, near, pairs, passed, tokens)
        if c == chunks - 1:
            before = tokens[-2:-1]
        xact, bmap, run, dt, cum, new, lead = state_chunk(
            c, chunks, got, w, bias, rate, state, lead, before, dims
        )
        after = []
        if c == chunks - 1:
            entering = relay(exchange(new), tokens[-1], piece_heads)
            after = [entering]
        *result, token = block_chunk(
            c, chunks, got, w, xact, bmap, run, dt, cum, state, skip, after, dims
        )
        results.append(result)
        tokens.append(token)
        state = new
    return finish(*zip(*results), exchange(entering), gain)


def solution(mesh):
    in_specs = (P(("tp", "seq"), None), P(None, "tp", None), P("tp"), P("tp"), P("tp"), P("tp"))
    return jax.shard_map(
        per_device, mesh=mesh, in_specs=in_specs, out_specs=P("seq", "tp"), check_vma=False
    )
```

```python
import functools

import jax
import jax.numpy as jnp
from jax import lax
from jax.experimental import pallas as pl
from jax.experimental.pallas import tpu as pltpu
from jax.sharding import PartitionSpec as P

HEAD_DIM = 64
STATE_WIDTH = 128
BLOCK = 256
LANES = 128
HALF = BLOCK // 2
WIDE = 256
LOG2E = 1.4426950408889634
CAP = 80.0
EPSILON = 1e-05

f32 = jnp.float32
bf16 = jnp.bfloat16
NT = (((1,), (1,)), ((), ()))


def params(mib=60):
    return pltpu.CompilerParams(vmem_limit_bytes=mib * 2**20)


def silu(v):
    half = 0.5 * v
    return half + half * jnp.tanh(half)


def softplus(v):
    e = jnp.exp(-jnp.abs(v))
    u = 1.0 + e
    gap = u - 1.0
    tiny = gap == 0.0
    log_part = jnp.where(tiny, e, jnp.log(u) * (e / jnp.where(tiny, 1.0, gap)))
    return jnp.maximum(v, 0.0) + log_part


def in_hbm(*arrays):
    return [pltpu.with_memory_space_constraint(array, pltpu.HBM) for array in arrays]


def in_vmem(*arrays):
    return [pltpu.with_memory_space_constraint(array, pltpu.VMEM) for array in arrays]


def per_group(*shape):
    return pl.BlockSpec((1,) + shape, lambda g: (g,) + (0,) * len(shape))


RIM = 4


def rim_rows(rows, width):
    base = rows // 16 * 16
    height = -(-(rows - base + RIM * -(-rows // width)) // 8) * 8
    assert height <= 16
    return base, height


def first_kernel(src, dst, held, windows, ends, in_sems, rim_sems, out_sems, end_sems):
    rows, all_tokens = src.shape
    count, _, width = dst.shape
    tokens = all_tokens // count
    base, height = rim_rows(rows, width)

    def fetch(d):
        at = d * tokens
        return pltpu.make_async_copy(src.at[:, at : at + width], held.at[d], in_sems.at[d])

    def window(d):
        at = d * tokens - LANES
        return pltpu.make_async_copy(src.at[:, at : at + LANES], windows.at[d], rim_sems.at[d])

    def place(d):
        return pltpu.make_async_copy(
            held.at[d, :base, :], dst.at[d, :base, :], out_sems.at[d]
        )

    def place_end(d):
        return pltpu.make_async_copy(
            ends.at[d], dst.at[d, base : base + height, :], end_sems.at[d]
        )

    for d in range(count):
        fetch(d).start()
        if d:
            window(d).start()
    row = lax.broadcasted_iota(jnp.int32, (height, LANES), 0) - (rows - base)
    col = lax.broadcasted_iota(jnp.int32, (height, LANES), 1)
    hit = (row >= 0) & (col == lax.rem(row + 16, RIM) + LANES - RIM)
    pick = jnp.where(hit, 1.0, 0.0).astype(bf16)
    which = lax.broadcasted_iota(jnp.int32, (height, width), 0) - (rows - base)
    for d in range(count):
        fetch(d).wait()
        place(d).start()
        end = held[d, base:rows, :].astype(f32)
        end = jnp.concatenate([end, jnp.zeros((height - end.shape[0], width), f32)], axis=0)
        if d:
            window(d).wait()
            rims = lax.dot_general(pick, windows[d], NT, preferred_element_type=f32)
            for j in range(-(-rows // width)):
                part = rims[:, j * width : min((j + 1) * width, rows)]
                if part.shape[1] < width:
                    fill = jnp.zeros((height, width - part.shape[1]), f32)
                    part = jnp.concatenate([part, fill], axis=1)
                end = jnp.where((which >= RIM * j) & (which < RIM * (j + 1)), part, end)
        ends[d] = end.astype(bf16)
        place_end(d).start()
    for d in range(count):
        place(d).wait()
        place_end(d).wait()


def cut_first(projected, count, width):
    rows = projected.shape[0]
    base, height = rim_rows(rows, width)
    sems = pltpu.SemaphoreType.DMA((count,))
    anywhere = pl.BlockSpec(memory_space=pl.ANY)
    return pl.pallas_call(
        first_kernel,
        in_specs=[anywhere],
        out_specs=anywhere,
        out_shape=pltpu.HBM((count, base + height, width), bf16),
        scratch_shapes=[
            pltpu.VMEM((count, rows, width), bf16),
            pltpu.VMEM((count, rows, LANES), bf16),
            pltpu.VMEM((count, height, width), bf16),
            sems,
            sems,
            sems,
            sems,
        ],
        compiler_params=params(),
        name="cut_first",
    )(*in_hbm(projected))


def staged(moves, held, in_sems, out_sems):
    for i, (source, _) in enumerate(moves):
        pltpu.make_async_copy(source, held.at[i], in_sems.at[i]).start()
    for i, (source, target) in enumerate(moves):
        pltpu.make_async_copy(source, held.at[i], in_sems.at[i]).wait()
        pltpu.make_async_copy(held.at[i], target, out_sems.at[i]).start()
    for i, (_, target) in enumerate(moves):
        pltpu.make_async_copy(held.at[i], target, out_sems.at[i]).wait()


def staging(count, rows):
    sems = pltpu.SemaphoreType.DMA((count,))
    return [pltpu.VMEM((count, rows, BLOCK), bf16), sems, sems]


def cut_kernel(low, count, src, *refs):
    dst = refs[-4]
    tokens = src.shape[1] // count
    moves = []
    for d in range(count):
        at = d * tokens + low
        moves.append((src.at[:, at : at + BLOCK], dst.at[d]))
    staged(moves, *refs[-3:])


def cut_block(projected, count, low, after):
    rows = projected.shape[0]
    args = in_hbm(projected, *after)
    anywhere = pl.BlockSpec(memory_space=pl.ANY)
    return pl.pallas_call(
        functools.partial(cut_kernel, low, count),
        in_specs=[anywhere] * len(args),
        out_specs=anywhere,
        out_shape=pltpu.HBM((count, rows, BLOCK), bf16),
        scratch_shapes=staging(count, rows),
        compiler_params=params(),
        name="cut_block",
    )(*args)


def pairs_kernel(low, count, me_ref, src, *refs):
    own, near, *far = refs[-(count // 2 + 4) : -3]
    tokens = src.shape[1] // count
    me = me_ref[0]
    targets = [own, near]
    for pair in far:
        targets += [pair.at[:, :BLOCK], pair.at[:, BLOCK:]]
    moves = []
    for k, target in enumerate(targets):
        at = pl.multiple_of((me ^ k) * tokens + low, LANES)
        moves.append((src.at[:, pl.ds(at, BLOCK)], target))
    staged(moves[2:] + moves[:2], *refs[-3:])


def cut_pairs(projected, me, count, low, after):
    rows = projected.shape[0]
    anywhere = pl.BlockSpec(memory_space=pl.ANY)
    one, two = pltpu.HBM((rows, BLOCK), bf16), pltpu.HBM((rows, 2 * BLOCK), bf16)
    return pl.pallas_call(
        functools.partial(pairs_kernel, low, count),
        in_specs=[pl.BlockSpec(memory_space=pltpu.SMEM)] + [anywhere] * (1 + len(after)),
        out_specs=[anywhere] * (count // 2 + 1),
        out_shape=[one, one] + [two] * (count // 2 - 1),
        scratch_shapes=staging(count, rows),
        compiler_params=params(),
        name="cut_pairs",
    )(me, *in_hbm(projected, *after))


def forward_kernel(count, *refs):
    dst = refs[-4]
    moves = [
        (refs[j].at[:, BLOCK:], dst.at[:, j * BLOCK : (j + 1) * BLOCK])
        for j in range(count // 2 - 1)
    ]
    staged(moves, *refs[-3:])


def forward(pairs, after):
    count = 2 * len(pairs) + 2
    rows = pairs[0].shape[0]
    anywhere = pl.BlockSpec(memory_space=pl.ANY)
    return pl.pallas_call(
        functools.partial(forward_kernel, count),
        in_specs=[anywhere] * (len(pairs) + len(after)),
        out_specs=anywhere,
        out_shape=pltpu.HBM((rows, len(pairs) * BLOCK), bf16),
        scratch_shapes=staging(len(pairs), rows),
        compiler_params=params(),
        name="forward",
    )(*pairs, *in_hbm(*after))


def join_kernel(count, me_ref, own, near, *refs):
    others = count // 2 - 1
    pairs, passed, dst = refs[:others], refs[others], refs[-4]
    me = me_ref[0]
    sources = [own, near]
    for j in range(others):
        sources += [pairs[j].at[:, :BLOCK], passed.at[:, j * BLOCK : (j + 1) * BLOCK]]
    staged([(source, dst.at[me ^ k]) for k, source in enumerate(sources)], *refs[-3:])


def join(me, own, near, pairs, passed, after):
    count = 2 * len(pairs) + 2
    rows = own.shape[0]
    anywhere = pl.BlockSpec(memory_space=pl.ANY)
    args = [own, near, *pairs, passed, *in_hbm(*after)]
    return pl.pallas_call(
        functools.partial(join_kernel, count),
        in_specs=[pl.BlockSpec(memory_space=pltpu.SMEM)] + [anywhere] * len(args),
        out_specs=anywhere,
        out_shape=pltpu.HBM((count, rows, BLOCK), bf16),
        scratch_shapes=staging(count, rows),
        compiler_params=params(),
        name="join",
    )(me, *args)


def gather_rows(recv, prev, first, raw, rows, low, high, ahead=True, only=None):
    for s in range(recv.shape[0]):
        a = max(low - s * rows, 0) // 16 * 16
        b = min(-(-(high - s * rows) // 16) * 16, rows)
        if b <= a:
            continue
        at = s * rows + a
        raw[at : at + b - a, LANES:] = recv[s, a:b, :].astype(f32)
        if not ahead:
            continue
        if not first:
            raw[at : at + b - a, :LANES] = prev[s if only is None else 0, a:b, :].astype(f32)
            continue
        width = prev.shape[2]
        base, height = rim_rows(rows, width)
        rims = prev[s if only is None else 0, :height, :].astype(f32)
        tall = jnp.concatenate([jnp.zeros((LANES - height, width), f32), rims], axis=0)
        for j in range(-(-rows // width)):
            c, d = max(a, j * width), min(b, (j + 1) * width)
            if d <= c:
                continue
            shift = height - RIM - (rows - base) - RIM * j
            moved = (pltpu.roll(tall, shift, 0) if shift else tall).T
            raw[s * rows + c : s * rows + d, :LANES] = moved[c - j * width : d - j * width]


def band():
    row = lax.broadcasted_iota(jnp.int32, (2 * LANES, 3 * LANES), 0)
    col = lax.broadcasted_iota(jnp.int32, (2 * LANES, 3 * LANES), 1)
    tap = col // LANES
    return jnp.where(row == col - tap * LANES + LANES - 3 + tap, 1.0, 0.0).astype(bf16)


def shift_rows(raw, low, shifted, at):
    low[...] = raw[at : at + low.shape[0], :].astype(bf16)
    picks = band()
    for i in range(BLOCK // LANES):
        window = low[:, i * LANES : (i + 2) * LANES]
        shifted[i] = jnp.dot(window, picks, preferred_element_type=f32)


def conv_tile(raw, shifted, w, at, r):
    rows = slice(r, r + HEAD_DIM)
    taps = [jnp.broadcast_to(w[0, rows, k : k + 1], (HEAD_DIM, LANES)) for k in range(4)]
    parts = []
    for i in range(BLOCK // LANES):
        summed = None
        for k in range(3):
            part = taps[k] * shifted[i, rows, k * LANES : (k + 1) * LANES]
            summed = part if summed is None else summed + part
        own = raw[at + r : at + r + HEAD_DIM, (i + 1) * LANES : (i + 2) * LANES]
        parts.append(silu(summed + taps[3] * own).astype(bf16))
    return jnp.concatenate(parts, axis=1)


def state_kernel(dims, first, last, recv, *refs):
    spg, rows, heads, span, piece_heads = dims
    prev, refs = refs[0], refs[1:]
    w, bias, a_log, state_in, lead_in = refs[:5]
    xact, bmap, run_out, dt_out, cum_out, state_out, lead_out = refs[-11:-4]
    raw, xw, low, shifted = refs[-4:]
    steps = 2 * span + 2 * STATE_WIDTH

    gather_rows(recv, prev, first, raw, rows, steps, steps + heads, False)
    gather_rows(recv, prev, first, raw, rows, span, 2 * span + STATE_WIDTH)
    dt = softplus(raw[steps : steps + heads, LANES:] + bias[0])
    log_decay = -jnp.exp(a_log[0]) * dt
    lane = lax.broadcasted_iota(jnp.int32, (heads, BLOCK), 1)
    run = log_decay
    shift = 1
    while shift < BLOCK:
        run = run + jnp.where(lane >= shift, pltpu.roll(run, shift, 1), 0.0)
        shift *= 2
    final = run[:, BLOCK - 1 :]
    scale = jnp.exp(final - run) * dt
    cum = run + lead_in[0][:, :1]
    run_out[0] = run
    dt_out[0] = dt
    cum_out[0] = cum
    lead = jnp.broadcast_to(cum[:, BLOCK - 1 :], (heads, LANES))
    lead_out[0] = lead
    keep = jnp.broadcast_to(jnp.exp(final), (heads, LANES))

    shift_rows(raw, low, shifted, span)
    for r in range(0, STATE_WIDTH, HEAD_DIM):
        bmap[0, r : r + HEAD_DIM, :] = conv_tile(raw, shifted, w, span, span + r)
    for h in range(heads):
        r = h * HEAD_DIM
        tile = conv_tile(raw, shifted, w, span, r)
        xact[0, r : r + HEAD_DIM, :] = tile
        xw[r : r + HEAD_DIM, :] = (tile.astype(f32) * scale[h : h + 1, :]).astype(bf16)
    update = lax.dot_general(xw[...], bmap[0], NT, preferred_element_type=f32)
    for h in range(heads):
        r = h * HEAD_DIM
        new = update[r : r + HEAD_DIM, :]
        if not first:
            new = keep[h : h + 1, :] * state_in[0, r : r + HEAD_DIM, :] + new
        if last:
            at = (h % piece_heads) * HEAD_DIM
            state_out[h // piece_heads, at : at + HEAD_DIM, :] = new.astype(bf16)
        else:
            state_out[0, r : r + HEAD_DIM, :] = new
    if last:
        high, low = split(jnp.exp(lead))
        fill = jnp.zeros((8 - piece_heads, LANES), f32)
        for i in range(heads // piece_heads):
            mine = slice(i * piece_heads, (i + 1) * piece_heads)
            parts = [high[mine].astype(f32), fill, low[mine].astype(f32), fill]
            at = piece_heads * HEAD_DIM
            state_out[i, at : at + 16, :] = jnp.concatenate(parts, axis=0).astype(bf16)


def chunk_specs(got, chunk, dims, only=None):
    spg, rows = dims[:2]
    slabs = spg if only is None else 1

    def ahead(source, shape, row, lane):
        def index(g):
            return (g if only is None else g * spg + only, row, lane)

        return source, pl.BlockSpec((slabs,) + shape, index)

    def lane_of(block):
        first, middle, last = got
        ahead_of = first.shape[2] // BLOCK
        if block < ahead_of:
            return first, block
        return (middle if block == ahead_of else last), 0

    source, at = lane_of(chunk)
    block = pl.BlockSpec((spg, source.shape[1], BLOCK), lambda g: (g, 0, at))
    if chunk == 0:
        width = source.shape[2]
        prev, prev_spec = ahead(source, (16, width), rim_rows(rows, width)[0] // 16, 0)
    else:
        prev, place = lane_of(chunk - 1)
        lane = (place + 1) * (BLOCK // LANES) - 1
        prev, prev_spec = ahead(prev, (prev.shape[1], LANES), 0, lane)
    return [source, prev], [block, prev_spec]


def state_chunk(chunk, chunks, got, w, bias, a_log, state, lead, before, dims):
    spg, rows, heads, span, piece_heads = dims
    groups = w.shape[0]
    last = chunk == chunks - 1
    if last:
        packed = piece_heads * HEAD_DIM + 16
        state_shape = pltpu.HBM((groups * spg, packed, STATE_WIDTH), bf16)
        state_spec = pl.BlockSpec((spg, packed, STATE_WIDTH), lambda g: (g, 0, 0))
    else:
        state_shape = pltpu.HBM((groups, span, STATE_WIDTH), f32)
        state_spec = per_group(span, STATE_WIDTH)

    def out(dtype, *shape):
        return pltpu.HBM((groups,) + shape, dtype)

    args, specs = chunk_specs(got, chunk, dims)
    args[1:] = in_hbm(args[1])
    args[:1] = in_vmem(args[0]) if last else in_hbm(args[0])
    after = in_hbm(*before)
    return pl.pallas_call(
        functools.partial(state_kernel, dims, chunk == 0, last),
        grid=(groups,),
        in_specs=specs
        + [
            per_group(span + STATE_WIDTH, 4),
            per_group(heads, 1),
            per_group(heads, 1),
            per_group(span, STATE_WIDTH),
            per_group(heads, LANES),
        ]
        + [pl.BlockSpec(memory_space=pl.ANY)] * len(after),
        out_specs=[
            per_group(span, BLOCK),
            per_group(STATE_WIDTH, BLOCK),
            per_group(heads, BLOCK),
            per_group(heads, BLOCK),
            per_group(heads, BLOCK),
            state_spec,
            per_group(heads, LANES),
        ],
        out_shape=[
            out(bf16, span, BLOCK),
            out(bf16, STATE_WIDTH, BLOCK),
            out(f32, heads, BLOCK),
            out(f32, heads, BLOCK),
            out(f32, heads, BLOCK),
            state_shape,
            out(f32, heads, LANES),
        ],
        scratch_shapes=[
            pltpu.VMEM((rows * spg, LANES + BLOCK), f32),
            pltpu.VMEM((span, BLOCK), bf16),
            pltpu.VMEM((span + STATE_WIDTH, LANES + BLOCK), bf16),
            pltpu.VMEM((BLOCK // LANES, span + STATE_WIDTH, 3 * LANES), f32),
        ],
        compiler_params=params(48 if last else 60),
        cost_estimate=pl.CostEstimate(flops=4 * 10**9, bytes_accessed=10**7, transcendentals=10**6),
        name="state_chunk",
    )(*args, *in_hbm(w, bias, a_log, state, lead), *after)


def split(v):
    high = v.astype(bf16)
    return high, (v - high.astype(f32)).astype(bf16)


def block_kernel(dims, first, recv, *refs):
    spg, rows, heads, span, piece_heads = dims
    prev, refs = refs[0], refs[1:]
    w, xact, bmap, run_ref, dt_ref, cum_ref, state, skip = refs[:8]
    mixed, passed, c_out, token, raw, low, shifted = refs[-7:]
    at_c = 2 * span + STATE_WIDTH
    gather_rows(recv, prev, first, raw, rows, at_c, at_c + STATE_WIDTH, True, at_c // rows)
    gather_rows(recv, prev, first, raw, rows, 0, span, False)
    token[0] = cum_ref[0, :8, :LANES]
    shift_rows(raw, low, shifted, at_c)
    c = [conv_tile(raw, shifted, w, at_c, r) for r in range(0, STATE_WIDTH, HEAD_DIM)]
    c = jnp.concatenate(c, axis=0)
    b_rows = bmap[0].astype(f32).T.astype(bf16)
    scores = jnp.dot(b_rows, c, preferred_element_type=f32)
    src = lax.broadcasted_iota(jnp.int32, (HALF, HALF), 0)
    dst = lax.broadcasted_iota(jnp.int32, (HALF, HALF), 1)
    causal = src <= dst
    s00 = jnp.where(causal, scores[:HALF, :HALF], 0.0)
    s01 = scores[:HALF, HALF:]
    s11 = jnp.where(causal, scores[HALF:, HALF:], 0.0)
    r = run_ref[0] * LOG2E
    q = (r - jnp.log(dt_ref[0]) * LOG2E).T
    if not first:
        cc = jnp.concatenate([c, c], axis=0)
        entered = jnp.exp2(r)
    reach = jnp.exp(cum_ref[0])
    c_out[0] = c.astype(f32).T.astype(bf16)
    turned = []
    for h in range(heads):
        at = h * HEAD_DIM
        r0, r1 = r[h : h + 1, :HALF], r[h : h + 1, HALF:]
        q0, q1 = q[:HALF, h : h + 1], q[HALF:, h : h + 1]
        w00 = (s00 * jnp.exp2(jnp.minimum(r0 - q0, CAP))).astype(bf16)
        w01 = (s01 * jnp.exp2(r1 - q0)).astype(bf16)
        w11 = (s11 * jnp.exp2(jnp.minimum(r1 - q1, CAP))).astype(bf16)
        x = xact[0, at : at + HEAD_DIM, :]
        y0 = jnp.dot(x[:, :HALF], w00, preferred_element_type=f32)
        y1 = jnp.dot(x, jnp.concatenate([w01, w11], axis=0), preferred_element_type=f32)
        y = jnp.concatenate([y0, y1], axis=1) + skip[0, h : h + 1, :] * x.astype(f32)
        if not first:
            if at % WIDE == 0:
                both = jnp.concatenate(split(state[0, at : at + WIDE, :]), axis=1)
                carried = jnp.dot(both, cc, preferred_element_type=f32)
            y = y + entered[h : h + 1, :] * carried[at % WIDE : at % WIDE + HEAD_DIM, :]
        gate = silu(raw[at : at + HEAD_DIM, LANES:])
        turned.append((y * gate, gate * reach[h : h + 1, :]))
        if len(turned) * HEAD_DIM == LANES:
            lanes = slice(at + HEAD_DIM - LANES, at + HEAD_DIM)
            mixed[0, :, lanes] = jnp.concatenate([pair[0] for pair in turned], axis=0).T
            wide = jnp.concatenate([pair[1] for pair in turned], axis=0).T
            passed[0, :, lanes] = wide.astype(bf16)
            turned = []


def block_chunk(
    chunk, chunks, got, w, xact, bmap, run, dt, cum, state, skip, after, dims
):
    spg, rows, heads, span, piece_heads = dims
    groups = w.shape[0]

    at_c = 2 * span + STATE_WIDTH
    one = at_c // rows
    assert (at_c + STATE_WIDTH - 1) // rows == one
    args, specs = chunk_specs(got, chunk, dims, one)
    args = in_hbm(*args)
    args += in_hbm(w, xact, bmap, run, dt, cum, state, skip)
    specs += [
        pl.BlockSpec((1, STATE_WIDTH, 4), lambda g: (g, span // STATE_WIDTH + 1, 0)),
        per_group(span, BLOCK),
        per_group(STATE_WIDTH, BLOCK),
        per_group(heads, BLOCK),
        per_group(heads, BLOCK),
        per_group(heads, BLOCK),
        per_group(span, STATE_WIDTH),
        per_group(heads, 1),
    ]
    args += in_vmem(*after)
    specs += [pl.BlockSpec(memory_space=pl.ANY)] * len(after)

    def out(dtype, *shape):
        return pltpu.HBM((groups,) + shape, dtype)

    return pl.pallas_call(
        functools.partial(block_kernel, dims, chunk == 0),
        grid=(groups,),
        in_specs=specs,
        out_specs=[
            per_group(BLOCK, span),
            per_group(BLOCK, span),
            per_group(BLOCK, STATE_WIDTH),
            per_group(8, LANES),
        ],
        out_shape=[
            out(f32, BLOCK, span),
            out(bf16, BLOCK, span),
            out(bf16, BLOCK, STATE_WIDTH),
            out(f32, 8, LANES),
        ],
        scratch_shapes=[
            pltpu.VMEM((rows * spg, LANES + BLOCK), f32),
            pltpu.VMEM((STATE_WIDTH, LANES + BLOCK), bf16),
            pltpu.VMEM((BLOCK // LANES, STATE_WIDTH, 3 * LANES), f32),
        ],
        compiler_params=params(),
        cost_estimate=pl.CostEstimate(flops=4 * 10**9, bytes_accessed=10**7, transcendentals=10**6),
        name="block_chunk",
    )(*args)


def relay_kernel(piece_heads, src, token, dst):
    rows = piece_heads * HEAD_DIM
    held = jnp.zeros((rows, STATE_WIDTH), f32)
    for d in range(src.shape[0]):
        dst[d] = held.T.astype(bf16)
        both = src[d, rows:, :].astype(f32)
        decay = both[:8] + both[8:]
        spread = [
            jnp.broadcast_to(decay[h : h + 1, :], (HEAD_DIM, STATE_WIDTH))
            for h in range(piece_heads)
        ]
        held = jnp.concatenate(spread, axis=0) * held + src[d, :rows, :].astype(f32)


def relay(packed, token, piece_heads):
    count = packed.shape[0]
    rows = piece_heads * HEAD_DIM
    return pl.pallas_call(
        functools.partial(relay_kernel, piece_heads),
        in_specs=[pl.BlockSpec(memory_space=pltpu.VMEM), pl.BlockSpec(memory_space=pl.ANY)],
        out_shape=pltpu.VMEM((count, STATE_WIDTH, rows), bf16),
        compiler_params=params(16),
        name="relay",
    )(packed, *in_hbm(token))


DEEP = 3


def final_kernel(chunks, groups, *refs):
    mixed, passed, maps = (refs[i * chunks : (i + 1) * chunks] for i in range(3))
    state_src, gain_src, out = refs[3 * chunks : 3 * chunks + 3]
    held, passed_held, map_held, state, gain, kept, done = refs[3 * chunks + 3 : -3]
    sems, few_sems, out_sems = refs[-3:]
    span = kept.shape[1]
    piece = state.shape[2]
    spg = state.shape[0] // groups
    half = BLOCK // 2
    steps = [(g, c) for g in range(groups) for c in range(chunks)]

    def loads(i):
        g, c = steps[i]
        moves = [
            (maps[c].at[g], map_held.at[i]),
            (mixed[c].at[g], held.at[i]),
            (passed[c].at[g], passed_held.at[i]),
        ]
        return [pltpu.make_async_copy(a, b, sems.at[i, j]) for j, (a, b) in enumerate(moves)]

    def store(i):
        g, c = steps[i]
        return pltpu.make_async_copy(
            done.at[i],
            out.at[c * BLOCK : (c + 1) * BLOCK, g * span : (g + 1) * span],
            out_sems.at[i],
        )

    few = [
        pltpu.make_async_copy(state_src, state, few_sems.at[0]),
        pltpu.make_async_copy(gain_src, gain, few_sems.at[1]),
    ]
    for move in few:
        move.start()
    for i in range(min(DEEP, len(steps))):
        for move in loads(i):
            move.start()
    for move in few:
        move.wait()
    for i, (g, c) in enumerate(steps):
        for move in loads(i):
            move.wait()
        if i + DEEP < len(steps):
            for move in loads(i + DEEP):
                move.start()
        for q in range(0, BLOCK, half):
            rows = slice(q, q + half)
            total = jnp.zeros((half, LANES), f32)
            for j in range(spg):
                piece_lanes = slice(j * piece, (j + 1) * piece)
                carried = jnp.dot(
                    map_held[i, rows, :], state[g * spg + j], preferred_element_type=f32
                )
                scale = passed_held[i, rows, piece_lanes].astype(f32)
                v = held[i, rows, piece_lanes] + scale * carried
                kept[rows, piece_lanes] = v
                for at in range(0, piece, LANES):
                    t = v[:, at : at + LANES]
                    if piece < LANES:
                        t = jnp.concatenate([t, jnp.zeros((half, LANES - piece), f32)], axis=1)
                    total = total + t * t
            mean = jnp.sum(total, axis=1, keepdims=True) * (1.0 / span)
            factor = lax.rsqrt(mean + EPSILON)
            for at in range(0, span, LANES):
                lanes = slice(at, at + LANES)
                scaled = kept[rows, lanes] * factor * gain[g, :, lanes]
                done[i, rows, lanes] = scaled.astype(bf16)
        store(i).start()
    for i in range(len(steps)):
        store(i).wait()


def finish(mixed, passed, maps, state, gain):
    chunks = len(mixed)
    groups, _, span = mixed[0].shape
    steps = groups * chunks
    anywhere = pl.BlockSpec(memory_space=pl.ANY)
    return pl.pallas_call(
        functools.partial(final_kernel, chunks, groups),
        in_specs=[anywhere] * (3 * chunks + 2),
        out_specs=anywhere,
        out_shape=jax.ShapeDtypeStruct((chunks * BLOCK, groups * span), bf16),
        scratch_shapes=[
            pltpu.VMEM((steps, BLOCK, span), f32),
            pltpu.VMEM((steps, BLOCK, span), bf16),
            pltpu.VMEM((steps, BLOCK, STATE_WIDTH), bf16),
            pltpu.VMEM(state.shape, bf16),
            pltpu.VMEM(gain.shape, f32),
            pltpu.VMEM((BLOCK, span), f32),
            pltpu.VMEM((steps, BLOCK, span), bf16),
            pltpu.SemaphoreType.DMA((steps, 3)),
            pltpu.SemaphoreType.DMA((2,)),
            pltpu.SemaphoreType.DMA((steps,)),
        ],
        compiler_params=params(40),
        name="finish",
    )(*in_hbm(*mixed, *passed, *maps), state, gain)


def swap(array, k):
    count = lax.axis_size("seq")
    return lax.ppermute(array, "seq", [(i, i ^ k) for i in range(count)])


def exchange(array):
    return lax.all_to_all(array, "seq", split_axis=0, concat_axis=0, tiled=True)


def per_device(projected, conv_weight, dt_bias, a_log, d_skip, norm_gain):
    seq_count = lax.axis_size("seq")
    groups = conv_weight.shape[1]
    heads = dt_bias.shape[0] // groups
    span = heads * HEAD_DIM
    rows, all_tokens = projected.shape
    local_tokens = all_tokens // seq_count
    chunks = local_tokens // BLOCK
    spg = seq_count // groups
    piece_heads = groups * heads // seq_count
    dims = (spg, rows, heads, span, piece_heads)

    w = jnp.transpose(conv_weight, (1, 2, 0))
    bias = dt_bias.reshape(groups, heads, 1)
    rate = a_log.reshape(groups, heads, 1)
    skip = d_skip.reshape(groups, heads, 1)
    gain = norm_gain.reshape(groups, 1, span)
    state = jnp.zeros((groups, span, STATE_WIDTH), f32)
    lead = jnp.zeros((groups, heads, LANES), f32)

    me = lax.axis_index("seq").astype(jnp.int32).reshape(1)
    assert chunks > 2 and seq_count & (seq_count - 1) == 0
    cut = cut_first(projected, seq_count, local_tokens - 2 * BLOCK)
    got = [exchange(cut)]
    own, near, *pairs = cut_pairs(projected, me, seq_count, local_tokens - 2 * BLOCK, [cut])
    near = swap(near, 1)
    pairs = [swap(pair, 2 * j + 2) for j, pair in enumerate(pairs)]
    ready = [own, w, bias, rate, skip, gain, state, lead]
    cut = cut_block(projected, seq_count, local_tokens - BLOCK, ready)
    got += [None, exchange(cut)]

    results, tokens = [], []
    for c in range(chunks):
        before = []
        if c == chunks - 2:
            passed = swap(forward(pairs, [lead, tokens[0]]), 1)
            got[1] = join(me, own, near, pairs, passed, tokens)
        if c == chunks - 1:
            before = tokens[-2:-1]
        xact, bmap, run, dt, cum, new, lead = state_chunk(
            c, chunks, got, w, bias, rate, state, lead, before, dims
        )
        after = []
        if c == chunks - 1:
            entering = relay(exchange(new), tokens[-1], piece_heads)
            after = [entering]
        *result, token = block_chunk(
            c, chunks, got, w, xact, bmap, run, dt, cum, state, skip, after, dims
        )
        results.append(result)
        tokens.append(token)
        state = new
    return finish(*zip(*results), exchange(entering), gain)


def solution(mesh):
    in_specs = (P(("tp", "seq"), None), P(None, "tp", None), P("tp"), P("tp"), P("tp"), P("tp"))
    return jax.shard_map(
        per_device, mesh=mesh, in_specs=in_specs, out_specs=P("seq", "tp"), check_vma=False
    )
```
